32 devices in a mesh: fsdp: 8 (over y, x, core), ctx: 4 (over z).
Axes of the slice: x: 2, y: 2, z: 4, core: 2. Of those that a mesh axis runs over, the one named last changes fastest.
Arguments:
- tokens: bfloat16 [8, 1024, 1024], P('fsdp', 'ctx'), may hold values from -6 to 6
- doc_lengths: int32 [8, 4], P('fsdp'), may hold values from 1 to 1021, as said below
- cotangent: bfloat16 [8, 1024, 1024], P('fsdp', 'ctx'), may hold values from -6 to 6
- gains: bfloat16 [2, 2, 1024], P(None, None, 'fsdp'), may hold values from 0.099609375 to 1.8984375
- w_qkv: bfloat16 [2, 1024, 3072], P(None, 'fsdp'), may hold values from -0.1875 to 0.1875
- w_out: bfloat16 [2, 1024, 1024], P(None, 'fsdp'), may hold values from -2 to 2
- w_gate: bfloat16 [2, 1024, 2816], P(None, 'fsdp'), may hold values from -0.1875 to 0.1875
- w_up: bfloat16 [2, 1024, 2816], P(None, 'fsdp'), may hold values from -0.1875 to 0.1875
- w_down: bfloat16 [2, 2816, 1024], P(None, 'fsdp'), may hold values from -0.109375 to 0.109375
Outputs:
- out_tokens: bfloat16 [8, 1024, 1024], P('fsdp', 'ctx')
- grad_tokens: float32 [8, 1024, 1024], P('fsdp', 'ctx')
- grad_gains: float32 [2, 2, 1024], P(None, None, 'fsdp')
- grad_qkv: float32 [2, 1024, 3072], P(None, 'fsdp')
- grad_out: float32 [2, 1024, 1024], P(None, 'fsdp')
- grad_gate: float32 [2, 1024, 2816], P(None, 'fsdp')
- grad_up: float32 [2, 1024, 2816], P(None, 'fsdp')
- grad_down: float32 [2, 2816, 1024], P(None, 'fsdp')
The draws below stay inside these ranges and needn't reach their ends.
Inputs may be any that keep to these rules, and one draw needn't show every extreme that they name: `doc_lengths`: each row's 4 lengths are at least 1 and sum to 1024; one document of each row starts among its first 256 positions and ends among its last 256.
All inputs are finite; a program needn't handle non-finite values.
Results may differ from the reference program's by a relative error of at most 0.02.
Values may be sent and summed in bfloat16 or wider, within the bound.
A program may use at most 320 MiB of HBM per device.

```python
import math
from functools import partial
import jax
import jax.numpy as jnp
from jax import lax

HEADS = 16
HD = 64
FF = 2816
CTX_TOK = 256
DOCS = 4
LAYERS = 2
D = 1024
SEQ = 1024
ROWS = 8


def draw_doc_lengths(key, part):
    key = jax.random.fold_in(key, 7)
    short_key, place_key = jax.random.split(key)
    shorts = jax.random.randint(short_key, (ROWS, DOCS - 1), 1, CTX_TOK // DOCS + 1).astype(jnp.int32)
    longest = (SEQ - jnp.sum(shorts, axis=1, keepdims=True)).astype(jnp.int32)
    place = jax.random.randint(place_key, (ROWS, 1), 0, DOCS).astype(jnp.int32)
    column = jnp.arange(DOCS, dtype=jnp.int32)[None, :]
    filler = jnp.zeros((ROWS, 1), jnp.int32)
    before = jnp.concatenate([shorts, filler], axis=1)
    after = jnp.concatenate([filler, shorts], axis=1)
    return jnp.where(column < place, before, jnp.where(column == place, longest, after)).astype(jnp.int32)


def levels(key, shape, cuts, low, largest):
    level = 1.0
    for dim, shards_of in cuts:
        draws = jax.random.uniform(jax.random.fold_in(jax.random.fold_in(key, 6), dim), (shards_of,), jnp.float32, low / len(cuts), largest / len(cuts))
        level = level * jnp.repeat(jnp.exp(draws), shape[dim] // shards_of).reshape((-1,) + (1,) * (len(shape) - 1 - dim))
    return level


def centred(own_key, shape, scale, reach, pieces=(), kind=jnp.bfloat16):
    drawn = scale * jax.random.normal(own_key, shape, jnp.float32)
    if pieces:
        drawn = drawn * levels(own_key, shape, pieces, -0.22, 0.18)
    return jnp.clip(drawn, -reach, reach).astype(kind)


def setup_inputs(seed: int = 0) -> dict:
    splits = jax.random.split(jax.random.key(seed), 10)
    tokens = centred(splits[0], (ROWS, SEQ, D), 1.0, 6.0, ((0, 8), (1, 4)))
    doc_lengths = draw_doc_lengths(jax.random.fold_in(splits[9], 71), 0)
    cotangent = centred(splits[2], (ROWS, SEQ, D), 1.0, 6.0, ((0, 8), (1, 4)))
    gains = jnp.clip(1.0 + 0.18 * jax.random.normal(splits[3], (LAYERS, 2, D), jnp.float32), 0.099609375, 1.8984375).astype(jnp.bfloat16)
    w_qkv = centred(splits[4], (LAYERS, D, 3 * D), D ** -0.5, 0.1875, ((1, 8),))
    w_out = centred(splits[5], (LAYERS, D, D), (max(1, 8 * D // SEQ)) ** -0.5, 2.0, ((1, 8),))
    w_gate = centred(splits[6], (LAYERS, D, FF), D ** -0.5, 0.1875, ((1, 8),))
    w_up = centred(splits[7], (LAYERS, D, FF), D ** -0.5, 0.1875, ((1, 8),))
    w_down = centred(splits[8], (LAYERS, FF, D), FF ** -0.5, 0.109375, ((1, 8),))
    return {"tokens": tokens, "doc_lengths": doc_lengths, "cotangent": cotangent, "gains": gains, "w_qkv": w_qkv, "w_out": w_out, "w_gate": w_gate, "w_up": w_up, "w_down": w_down}


@jax.custom_vjp
def low(v):
    return lax.optimization_barrier(v.astype(jnp.bfloat16)).astype(jnp.float32)

@jax.custom_vjp
def low_back(v):
    return v

def low_keep(v):
    return (low(v), None)

def low_pass(kept, grad):
    return (grad,)

def back_keep(v):
    return (v, None)

def back_low(kept, grad):
    return (low(grad),)
low.defvjp(low_keep, low_pass)
low_back.defvjp(back_keep, back_low)
EPSILON = 1e-06
SCORE_SCALE = 0.125
MASK_FILL = -1e+30

def product(left, right):
    return jnp.einsum('rsd,de->rse', left, right, precision=lax.Precision.HIGHEST)

def normalize(hidden, gain):
    return hidden * lax.rsqrt(lax.optimization_barrier(jnp.mean(hidden * hidden, axis=-1, keepdims=True)) + EPSILON) * gain

def documents(lengths, index):
    doc_ends = jnp.cumsum(lengths).astype(jnp.int32)
    passed = index[:, None] >= doc_ends[None, :]
    segment = lax.optimization_barrier(jnp.sum(passed.astype(jnp.int32), axis=1)).astype(jnp.int32)
    doc_start = lax.optimization_barrier(jnp.max(jnp.where(passed, doc_ends[None, :], 0), axis=1)).astype(jnp.int32)
    return (segment, (index - doc_start).astype(jnp.int32))

def rotary_tables(positions, head_width):
    half_width = head_width // 2
    frequency = jnp.exp(-math.log(10000.0) * jnp.arange(half_width, dtype=jnp.float32) / half_width)
    angles = positions.astype(jnp.float32)[..., None] * frequency
    return (jnp.cos(angles)[..., None, :], jnp.sin(angles)[..., None, :])

def rotate(vectors, cosines, sine_table):
    half_width = vectors.shape[-1] // 2
    first_half = vectors[..., :half_width]
    second_half = vectors[..., half_width:]
    return jnp.concatenate([first_half * cosines - second_half * sine_table, second_half * cosines + first_half * sine_table], axis=-1)

def attend_row(row_inputs):
    queries, keys_rot, values_row, segment = row_inputs
    index = jnp.arange(segment.shape[0], dtype=jnp.int32)
    scores = low_back(jnp.einsum('qhd,khd->hqk', queries, keys_rot, precision=lax.Precision.HIGHEST) * SCORE_SCALE)
    allowed = (segment[None, :] == segment[:, None]) & (index[None, :] <= index[:, None])
    prob_rows = low(jax.nn.softmax(jnp.where(allowed[None], scores, MASK_FILL), axis=-1))
    return jnp.einsum('hqk,khd->qhd', prob_rows, values_row, precision=lax.Precision.HIGHEST)

def forward(cosines, sine_table, segment, tokens, gains, w_qkv, w_out, w_gate, w_up, w_down):
    rows_count, full_span, model_width = tokens.shape
    head_shape = (rows_count, full_span, HEADS, HD)
    hidden = tokens
    first_value = None
    for layer_index in range(LAYERS):
        normed = low(normalize(hidden, gains[layer_index, 0]))
        projected = low_back(product(normed, w_qkv[layer_index]))
        queries = low(rotate(projected[..., :model_width].reshape(head_shape), cosines, sine_table))
        keys_rot = low(rotate(projected[..., model_width:2 * model_width].reshape(head_shape), cosines, sine_table))
        if layer_index == 0:
            values_low = low(projected[..., 2 * model_width:])
            first_value = values_low
        else:
            values_low = low(0.5 * projected[..., 2 * model_width:] + 0.5 * first_value)
        attended = lax.map(jax.checkpoint(attend_row), (queries, keys_rot, values_low.reshape(head_shape), segment))
        attended = low_back(low(attended.reshape(rows_count, full_span, model_width)))
        hidden = hidden + low_back(product(attended, w_out[layer_index]))
        normed = low(normalize(hidden, gains[layer_index, 1]))
        gate_value = low_back(product(normed, w_gate[layer_index]))
        up_value = low_back(product(normed, w_up[layer_index]))
        activated = low(jax.nn.silu(gate_value) * up_value)
        hidden = hidden + low_back(product(activated, w_down[layer_index]))
    return hidden

def reference(tokens, doc_lengths, cotangent, gains, w_qkv, w_out, w_gate, w_up, w_down):
    index = jnp.arange(SEQ, dtype=jnp.int32)
    segment, position = jax.vmap(partial(documents, index=index))(doc_lengths)
    cosines, sine_table = rotary_tables(position, HD)
    params = (tokens, gains, w_qkv, w_out, w_gate, w_up, w_down)
    params = tuple((item.astype(jnp.float32) for item in params))
    result, pullback = jax.vjp(partial(forward, cosines, sine_table, segment), *params)
    grads_all = pullback(cotangent.astype(jnp.float32))
    return (result.astype(jnp.bfloat16), grads_all[0], grads_all[1], grads_all[2], grads_all[3], grads_all[4], grads_all[5], grads_all[6])
```

```python
import math

import jax
import jax.numpy as jnp
from jax import lax
from jax.experimental import pallas as pl
from jax.experimental.pallas import tpu as pltpu
from jax.sharding import PartitionSpec as P

HEADS = 16
HD = 64
EPSILON = 1e-06
SCORE_SCALE = 0.125
MASK_FILL = -1e30
BF = jnp.bfloat16
F32 = jnp.float32
MIB = 1024 * 1024
ANY = pl.BlockSpec(memory_space=pl.ANY)
VM = pl.BlockSpec(memory_space=pltpu.VMEM)
NT = (((1,), (1,)), ((), ()))
TN = (((0,), (0,)), ((), ()))


def dot(left, right):
    return jnp.dot(left, right, preferred_element_type=F32)


def dot_nt(left, right):
    return lax.dot_general(left, right, NT, preferred_element_type=F32)


def dot_tn(left, right):
    return lax.dot_general(left, right, TN, preferred_element_type=F32)


def swap(array, axis, bit):
    size = lax.axis_size(axis)
    return lax.ppermute(array, axis, [(i, i ^ bit) for i in range(size)])


def call(kernel, outs, out_specs, scratch, args, in_specs, flops, vmem):
    nbytes = sum(a.size * a.dtype.itemsize for a in args)
    nbytes += sum(math.prod(o.shape) * o.dtype.itemsize for o in outs)
    return pl.pallas_call(
        kernel,
        out_shape=outs,
        in_specs=in_specs,
        out_specs=out_specs,
        scratch_shapes=scratch,
        compiler_params=pltpu.CompilerParams(vmem_limit_bytes=vmem * MIB),
        cost_estimate=pl.CostEstimate(flops=flops, bytes_accessed=nbytes, transcendentals=0),
    )(*args)


def shape(dims, kind):
    return jax.ShapeDtypeStruct(tuple(dims), kind)


def chip_index():
    return lax.axis_index("fsdp") // 2


def run_copies(copies):
    for copy in copies:
        copy.start()
    for copy in copies:
        copy.wait()


def weight_copies(plan, refs, buffer, sems, first):
    chip = chip_index()
    rows = plan[0][2]
    copies = []
    for number, ((k, offset, count), ref) in enumerate(zip(plan[1], refs)):
        start = pl.multiple_of(lax.bitwise_xor(chip, k) * rows + offset, 16)
        copies.append(
            pltpu.make_async_copy(
                ref, buffer.at[pl.ds(start, count), :], sems.at[first + number]
            )
        )
    return copies


class Pieces:
    def __init__(self, arrays, where, rows):
        self.arrays = arrays
        self.where = where
        self.rows = rows

    @property
    def plan(self):
        return ((0, 0, self.rows), self.where)


def gather(piece, chips):
    rows = piece.shape[0]
    if chips == 4:
        half = rows // 2
        from_x = swap(piece, "fsdp", 2)
        from_y = swap(piece, "fsdp", 4)
        far_one = swap(from_x[:half], "fsdp", 4)
        far_two = swap(from_y[half:], "fsdp", 2)
        return Pieces(
            [piece, from_x, from_y, far_one, far_two],
            [(0, 0, rows), (1, 0, rows), (2, 0, rows), (3, 0, half), (3, half, rows - half)],
            rows,
        )
    arrays = [piece] + [swap(piece, "fsdp", 2 * k) for k in range(1, chips)]
    return Pieces(arrays, [(k, 0, rows) for k in range(chips)], rows)


def rope(x, cosines, low_sine, high_sine):
    width = x.shape[-1]
    return (
        x * cosines
        + pltpu.roll(x, width - HD // 2, 1) * low_sine
        + pltpu.roll(x, HD // 2, 1) * high_sine
    )


def project(n_own, n_other, tables, first_value, weight, ctx, last):
    local, width = n_own.shape
    half = width // 2
    group = half // ctx
    pieces = len(weight.arrays)
    plan = weight.plan

    def kernel(*refs):
        own, other, cos, low, high = refs[:5]
        at = 5
        v_in = None
        if first_value is not None:
            v_in = refs[at]
            at += 1
        w_refs = refs[at : at + pieces]
        at += pieces
        slabs = refs[at : at + ctx]
        at += ctx
        v_out = None
        if first_value is None:
            v_out = refs[at]
            at += 1
        buffer, tokens, slab, sems, out_sems = refs[at:]
        copies = weight_copies(plan, w_refs, buffer, sems, 0)
        for copy in copies:
            copy.start()
        tokens[:local] = own[...]
        tokens[local:] = other[...]
        tables_now = [t[...].reshape(2 * local, 128) for t in (cos, low, high)]
        for copy in copies:
            copy.wait()
        for tile in range(3 * half // 256):
            acc = dot(tokens[...], buffer[:, tile * 256 : (tile + 1) * 256])
            kind = tile * 256 // half
            base = tile * 256 - kind * half
            for sub in range(2):
                x = acc[:, sub * 128 : (sub + 1) * 128]
                column = base + sub * 128
                if kind < 2:
                    x = rope(x, *tables_now)
                elif first_value is not None:
                    x = 0.5 * x + 0.5 * v_in[:, column : column + 128].astype(F32)
                x = x.astype(BF)
                if kind == 2 and v_out is not None:
                    v_out[:, column : column + 128] = x
                for part in range(128 // group):
                    slab[column // group + part, kind] = x[
                        :, part * group : (part + 1) * group
                    ].reshape(2, local, group)
        z = lax.axis_index("ctx")
        run_copies(
            [
                pltpu.make_async_copy(slab.at[lax.bitwise_xor(z, k)], slabs[k], out_sems.at[k])
                for k in range(ctx)
            ]
        )

    args = [n_own, n_other, *tables]
    specs = [VM] * 5
    outs = [shape((3, 2, local, group), BF)] * ctx
    out_specs = [ANY] * ctx
    if first_value is not None:
        args.append(first_value)
        specs.append(VM)
    else:
        outs.append(shape((2 * local, half), BF))
        out_specs.append(VM)
    args += weight.arrays
    specs += [ANY] * pieces
    got = call(
        kernel,
        outs,
        out_specs,
        [
            pltpu.VMEM((width, 3 * half), BF),
            pltpu.VMEM((2 * local, width), BF),
            pltpu.VMEM((ctx, 3, 2, local, group), BF),
            pltpu.SemaphoreType.DMA((pieces,)),
            pltpu.SemaphoreType.DMA((ctx,)),
        ],
        args,
        specs,
        2 * 2 * local * width * 3 * half,
        40,
    )
    return got[:ctx], (first_value if first_value is not None else got[ctx])


def exchange(slabs):
    return [slabs[0]] + [swap(slabs[k], "ctx", k) for k in range(1, len(slabs))]


def attend(slabs, start_column):
    ctx = len(slabs)
    _, _, local, group = slabs[0].shape
    span = ctx * local
    heads = group // HD

    def kernel(*refs):
        starts = refs[0]
        ins = refs[1 : 1 + ctx]
        outs = refs[1 + ctx : 1 + 2 * ctx]
        whole, mixed, sems, out_sems = refs[1 + 2 * ctx :]
        z = lax.axis_index("ctx")
        copies = []
        for k in range(ctx):
            at = pl.multiple_of(lax.bitwise_xor(z, k) * local, 16)
            copies.append(
                pltpu.make_async_copy(
                    ins[k], whole.at[:, :, pl.ds(at, local), :], sems.at[k]
                )
            )
        run_copies(copies)
        lane = lax.broadcasted_iota(jnp.int32, (1, group), 1) // HD

        def row_step(row, carry):
            for block in range(ctx):
                keys = (block + 1) * local
                here = slice(block * local, keys)
                query = whole[0, row, here, :] * SCORE_SCALE
                key = whole[1, row, :keys, :]
                value = whole[2, row, :keys, :]
                k_at = lax.broadcasted_iota(jnp.int32, (local, keys), 1)
                q_at = lax.broadcasted_iota(jnp.int32, (local, keys), 0) + block * local
                allowed = (k_at <= q_at) & (k_at >= starts[row, here, :])
                result = None
                for head in range(heads):
                    q_head = jnp.where(lane == head, query, jnp.zeros_like(query))
                    scores = jnp.where(allowed, dot_nt(q_head, key), MASK_FILL)
                    top = jnp.max(scores, axis=1, keepdims=True)
                    powers = jnp.exp(scores - top)
                    total = jnp.sum(powers, axis=1, keepdims=True)
                    probs = (powers * (1.0 / total)).astype(BF)
                    out = dot(probs, value)
                    result = out if result is None else jnp.where(lane == head, out, result)
                mixed[block, row] = result.astype(BF)
            return carry

        lax.fori_loop(0, 2, row_step, 0)
        run_copies(
            [
                pltpu.make_async_copy(mixed.at[lax.bitwise_xor(z, k)], outs[k], out_sems.at[k])
                for k in range(ctx)
            ]
        )

    return call(
        kernel,
        [shape((2, local, group), BF)] * ctx,
        [ANY] * ctx,
        [
            pltpu.VMEM((3, 2, span, group), BF),
            pltpu.VMEM((ctx, 2, local, group), BF),
            pltpu.SemaphoreType.DMA((ctx,)),
            pltpu.SemaphoreType.DMA((ctx,)),
        ],
        [start_column, *slabs],
        [VM] + [ANY] * ctx,
        2 * 2 * 2 * heads * span * span * 128,
        40,
    )


def halves_out(product, own_ref, other_ref, columns, local):
    own_ref[:, columns] = product[:local]
    other_ref[:, columns] = product[local:].astype(BF)


def mix_out(slabs, weight):
    ctx = len(slabs)
    _, local, group = slabs[0].shape
    half = ctx * group
    width = weight.arrays[0].shape[1]
    pieces = len(weight.arrays)
    plan = weight.plan

    def kernel(*refs):
        ins = refs[:ctx]
        w_refs = refs[ctx : ctx + pieces]
        own, other, joined, buffer, landed, sems = refs[ctx + pieces :]
        z = lax.axis_index("ctx")
        copies = weight_copies(plan, w_refs, buffer, sems, ctx)
        for k in range(ctx):
            copies.append(
                pltpu.make_async_copy(ins[k], landed.at[lax.bitwise_xor(z, k)], sems.at[k])
            )
        run_copies(copies)
        for k in range(ctx):
            joined[:, k * group : (k + 1) * group] = landed[k].reshape(2 * local, group)
        for tile in range(width // 256):
            columns = slice(tile * 256, (tile + 1) * 256)
            halves_out(dot(joined[...], buffer[:, columns]), own, other, columns, local)

    return call(
        kernel,
        [shape((local, width), F32), shape((local, width), BF), shape((2 * local, half), BF)],
        [VM] * 3,
        [
            pltpu.VMEM((half, width), BF),
            pltpu.VMEM((ctx, 2, local, group), BF),
            pltpu.SemaphoreType.DMA((ctx + pieces,)),
        ],
        [*slabs, *weight.arrays],
        [ANY] * (ctx + pieces),
        2 * 2 * local * half * width,
        24,
    )


def join_norm(base, own, other, gain):
    local, width = base.shape
    fresh = own is not None

    def kernel(*refs):
        if fresh:
            base_ref, own_ref, other_ref, gain_ref, sum_ref, low_ref = refs
            total = base_ref[...].astype(F32) + own_ref[...] + other_ref[...].astype(F32)
            sum_ref[...] = total
        else:
            base_ref, gain_ref, low_ref = refs
            total = base_ref[...].astype(F32)
        factor = lax.rsqrt(jnp.mean(total * total, axis=1, keepdims=True) + EPSILON)
        low_ref[...] = (total * factor * gain_ref[...].astype(F32)).astype(BF)

    outs = [shape((local, width), BF)]
    args = [base, gain]
    if fresh:
        outs = [shape((local, width), F32)] + outs
        args = [base, own, other, gain]
    return call(
        kernel, outs, [VM] * len(outs), [], args, [VM] * len(args), 8 * local * width, 16
    )


def gate_up(n_own, n_other, weight):
    local, width = n_own.shape
    hidden2 = weight.arrays[0].shape[1]
    hidden = hidden2 // 2
    pieces = len(weight.arrays)
    plan = weight.plan

    def kernel(*refs):
        own, other = refs[:2]
        w_refs = refs[2 : 2 + pieces]
        active, kept, buffer, tokens, sems = refs[2 + pieces :]
        copies = weight_copies(plan, w_refs, buffer, sems, 0)
        for copy in copies:
            copy.start()
        tokens[:local] = own[...]
        tokens[local:] = other[...]
        for copy in copies:
            copy.wait()

        def step(tile, carry):
            wide = pl.ds(pl.multiple_of(tile * 256, 256), 256)
            acc = dot(tokens[...], buffer[:, wide])
            kept[:, wide] = acc
            gate = acc[:, :128]
            active[:, pl.ds(pl.multiple_of(tile * 128, 128), 128)] = (
                gate * jax.nn.sigmoid(gate) * acc[:, 128:]
            ).astype(BF)
            return carry

        lax.fori_loop(0, hidden2 // 256, step, 0)

    return call(
        kernel,
        [shape((2 * local, hidden), BF), shape((2 * local, hidden2), F32)],
        [VM] * 2,
        [
            pltpu.VMEM((width, hidden2), BF),
            pltpu.VMEM((2 * local, width), BF),
            pltpu.SemaphoreType.DMA((pieces,)),
        ],
        [n_own, n_other, *weight.arrays],
        [VM] * 2 + [ANY] * pieces,
        2 * 2 * local * width * hidden2,
        40,
    )


def down(active, weight):
    tokens, hidden = active.shape
    local = tokens // 2
    width = weight.arrays[0].shape[1]
    pieces = len(weight.arrays)
    plan = weight.plan

    def kernel(*refs):
        left = refs[0]
        w_refs = refs[1 : 1 + pieces]
        own, other, buffer, sems = refs[1 + pieces :]
        run_copies(weight_copies(plan, w_refs, buffer, sems, 0))

        def step(tile, carry):
            columns = pl.ds(pl.multiple_of(tile * 256, 256), 256)
            halves_out(dot(left[...], buffer[:, columns]), own, other, columns, local)
            return carry

        lax.fori_loop(0, width // 256, step, 0)

    return call(
        kernel,
        [shape((local, width), F32), shape((local, width), BF)],
        [VM] * 2,
        [pltpu.VMEM((hidden, width), BF), pltpu.SemaphoreType.DMA((pieces,))],
        [active, *weight.arrays],
        [VM] + [ANY] * pieces,
        2 * tokens * hidden * width,
        24,
    )


def mlp_back(e_own, e_other, kept, gu_weight, down_weight):
    local, width = e_own.shape
    hidden2 = kept.shape[1]
    hidden = hidden2 // 2
    pieces = len(gu_weight.arrays)
    more = len(down_weight.arrays)
    gu_plan, down_plan = gu_weight.plan, down_weight.plan

    def kernel(*refs):
        e_one, e_two, kept_ref = refs[:3]
        gu_refs = refs[3 : 3 + pieces]
        down_refs = refs[3 + pieces : 3 + pieces + more]
        grads, own, other, gu, wd, tokens, sems = refs[3 + pieces + more :]
        first = weight_copies(down_plan, down_refs, wd, sems, pieces)
        second = weight_copies(gu_plan, gu_refs, gu, sems, 0)
        for copy in first + second:
            copy.start()
        tokens[:local] = e_one[...]
        tokens[local:] = e_two[...]
        for copy in first:
            copy.wait()

        def span_step(base, count):
            rows = pl.ds(base, count * 128)
            flow = dot_nt(tokens[...], wd[rows, :])
            for sub in range(count):
                start = pl.multiple_of(2 * base + sub * 256, 256)
                gate = kept_ref[:, pl.ds(start, 128)]
                up = kept_ref[:, pl.ds(start + 128, 128)]
                sig = jax.nn.sigmoid(gate)
                here = flow[:, sub * 128 : (sub + 1) * 128]
                grads[:, pl.ds(start, 128)] = (
                    here * up * sig * (1.0 + gate * (1.0 - sig))
                ).astype(BF)
                grads[:, pl.ds(start + 128, 128)] = (here * gate * sig).astype(BF)

        def step(tile, carry):
            span_step(pl.multiple_of(tile * 256, 256), 2)
            return carry

        lax.fori_loop(0, hidden // 256, step, 0)
        if hidden % 256:
            span_step(hidden // 256 * 256, 1)
        for copy in second:
            copy.wait()

        def back_step(tile, carry):
            rows = pl.ds(pl.multiple_of(tile * 256, 256), 256)
            halves_out(dot_nt(grads[...], gu[rows, :]), own, other, rows, local)
            return carry

        lax.fori_loop(0, width // 256, back_step, 0)

    return call(
        kernel,
        [
            shape((2 * local, hidden2), BF),
            shape((local, width), F32),
            shape((local, width), BF),
        ],
        [VM] * 3,
        [
            pltpu.VMEM((width, hidden2), BF),
            pltpu.VMEM((hidden, width), BF),
            pltpu.VMEM((2 * local, width), BF),
            pltpu.SemaphoreType.DMA((pieces + more,)),
        ],
        [e_own, e_other, kept, *gu_weight.arrays, *down_weight.arrays],
        [VM] * 3 + [ANY] * (pieces + more),
        2 * 2 * local * width * hidden * 3,
        48,
    )


def norm_back(stream, own, other, gain, grad):
    local, width = stream.shape

    def kernel(x_ref, own_ref, other_ref, gain_ref, grad_ref, out_ref, low_ref, gain_out):
        x = x_ref[...].astype(F32)
        factor = lax.rsqrt(jnp.mean(x * x, axis=1, keepdims=True) + EPSILON)
        flow = own_ref[...] + other_ref[...].astype(F32)
        scaled = flow * gain_ref[...].astype(F32)
        gain_out[...] = jnp.sum(flow * x * factor, axis=0, keepdims=True)
        mean_term = jnp.mean(scaled * x, axis=1, keepdims=True)
        result = (
            grad_ref[...].astype(F32)
            + factor * scaled
            - x * (factor * factor * factor * mean_term)
        )
        out_ref[...] = result
        low_ref[...] = result.astype(BF)

    return call(
        kernel,
        [shape((local, width), F32), shape((local, width), BF), shape((1, width), F32)],
        [VM] * 3,
        [],
        [stream, own, other, gain, grad],
        [VM] * 5,
        12 * local * width,
        24,
    )


def mix_back(f_own, f_other, weight, ctx):
    local, width = f_own.shape
    half = width // 2
    group = half // ctx
    pieces = len(weight.arrays)
    plan = weight.plan

    def kernel(*refs):
        own, other = refs[:2]
        w_refs = refs[2 : 2 + pieces]
        slabs = refs[2 + pieces : 2 + pieces + ctx]
        buffer, tokens, slab, sems, out_sems = refs[2 + pieces + ctx :]
        copies = weight_copies(plan, w_refs, buffer, sems, 0)
        for copy in copies:
            copy.start()
        tokens[:local] = own[...]
        tokens[local:] = other[...]
        for copy in copies:
            copy.wait()
        for tile in range(half // 256):
            flow = dot_nt(tokens[...], buffer[tile * 256 : (tile + 1) * 256, :]).astype(BF)
            for part in range(256 // group):
                slab[tile * 256 // group + part] = flow[
                    :, part * group : (part + 1) * group
                ].reshape(2, local, group)
        z = lax.axis_index("ctx")
        run_copies(
            [
                pltpu.make_async_copy(slab.at[lax.bitwise_xor(z, k)], slabs[k], out_sems.at[k])
                for k in range(ctx)
            ]
        )

    return call(
        kernel,
        [shape((2, local, group), BF)] * ctx,
        [ANY] * ctx,
        [
            pltpu.VMEM((half, width), BF),
            pltpu.VMEM((2 * local, width), BF),
            pltpu.VMEM((ctx, 2, local, group), BF),
            pltpu.SemaphoreType.DMA((pieces,)),
            pltpu.SemaphoreType.DMA((ctx,)),
        ],
        [f_own, f_other, *weight.arrays],
        [VM] * 2 + [ANY] * pieces,
        2 * 2 * local * half * width,
        24,
    )


def attend_back(slabs, grad_slabs, start_row, tables, carried):
    ctx = len(slabs)
    _, _, local, group = slabs[0].shape
    span = ctx * local
    heads = group // HD
    first = carried is not None

    def kernel(*refs):
        starts, cos, low, high = refs[:4]
        at = 4
        carry_in = None
        if first:
            carry_in = refs[at]
            at += 1
        ins = refs[at : at + ctx]
        grads = refs[at + ctx : at + 2 * ctx]
        outs = refs[at + 2 * ctx : at + 3 * ctx]
        at += 3 * ctx
        carry_out = None
        if not first:
            carry_out = refs[at]
            at += 1
        whole, flow_in, slab, key_sum, value_sum, sems, out_sems = refs[at:]
        z = lax.axis_index("ctx")
        copies = []
        for k in range(ctx):
            to = pl.ds(pl.multiple_of(lax.bitwise_xor(z, k) * local, 16), local)
            copies.append(
                pltpu.make_async_copy(ins[k], whole.at[:, :, to, :], sems.at[k])
            )
            copies.append(
                pltpu.make_async_copy(grads[k], flow_in.at[:, to, :], sems.at[ctx + k])
            )
        run_copies(copies)
        lane = lax.broadcasted_iota(jnp.int32, (1, group), 1) // HD
        line = lax.broadcasted_iota(jnp.int32, (group, 1), 0) // HD

        def row_step(row, carry):
            key_sum[...] = jnp.zeros_like(key_sum)
            value_sum[...] = jnp.zeros_like(value_sum)
            key_turned = whole[1, row].astype(F32).T.astype(BF)
            for block in range(ctx):
                keys = (block + 1) * local
                here = slice(block * local, keys)
                query = whole[0, row, here, :] * SCORE_SCALE
                grad = flow_in[row, here, :]
                key = whole[1, row, :keys, :]
                value = whole[2, row, :keys, :]
                k_at = lax.broadcasted_iota(jnp.int32, (keys, local), 0)
                q_at = lax.broadcasted_iota(jnp.int32, (keys, local), 1) + block * local
                allowed = (k_at <= q_at) & (k_at >= starts[row, :, here])
                turned = None
                for head in range(heads):
                    mine = lane == head
                    q_head = jnp.where(mine, query, jnp.zeros_like(query))
                    g_head = jnp.where(mine, grad, jnp.zeros_like(grad))
                    scores = jnp.where(allowed, dot_nt(key, q_head), MASK_FILL)
                    top = jnp.max(scores, axis=0, keepdims=True)
                    powers = jnp.exp(scores - top)
                    total = jnp.sum(powers, axis=0, keepdims=True)
                    probs = powers * (1.0 / total)
                    grad_probs = dot_nt(value, g_head)
                    delta = jnp.sum(probs * grad_probs, axis=0, keepdims=True)
                    grad_scores = (probs * (grad_probs - delta)).astype(BF)
                    value_sum[:keys] += dot(probs.astype(BF), g_head)
                    key_sum[:keys] += dot(grad_scores, q_head)
                    part = dot(key_turned[:, :keys], grad_scores)
                    turned = part if turned is None else jnp.where(line == head, part, turned)
                grad_query = turned.T * SCORE_SCALE
                slab[block, 0, row] = rope(
                    grad_query, cos[row, here, :], -low[row, here, :], -high[row, here, :]
                ).astype(BF)
            for block in range(ctx):
                here = slice(block * local, (block + 1) * local)
                slab[block, 1, row] = rope(
                    key_sum[here, :], cos[row, here, :], -low[row, here, :], -high[row, here, :]
                ).astype(BF)
                if first:
                    total_value = value_sum[here, :] + carry_in[row, here, :]
                else:
                    total_value = 0.5 * value_sum[here, :]
                    carry_out[row, here, :] = total_value
                slab[block, 2, row] = total_value.astype(BF)
            return carry

        lax.fori_loop(0, 2, row_step, 0)
        run_copies(
            [
                pltpu.make_async_copy(slab.at[lax.bitwise_xor(z, k)], outs[k], out_sems.at[k])
                for k in range(ctx)
            ]
        )

    args = [start_row, *tables]
    specs = [VM] * 4
    outs = [shape((3, 2, local, group), BF)] * ctx
    out_specs = [ANY] * ctx
    if first:
        args.append(carried)
        specs.append(VM)
    else:
        outs.append(shape((2, span, group), F32))
        out_specs.append(VM)
    got = call(
        kernel,
        outs,
        out_specs,
        [
            pltpu.VMEM((3, 2, span, group), BF),
            pltpu.VMEM((2, span, group), BF),
            pltpu.VMEM((ctx, 3, 2, local, group), BF),
            pltpu.VMEM((span, group), F32),
            pltpu.VMEM((span, group), F32),
            pltpu.SemaphoreType.DMA((2 * ctx,)),
            pltpu.SemaphoreType.DMA((ctx,)),
        ],
        [*args, *slabs, *grad_slabs],
        specs + [ANY] * (2 * ctx),
        2 * 5 * 2 * heads * span * span * 128,
        48,
    )
    return got[:ctx], (None if first else got[ctx])


def project_back(slabs, weight):
    ctx = len(slabs)
    _, _, local, group = slabs[0].shape
    half = ctx * group
    width = 2 * half
    pieces = len(weight.arrays)
    plan = weight.plan

    def kernel(*refs):
        ins = refs[:ctx]
        w_refs = refs[ctx : ctx + pieces]
        own, other, joined, buffer, landed, sems = refs[ctx + pieces :]
        z = lax.axis_index("ctx")
        copies = weight_copies(plan, w_refs, buffer, sems, ctx)
        for k in range(ctx):
            copies.append(
                pltpu.make_async_copy(ins[k], landed.at[lax.bitwise_xor(z, k)], sems.at[k])
            )
        run_copies(copies)
        for k in range(ctx):
            for kind in range(3):
                base = kind * half + k * group
                joined[:, base : base + group] = landed[k, kind].reshape(2 * local, group)

        def step(tile, carry):
            rows = pl.ds(pl.multiple_of(tile * 256, 256), 256)
            halves_out(dot_nt(joined[...], buffer[rows, :]), own, other, rows, local)
            return carry

        lax.fori_loop(0, width // 256, step, 0)

    return call(
        kernel,
        [
            shape((local, width), F32),
            shape((local, width), BF),
            shape((2 * local, 3 * half), BF),
        ],
        [VM] * 3,
        [
            pltpu.VMEM((width, 3 * half), BF),
            pltpu.VMEM((ctx, 3, 2, local, group), BF),
            pltpu.SemaphoreType.DMA((ctx + pieces,)),
        ],
        [*slabs, *weight.arrays],
        [ANY] * (ctx + pieces),
        2 * 2 * local * 3 * half * width,
        40,
    )


def weight_grad(left, right, chips):
    lefts, rights = list(left), list(right)
    tall = lefts[0].shape[1]
    wide = rights[0].shape[1]
    tokens = lefts[0].shape[0] * len(lefts)
    rows = tall // chips
    halved = wide // 2
    split = chips == 4

    def kernel(*refs):
        l_refs = refs[: len(lefts)]
        r_refs = refs[len(lefts) : len(lefts) + len(rights)]
        at = len(lefts) + len(rights)
        count = 4 if split else chips
        outs = refs[at : at + count]
        grads, l_buf, r_buf, sems = refs[at + count :]
        if len(lefts) == 2:
            l_buf[: tokens // 2] = l_refs[0][...]
            l_buf[tokens // 2 :] = l_refs[1][...]
            l_now = l_buf
        else:
            l_now = l_refs[0]
        if len(rights) == 2:
            r_buf[: tokens // 2] = r_refs[0][...]
            r_buf[tokens // 2 :] = r_refs[1][...]
            r_now = r_buf
        else:
            r_now = r_refs[0]

        def tile_step(base, size):
            turned = l_now[:, pl.ds(base, size)]
            for start in range(0, wide, 512):
                stop = min(start + 512, wide)
                grads[pl.ds(base, size), start:stop] = dot_tn(
                    turned, r_now[:, start:stop]
                ).astype(BF)

        def step(tile, carry):
            tile_step(pl.multiple_of(tile * 256, 256), 256)
            return carry

        lax.fori_loop(0, tall // 256, step, 0)
        if tall % 256:
            tile_step(tall // 256 * 256, tall % 256)
        chip = chip_index()

        def block(k):
            return pl.ds(pl.multiple_of(lax.bitwise_xor(chip, k) * rows, 16), rows)

        copies = []
        if split:
            for which, order in enumerate(((1, 3), (0, 2), (2, 3), (0, 1))):
                columns = pl.ds((which // 2) * halved, halved)
                for slot, k in enumerate(order):
                    copies.append(
                        pltpu.make_async_copy(
                            grads.at[block(k), columns],
                            outs[which].at[slot],
                            sems.at[2 * which + slot],
                        )
                    )
        else:
            for k in range(chips):
                copies.append(
                    pltpu.make_async_copy(grads.at[block(k), :], outs[k], sems.at[k])
                )
        run_copies(copies)

    if split:
        outs = [shape((2, rows, halved), BF)] * 4
    else:
        outs = [shape((rows, wide), BF)] * chips
    small = (16, 128)
    return call(
        kernel,
        outs,
        [ANY] * len(outs),
        [
            pltpu.VMEM((tall, wide), BF),
            pltpu.VMEM((tokens, tall) if len(lefts) == 2 else small, BF),
            pltpu.VMEM((tokens, wide) if len(rights) == 2 else small, BF),
            pltpu.SemaphoreType.DMA((8 if split else chips,)),
        ],
        [*lefts, *rights],
        [VM] * (len(lefts) + len(rights)),
        2 * tokens * tall * wide,
        48,
    )


def add_low(left, right):
    return (left.astype(F32) + right.astype(F32)).astype(BF)


def reduce_chips(blocks, chips):
    if chips != 4:
        total = blocks[0].astype(F32)
        for k in range(1, chips):
            total = total + swap(blocks[k], "fsdp", 2 * k).astype(F32)
        return total.astype(BF)
    send_x, keep_x, send_y, keep_y = blocks
    got_x = swap(send_x, "fsdp", 2)
    got_y = swap(send_y, "fsdp", 4)
    on_x = swap(add_low(keep_x[1], got_x[1]), "fsdp", 4)
    on_y = swap(add_low(keep_y[1], got_y[1]), "fsdp", 2)
    first = add_low(add_low(keep_x[0], got_x[0]), on_x)
    second = add_low(add_low(keep_y[0], got_y[0]), on_y)
    return jnp.concatenate([first, second], axis=1)


def reduce_line(block):
    if lax.axis_size("ctx") != 4:
        return lax.psum(block, "ctx")
    z = lax.axis_index("ctx")
    inner = (z == 1) | (z == 2)
    inward = lax.ppermute(block, "ctx", [(0, 1), (3, 2)])
    pair = jnp.where(inner, add_low(block, inward), block)
    across = lax.ppermute(pair, "ctx", [(1, 2), (2, 1)])
    total = add_low(pair, across)
    outward = lax.ppermute(total, "ctx", [(1, 0), (2, 3)])
    return jnp.where(inner, total, outward)


def own_rows(block):
    core = lax.axis_index("fsdp") % 2
    rows = block.shape[0] // 2
    mine = lax.dynamic_slice_in_dim(block, core * rows, rows)
    theirs = swap(lax.dynamic_slice_in_dim(block, (1 - core) * rows, rows), "fsdp", 1)
    low = jnp.where(core == 0, mine, theirs)
    high = jnp.where(core == 0, theirs, mine)
    return jnp.stack([low, high])


def chip_piece(mine, other):
    core = lax.axis_index("fsdp") % 2
    got = swap(other, "fsdp", 1)
    return jnp.where(
        core == 0, jnp.concatenate([mine, got]), jnp.concatenate([got, mine])
    )


def document_starts(lengths, index):
    ends = []
    total = jnp.int32(0)
    for j in range(lengths.shape[0]):
        total = total + lengths[j]
        ends.append(total)
    start = jnp.zeros_like(index)
    for end in ends:
        start = jnp.where(index >= end, end, start)
    return start


def rotary(positions):
    pairs = HD // 2
    lane = jnp.arange(128, dtype=jnp.int32)
    frequency = jnp.exp(-math.log(10000.0) * jnp.arange(pairs, dtype=F32) / pairs)
    angles = positions.astype(F32)[..., None] * frequency
    cosines = jnp.tile(jnp.cos(angles), 128 // pairs)
    sines = jnp.tile(jnp.sin(angles), 128 // pairs)
    low = jnp.where(lane % HD < pairs, -sines, 0.0)
    high = jnp.where(lane % HD >= pairs, sines, 0.0)
    return [cosines, low, high]


def body(tokens, doc_lengths, cotangent, gains, w_qkv, w_out, w_gate, w_up, w_down):
    _, local, width = tokens.shape
    layers = gains.shape[0]
    shards = lax.axis_size("fsdp")
    ctx = lax.axis_size("ctx")
    chips = shards // 2
    block = width // shards
    hidden = w_gate.shape[2]
    hidden_half = hidden // 2
    hidden_block = hidden // shards
    core = lax.axis_index("fsdp") % 2
    z = lax.axis_index("ctx")
    span = local * ctx

    def pick(array, axis, which):
        return lax.dynamic_index_in_dim(array, which, axis, keepdims=False)

    qkv_weights, out_weights, gu_weights, down_weights = [], [], [], []
    for layer in range(layers):
        qkv = w_qkv[layer].reshape(block, 3, chips, 2, block)
        sides = [pick(qkv, 3, which).reshape(block, -1) for which in (core, 1 - core)]
        qkv_weights.append(gather(chip_piece(*sides), chips))
        out_weights.append(gather(w_out[layer], chips))
        sides = []
        for which in (core, 1 - core):
            both = [
                pick(w[layer].reshape(block, chips, 2, hidden_block), 2, which).reshape(
                    block, hidden_half // 128, 128
                )
                for w in (w_gate, w_up)
            ]
            sides.append(jnp.stack(both, axis=2).reshape(block, 2 * hidden_half))
        gu_weights.append(gather(chip_piece(*sides), chips))
        down_weights.append(gather(w_down[layer], chips))

    all_gains = lax.all_gather(gains, "fsdp", axis=2, tiled=True)
    gain_rows = [[all_gains[layer, n][None] for n in range(2)] for layer in range(layers)]

    index = jnp.arange(span, dtype=jnp.int32)
    lengths = [doc_lengths[0], swap(doc_lengths, "fsdp", 1)[0]]
    starts = jnp.stack([document_starts(row, index) for row in lengths])
    row_tables = rotary(index[None] - starts)
    here_tables = [lax.dynamic_slice_in_dim(t, z * local, local, axis=1) for t in row_tables]
    head_lanes = min(128, width // 2 // ctx)
    head_tables = [t[:, :, :head_lanes] for t in row_tables]
    start_column = starts[:, :, None]
    start_row = starts[:, None, :]

    def pair(array):
        return (array, swap(array, "fsdp", 1))

    stream = tokens[0]
    kept = []
    first_value = None
    (low,) = join_norm(stream, None, None, gain_rows[0][0])
    for layer in range(layers):
        normed = pair(low)
        slabs, first_value = project(
            *normed, here_tables, first_value, qkv_weights[layer], ctx, layer == layers - 1
        )
        slabs = exchange(slabs)
        mixed = exchange(attend(slabs, start_column))
        own, other, joined = mix_out(mixed, out_weights[layer])
        middle, low = join_norm(stream, own, swap(other, "fsdp", 1), gain_rows[layer][1])
        normed_two = pair(low)
        active, gu_kept = gate_up(*normed_two, gu_weights[layer])
        own, other = down(active, down_weights[layer])
        after = gain_rows[min(layer + 1, layers - 1)][0]
        kept.append((stream, normed, slabs, joined, middle, normed_two, active, gu_kept))
        stream, low = join_norm(middle, own, swap(other, "fsdp", 1), after)
    out_tokens = stream.astype(BF)[None]

    grad = cotangent[0]
    low = cotangent[0]
    carried = None
    gain_grads = [[None, None] for _ in range(layers)]
    done = [None] * layers
    for layer in reversed(range(layers)):
        stream, normed, slabs, joined, middle, normed_two, active, gu_kept = kept[layer]
        sent = pair(low)
        down_blocks = weight_grad([active], sent, chips)
        gu_grads, own, other = mlp_back(
            *sent, gu_kept, gu_weights[layer], down_weights[layer]
        )
        grad, low, gain_grads[layer][1] = norm_back(
            middle, own, swap(other, "fsdp", 1), gain_rows[layer][1], grad
        )
        gu_blocks = weight_grad(normed_two, [gu_grads], chips)
        mixed_back = pair(low)
        grad_slabs = exchange(mix_back(*mixed_back, out_weights[layer], ctx))
        out_blocks = weight_grad([joined], mixed_back, chips)
        grad_slabs, carry_out = attend_back(slabs, grad_slabs, start_row, head_tables, carried)
        carried = carry_out
        own, other, qkv_grads = project_back(exchange(grad_slabs), qkv_weights[layer])
        qkv_blocks = weight_grad(normed, [qkv_grads], chips)
        grad, low, gain_grads[layer][0] = norm_back(
            stream, own, swap(other, "fsdp", 1), gain_rows[layer][0], grad
        )
        down_sum = reduce_line(reduce_chips(down_blocks, chips)).astype(F32)
        gu_sum = own_rows(reduce_line(reduce_chips(gu_blocks, chips)))
        out_sum = reduce_line(reduce_chips(out_blocks, chips)).astype(F32)
        qkv_sum = own_rows(reduce_line(reduce_chips(qkv_blocks, chips)))
        qkv_sum = qkv_sum.reshape(2, block, 3, chips, block).transpose(1, 2, 3, 0, 4)
        qkv_sum = qkv_sum.reshape(block, 3 * width).astype(F32)
        gu_sum = gu_sum.reshape(2, block, hidden_half // 128, 2, 128).transpose(3, 1, 0, 2, 4)
        gu_sum = gu_sum.reshape(2, block, 2, chips, hidden_block).transpose(0, 1, 3, 2, 4)
        gu_sum = gu_sum.reshape(2, block, hidden).astype(F32)
        done[layer] = (qkv_sum, out_sum, gu_sum[0], gu_sum[1], down_sum)

    gain_sum = jnp.stack([jnp.concatenate(rows) for rows in gain_grads])
    gain_sum = lax.psum_scatter(gain_sum, "fsdp", scatter_dimension=2, tiled=True)
    gain_sum = lax.psum(gain_sum, "ctx")
    stacked = [jnp.stack([done[layer][n] for layer in range(layers)]) for n in range(5)]
    return (out_tokens, grad[None], gain_sum, *stacked)


def solution(mesh):
    rows = P(None, "fsdp", None)
    tokens = P("fsdp", "ctx", None)
    gains = P(None, None, "fsdp")
    return jax.shard_map(
        body,
        mesh=mesh,
        in_specs=(tokens, P("fsdp", None), tokens, gains, rows, rows, rows, rows, rows),
        out_specs=(tokens, tokens, gains, rows, rows, rows, rows, rows),
        check_vma=False,
    )
```

```python
import math

import jax
import jax.numpy as jnp
from jax import lax
from jax.experimental import pallas as pl
from jax.experimental.pallas import tpu as pltpu
from jax.sharding import PartitionSpec as P

HEADS = 16
HD = 64
EPSILON = 1e-06
SCORE_SCALE = 0.125
MASK_FILL = -1e30
BF = jnp.bfloat16
F32 = jnp.float32
MIB = 1024 * 1024
ANY = pl.BlockSpec(memory_space=pl.ANY)
VM = pl.BlockSpec(memory_space=pltpu.VMEM)
NT = (((1,), (1,)), ((), ()))
TN = (((0,), (0,)), ((), ()))


def dot(left, right):
    return jnp.dot(left, right, preferred_element_type=F32)


def dot_nt(left, right):
    return lax.dot_general(left, right, NT, preferred_element_type=F32)


def dot_tn(left, right):
    return lax.dot_general(left, right, TN, preferred_element_type=F32)


def swap(array, axis, bit):
    size = lax.axis_size(axis)
    return lax.ppermute(array, axis, [(i, i ^ bit) for i in range(size)])


def call(kernel, outs, out_specs, scratch, args, in_specs, flops, vmem):
    nbytes = sum(a.size * a.dtype.itemsize for a in args)
    nbytes += sum(math.prod(o.shape) * o.dtype.itemsize for o in outs)
    return pl.pallas_call(
        kernel,
        out_shape=outs,
        in_specs=in_specs,
        out_specs=out_specs,
        scratch_shapes=scratch,
        compiler_params=pltpu.CompilerParams(vmem_limit_bytes=vmem * MIB),
        cost_estimate=pl.CostEstimate(flops=flops, bytes_accessed=nbytes, transcendentals=0),
    )(*args)


def shape(dims, kind):
    return jax.ShapeDtypeStruct(tuple(dims), kind)


def chip_index():
    return lax.axis_index("fsdp") // 2


def run_copies(copies):
    for copy in copies:
        copy.start()
    for copy in copies:
        copy.wait()


def weight_copies(plan, refs, buffer, sems, first):
    if plan[1] is None:
        return [pltpu.make_async_copy(refs[0], buffer, sems.at[first])]
    chip = chip_index()
    rows = plan[0][2]
    copies = []
    for number, ((k, offset, count), ref) in enumerate(zip(plan[1], refs)):
        start = pl.multiple_of(lax.bitwise_xor(chip, k) * rows + offset, 16)
        copies.append(
            pltpu.make_async_copy(
                ref, buffer.at[pl.ds(start, count), :], sems.at[first + number]
            )
        )
    return copies


class Pieces:
    def __init__(self, arrays, where, rows):
        self.arrays = arrays
        self.where = where
        self.rows = rows

    @property
    def plan(self):
        return ((0, 0, self.rows), self.where)


def gather(piece, chips):
    rows = piece.shape[0]
    if chips == 4:
        half = rows // 2
        from_x = swap(piece, "fsdp", 2)
        from_y = swap(piece, "fsdp", 4)
        far_one = swap(from_x[:half], "fsdp", 4)
        far_two = swap(from_y[half:], "fsdp", 2)
        return Pieces(
            [piece, from_x, from_y, far_one, far_two],
            [(0, 0, rows), (1, 0, rows), (2, 0, rows), (3, 0, half), (3, half, rows - half)],
            rows,
        )
    arrays = [piece] + [swap(piece, "fsdp", 2 * k) for k in range(1, chips)]
    return Pieces(arrays, [(k, 0, rows) for k in range(chips)], rows)


def rope(x, cosines, low_sine, high_sine):
    width = x.shape[-1]
    return (
        x * cosines
        + pltpu.roll(x, width - HD // 2, 1) * low_sine
        + pltpu.roll(x, HD // 2, 1) * high_sine
    )


def project(n_own, n_other, tables, first_value, weight, ctx, last):
    local, width = n_own.shape
    half = width // 2
    group = half // ctx
    pieces = len(weight.arrays)
    plan = weight.plan

    def kernel(*refs):
        own, other, cos, low, high = refs[:5]
        at = 5
        v_in = None
        if first_value is not None:
            v_in = refs[at]
            at += 1
        w_refs = refs[at : at + pieces]
        at += pieces
        slabs = refs[at : at + ctx]
        at += ctx
        v_out = None
        if first_value is None:
            v_out = refs[at]
            at += 1
        buffer, tokens, slab, sems, out_sems = refs[at:]
        copies = weight_copies(plan, w_refs, buffer, sems, 0)
        for copy in copies:
            copy.start()
        tokens[:local] = own[...]
        tokens[local:] = other[...]
        tables_now = [t[...].reshape(2 * local, 128) for t in (cos, low, high)]
        for copy in copies:
            copy.wait()
        for tile in range(3 * half // 256):
            acc = dot(tokens[...], buffer[:, tile * 256 : (tile + 1) * 256])
            kind = tile * 256 // half
            base = tile * 256 - kind * half
            for sub in range(2):
                x = acc[:, sub * 128 : (sub + 1) * 128]
                column = base + sub * 128
                if kind < 2:
                    x = rope(x, *tables_now)
                elif first_value is not None:
                    x = 0.5 * x + 0.5 * v_in[:, column : column + 128].astype(F32)
                x = x.astype(BF)
                if kind == 2 and v_out is not None:
                    v_out[:, column : column + 128] = x
                for part in range(128 // group):
                    slab[column // group + part, kind] = x[
                        :, part * group : (part + 1) * group
                    ].reshape(2, local, group)
        z = lax.axis_index("ctx")
        run_copies(
            [
                pltpu.make_async_copy(slab.at[lax.bitwise_xor(z, k)], slabs[k], out_sems.at[k])
                for k in range(ctx)
            ]
        )

    args = [n_own, n_other, *tables]
    specs = [VM] * 5
    outs = [shape((3, 2, local, group), BF)] * ctx
    out_specs = [ANY] * ctx
    if first_value is not None:
        args.append(first_value)
        specs.append(VM)
    else:
        outs.append(shape((2 * local, half), BF))
        out_specs.append(VM)
    args += weight.arrays
    specs += [ANY] * pieces
    got = call(
        kernel,
        outs,
        out_specs,
        [
            pltpu.VMEM((width, 3 * half), BF),
            pltpu.VMEM((2 * local, width), BF),
            pltpu.VMEM((ctx, 3, 2, local, group), BF),
            pltpu.SemaphoreType.DMA((pieces,)),
            pltpu.SemaphoreType.DMA((ctx,)),
        ],
        args,
        specs,
        2 * 2 * local * width * 3 * half,
        40,
    )
    return got[:ctx], (first_value if first_value is not None else got[ctx])


def exchange(slabs):
    return [slabs[0]] + [swap(slabs[k], "ctx", k) for k in range(1, len(slabs))]


def attend(slabs, start_column):
    ctx = len(slabs)
    _, _, local, group = slabs[0].shape
    span = ctx * local
    heads = group // HD

    def kernel(*refs):
        starts = refs[0]
        ins = refs[1 : 1 + ctx]
        outs = refs[1 + ctx : 1 + 2 * ctx]
        whole, mixed, sems, out_sems = refs[1 + 2 * ctx :]
        z = lax.axis_index("ctx")
        copies = []
        for k in range(ctx):
            at = pl.multiple_of(lax.bitwise_xor(z, k) * local, 16)
            copies.append(
                pltpu.make_async_copy(
                    ins[k], whole.at[:, :, pl.ds(at, local), :], sems.at[k]
                )
            )
        run_copies(copies)
        lane = lax.broadcasted_iota(jnp.int32, (1, group), 1) // HD

        def row_step(row, carry):
            for block in range(ctx):
                keys = (block + 1) * local
                here = slice(block * local, keys)
                query = whole[0, row, here, :] * SCORE_SCALE
                key = whole[1, row, :keys, :]
                value = whole[2, row, :keys, :]
                k_at = lax.broadcasted_iota(jnp.int32, (local, keys), 1)
                q_at = lax.broadcasted_iota(jnp.int32, (local, keys), 0) + block * local
                allowed = (k_at <= q_at) & (k_at >= starts[row, here, :])
                result = None
                for head in range(heads):
                    q_head = jnp.where(lane == head, query, jnp.zeros_like(query))
                    scores = jnp.where(allowed, dot_nt(q_head, key), MASK_FILL)
                    top = jnp.max(scores, axis=1, keepdims=True)
                    powers = jnp.exp(scores - top)
                    total = jnp.sum(powers, axis=1, keepdims=True)
                    probs = (powers * (1.0 / total)).astype(BF)
                    out = dot(probs, value)
                    result = out if result is None else jnp.where(lane == head, out, result)
                mixed[block, row] = result.astype(BF)
            return carry

        lax.fori_loop(0, 2, row_step, 0)
        run_copies(
            [
                pltpu.make_async_copy(mixed.at[lax.bitwise_xor(z, k)], outs[k], out_sems.at[k])
                for k in range(ctx)
            ]
        )

    return call(
        kernel,
        [shape((2, local, group), BF)] * ctx,
        [ANY] * ctx,
        [
            pltpu.VMEM((3, 2, span, group), BF),
            pltpu.VMEM((ctx, 2, local, group), BF),
            pltpu.SemaphoreType.DMA((ctx,)),
            pltpu.SemaphoreType.DMA((ctx,)),
        ],
        [start_column, *slabs],
        [VM] + [ANY] * ctx,
        2 * 2 * 2 * heads * span * span * 128,
        40,
    )


def halves_out(product, own_ref, other_ref, columns, local):
    own_ref[:, columns] = product[:local]
    other_ref[:, columns] = product[local:].astype(BF)


def mix_out(slabs, weight):
    ctx = len(slabs)
    _, local, group = slabs[0].shape
    half = ctx * group
    width = weight.arrays[0].shape[1]
    pieces = len(weight.arrays)
    plan = weight.plan

    def kernel(*refs):
        ins = refs[:ctx]
        w_refs = refs[ctx : ctx + pieces]
        own, other, joined, buffer, landed, sems = refs[ctx + pieces :]
        z = lax.axis_index("ctx")
        copies = weight_copies(plan, w_refs, buffer, sems, ctx)
        for k in range(ctx):
            copies.append(
                pltpu.make_async_copy(ins[k], landed.at[lax.bitwise_xor(z, k)], sems.at[k])
            )
        run_copies(copies)
        for k in range(ctx):
            joined[:, k * group : (k + 1) * group] = landed[k].reshape(2 * local, group)
        for tile in range(width // 256):
            columns = slice(tile * 256, (tile + 1) * 256)
            halves_out(dot(joined[...], buffer[:, columns]), own, other, columns, local)

    return call(
        kernel,
        [shape((local, width), F32), shape((local, width), BF), shape((2 * local, half), BF)],
        [VM] * 3,
        [
            pltpu.VMEM((half, width), BF),
            pltpu.VMEM((ctx, 2, local, group), BF),
            pltpu.SemaphoreType.DMA((ctx + pieces,)),
        ],
        [*slabs, *weight.arrays],
        [ANY] * (ctx + pieces),
        2 * 2 * local * half * width,
        24,
    )


def join_norm(base, own, other, gain):
    local, width = base.shape
    fresh = own is not None

    def kernel(*refs):
        if fresh:
            base_ref, own_ref, other_ref, gain_ref, sum_ref, low_ref = refs
            total = base_ref[...].astype(F32) + own_ref[...] + other_ref[...].astype(F32)
            sum_ref[...] = total
        else:
            base_ref, gain_ref, low_ref = refs
            total = base_ref[...].astype(F32)
        factor = lax.rsqrt(jnp.mean(total * total, axis=1, keepdims=True) + EPSILON)
        low_ref[...] = (total * factor * gain_ref[...].astype(F32)).astype(BF)

    outs = [shape((local, width), BF)]
    args = [base, gain]
    if fresh:
        outs = [shape((local, width), F32)] + outs
        args = [base, own, other, gain]
    return call(
        kernel, outs, [VM] * len(outs), [], args, [VM] * len(args), 8 * local * width, 16
    )


def gate_up(n_own, n_other, weight):
    local, width = n_own.shape
    hidden2 = weight.arrays[0].shape[1]
    hidden = hidden2 // 2
    pieces = len(weight.arrays)
    plan = weight.plan

    def kernel(*refs):
        own, other = refs[:2]
        w_refs = refs[2 : 2 + pieces]
        active, kept, buffer, tokens, sems = refs[2 + pieces :]
        copies = weight_copies(plan, w_refs, buffer, sems, 0)
        for copy in copies:
            copy.start()
        tokens[:local] = own[...]
        tokens[local:] = other[...]
        for copy in copies:
            copy.wait()

        def span_step(base, count):
            here, there = pl.ds(base, count), pl.ds(hidden + base, count)
            gate = dot(tokens[...], buffer[:, here])
            up = dot(tokens[...], buffer[:, there])
            kept[:, here] = gate.astype(BF)
            kept[:, there] = up.astype(BF)
            active[:, here] = (gate * jax.nn.sigmoid(gate) * up).astype(BF)

        def step(tile, carry):
            span_step(pl.multiple_of(tile * 256, 128), 256)
            return carry

        lax.fori_loop(0, hidden // 256, step, 0)
        if hidden % 256:
            span_step(hidden // 256 * 256, hidden % 256)

    return call(
        kernel,
        [shape((2 * local, hidden), BF), shape((2 * local, hidden2), BF)],
        [VM] * 2,
        [
            pltpu.VMEM((width, hidden2), BF),
            pltpu.VMEM((2 * local, width), BF),
            pltpu.SemaphoreType.DMA((pieces,)),
        ],
        [n_own, n_other, *weight.arrays],
        [VM] * 2 + [ANY] * pieces,
        2 * 2 * local * width * hidden2,
        40,
    )


def down(active, weight):
    tokens, hidden = active.shape
    local = tokens // 2
    width = weight.arrays[0].shape[1]
    pieces = len(weight.arrays)
    plan = weight.plan

    def kernel(*refs):
        left = refs[0]
        w_refs = refs[1 : 1 + pieces]
        own, other, buffer, sems = refs[1 + pieces :]
        run_copies(weight_copies(plan, w_refs, buffer, sems, 0))

        def step(tile, carry):
            columns = pl.ds(pl.multiple_of(tile * 256, 256), 256)
            halves_out(dot(left[...], buffer[:, columns]), own, other, columns, local)
            return carry

        lax.fori_loop(0, width // 256, step, 0)

    return call(
        kernel,
        [shape((local, width), F32), shape((local, width), BF)],
        [VM] * 2,
        [pltpu.VMEM((hidden, width), BF), pltpu.SemaphoreType.DMA((pieces,))],
        [active, *weight.arrays],
        [VM] + [ANY] * pieces,
        2 * tokens * hidden * width,
        24,
    )


def mlp_back(e_own, e_other, kept, gu_weight, down_weight):
    local, width = e_own.shape
    hidden2 = kept.shape[1]
    hidden = hidden2 // 2
    pieces = len(gu_weight.arrays)
    more = len(down_weight.arrays)
    gu_plan, down_plan = gu_weight.plan, down_weight.plan

    def kernel(*refs):
        e_one, e_two, kept_ref = refs[:3]
        gu_refs = refs[3 : 3 + pieces]
        down_refs = refs[3 + pieces : 3 + pieces + more]
        grads, own, other, gu, wd, tokens, sems = refs[3 + pieces + more :]
        first = weight_copies(down_plan, down_refs, wd, sems, pieces)
        second = weight_copies(gu_plan, gu_refs, gu, sems, 0)
        for copy in first + second:
            copy.start()
        tokens[:local] = e_one[...]
        tokens[local:] = e_two[...]
        for copy in first:
            copy.wait()

        def span_step(base, count):
            here, there = pl.ds(base, count), pl.ds(hidden + base, count)
            flow = dot_nt(tokens[...], wd[here, :])
            gate = kept_ref[:, here].astype(F32)
            up = kept_ref[:, there].astype(F32)
            sig = jax.nn.sigmoid(gate)
            grads[:, here] = (flow * up * sig * (1.0 + gate * (1.0 - sig))).astype(BF)
            grads[:, there] = (flow * gate * sig).astype(BF)

        def step(tile, carry):
            span_step(pl.multiple_of(tile * 256, 128), 256)
            return carry

        lax.fori_loop(0, hidden // 256, step, 0)
        if hidden % 256:
            span_step(hidden // 256 * 256, hidden % 256)
        for copy in second:
            copy.wait()

        def back_step(tile, carry):
            rows = pl.ds(pl.multiple_of(tile * 256, 256), 256)
            halves_out(dot_nt(grads[...], gu[rows, :]), own, other, rows, local)
            return carry

        lax.fori_loop(0, width // 256, back_step, 0)

    return call(
        kernel,
        [
            shape((2 * local, hidden2), BF),
            shape((local, width), F32),
            shape((local, width), BF),
        ],
        [VM] * 3,
        [
            pltpu.VMEM((width, hidden2), BF),
            pltpu.VMEM((hidden, width), BF),
            pltpu.VMEM((2 * local, width), BF),
            pltpu.SemaphoreType.DMA((pieces + more,)),
        ],
        [e_own, e_other, kept, *gu_weight.arrays, *down_weight.arrays],
        [VM] * 3 + [ANY] * (pieces + more),
        2 * 2 * local * width * hidden * 3,
        48,
    )


def norm_back(stream, own, other, gain, grad):
    local, width = stream.shape

    def kernel(x_ref, own_ref, other_ref, gain_ref, grad_ref, out_ref, low_ref, gain_out):
        x = x_ref[...].astype(F32)
        factor = lax.rsqrt(jnp.mean(x * x, axis=1, keepdims=True) + EPSILON)
        flow = own_ref[...] + other_ref[...].astype(F32)
        scaled = flow * gain_ref[...].astype(F32)
        gain_out[...] = jnp.sum(flow * x * factor, axis=0, keepdims=True)
        mean_term = jnp.mean(scaled * x, axis=1, keepdims=True)
        result = (
            grad_ref[...].astype(F32)
            + factor * scaled
            - x * (factor * factor * factor * mean_term)
        )
        out_ref[...] = result
        low_ref[...] = result.astype(BF)

    return call(
        kernel,
        [shape((local, width), F32), shape((local, width), BF), shape((1, width), F32)],
        [VM] * 3,
        [],
        [stream, own, other, gain, grad],
        [VM] * 5,
        12 * local * width,
        24,
    )


def mix_back(f_own, f_other, weight, ctx):
    local, width = f_own.shape
    half = width // 2
    group = half // ctx
    pieces = len(weight.arrays)
    plan = weight.plan

    def kernel(*refs):
        own, other = refs[:2]
        w_refs = refs[2 : 2 + pieces]
        slabs = refs[2 + pieces : 2 + pieces + ctx]
        buffer, tokens, slab, sems, out_sems = refs[2 + pieces + ctx :]
        copies = weight_copies(plan, w_refs, buffer, sems, 0)
        for copy in copies:
            copy.start()
        tokens[:local] = own[...]
        tokens[local:] = other[...]
        for copy in copies:
            copy.wait()
        for tile in range(half // 256):
            flow = dot_nt(tokens[...], buffer[tile * 256 : (tile + 1) * 256, :]).astype(BF)
            for part in range(256 // group):
                slab[tile * 256 // group + part] = flow[
                    :, part * group : (part + 1) * group
                ].reshape(2, local, group)
        z = lax.axis_index("ctx")
        run_copies(
            [
                pltpu.make_async_copy(slab.at[lax.bitwise_xor(z, k)], slabs[k], out_sems.at[k])
                for k in range(ctx)
            ]
        )

    return call(
        kernel,
        [shape((2, local, group), BF)] * ctx,
        [ANY] * ctx,
        [
            pltpu.VMEM((half, width), BF),
            pltpu.VMEM((2 * local, width), BF),
            pltpu.VMEM((ctx, 2, local, group), BF),
            pltpu.SemaphoreType.DMA((pieces,)),
            pltpu.SemaphoreType.DMA((ctx,)),
        ],
        [f_own, f_other, *weight.arrays],
        [VM] * 2 + [ANY] * pieces,
        2 * 2 * local * half * width,
        24,
    )


def attend_back(slabs, grad_slabs, start_row, tables, carried):
    ctx = len(grad_slabs)
    _, local, group = grad_slabs[0].shape
    span = ctx * local
    parts = len(slabs)
    heads = group // HD
    first = carried is not None

    def kernel(*refs):
        starts, cos, low, high = refs[:4]
        at = 4
        carry_in = None
        if first:
            carry_in = refs[at]
            at += 1
        ins = refs[at : at + parts]
        at += parts
        grads = refs[at : at + ctx]
        outs = refs[at + ctx : at + 2 * ctx]
        at += 2 * ctx
        carry_out = None
        if not first:
            carry_out = refs[at]
            at += 1
        whole, flow_in, slab, key_sum, value_sum, sems, out_sems = refs[at:]
        z = lax.axis_index("ctx")
        copies = []
        if parts == 1:
            copies.append(pltpu.make_async_copy(ins[0], whole, sems.at[0]))
        for k in range(ctx):
            to = pl.ds(pl.multiple_of(lax.bitwise_xor(z, k) * local, 16), local)
            if parts > 1:
                copies.append(
                    pltpu.make_async_copy(ins[k], whole.at[:, :, to, :], sems.at[k])
                )
            copies.append(
                pltpu.make_async_copy(grads[k], flow_in.at[:, to, :], sems.at[ctx + k])
            )
        run_copies(copies)
        lane = lax.broadcasted_iota(jnp.int32, (1, group), 1) // HD
        line = lax.broadcasted_iota(jnp.int32, (group, 1), 0) // HD

        def row_step(row, carry):
            key_sum[...] = jnp.zeros_like(key_sum)
            value_sum[...] = jnp.zeros_like(value_sum)
            key_turned = whole[1, row].astype(F32).T.astype(BF)
            for block in range(ctx):
                keys = (block + 1) * local
                here = slice(block * local, keys)
                query = whole[0, row, here, :] * SCORE_SCALE
                grad = flow_in[row, here, :]
                key = whole[1, row, :keys, :]
                value = whole[2, row, :keys, :]
                k_at = lax.broadcasted_iota(jnp.int32, (keys, local), 0)
                q_at = lax.broadcasted_iota(jnp.int32, (keys, local), 1) + block * local
                allowed = (k_at <= q_at) & (k_at >= starts[row, :, here])
                turned = None
                for head in range(heads):
                    mine = lane == head
                    q_head = jnp.where(mine, query, jnp.zeros_like(query))
                    g_head = jnp.where(mine, grad, jnp.zeros_like(grad))
                    scores = jnp.where(allowed, dot_nt(key, q_head), MASK_FILL)
                    top = jnp.max(scores, axis=0, keepdims=True)
                    powers = jnp.exp(scores - top)
                    total = jnp.sum(powers, axis=0, keepdims=True)
                    probs = powers * (1.0 / total)
                    grad_probs = dot_nt(value, g_head)
                    delta = jnp.sum(probs * grad_probs, axis=0, keepdims=True)
                    grad_scores = (probs * (grad_probs - delta)).astype(BF)
                    value_sum[:keys] += dot(probs.astype(BF), g_head)
                    key_sum[:keys] += dot(grad_scores, q_head)
                    part = dot(key_turned[:, :keys], grad_scores)
                    turned = part if turned is None else jnp.where(line == head, part, turned)
                grad_query = turned.T * SCORE_SCALE
                slab[block, 0, row] = rope(
                    grad_query, cos[row, here, :], -low[row, here, :], -high[row, here, :]
                ).astype(BF)
            for block in range(ctx):
                here = slice(block * local, (block + 1) * local)
                slab[block, 1, row] = rope(
                    key_sum[here, :], cos[row, here, :], -low[row, here, :], -high[row, here, :]
                ).astype(BF)
                if first:
                    total_value = value_sum[here, :] + carry_in[row, here, :]
                else:
                    total_value = 0.5 * value_sum[here, :]
                    carry_out[row, here, :] = total_value
                slab[block, 2, row] = total_value.astype(BF)
            return carry

        lax.fori_loop(0, 2, row_step, 0)
        run_copies(
            [
                pltpu.make_async_copy(slab.at[lax.bitwise_xor(z, k)], outs[k], out_sems.at[k])
                for k in range(ctx)
            ]
        )

    args = [start_row, *tables]
    specs = [VM] * 4
    outs = [shape((3, 2, local, group), BF)] * ctx
    out_specs = [ANY] * ctx
    if first:
        args.append(carried)
        specs.append(VM)
    else:
        outs.append(shape((2, span, group), F32))
        out_specs.append(VM)
    got = call(
        kernel,
        outs,
        out_specs,
        [
            pltpu.VMEM((3, 2, span, group), BF),
            pltpu.VMEM((2, span, group), BF),
            pltpu.VMEM((ctx, 3, 2, local, group), BF),
            pltpu.VMEM((span, group), F32),
            pltpu.VMEM((span, group), F32),
            pltpu.SemaphoreType.DMA((2 * ctx,)),
            pltpu.SemaphoreType.DMA((ctx,)),
        ],
        [*args, *slabs, *grad_slabs],
        specs + [ANY] * (parts + ctx),
        2 * 5 * 2 * heads * span * span * 128,
        48,
    )
    return got[:ctx], (None if first else got[ctx])


def project_back(slabs, weight):
    ctx = len(slabs)
    _, _, local, group = slabs[0].shape
    half = ctx * group
    width = 2 * half
    pieces = len(weight.arrays)
    plan = weight.plan

    def kernel(*refs):
        ins = refs[:ctx]
        w_refs = refs[ctx : ctx + pieces]
        own, other, joined, buffer, landed, sems = refs[ctx + pieces :]
        z = lax.axis_index("ctx")
        copies = weight_copies(plan, w_refs, buffer, sems, ctx)
        for k in range(ctx):
            copies.append(
                pltpu.make_async_copy(ins[k], landed.at[lax.bitwise_xor(z, k)], sems.at[k])
            )
        run_copies(copies)
        for k in range(ctx):
            for kind in range(3):
                base = kind * half + k * group
                joined[:, base : base + group] = landed[k, kind].reshape(2 * local, group)

        def step(tile, carry):
            rows = pl.ds(pl.multiple_of(tile * 256, 256), 256)
            halves_out(dot_nt(joined[...], buffer[rows, :]), own, other, rows, local)
            return carry

        lax.fori_loop(0, width // 256, step, 0)

    return call(
        kernel,
        [
            shape((local, width), F32),
            shape((local, width), BF),
            shape((2 * local, 3 * half), BF),
        ],
        [VM] * 3,
        [
            pltpu.VMEM((width, 3 * half), BF),
            pltpu.VMEM((ctx, 3, 2, local, group), BF),
            pltpu.SemaphoreType.DMA((ctx + pieces,)),
        ],
        [*slabs, *weight.arrays],
        [ANY] * (ctx + pieces),
        2 * 2 * local * 3 * half * width,
        40,
    )


def weight_grad(left, right, chips):
    lefts, rights = list(left), list(right)
    tall = lefts[0].shape[1]
    wide = rights[0].shape[1]
    tokens = lefts[0].shape[0] * len(lefts)
    rows = tall // chips
    halved = wide // 2
    split = chips == 4

    def kernel(*refs):
        l_refs = refs[: len(lefts)]
        r_refs = refs[len(lefts) : len(lefts) + len(rights)]
        at = len(lefts) + len(rights)
        count = 4 if split else chips
        outs = refs[at : at + count]
        grads, l_buf, r_buf, sems = refs[at + count :]
        if len(lefts) == 2:
            l_buf[: tokens // 2] = l_refs[0][...]
            l_buf[tokens // 2 :] = l_refs[1][...]
            l_now = l_buf
        else:
            l_now = l_refs[0]
        if len(rights) == 2:
            r_buf[: tokens // 2] = r_refs[0][...]
            r_buf[tokens // 2 :] = r_refs[1][...]
            r_now = r_buf
        else:
            r_now = r_refs[0]

        def tile_step(base, size):
            turned = l_now[:, pl.ds(base, size)]
            for start in range(0, wide, 512):
                stop = min(start + 512, wide)
                grads[pl.ds(base, size), start:stop] = dot_tn(
                    turned, r_now[:, start:stop]
                ).astype(BF)

        def step(tile, carry):
            tile_step(pl.multiple_of(tile * 256, 256), 256)
            return carry

        lax.fori_loop(0, tall // 256, step, 0)
        if tall % 256:
            tile_step(tall // 256 * 256, tall % 256)
        chip = chip_index()

        def block(k):
            return pl.ds(pl.multiple_of(lax.bitwise_xor(chip, k) * rows, 16), rows)

        copies = []
        if split:
            for which, order in enumerate(((1, 3), (0, 2), (2, 3), (0, 1))):
                columns = pl.ds((which // 2) * halved, halved)
                for slot, k in enumerate(order):
                    copies.append(
                        pltpu.make_async_copy(
                            grads.at[block(k), columns],
                            outs[which].at[slot],
                            sems.at[2 * which + slot],
                        )
                    )
        else:
            for k in range(chips):
                copies.append(
                    pltpu.make_async_copy(grads.at[block(k), :], outs[k], sems.at[k])
                )
        run_copies(copies)

    if split:
        outs = [shape((2, rows, halved), BF)] * 4
    else:
        outs = [shape((rows, wide), BF)] * chips
    small = (16, 128)
    return call(
        kernel,
        outs,
        [ANY] * len(outs),
        [
            pltpu.VMEM((tall, wide), BF),
            pltpu.VMEM((tokens, tall) if len(lefts) == 2 else small, BF),
            pltpu.VMEM((tokens, wide) if len(rights) == 2 else small, BF),
            pltpu.SemaphoreType.DMA((8 if split else chips,)),
        ],
        [*lefts, *rights],
        [VM] * (len(lefts) + len(rights)),
        2 * tokens * tall * wide,
        48,
    )


class Link:
    def __init__(self, source, target, arriving, sems, slot, axis, bit):
        device = {axis: lax.bitwise_xor(lax.axis_index(axis), bit)}

        def make(to):
            return pltpu.make_async_remote_copy(
                src_ref=source,
                dst_ref=to,
                send_sem=sems.at[0, slot],
                recv_sem=sems.at[1, slot],
                device_id=device,
                device_id_type=pl.DeviceIdType.MESH,
            )

        self.out = make(target)
        self.into = make(arriving)
        self.flying = False

    def start(self):
        self.out.start()
        self.flying = True
        return self

    def arrived(self):
        self.into.wait_recv()

    def sent(self):
        if self.flying:
            self.out.wait_send()
        self.flying = False


def enter(fsdp_bits, ctx_bits):
    barrier = pltpu.get_barrier_semaphore()
    for axis, bits in (("fsdp", fsdp_bits), ("ctx", ctx_bits)):
        for bit in bits:
            pl.semaphore_signal(
                barrier,
                inc=1,
                device_id={axis: lax.bitwise_xor(lax.axis_index(axis), bit)},
                device_id_type=pl.DeviceIdType.MESH,
            )
    pl.semaphore_wait(barrier, len(fsdp_bits) + len(ctx_bits))


def rms(total, gain):
    factor = lax.rsqrt(jnp.mean(total * total, axis=1, keepdims=True) + EPSILON)
    return (total * factor * gain).astype(BF)


def forward_pass(tokens, doc_lengths, gains, w_qkv, w_out, w_gate, w_up, w_down):
    local, width = tokens.shape
    layers, block, _ = w_qkv.shape
    hidden = w_gate.shape[2]
    hid = hidden // 2
    hid_block = w_down.shape[1]
    half = width // 2
    shards, ctx = lax.axis_size("fsdp"), lax.axis_size("ctx")
    chips = shards // 2
    group = half // ctx
    span = ctx * local
    heads = group // HD
    both = 2 * local
    documents = doc_lengths.shape[1]
    lengths = jnp.zeros((8, 128), jnp.int32).at[:documents].set(doc_lengths[0][:, None])
    gain_rows = jnp.zeros((8, block), F32).at[: 2 * layers].set(
        gains.reshape(2 * layers, block).astype(F32)
    )

    def kernel(*refs):
        (tok, lens, gain_in, qkv_in, out_in, gate_in, up_in, down_in) = refs[:8]
        (wq_o, wo_o, wg_o, wd_o, n1_o, n2_o, whole_o, mix_o, mid_o, stream_o) = refs[8:18]
        (act_o, kept_o, gain_o, cos_o, low_o, high_o, start_o, final_o) = refs[18:26]
        (wq, wo, wg, wd, qkv_raw, gu_raw, q_stage, g_stage) = refs[26:34]
        (n1, n2, whole, slab, mixed, landed, value, mix, mid, stream) = refs[34:44]
        (act, kept, part, other, got, gbuf, lens_all, cos, low, high, start) = refs[44:55]
        (sems, local_sems, save_sems) = refs[55:]
        f = lax.axis_index("fsdp")
        z = lax.axis_index("ctx")
        core = lax.rem(f, 2)
        chip = f // 2
        flights = []
        saves = []

        def link(source, target, arriving, axis, bit):
            made = Link(source, target, arriving, sems, len(flights), axis, bit)
            flights.append(made)
            return made

        def save(source, target):
            copy = pltpu.make_async_copy(source, target, save_sems.at[len(saves)])
            copy.start()
            saves.append(copy)
            return len(saves) - 1

        def saved(number):
            if saves[number] is not None:
                saves[number].wait()
            saves[number] = None

        def rows(index, count):
            return pl.ds(pl.multiple_of(index * count, 16), count)

        def fx(bit):
            return lax.bitwise_xor(f, bit)

        def cx(bit):
            return lax.bitwise_xor(chip, bit)

        class Halved:
            def __init__(self, buffer, stage):
                def at(index):
                    return buffer.at[rows(index, block), :]

                self.first = [
                    link(stage, at(f), at(fx(bit)), "fsdp", bit) for bit in (1, 3, 5)
                ] + [link(at(f), at(f), at(fx(bit)), "fsdp", bit) for bit in (2, 4)]
                over_y, over_x, far = 2 * cx(1), 2 * cx(2) + 1, 2 * cx(3)
                self.second = [
                    link(at(over_y), at(over_y), at(far), "fsdp", 4),
                    link(at(over_x), at(over_x), at(far + 1), "fsdp", 2),
                ]

        class Rowed:
            def __init__(self, buffer, source, count):
                small = count // 2

                def at(index):
                    return buffer.at[rows(index, count), :]

                def side(index, which):
                    begin = pl.multiple_of(index * count + which * small, 16)
                    return buffer.at[pl.ds(begin, small), :]

                self.first = [
                    link(source, at(chip), at(cx(bit // 2)), "fsdp", bit) for bit in (2, 4)
                ]
                self.second = [
                    link(side(cx(1), 0), side(cx(1), 0), side(cx(3), 0), "fsdp", 4),
                    link(side(cx(2), 1), side(cx(2), 1), side(cx(3), 1), "fsdp", 2),
                ]

        def begin(weight):
            for one in weight.first:
                one.start()

        def forward(weight):
            for one in weight.first:
                one.arrived()
            for one in weight.second:
                one.start()

        def finish(weight):
            for one in weight.second:
                one.arrived()

        q_of = [Halved(wq.at[n], q_stage.at[n]) for n in range(layers)]
        g_of = [Halved(wg.at[n], g_stage.at[n]) for n in range(layers)]
        o_of = [Rowed(wo.at[n], out_in.at[n], block) for n in range(layers)]
        d_of = [Rowed(wd.at[n], down_in.at[n], hid_block) for n in range(layers)]

        def local_copy(source, target, slot):
            copy = pltpu.make_async_copy(source, target, local_sems.at[slot])
            copy.start()
            return copy

        def choose(first, second):
            return lax.select(core == 0, first, second)

        def stage_qkv(n):
            for kind in range(3):
                for j in range(chips):
                    at = kind * width + 2 * j * block
                    even = qkv_raw[:, at : at + block]
                    odd = qkv_raw[:, at + block : at + 2 * block]
                    to = kind * half + j * block
                    wq[n, rows(f, block), to : to + block] = choose(even, odd)
                    q_stage[n, :, to : to + block] = choose(odd, even)

        def stage_gu(n):
            for which in range(2):
                sets = []
                for lane_core in range(2):
                    parts = []
                    for j in range(chips):
                        at = (2 * j + lane_core) * hid_block
                        parts.append(gu_raw[which, :, at : at + hid_block])
                    sets.append(jnp.concatenate(parts, axis=1))
                to = slice(which * hid, (which + 1) * hid)
                wg[n, rows(f, block), to] = choose(sets[0], sets[1])
                g_stage[n, :, to] = choose(sets[1], sets[0])

        def load(n):
            return [
                local_copy(qkv_in.at[n], qkv_raw, 0),
                local_copy(gate_in.at[n], gu_raw.at[0], 1),
                local_copy(up_in.at[n], gu_raw.at[1], 2),
            ]

        loads = load(0)
        mine = []
        for n in range(layers):
            mine.append(local_copy(out_in.at[n], wo.at[n, rows(chip, block), :], 3 + n))
            mine.append(
                local_copy(down_in.at[n], wd.at[n, rows(chip, hid_block), :], 3 + layers + n)
            )
        spare = 3 + 2 * layers
        loads[0].wait()
        stage_qkv(0)
        gain_links = [
            link(gain_in, gbuf.at[f], gbuf.at[fx(bit)], "fsdp", bit) for bit in range(1, shards)
        ]
        lens_link = link(lens, lens_all.at[1], lens_all.at[1], "fsdp", 1)
        enter(list(range(1, shards)), list(range(1, ctx)))
        for one in gain_links:
            one.start()
        lens_link.start()
        begin(q_of[0])
        gbuf[f] = gain_in[...]
        lens_all[0] = lens[...]
        for copy in mine + loads[1:]:
            copy.wait()
        stage_gu(0)
        loads = load(1)
        for one in gain_links:
            one.arrived()

        def gain_row(n):
            return jnp.concatenate([gbuf[s, n : n + 1, :] for s in range(shards)], axis=1)

        for n in range(2 * layers):
            gain_o[n : n + 1, :] = gain_row(n)

        def norm_link(buffer, n):
            upper = buffer.at[n, pl.ds(local, local), :]
            return link(buffer.at[n, pl.ds(0, local), :], upper, upper, "fsdp", 1)

        n1[0, :local] = rms(tok[...].astype(F32), gain_row(0))
        norm_now = norm_link(n1, 0).start()

        lens_link.arrived()
        pairs = HD // 2
        lane = lax.broadcasted_iota(jnp.int32, (1, 128), 1)
        frequency = jnp.exp((-math.log(10000.0) / pairs) * lax.rem(lane, pairs).astype(F32))
        is_low = lax.rem(lane, HD) < pairs

        def table_step(index, carry):
            r = index // ctx
            piece = lax.rem(index, ctx)
            to = rows(piece, local)
            at = lax.broadcasted_iota(jnp.int32, (local, 128), 0) + piece * local
            first = jnp.zeros((local, 128), jnp.int32)
            end = jnp.zeros((1, 128), jnp.int32)
            for j in range(documents):
                end = end + lens_all[r, j : j + 1, :]
                first = jnp.where(at >= end, end, first)
            start[r, to, :] = first
            angle = (at - first).astype(F32) * frequency
            sine = jnp.sin(angle)
            cos[r, to, :] = jnp.cos(angle)
            low[r, to, :] = jnp.where(is_low, -sine, 0.0)
            high[r, to, :] = jnp.where(is_low, 0.0, sine)
            return carry

        lax.fori_loop(0, 2 * ctx, table_step, 0)
        here_rows = rows(z, local)
        for source, target in ((cos, cos_o), (low, low_o), (high, high_o), (start, start_o)):
            save(source, target)
        lane_head = lax.broadcasted_iota(jnp.int32, (1, group), 1) // HD

        def do_project(n):
            for tile in range(3 * half // 256):
                acc = dot(n1[n], wq[n, :, tile * 256 : (tile + 1) * 256])
                kind = tile * 256 // half
                for sub in range(256 // group):
                    column = tile * 256 - kind * half + sub * group
                    for r in range(2):
                        x = acc[r * local : (r + 1) * local, sub * group : (sub + 1) * group]
                        at = (slice(r * local, (r + 1) * local), slice(column, column + group))
                        if kind < 2:
                            x = rope(
                                x, cos[r, here_rows, :], low[r, here_rows, :], high[r, here_rows, :]
                            )
                        elif n > 0:
                            x = 0.5 * x + 0.5 * value[at].astype(F32)
                        x = x.astype(BF)
                        if kind == 2 and n == 0:
                            value[at] = x
                        slab[column // group, kind, r] = x

        def slab_links(n):
            made = []
            for bit in range(1, ctx):
                to = lax.bitwise_xor(z, bit)
                made.append(
                    link(
                        slab.at[to],
                        whole.at[n, :, :, rows(z, local), :],
                        whole.at[n, :, :, rows(to, local), :],
                        "ctx",
                        bit,
                    )
                )
            return made

        def mixed_links(n):
            made = []
            for bit in range(1, ctx):
                to = lax.bitwise_xor(z, bit)
                made.append(link(mixed.at[n, to], landed.at[n, z], landed.at[n, to], "ctx", bit))
            return made

        def do_attend(n):
            def row_step(r, carry):
                for piece in range(ctx):
                    keys = (piece + 1) * local
                    here = slice(piece * local, keys)
                    query = whole[n, 0, r, here, :] * SCORE_SCALE
                    key = whole[n, 1, r, :keys, :]
                    val = whole[n, 2, r, :keys, :]
                    k_at = lax.broadcasted_iota(jnp.int32, (local, keys), 1)
                    q_at = lax.broadcasted_iota(jnp.int32, (local, keys), 0) + piece * local
                    allowed = (k_at <= q_at) & (k_at >= start[r, here, 0:1])
                    result = None
                    for head in range(heads):
                        q_head = jnp.where(lane_head == head, query, jnp.zeros_like(query))
                        scores = jnp.where(allowed, dot_nt(q_head, key), MASK_FILL)
                        top = jnp.max(scores, axis=1, keepdims=True)
                        powers = jnp.exp(scores - top)
                        total = jnp.sum(powers, axis=1, keepdims=True)
                        probs = (powers * (1.0 / total)).astype(BF)
                        out = dot(probs, val)
                        result = out if head == 0 else jnp.where(lane_head == head, out, result)
                    mixed[n, piece, r] = result.astype(BF)
                return carry

            lax.fori_loop(0, 2, row_step, 0)

        last_sum = [None]

        def partial_sums(n, which, left, weight):
            if last_sum[0] is not None:
                last_sum[0].sent()

            def step(tile, carry):
                columns = rows(tile, 256)
                product = dot(left[...], weight[:, columns])
                part[:, columns] = product[:local]
                other[:, columns] = product[local:].astype(BF)
                return carry

            lax.fori_loop(0, width // 256, step, 0)
            to = got.at[n, which]
            last_sum[0] = link(other, to, to, "fsdp", 1).start()
            return last_sum[0]

        def gate_up(n):
            def span_step(base, count):
                here, there = pl.ds(base, count), pl.ds(hid + base, count)
                gate = dot(n2[n], wg[n, :, here])
                up = dot(n2[n], wg[n, :, there])
                kept[:, here] = gate.astype(BF)
                kept[:, there] = up.astype(BF)
                act[:, here] = (gate * jax.nn.sigmoid(gate) * up).astype(BF)

            def step(tile, carry):
                span_step(pl.multiple_of(tile * 256, 128), 256)
                return carry

            lax.fori_loop(0, hid // 256, step, 0)
            if hid % 256:
                span_step(hid // 256 * 256, hid % 256)

        slab_flights = []
        held = []
        for n in range(layers):
            if n == 0:
                forward(q_of[0])
                begin(o_of[0])
            finish(q_of[n])
            save(wq.at[n], wq_o.at[n])
            begin(g_of[n])
            norm_now.arrived()
            save(n1.at[n], n1_o.at[n])
            for one in slab_flights:
                one.sent()
            do_project(n)
            slab_flights = slab_links(n)
            for one in slab_flights:
                one.start()
            own = local_copy(slab.at[z], whole.at[n, :, :, here_rows, :], spare)
            if n == 0:
                for copy in loads:
                    copy.wait()
                stage_qkv(1)
                stage_gu(1)
            forward(o_of[n])
            finish(o_of[n])
            save(wo.at[n], wo_o.at[n])
            if n > 0:
                forward(g_of[n])
                begin(d_of[n])
            own.wait()
            for one in slab_flights:
                one.arrived()
            save(whole.at[n], whole_o.at[n])
            if n == 0:
                forward(g_of[n])
                begin(d_of[n])
            do_attend(n)
            back = mixed_links(n)
            for one in back:
                one.start()
            own = local_copy(mixed.at[n, z], landed.at[n, z], spare)
            if n == 0:
                begin(q_of[1])
            own.wait()
            for one in back:
                one.arrived()
            for k in range(ctx):
                mix[n, :, k * group : (k + 1) * group] = landed[n, k].reshape(both, group)
            save(mix.at[n], mix_o.at[n])
            sums = partial_sums(n, 0, mix.at[n], wo.at[n])
            forward(d_of[n])
            base = tok[...].astype(F32) if n == 0 else stream[...]
            sums.arrived()
            total = base + part[...] + got[n, 0].astype(F32)
            mid[n] = total
            n2[n, :local] = rms(total, gain_row(2 * n + 1))
            norm_now = norm_link(n2, n).start()
            save(mid.at[n], mid_o.at[n])
            finish(g_of[n])
            save(wg.at[n], wg_o.at[n])
            for number in held:
                saved(number)
            norm_now.arrived()
            save(n2.at[n], n2_o.at[n])
            gate_up(n)
            held = [save(act, act_o.at[n]), save(kept, kept_o.at[n])]
            if n == 0:
                forward(q_of[1])
                begin(o_of[1])
            finish(d_of[n])
            save(wd.at[n], wd_o.at[n])
            sums = partial_sums(n, 1, act, wd.at[n])
            sums.arrived()
            total = mid[n] + part[...] + got[n, 1].astype(F32)
            if n + 1 < layers:
                stream[...] = total
                n1[n + 1, :local] = rms(total, gain_row(2 * n + 2))
                norm_now = norm_link(n1, n + 1).start()
                save(stream, stream_o)
            else:
                final_o[...] = total.astype(BF)
        for one in flights:
            one.sent()
        for number in range(len(saves)):
            saved(number)

    def stacked(*dims):
        return (layers, *dims)

    outs = [
        shape(stacked(width, 3 * half), BF),
        shape(stacked(half, width), BF),
        shape(stacked(width, 2 * hid), BF),
        shape(stacked(hid, width), BF),
        shape(stacked(both, width), BF),
        shape(stacked(both, width), BF),
        shape(stacked(3, 2, span, group), BF),
        shape(stacked(both, half), BF),
        shape(stacked(local, width), F32),
        shape((local, width), F32),
        shape(stacked(both, hid), BF),
        shape(stacked(both, 2 * hid), BF),
        shape((2 * layers, width), F32),
        shape((2, span, 128), F32),
        shape((2, span, 128), F32),
        shape((2, span, 128), F32),
        shape((2, span, 128), jnp.int32),
        shape((local, width), BF),
    ]
    out_specs = [ANY] * 18
    out_specs[12] = out_specs[17] = VM
    scratch = [
        pltpu.VMEM(stacked(width, 3 * half), BF),
        pltpu.VMEM(stacked(half, width), BF),
        pltpu.VMEM(stacked(width, 2 * hid), BF),
        pltpu.VMEM(stacked(hid, width), BF),
        pltpu.VMEM((block, 3 * width), BF),
        pltpu.VMEM((2, block, hidden), BF),
        pltpu.VMEM(stacked(block, 3 * half), BF),
        pltpu.VMEM(stacked(block, 2 * hid), BF),
        pltpu.VMEM(stacked(both, width), BF),
        pltpu.VMEM(stacked(both, width), BF),
        pltpu.VMEM(stacked(3, 2, span, group), BF),
        pltpu.VMEM((ctx, 3, 2, local, group), BF),
        pltpu.VMEM(stacked(ctx, 2, local, group), BF),
        pltpu.VMEM(stacked(ctx, 2, local, group), BF),
        pltpu.VMEM((both, half), BF),
        pltpu.VMEM(stacked(both, half), BF),
        pltpu.VMEM(stacked(local, width), F32),
        pltpu.VMEM((local, width), F32),
        pltpu.VMEM((both, hid), BF),
        pltpu.VMEM((both, 2 * hid), BF),
        pltpu.VMEM((local, width), F32),
        pltpu.VMEM((local, width), BF),
        pltpu.VMEM(stacked(2, local, width), BF),
        pltpu.VMEM((shards, 8, block), F32),
        pltpu.VMEM((2, 8, 128), jnp.int32),
        pltpu.VMEM((2, span, 128), F32),
        pltpu.VMEM((2, span, 128), F32),
        pltpu.VMEM((2, span, 128), F32),
        pltpu.VMEM((2, span, 128), jnp.int32),
        pltpu.SemaphoreType.DMA((2, 80)),
        pltpu.SemaphoreType.DMA((8,)),
        pltpu.SemaphoreType.DMA((32,)),
    ]
    return pl.pallas_call(
        kernel,
        out_shape=outs,
        in_specs=[VM] * 3 + [ANY] * 5,
        out_specs=out_specs,
        scratch_shapes=scratch,
        compiler_params=pltpu.CompilerParams(
            vmem_limit_bytes=62 * MIB, collective_id=0, has_side_effects=True
        ),
        cost_estimate=pl.CostEstimate(
            flops=14 * 10**9, bytes_accessed=60 * MIB, transcendentals=0
        ),
    )(tokens, lengths, gain_rows, w_qkv, w_out, w_gate, w_up, w_down)


def add_low(left, right):
    return (left.astype(F32) + right.astype(F32)).astype(BF)


def reduce_chips(blocks, chips):
    if chips != 4:
        total = blocks[0].astype(F32)
        for k in range(1, chips):
            total = total + swap(blocks[k], "fsdp", 2 * k).astype(F32)
        return total.astype(BF)
    send_x, keep_x, send_y, keep_y = blocks
    got_x = swap(send_x, "fsdp", 2)
    got_y = swap(send_y, "fsdp", 4)
    on_x = swap(add_low(keep_x[1], got_x[1]), "fsdp", 4)
    on_y = swap(add_low(keep_y[1], got_y[1]), "fsdp", 2)
    first = add_low(add_low(keep_x[0], got_x[0]), on_x)
    second = add_low(add_low(keep_y[0], got_y[0]), on_y)
    return jnp.concatenate([first, second], axis=1)


def reduce_line(block):
    if lax.axis_size("ctx") != 4:
        return lax.psum(block, "ctx")
    z = lax.axis_index("ctx")
    inner = (z == 1) | (z == 2)
    inward = lax.ppermute(block, "ctx", [(0, 1), (3, 2)])
    pair = jnp.where(inner, add_low(block, inward), block)
    across = lax.ppermute(pair, "ctx", [(1, 2), (2, 1)])
    total = add_low(pair, across)
    outward = lax.ppermute(total, "ctx", [(1, 0), (2, 3)])
    return jnp.where(inner, total, outward)


def own_rows(block):
    core = lax.axis_index("fsdp") % 2
    rows = block.shape[0] // 2
    mine = lax.dynamic_slice_in_dim(block, core * rows, rows)
    theirs = swap(lax.dynamic_slice_in_dim(block, (1 - core) * rows, rows), "fsdp", 1)
    low = jnp.where(core == 0, mine, theirs)
    high = jnp.where(core == 0, theirs, mine)
    return jnp.stack([low, high])


def chip_piece(mine, other):
    core = lax.axis_index("fsdp") % 2
    got = swap(other, "fsdp", 1)
    return jnp.where(
        core == 0, jnp.concatenate([mine, got]), jnp.concatenate([got, mine])
    )


def document_starts(lengths, index):
    ends = []
    total = jnp.int32(0)
    for j in range(lengths.shape[0]):
        total = total + lengths[j]
        ends.append(total)
    start = jnp.zeros_like(index)
    for end in ends:
        start = jnp.where(index >= end, end, start)
    return start


def rotary(positions):
    pairs = HD // 2
    lane = jnp.arange(128, dtype=jnp.int32)
    frequency = jnp.exp(-math.log(10000.0) * jnp.arange(pairs, dtype=F32) / pairs)
    angles = positions.astype(F32)[..., None] * frequency
    cosines = jnp.tile(jnp.cos(angles), 128 // pairs)
    sines = jnp.tile(jnp.sin(angles), 128 // pairs)
    low = jnp.where(lane % HD < pairs, -sines, 0.0)
    high = jnp.where(lane % HD >= pairs, sines, 0.0)
    return [cosines, low, high]


def body(tokens, doc_lengths, cotangent, gains, w_qkv, w_out, w_gate, w_up, w_down):
    _, local, width = tokens.shape
    layers = gains.shape[0]
    shards = lax.axis_size("fsdp")
    ctx = lax.axis_size("ctx")
    chips = shards // 2
    block = width // shards
    hidden = w_gate.shape[2]
    hidden_half = hidden // 2
    hidden_block = hidden // shards
    core = lax.axis_index("fsdp") % 2
    z = lax.axis_index("ctx")
    span = local * ctx

    def pick(array, axis, which):
        return lax.dynamic_index_in_dim(array, which, axis, keepdims=False)

    if chips == 4 and ctx == 4:
        saved = forward_pass(
            tokens[0], doc_lengths, gains, w_qkv, w_out, w_gate, w_up, w_down
        )
        wq, wo, wg, wd, n1, n2, whole, mix, mid, stream, act, kept_gu, gain_all = saved[:13]
        cosines, low_sine, high_sine, starts, out_low = saved[13:]
        head_tables = [cosines, low_sine, high_sine]
        start_row = starts[:, :, 0][:, None, :]
        qkv_weights, out_weights, gu_weights, down_weights = [
            [Pieces([w[layer]], None, 0) for layer in range(layers)] for w in (wq, wo, wg, wd)
        ]
        gain_rows = [
            [gain_all[2 * layer + n][None] for n in range(2)] for layer in range(layers)
        ]
        kept = [
            (
                tokens[0] if layer == 0 else stream,
                (n1[layer, :local], n1[layer, local:]),
                [whole[layer]],
                mix[layer],
                mid[layer],
                (n2[layer, :local], n2[layer, local:]),
                act[layer],
                kept_gu[layer],
            )
            for layer in range(layers)
        ]
        out_tokens = out_low[None]
    else:
        qkv_weights, out_weights, gu_weights, down_weights = [], [], [], []
        for layer in range(layers):
            qkv = w_qkv[layer].reshape(block, 3, chips, 2, block)
            sides = [pick(qkv, 3, which).reshape(block, -1) for which in (core, 1 - core)]
            qkv_weights.append(gather(chip_piece(*sides), chips))
            out_weights.append(gather(w_out[layer], chips))
            sides = []
            for which in (core, 1 - core):
                both = [
                    pick(w[layer].reshape(block, chips, 2, hidden_block), 2, which).reshape(
                        block, hidden_half
                    )
                    for w in (w_gate, w_up)
                ]
                sides.append(jnp.concatenate(both, axis=1))
            gu_weights.append(gather(chip_piece(*sides), chips))
            down_weights.append(gather(w_down[layer], chips))

        all_gains = lax.all_gather(gains, "fsdp", axis=2, tiled=True)
        gain_rows = [[all_gains[layer, n][None] for n in range(2)] for layer in range(layers)]

        index = jnp.arange(span, dtype=jnp.int32)
        lengths = [doc_lengths[0], swap(doc_lengths, "fsdp", 1)[0]]
        starts = jnp.stack([document_starts(row, index) for row in lengths])
        row_tables = rotary(index[None] - starts)
        here_tables = [lax.dynamic_slice_in_dim(t, z * local, local, axis=1) for t in row_tables]
        head_lanes = min(128, width // 2 // ctx)
        head_tables = [t[:, :, :head_lanes] for t in row_tables]
        start_column = starts[:, :, None]
        start_row = starts[:, None, :]

        def pair(array):
            return (array, swap(array, "fsdp", 1))

        stream = tokens[0]
        kept = []
        first_value = None
        (low,) = join_norm(stream, None, None, gain_rows[0][0])
        for layer in range(layers):
            normed = pair(low)
            slabs, first_value = project(
                *normed, here_tables, first_value, qkv_weights[layer], ctx, layer == layers - 1
            )
            slabs = exchange(slabs)
            mixed = exchange(attend(slabs, start_column))
            own, other, joined = mix_out(mixed, out_weights[layer])
            middle, low = join_norm(stream, own, swap(other, "fsdp", 1), gain_rows[layer][1])
            normed_two = pair(low)
            active, gu_kept = gate_up(*normed_two, gu_weights[layer])
            own, other = down(active, down_weights[layer])
            after = gain_rows[min(layer + 1, layers - 1)][0]
            kept.append((stream, normed, slabs, joined, middle, normed_two, active, gu_kept))
            stream, low = join_norm(middle, own, swap(other, "fsdp", 1), after)
        out_tokens = stream.astype(BF)[None]

    def pair(array):
        return (array, swap(array, "fsdp", 1))


    grad = cotangent[0]
    low = cotangent[0]
    carried = None
    gain_grads = [[None, None] for _ in range(layers)]
    done = [None] * layers
    for layer in reversed(range(layers)):
        stream, normed, slabs, joined, middle, normed_two, active, gu_kept = kept[layer]
        sent = pair(low)
        down_blocks = weight_grad([active], sent, chips)
        gu_grads, own, other = mlp_back(
            *sent, gu_kept, gu_weights[layer], down_weights[layer]
        )
        grad, low, gain_grads[layer][1] = norm_back(
            middle, own, swap(other, "fsdp", 1), gain_rows[layer][1], grad
        )
        gu_blocks = weight_grad(normed_two, [gu_grads], chips)
        mixed_back = pair(low)
        grad_slabs = exchange(mix_back(*mixed_back, out_weights[layer], ctx))
        out_blocks = weight_grad([joined], mixed_back, chips)
        grad_slabs, carry_out = attend_back(slabs, grad_slabs, start_row, head_tables, carried)
        carried = carry_out
        own, other, qkv_grads = project_back(exchange(grad_slabs), qkv_weights[layer])
        qkv_blocks = weight_grad(normed, [qkv_grads], chips)
        grad, low, gain_grads[layer][0] = norm_back(
            stream, own, swap(other, "fsdp", 1), gain_rows[layer][0], grad
        )
        down_sum = reduce_line(reduce_chips(down_blocks, chips)).astype(F32)
        gu_sum = own_rows(reduce_line(reduce_chips(gu_blocks, chips)))
        out_sum = reduce_line(reduce_chips(out_blocks, chips)).astype(F32)
        qkv_sum = own_rows(reduce_line(reduce_chips(qkv_blocks, chips)))
        qkv_sum = qkv_sum.reshape(2, block, 3, chips, block).transpose(1, 2, 3, 0, 4)
        qkv_sum = qkv_sum.reshape(block, 3 * width).astype(F32)
        gu_sum = gu_sum.reshape(2, block, 2, chips, hidden_block).transpose(2, 1, 3, 0, 4)
        gu_sum = gu_sum.reshape(2, block, hidden).astype(F32)
        done[layer] = (qkv_sum, out_sum, gu_sum[0], gu_sum[1], down_sum)

    gain_sum = jnp.stack([jnp.concatenate(rows) for rows in gain_grads])
    gain_sum = lax.psum_scatter(gain_sum, "fsdp", scatter_dimension=2, tiled=True)
    gain_sum = lax.psum(gain_sum, "ctx")
    stacked = [jnp.stack([done[layer][n] for layer in range(layers)]) for n in range(5)]
    return (out_tokens, grad[None], gain_sum, *stacked)


def solution(mesh):
    rows = P(None, "fsdp", None)
    tokens = P("fsdp", "ctx", None)
    gains = P(None, None, "fsdp")
    return jax.shard_map(
        body,
        mesh=mesh,
        in_specs=(tokens, P("fsdp", None), tokens, gains, rows, rows, rows, rows, rows),
        out_specs=(tokens, tokens, gains, rows, rows, rows, rows, rows),
        check_vma=False,
    )
```

```python
import math

import jax
import jax.numpy as jnp
from jax import lax
from jax.experimental import pallas as pl
from jax.experimental.pallas import tpu as pltpu
from jax.sharding import PartitionSpec as P

HEADS = 16
HD = 64
EPSILON = 1e-06
SCORE_SCALE = 0.125
MASK_FILL = -1e30
BF = jnp.bfloat16
F32 = jnp.float32
MIB = 1024 * 1024
ANY = pl.BlockSpec(memory_space=pl.ANY)
VM = pl.BlockSpec(memory_space=pltpu.VMEM)
NT = (((1,), (1,)), ((), ()))
TN = (((0,), (0,)), ((), ()))


def dot(left, right):
    return jnp.dot(left, right, preferred_element_type=F32)


def dot_nt(left, right):
    return lax.dot_general(left, right, NT, preferred_element_type=F32)


def dot_tn(left, right):
    return lax.dot_general(left, right, TN, preferred_element_type=F32)


def swap(array, axis, bit):
    size = lax.axis_size(axis)
    return lax.ppermute(array, axis, [(i, i ^ bit) for i in range(size)])


def call(kernel, outs, out_specs, scratch, args, in_specs, flops, vmem):
    nbytes = sum(a.size * a.dtype.itemsize for a in args)
    nbytes += sum(math.prod(o.shape) * o.dtype.itemsize for o in outs)
    return pl.pallas_call(
        kernel,
        out_shape=outs,
        in_specs=in_specs,
        out_specs=out_specs,
        scratch_shapes=scratch,
        compiler_params=pltpu.CompilerParams(vmem_limit_bytes=vmem * MIB),
        cost_estimate=pl.CostEstimate(flops=flops, bytes_accessed=nbytes, transcendentals=0),
    )(*args)


def shape(dims, kind):
    return jax.ShapeDtypeStruct(tuple(dims), kind)


def chip_index():
    return lax.axis_index("fsdp") // 2


def run_copies(copies):
    for copy in copies:
        copy.start()
    for copy in copies:
        copy.wait()


def weight_copies(plan, refs, buffer, sems, first):
    chip = chip_index()
    rows = plan[0][2]
    copies = []
    for number, ((k, offset, count), ref) in enumerate(zip(plan[1], refs)):
        start = pl.multiple_of(lax.bitwise_xor(chip, k) * rows + offset, 16)
        copies.append(
            pltpu.make_async_copy(
                ref, buffer.at[pl.ds(start, count), :], sems.at[first + number]
            )
        )
    return copies


class Pieces:
    def __init__(self, arrays, where, rows):
        self.arrays = arrays
        self.where = where
        self.rows = rows

    @property
    def plan(self):
        return ((0, 0, self.rows), self.where)


def gather(piece, chips):
    rows = piece.shape[0]
    if chips == 4:
        half = rows // 2
        from_x = swap(piece, "fsdp", 2)
        from_y = swap(piece, "fsdp", 4)
        far_one = swap(from_x[:half], "fsdp", 4)
        far_two = swap(from_y[half:], "fsdp", 2)
        return Pieces(
            [piece, from_x, from_y, far_one, far_two],
            [(0, 0, rows), (1, 0, rows), (2, 0, rows), (3, 0, half), (3, half, rows - half)],
            rows,
        )
    arrays = [piece] + [swap(piece, "fsdp", 2 * k) for k in range(1, chips)]
    return Pieces(arrays, [(k, 0, rows) for k in range(chips)], rows)


def rope(x, cosines, low_sine, high_sine):
    width = x.shape[-1]
    return (
        x * cosines
        + pltpu.roll(x, width - HD // 2, 1) * low_sine
        + pltpu.roll(x, HD // 2, 1) * high_sine
    )


def project(n_own, n_other, tables, first_value, weight, ctx, last):
    local, width = n_own.shape
    half = width // 2
    group = half // ctx
    pieces = len(weight.arrays)
    plan = weight.plan

    def kernel(*refs):
        own, other, cos, low, high = refs[:5]
        at = 5
        v_in = None
        if first_value is not None:
            v_in = refs[at]
            at += 1
        w_refs = refs[at : at + pieces]
        at += pieces
        slabs = refs[at : at + ctx]
        at += ctx
        v_out = None
        if first_value is None:
            v_out = refs[at]
            at += 1
        buffer, tokens, slab, sems, out_sems = refs[at:]
        copies = weight_copies(plan, w_refs, buffer, sems, 0)
        for copy in copies:
            copy.start()
        tokens[:local] = own[...]
        tokens[local:] = other[...]
        tables_now = [t[...].reshape(2 * local, 128) for t in (cos, low, high)]
        for copy in copies:
            copy.wait()
        for tile in range(3 * half // 256):
            acc = dot(tokens[...], buffer[:, tile * 256 : (tile + 1) * 256])
            kind = tile * 256 // half
            base = tile * 256 - kind * half
            for sub in range(2):
                x = acc[:, sub * 128 : (sub + 1) * 128]
                column = base + sub * 128
                if kind < 2:
                    x = rope(x, *tables_now)
                elif first_value is not None:
                    x = 0.5 * x + 0.5 * v_in[:, column : column + 128].astype(F32)
                x = x.astype(BF)
                if kind == 2 and v_out is not None:
                    v_out[:, column : column + 128] = x
                for part in range(128 // group):
                    slab[column // group + part, kind] = x[
                        :, part * group : (part + 1) * group
                    ].reshape(2, local, group)
        z = lax.axis_index("ctx")
        run_copies(
            [
                pltpu.make_async_copy(slab.at[lax.bitwise_xor(z, k)], slabs[k], out_sems.at[k])
                for k in range(ctx)
            ]
        )

    args = [n_own, n_other, *tables]
    specs = [VM] * 5
    outs = [shape((3, 2, local, group), BF)] * ctx
    out_specs = [ANY] * ctx
    if first_value is not None:
        args.append(first_value)
        specs.append(VM)
    else:
        outs.append(shape((2 * local, half), BF))
        out_specs.append(VM)
    args += weight.arrays
    specs += [ANY] * pieces
    got = call(
        kernel,
        outs,
        out_specs,
        [
            pltpu.VMEM((width, 3 * half), BF),
            pltpu.VMEM((2 * local, width), BF),
            pltpu.VMEM((ctx, 3, 2, local, group), BF),
            pltpu.SemaphoreType.DMA((pieces,)),
            pltpu.SemaphoreType.DMA((ctx,)),
        ],
        args,
        specs,
        2 * 2 * local * width * 3 * half,
        40,
    )
    return got[:ctx], (first_value if first_value is not None else got[ctx])


def exchange(slabs):
    return [slabs[0]] + [swap(slabs[k], "ctx", k) for k in range(1, len(slabs))]


def attend(slabs, start_column):
    ctx = len(slabs)
    _, _, local, group = slabs[0].shape
    span = ctx * local
    heads = group // HD

    def kernel(*refs):
        starts = refs[0]
        ins = refs[1 : 1 + ctx]
        outs = refs[1 + ctx : 1 + 2 * ctx]
        whole, mixed, sems, out_sems = refs[1 + 2 * ctx :]
        z = lax.axis_index("ctx")
        copies = []
        for k in range(ctx):
            at = pl.multiple_of(lax.bitwise_xor(z, k) * local, 16)
            copies.append(
                pltpu.make_async_copy(
                    ins[k], whole.at[:, :, pl.ds(at, local), :], sems.at[k]
                )
            )
        run_copies(copies)
        lane = lax.broadcasted_iota(jnp.int32, (1, group), 1) // HD

        def row_step(row, carry):
            for block in range(ctx):
                keys = (block + 1) * local
                here = slice(block * local, keys)
                query = whole[0, row, here, :] * SCORE_SCALE
                key = whole[1, row, :keys, :]
                value = whole[2, row, :keys, :]
                k_at = lax.broadcasted_iota(jnp.int32, (local, keys), 1)
                q_at = lax.broadcasted_iota(jnp.int32, (local, keys), 0) + block * local
                allowed = (k_at <= q_at) & (k_at >= starts[row, here, :])
                result = None
                for head in range(heads):
                    q_head = jnp.where(lane == head, query, jnp.zeros_like(query))
                    scores = jnp.where(allowed, dot_nt(q_head, key), MASK_FILL)
                    top = jnp.max(scores, axis=1, keepdims=True)
                    powers = jnp.exp(scores - top)
                    total = jnp.sum(powers, axis=1, keepdims=True)
                    probs = (powers * (1.0 / total)).astype(BF)
                    out = dot(probs, value)
                    result = out if result is None else jnp.where(lane == head, out, result)
                mixed[block, row] = result.astype(BF)
            return carry

        lax.fori_loop(0, 2, row_step, 0)
        run_copies(
            [
                pltpu.make_async_copy(mixed.at[lax.bitwise_xor(z, k)], outs[k], out_sems.at[k])
                for k in range(ctx)
            ]
        )

    return call(
        kernel,
        [shape((2, local, group), BF)] * ctx,
        [ANY] * ctx,
        [
            pltpu.VMEM((3, 2, span, group), BF),
            pltpu.VMEM((ctx, 2, local, group), BF),
            pltpu.SemaphoreType.DMA((ctx,)),
            pltpu.SemaphoreType.DMA((ctx,)),
        ],
        [start_column, *slabs],
        [VM] + [ANY] * ctx,
        2 * 2 * 2 * heads * span * span * 128,
        40,
    )


def halves_out(product, own_ref, other_ref, columns, local):
    own_ref[:, columns] = product[:local]
    other_ref[:, columns] = product[local:].astype(BF)


def mix_out(slabs, weight):
    ctx = len(slabs)
    _, local, group = slabs[0].shape
    half = ctx * group
    width = weight.arrays[0].shape[1]
    pieces = len(weight.arrays)
    plan = weight.plan

    def kernel(*refs):
        ins = refs[:ctx]
        w_refs = refs[ctx : ctx + pieces]
        own, other, joined, buffer, landed, sems = refs[ctx + pieces :]
        z = lax.axis_index("ctx")
        copies = weight_copies(plan, w_refs, buffer, sems, ctx)
        for k in range(ctx):
            copies.append(
                pltpu.make_async_copy(ins[k], landed.at[lax.bitwise_xor(z, k)], sems.at[k])
            )
        run_copies(copies)
        for k in range(ctx):
            joined[:, k * group : (k + 1) * group] = landed[k].reshape(2 * local, group)
        for tile in range(width // 256):
            columns = slice(tile * 256, (tile + 1) * 256)
            halves_out(dot(joined[...], buffer[:, columns]), own, other, columns, local)

    return call(
        kernel,
        [shape((local, width), F32), shape((local, width), BF), shape((2 * local, half), BF)],
        [VM] * 3,
        [
            pltpu.VMEM((half, width), BF),
            pltpu.VMEM((ctx, 2, local, group), BF),
            pltpu.SemaphoreType.DMA((ctx + pieces,)),
        ],
        [*slabs, *weight.arrays],
        [ANY] * (ctx + pieces),
        2 * 2 * local * half * width,
        24,
    )


def join_norm(base, own, other, gain):
    local, width = base.shape
    fresh = own is not None

    def kernel(*refs):
        if fresh:
            base_ref, own_ref, other_ref, gain_ref, sum_ref, low_ref = refs
            total = base_ref[...].astype(F32) + own_ref[...] + other_ref[...].astype(F32)
            sum_ref[...] = total
        else:
            base_ref, gain_ref, low_ref = refs
            total = base_ref[...].astype(F32)
        factor = lax.rsqrt(jnp.mean(total * total, axis=1, keepdims=True) + EPSILON)
        low_ref[...] = (total * factor * gain_ref[...].astype(F32)).astype(BF)

    outs = [shape((local, width), BF)]
    args = [base, gain]
    if fresh:
        outs = [shape((local, width), F32)] + outs
        args = [base, own, other, gain]
    return call(
        kernel, outs, [VM] * len(outs), [], args, [VM] * len(args), 8 * local * width, 16
    )


def gate_up(n_own, n_other, weight):
    local, width = n_own.shape
    hidden2 = weight.arrays[0].shape[1]
    hidden = hidden2 // 2
    pieces = len(weight.arrays)
    plan = weight.plan

    def kernel(*refs):
        own, other = refs[:2]
        w_refs = refs[2 : 2 + pieces]
        active, kept, buffer, tokens, sems = refs[2 + pieces :]
        copies = weight_copies(plan, w_refs, buffer, sems, 0)
        for copy in copies:
            copy.start()
        tokens[:local] = own[...]
        tokens[local:] = other[...]
        for copy in copies:
            copy.wait()

        def span_step(base, count):
            here, there = pl.ds(base, count), pl.ds(hidden + base, count)
            gate = dot(tokens[...], buffer[:, here])
            up = dot(tokens[...], buffer[:, there])
            kept[:, here] = gate.astype(BF)
            kept[:, there] = up.astype(BF)
            active[:, here] = (gate * jax.nn.sigmoid(gate) * up).astype(BF)

        def step(tile, carry):
            span_step(pl.multiple_of(tile * 256, 128), 256)
            return carry

        lax.fori_loop(0, hidden // 256, step, 0)
        if hidden % 256:
            span_step(hidden // 256 * 256, hidden % 256)

    return call(
        kernel,
        [shape((2 * local, hidden), BF), shape((2 * local, hidden2), BF)],
        [VM] * 2,
        [
            pltpu.VMEM((width, hidden2), BF),
            pltpu.VMEM((2 * local, width), BF),
            pltpu.SemaphoreType.DMA((pieces,)),
        ],
        [n_own, n_other, *weight.arrays],
        [VM] * 2 + [ANY] * pieces,
        2 * 2 * local * width * hidden2,
        40,
    )


def down(active, weight):
    tokens, hidden = active.shape
    local = tokens // 2
    width = weight.arrays[0].shape[1]
    pieces = len(weight.arrays)
    plan = weight.plan

    def kernel(*refs):
        left = refs[0]
        w_refs = refs[1 : 1 + pieces]
        own, other, buffer, sems = refs[1 + pieces :]
        run_copies(weight_copies(plan, w_refs, buffer, sems, 0))

        def step(tile, carry):
            columns = pl.ds(pl.multiple_of(tile * 256, 256), 256)
            halves_out(dot(left[...], buffer[:, columns]), own, other, columns, local)
            return carry

        lax.fori_loop(0, width // 256, step, 0)

    return call(
        kernel,
        [shape((local, width), F32), shape((local, width), BF)],
        [VM] * 2,
        [pltpu.VMEM((hidden, width), BF), pltpu.SemaphoreType.DMA((pieces,))],
        [active, *weight.arrays],
        [VM] + [ANY] * pieces,
        2 * tokens * hidden * width,
        24,
    )


def mlp_back(e_own, e_other, kept, gu_weight, down_weight):
    local, width = e_own.shape
    hidden2 = kept.shape[1]
    hidden = hidden2 // 2
    pieces = len(gu_weight.arrays)
    more = len(down_weight.arrays)
    gu_plan, down_plan = gu_weight.plan, down_weight.plan

    def kernel(*refs):
        e_one, e_two, kept_ref = refs[:3]
        gu_refs = refs[3 : 3 + pieces]
        down_refs = refs[3 + pieces : 3 + pieces + more]
        grads, own, other, gu, wd, tokens, sems = refs[3 + pieces + more :]
        first = weight_copies(down_plan, down_refs, wd, sems, pieces)
        second = weight_copies(gu_plan, gu_refs, gu, sems, 0)
        for copy in first + second:
            copy.start()
        tokens[:local] = e_one[...]
        tokens[local:] = e_two[...]
        for copy in first:
            copy.wait()

        def span_step(base, count):
            here, there = pl.ds(base, count), pl.ds(hidden + base, count)
            flow = dot_nt(tokens[...], wd[here, :])
            gate = kept_ref[:, here].astype(F32)
            up = kept_ref[:, there].astype(F32)
            sig = jax.nn.sigmoid(gate)
            grads[:, here] = (flow * up * sig * (1.0 + gate * (1.0 - sig))).astype(BF)
            grads[:, there] = (flow * gate * sig).astype(BF)

        def step(tile, carry):
            span_step(pl.multiple_of(tile * 256, 128), 256)
            return carry

        lax.fori_loop(0, hidden // 256, step, 0)
        if hidden % 256:
            span_step(hidden // 256 * 256, hidden % 256)
        for copy in second:
            copy.wait()

        def back_step(tile, carry):
            rows = pl.ds(pl.multiple_of(tile * 256, 256), 256)
            halves_out(dot_nt(grads[...], gu[rows, :]), own, other, rows, local)
            return carry

        lax.fori_loop(0, width // 256, back_step, 0)

    return call(
        kernel,
        [
            shape((2 * local, hidden2), BF),
            shape((local, width), F32),
            shape((local, width), BF),
        ],
        [VM] * 3,
        [
            pltpu.VMEM((width, hidden2), BF),
            pltpu.VMEM((hidden, width), BF),
            pltpu.VMEM((2 * local, width), BF),
            pltpu.SemaphoreType.DMA((pieces + more,)),
        ],
        [e_own, e_other, kept, *gu_weight.arrays, *down_weight.arrays],
        [VM] * 3 + [ANY] * (pieces + more),
        2 * 2 * local * width * hidden * 3,
        48,
    )


def norm_back(stream, own, other, gain, grad):
    local, width = stream.shape

    def kernel(x_ref, own_ref, other_ref, gain_ref, grad_ref, out_ref, low_ref, gain_out):
        x = x_ref[...].astype(F32)
        factor = lax.rsqrt(jnp.mean(x * x, axis=1, keepdims=True) + EPSILON)
        flow = own_ref[...] + other_ref[...].astype(F32)
        scaled = flow * gain_ref[...].astype(F32)
        gain_out[...] = jnp.sum(flow * x * factor, axis=0, keepdims=True)
        mean_term = jnp.mean(scaled * x, axis=1, keepdims=True)
        result = (
            grad_ref[...].astype(F32)
            + factor * scaled
            - x * (factor * factor * factor * mean_term)
        )
        out_ref[...] = result
        low_ref[...] = result.astype(BF)

    return call(
        kernel,
        [shape((local, width), F32), shape((local, width), BF), shape((1, width), F32)],
        [VM] * 3,
        [],
        [stream, own, other, gain, grad],
        [VM] * 5,
        12 * local * width,
        24,
    )


def mix_back(f_own, f_other, weight, ctx):
    local, width = f_own.shape
    half = width // 2
    group = half // ctx
    pieces = len(weight.arrays)
    plan = weight.plan

    def kernel(*refs):
        own, other = refs[:2]
        w_refs = refs[2 : 2 + pieces]
        slabs = refs[2 + pieces : 2 + pieces + ctx]
        buffer, tokens, slab, sems, out_sems = refs[2 + pieces + ctx :]
        copies = weight_copies(plan, w_refs, buffer, sems, 0)
        for copy in copies:
            copy.start()
        tokens[:local] = own[...]
        tokens[local:] = other[...]
        for copy in copies:
            copy.wait()
        for tile in range(half // 256):
            flow = dot_nt(tokens[...], buffer[tile * 256 : (tile + 1) * 256, :]).astype(BF)
            for part in range(256 // group):
                slab[tile * 256 // group + part] = flow[
                    :, part * group : (part + 1) * group
                ].reshape(2, local, group)
        z = lax.axis_index("ctx")
        run_copies(
            [
                pltpu.make_async_copy(slab.at[lax.bitwise_xor(z, k)], slabs[k], out_sems.at[k])
                for k in range(ctx)
            ]
        )

    return call(
        kernel,
        [shape((2, local, group), BF)] * ctx,
        [ANY] * ctx,
        [
            pltpu.VMEM((half, width), BF),
            pltpu.VMEM((2 * local, width), BF),
            pltpu.VMEM((ctx, 2, local, group), BF),
            pltpu.SemaphoreType.DMA((pieces,)),
            pltpu.SemaphoreType.DMA((ctx,)),
        ],
        [f_own, f_other, *weight.arrays],
        [VM] * 2 + [ANY] * pieces,
        2 * 2 * local * half * width,
        24,
    )


def attend_back(slabs, grad_slabs, start_row, tables, carried):
    ctx = len(grad_slabs)
    _, local, group = grad_slabs[0].shape
    span = ctx * local
    parts = len(slabs)
    heads = group // HD
    first = carried is not None

    def kernel(*refs):
        starts, cos, low, high = refs[:4]
        at = 4
        carry_in = None
        if first:
            carry_in = refs[at]
            at += 1
        ins = refs[at : at + parts]
        at += parts
        grads = refs[at : at + ctx]
        outs = refs[at + ctx : at + 2 * ctx]
        at += 2 * ctx
        carry_out = None
        if not first:
            carry_out = refs[at]
            at += 1
        whole, flow_in, slab, key_sum, value_sum, sems, out_sems = refs[at:]
        z = lax.axis_index("ctx")
        copies = []
        if parts == 1:
            copies.append(pltpu.make_async_copy(ins[0], whole, sems.at[0]))
        for k in range(ctx):
            to = pl.ds(pl.multiple_of(lax.bitwise_xor(z, k) * local, 16), local)
            if parts > 1:
                copies.append(
                    pltpu.make_async_copy(ins[k], whole.at[:, :, to, :], sems.at[k])
                )
            copies.append(
                pltpu.make_async_copy(grads[k], flow_in.at[:, to, :], sems.at[ctx + k])
            )
        run_copies(copies)
        lane = lax.broadcasted_iota(jnp.int32, (1, group), 1) // HD
        line = lax.broadcasted_iota(jnp.int32, (group, 1), 0) // HD

        def row_step(row, carry):
            key_sum[...] = jnp.zeros_like(key_sum)
            value_sum[...] = jnp.zeros_like(value_sum)
            key_turned = whole[1, row].astype(F32).T.astype(BF)
            for block in range(ctx):
                keys = (block + 1) * local
                here = slice(block * local, keys)
                query = whole[0, row, here, :] * SCORE_SCALE
                grad = flow_in[row, here, :]
                key = whole[1, row, :keys, :]
                value = whole[2, row, :keys, :]
                k_at = lax.broadcasted_iota(jnp.int32, (keys, local), 0)
                q_at = lax.broadcasted_iota(jnp.int32, (keys, local), 1) + block * local
                allowed = (k_at <= q_at) & (k_at >= starts[row, :, here])
                turned = None
                for head in range(heads):
                    mine = lane == head
                    q_head = jnp.where(mine, query, jnp.zeros_like(query))
                    g_head = jnp.where(mine, grad, jnp.zeros_like(grad))
                    scores = jnp.where(allowed, dot_nt(key, q_head), MASK_FILL)
                    top = jnp.max(scores, axis=0, keepdims=True)
                    powers = jnp.exp(scores - top)
                    total = jnp.sum(powers, axis=0, keepdims=True)
                    probs = powers * (1.0 / total)
                    grad_probs = dot_nt(value, g_head)
                    delta = jnp.sum(probs * grad_probs, axis=0, keepdims=True)
                    grad_scores = (probs * (grad_probs - delta)).astype(BF)
                    value_sum[:keys] += dot(probs.astype(BF), g_head)
                    key_sum[:keys] += dot(grad_scores, q_head)
                    part = dot(key_turned[:, :keys], grad_scores)
                    turned = part if turned is None else jnp.where(line == head, part, turned)
                grad_query = turned.T * SCORE_SCALE
                slab[block, 0, row] = rope(
                    grad_query, cos[row, here, :], -low[row, here, :], -high[row, here, :]
                ).astype(BF)
            for block in range(ctx):
                here = slice(block * local, (block + 1) * local)
                slab[block, 1, row] = rope(
                    key_sum[here, :], cos[row, here, :], -low[row, here, :], -high[row, here, :]
                ).astype(BF)
                if first:
                    total_value = value_sum[here, :] + carry_in[row, here, :]
                else:
                    total_value = 0.5 * value_sum[here, :]
                    carry_out[row, here, :] = total_value
                slab[block, 2, row] = total_value.astype(BF)
            return carry

        lax.fori_loop(0, 2, row_step, 0)
        run_copies(
            [
                pltpu.make_async_copy(slab.at[lax.bitwise_xor(z, k)], outs[k], out_sems.at[k])
                for k in range(ctx)
            ]
        )

    args = [start_row, *tables]
    specs = [VM] * 4
    outs = [shape((3, 2, local, group), BF)] * ctx
    out_specs = [ANY] * ctx
    if first:
        args.append(carried)
        specs.append(VM)
    else:
        outs.append(shape((2, span, group), F32))
        out_specs.append(VM)
    got = call(
        kernel,
        outs,
        out_specs,
        [
            pltpu.VMEM((3, 2, span, group), BF),
            pltpu.VMEM((2, span, group), BF),
            pltpu.VMEM((ctx, 3, 2, local, group), BF),
            pltpu.VMEM((span, group), F32),
            pltpu.VMEM((span, group), F32),
            pltpu.SemaphoreType.DMA((2 * ctx,)),
            pltpu.SemaphoreType.DMA((ctx,)),
        ],
        [*args, *slabs, *grad_slabs],
        specs + [ANY] * (parts + ctx),
        2 * 5 * 2 * heads * span * span * 128,
        48,
    )
    return got[:ctx], (None if first else got[ctx])


def project_back(slabs, weight):
    ctx = len(slabs)
    _, _, local, group = slabs[0].shape
    half = ctx * group
    width = 2 * half
    pieces = len(weight.arrays)
    plan = weight.plan

    def kernel(*refs):
        ins = refs[:ctx]
        w_refs = refs[ctx : ctx + pieces]
        own, other, joined, buffer, landed, sems = refs[ctx + pieces :]
        z = lax.axis_index("ctx")
        copies = weight_copies(plan, w_refs, buffer, sems, ctx)
        for k in range(ctx):
            copies.append(
                pltpu.make_async_copy(ins[k], landed.at[lax.bitwise_xor(z, k)], sems.at[k])
            )
        run_copies(copies)
        for k in range(ctx):
            for kind in range(3):
                base = kind * half + k * group
                joined[:, base : base + group] = landed[k, kind].reshape(2 * local, group)

        def step(tile, carry):
            rows = pl.ds(pl.multiple_of(tile * 256, 256), 256)
            halves_out(dot_nt(joined[...], buffer[rows, :]), own, other, rows, local)
            return carry

        lax.fori_loop(0, width // 256, step, 0)

    return call(
        kernel,
        [
            shape((local, width), F32),
            shape((local, width), BF),
            shape((2 * local, 3 * half), BF),
        ],
        [VM] * 3,
        [
            pltpu.VMEM((width, 3 * half), BF),
            pltpu.VMEM((ctx, 3, 2, local, group), BF),
            pltpu.SemaphoreType.DMA((ctx + pieces,)),
        ],
        [*slabs, *weight.arrays],
        [ANY] * (ctx + pieces),
        2 * 2 * local * 3 * half * width,
        40,
    )


def weight_grad(left, right, chips):
    lefts, rights = list(left), list(right)
    tall = lefts[0].shape[1]
    wide = rights[0].shape[1]
    tokens = lefts[0].shape[0] * len(lefts)
    rows = tall // chips
    halved = wide // 2
    split = chips == 4

    def kernel(*refs):
        l_refs = refs[: len(lefts)]
        r_refs = refs[len(lefts) : len(lefts) + len(rights)]
        at = len(lefts) + len(rights)
        count = 4 if split else chips
        outs = refs[at : at + count]
        grads, l_buf, r_buf, sems = refs[at + count :]
        if len(lefts) == 2:
            l_buf[: tokens // 2] = l_refs[0][...]
            l_buf[tokens // 2 :] = l_refs[1][...]
            l_now = l_buf
        else:
            l_now = l_refs[0]
        if len(rights) == 2:
            r_buf[: tokens // 2] = r_refs[0][...]
            r_buf[tokens // 2 :] = r_refs[1][...]
            r_now = r_buf
        else:
            r_now = r_refs[0]

        def tile_step(base, size):
            turned = l_now[:, pl.ds(base, size)]
            for start in range(0, wide, 512):
                stop = min(start + 512, wide)
                grads[pl.ds(base, size), start:stop] = dot_tn(
                    turned, r_now[:, start:stop]
                ).astype(BF)

        def step(tile, carry):
            tile_step(pl.multiple_of(tile * 256, 256), 256)
            return carry

        lax.fori_loop(0, tall // 256, step, 0)
        if tall % 256:
            tile_step(tall // 256 * 256, tall % 256)
        chip = chip_index()

        def block(k):
            return pl.ds(pl.multiple_of(lax.bitwise_xor(chip, k) * rows, 16), rows)

        copies = []
        if split:
            for which, order in enumerate(((1, 3), (0, 2), (2, 3), (0, 1))):
                columns = pl.ds((which // 2) * halved, halved)
                for slot, k in enumerate(order):
                    copies.append(
                        pltpu.make_async_copy(
                            grads.at[block(k), columns],
                            outs[which].at[slot],
                            sems.at[2 * which + slot],
                        )
                    )
        else:
            for k in range(chips):
                copies.append(
                    pltpu.make_async_copy(grads.at[block(k), :], outs[k], sems.at[k])
                )
        run_copies(copies)

    if split:
        outs = [shape((2, rows, halved), BF)] * 4
    else:
        outs = [shape((rows, wide), BF)] * chips
    small = (16, 128)
    return call(
        kernel,
        outs,
        [ANY] * len(outs),
        [
            pltpu.VMEM((tall, wide), BF),
            pltpu.VMEM((tokens, tall) if len(lefts) == 2 else small, BF),
            pltpu.VMEM((tokens, wide) if len(rights) == 2 else small, BF),
            pltpu.SemaphoreType.DMA((8 if split else chips,)),
        ],
        [*lefts, *rights],
        [VM] * (len(lefts) + len(rights)),
        2 * tokens * tall * wide,
        48,
    )


class Link:
    def __init__(self, source, target, arriving, sems, slot, axis, bit):
        device = {axis: lax.bitwise_xor(lax.axis_index(axis), bit)}

        def make(to):
            return pltpu.make_async_remote_copy(
                src_ref=source,
                dst_ref=to,
                send_sem=sems.at[0, slot],
                recv_sem=sems.at[1, slot],
                device_id=device,
                device_id_type=pl.DeviceIdType.MESH,
            )

        self.out = make(target)
        self.into = make(arriving)
        self.flying = False

    def start(self):
        self.out.start()
        self.flying = True
        return self

    def arrived(self):
        self.into.wait_recv()

    def sent(self):
        if self.flying:
            self.out.wait_send()
        self.flying = False


def enter(fsdp_bits, ctx_bits):
    barrier = pltpu.get_barrier_semaphore()
    for axis, bits in (("fsdp", fsdp_bits), ("ctx", ctx_bits)):
        for bit in bits:
            pl.semaphore_signal(
                barrier,
                inc=1,
                device_id={axis: lax.bitwise_xor(lax.axis_index(axis), bit)},
                device_id_type=pl.DeviceIdType.MESH,
            )
    pl.semaphore_wait(barrier, len(fsdp_bits) + len(ctx_bits))


def turn(x, cosines, sines, direction):
    width, pairs = x.shape[-1], HD // 2
    lane = lax.broadcasted_iota(jnp.int32, (1, width), 1)
    ahead = pltpu.roll(x, width - pairs, 1)
    behind = pltpu.roll(x, pairs, 1)
    other = jnp.where(lax.rem(lane, HD) < pairs, -ahead, behind)
    return x * cosines + other * (sines if direction > 0 else -sines)


def rms(total, gain):
    factor = lax.rsqrt(jnp.mean(total * total, axis=1, keepdims=True) + EPSILON)
    return (total * factor * gain).astype(BF)


def forward_pass(tokens, doc_lengths, gains, w_qkv, w_out, w_gate, w_up, w_down):
    local, width = tokens.shape
    layers, block, _ = w_qkv.shape
    hidden = w_gate.shape[2]
    hid = hidden // 2
    hid_block = w_down.shape[1]
    half = width // 2
    shards, ctx = lax.axis_size("fsdp"), lax.axis_size("ctx")
    chips = shards // 2
    group = half // ctx
    span = ctx * local
    heads = group // HD
    both = 2 * local
    documents = doc_lengths.shape[1]
    lengths = jnp.zeros((8, 128), jnp.int32).at[:documents].set(doc_lengths[0][:, None])
    gain_rows = jnp.zeros((8, block), F32).at[: 2 * layers].set(
        gains.reshape(2 * layers, block).astype(F32)
    )

    def kernel(*refs):
        (tok, lens, gain_in, qkv_in, out_in, gate_in, up_in, down_in) = refs[:8]
        (wq_o, wo_o, wg_o, wd_o, n1_o, n2_o, whole_o, mix_o, mid_o, stream_o) = refs[8:18]
        (act_o, kept_o, gain_o, cos_o, sin_o, start_o, final_o) = refs[18:25]
        (wq, wo, wg, wd, qkv_raw, gu_raw, q_stage, g_stage) = refs[25:33]
        (n1, n2, whole, slab, mixed, landed, value, mix, mid, stream) = refs[33:43]
        (act, kept, part, other, got, gbuf, lens_all, cos, sin, start) = refs[43:53]
        (sems, local_sems, save_sems) = refs[53:]
        f = lax.axis_index("fsdp")
        z = lax.axis_index("ctx")
        core = lax.rem(f, 2)
        chip = f // 2
        flights = []
        saves = []

        def link(source, target, arriving, axis, bit):
            made = Link(source, target, arriving, sems, len(flights), axis, bit)
            flights.append(made)
            return made

        def save(source, target):
            copy = pltpu.make_async_copy(source, target, save_sems.at[len(saves)])
            copy.start()
            saves.append(copy)
            return len(saves) - 1

        def saved(number):
            if saves[number] is not None:
                saves[number].wait()
            saves[number] = None

        def rows(index, count):
            return pl.ds(pl.multiple_of(index * count, 16), count)

        def fx(bit):
            return lax.bitwise_xor(f, bit)

        def cx(bit):
            return lax.bitwise_xor(chip, bit)

        class Halved:
            def __init__(self, buffer, stage):
                def at(index):
                    return buffer.at[rows(index, block), :]

                self.first = [
                    link(stage, at(f), at(fx(bit)), "fsdp", bit) for bit in (1, 3, 5)
                ] + [link(at(f), at(f), at(fx(bit)), "fsdp", bit) for bit in (2, 4)]
                over_y, over_x, far = 2 * cx(1), 2 * cx(2) + 1, 2 * cx(3)
                self.second = [
                    link(at(over_y), at(over_y), at(far), "fsdp", 4),
                    link(at(over_x), at(over_x), at(far + 1), "fsdp", 2),
                ]

        class Rowed:
            def __init__(self, buffer, source, count):
                small = count // 2

                def at(index):
                    return buffer.at[rows(index, count), :]

                def side(index, which):
                    begin = pl.multiple_of(index * count + which * small, 16)
                    return buffer.at[pl.ds(begin, small), :]

                self.first = [
                    link(source, at(chip), at(cx(bit // 2)), "fsdp", bit) for bit in (2, 4)
                ]
                self.second = [
                    link(side(cx(1), 0), side(cx(1), 0), side(cx(3), 0), "fsdp", 4),
                    link(side(cx(2), 1), side(cx(2), 1), side(cx(3), 1), "fsdp", 2),
                ]

        def begin(weight):
            for one in weight.first:
                one.start()

        def forward(weight):
            for one in weight.first:
                one.arrived()
            for one in weight.second:
                one.start()

        def finish(weight):
            for one in weight.second:
                one.arrived()

        q_of = [Halved(wq.at[n], q_stage.at[n]) for n in range(layers)]
        g_of = [Halved(wg.at[n], g_stage.at[n]) for n in range(layers)]
        o_of = [Rowed(wo.at[n], out_in.at[n], block) for n in range(layers)]
        d_of = [Rowed(wd.at[n], down_in.at[n], hid_block) for n in range(layers)]

        def local_copy(source, target, slot):
            copy = pltpu.make_async_copy(source, target, local_sems.at[slot])
            copy.start()
            return copy

        def choose(first, second):
            return lax.select(core == 0, first, second)

        def stage_qkv(n):
            for kind in range(3):
                for j in range(chips):
                    at = kind * width + 2 * j * block
                    even = qkv_raw[:, at : at + block]
                    odd = qkv_raw[:, at + block : at + 2 * block]
                    to = kind * half + j * block
                    wq[n, rows(f, block), to : to + block] = choose(even, odd)
                    q_stage[n, :, to : to + block] = choose(odd, even)

        def stage_gu(n):
            for which in range(2):
                sets = []
                for lane_core in range(2):
                    parts = []
                    for j in range(chips):
                        at = (2 * j + lane_core) * hid_block
                        parts.append(gu_raw[which, :, at : at + hid_block])
                    sets.append(jnp.concatenate(parts, axis=1))
                to = slice(which * hid, (which + 1) * hid)
                wg[n, rows(f, block), to] = choose(sets[0], sets[1])
                g_stage[n, :, to] = choose(sets[1], sets[0])

        def load(n):
            return [
                local_copy(qkv_in.at[n], qkv_raw, 0),
                local_copy(gate_in.at[n], gu_raw.at[0], 1),
                local_copy(up_in.at[n], gu_raw.at[1], 2),
            ]

        loads = load(0)
        mine = []
        for n in range(layers):
            mine.append(local_copy(out_in.at[n], wo.at[n, rows(chip, block), :], 3 + n))
            mine.append(
                local_copy(down_in.at[n], wd.at[n, rows(chip, hid_block), :], 3 + layers + n)
            )
        spare = 3 + 2 * layers
        loads[0].wait()
        stage_qkv(0)
        gain_links = [
            link(gain_in, gbuf.at[f], gbuf.at[fx(bit)], "fsdp", bit) for bit in range(1, shards)
        ]
        lens_link = link(lens, lens_all.at[1], lens_all.at[1], "fsdp", 1)
        enter(list(range(1, shards)), list(range(1, ctx)))
        for one in gain_links:
            one.start()
        lens_link.start()
        begin(q_of[0])
        gbuf[f] = gain_in[...]
        lens_all[0] = lens[...]
        for copy in mine + loads[1:]:
            copy.wait()
        stage_gu(0)
        loads = load(1)
        for one in gain_links:
            one.arrived()

        def gain_row(n):
            return jnp.concatenate([gbuf[s, n : n + 1, :] for s in range(shards)], axis=1)

        for n in range(2 * layers):
            gain_o[n : n + 1, :] = gain_row(n)

        def norm_link(buffer, n):
            upper = buffer.at[n, pl.ds(local, local), :]
            return link(buffer.at[n, pl.ds(0, local), :], upper, upper, "fsdp", 1)

        n1[0, :local] = rms(tok[...].astype(F32), gain_row(0))
        norm_now = norm_link(n1, 0).start()

        lens_link.arrived()
        pairs = HD // 2
        lane = lax.broadcasted_iota(jnp.int32, (1, 128), 1)
        frequency = jnp.exp((-math.log(10000.0) / pairs) * lax.rem(lane, pairs).astype(F32))

        def table_step(index, carry):
            r = index // ctx
            piece = lax.rem(index, ctx)
            to = rows(piece, local)
            at = lax.broadcasted_iota(jnp.int32, (local, 128), 0) + piece * local
            first = jnp.zeros((local, 128), jnp.int32)
            end = jnp.zeros((1, 128), jnp.int32)
            for j in range(documents):
                end = end + lens_all[r, j : j + 1, :]
                first = jnp.where(at >= end, end, first)
            start[r, to, :] = first
            angle = (at - first).astype(F32) * frequency
            sin[r, to, :] = jnp.sin(angle)
            cos[r, to, :] = jnp.cos(angle)
            return carry

        lax.fori_loop(0, 2 * ctx, table_step, 0)
        here_rows = rows(z, local)
        for source, target in ((cos, cos_o), (sin, sin_o), (lens_all, start_o)):
            save(source, target)
        lane_head = lax.broadcasted_iota(jnp.int32, (1, group), 1) // HD

        def do_project(n):
            for tile in range(3 * half // 256):
                acc = dot(n1[n], wq[n, :, tile * 256 : (tile + 1) * 256])
                kind = tile * 256 // half
                for sub in range(256 // group):
                    column = tile * 256 - kind * half + sub * group
                    for r in range(2):
                        x = acc[r * local : (r + 1) * local, sub * group : (sub + 1) * group]
                        at = (slice(r * local, (r + 1) * local), slice(column, column + group))
                        if kind < 2:
                            x = turn(x, cos[r, here_rows, :], sin[r, here_rows, :], 1)
                        elif n > 0:
                            x = 0.5 * x + 0.5 * value[at].astype(F32)
                        x = x.astype(BF)
                        if kind == 2 and n == 0:
                            value[at] = x
                        slab[column // group, kind, r] = x

        def slab_links(n):
            made = []
            for bit in range(1, ctx):
                to = lax.bitwise_xor(z, bit)
                made.append(
                    link(
                        slab.at[to],
                        whole.at[n, :, :, rows(z, local), :],
                        whole.at[n, :, :, rows(to, local), :],
                        "ctx",
                        bit,
                    )
                )
            return made

        def mixed_links(n):
            made = []
            for bit in range(1, ctx):
                to = lax.bitwise_xor(z, bit)
                made.append(link(mixed.at[n, to], landed.at[n, z], landed.at[n, to], "ctx", bit))
            return made

        def do_attend(n):
            def row_step(r, carry):
                for piece in range(ctx):
                    keys = (piece + 1) * local
                    here = slice(piece * local, keys)
                    query = whole[n, 0, r, here, :] * SCORE_SCALE
                    key = whole[n, 1, r, :keys, :]
                    val = whole[n, 2, r, :keys, :]
                    k_at = lax.broadcasted_iota(jnp.int32, (local, keys), 1)
                    q_at = lax.broadcasted_iota(jnp.int32, (local, keys), 0) + piece * local
                    allowed = (k_at <= q_at) & (k_at >= start[r, here, 0:1])
                    result = None
                    for head in range(heads):
                        q_head = jnp.where(lane_head == head, query, jnp.zeros_like(query))
                        scores = jnp.where(allowed, dot_nt(q_head, key), MASK_FILL)
                        top = jnp.max(scores, axis=1, keepdims=True)
                        powers = jnp.exp(scores - top)
                        total = jnp.sum(powers, axis=1, keepdims=True)
                        probs = (powers * (1.0 / total)).astype(BF)
                        out = dot(probs, val)
                        result = out if head == 0 else jnp.where(lane_head == head, out, result)
                    mixed[n, piece, r] = result.astype(BF)
                return carry

            lax.fori_loop(0, 2, row_step, 0)

        last_sum = [None]

        def partial_sums(n, which, left, weight):
            if last_sum[0] is not None:
                last_sum[0].sent()

            def step(tile, carry):
                columns = rows(tile, 256)
                product = dot(left[...], weight[:, columns])
                part[:, columns] = product[:local]
                other[:, columns] = product[local:].astype(BF)
                return carry

            lax.fori_loop(0, width // 256, step, 0)
            to = got.at[n, which]
            last_sum[0] = link(other, to, to, "fsdp", 1).start()
            return last_sum[0]

        def gate_up(n):
            def span_step(base, count):
                here, there = pl.ds(base, count), pl.ds(hid + base, count)
                gate = dot(n2[n], wg[n, :, here])
                up = dot(n2[n], wg[n, :, there])
                kept[:, here] = gate.astype(BF)
                kept[:, there] = up.astype(BF)
                act[:, here] = (gate * jax.nn.sigmoid(gate) * up).astype(BF)

            def step(tile, carry):
                span_step(pl.multiple_of(tile * 256, 128), 256)
                return carry

            lax.fori_loop(0, hid // 256, step, 0)
            if hid % 256:
                span_step(hid // 256 * 256, hid % 256)

        slab_flights = []
        held = []
        for n in range(layers):
            if n == 0:
                forward(q_of[0])
                begin(o_of[0])
            finish(q_of[n])
            save(wq.at[n], wq_o.at[n])
            begin(g_of[n])
            norm_now.arrived()
            save(n1.at[n], n1_o.at[n])
            for one in slab_flights:
                one.sent()
            do_project(n)
            slab_flights = slab_links(n)
            for one in slab_flights:
                one.start()
            own = local_copy(slab.at[z], whole.at[n, :, :, here_rows, :], spare)
            if n == 0:
                for copy in loads:
                    copy.wait()
                stage_qkv(1)
                stage_gu(1)
            forward(o_of[n])
            finish(o_of[n])
            save(wo.at[n], wo_o.at[n])
            if n > 0:
                forward(g_of[n])
                begin(d_of[n])
            own.wait()
            for one in slab_flights:
                one.arrived()
            save(whole.at[n], whole_o.at[n])
            if n == 0:
                forward(g_of[n])
                begin(d_of[n])
            do_attend(n)
            back = mixed_links(n)
            for one in back:
                one.start()
            own = local_copy(mixed.at[n, z], landed.at[n, z], spare)
            if n == 0:
                begin(q_of[1])
            own.wait()
            for one in back:
                one.arrived()
            for k in range(ctx):
                mix[n, :, k * group : (k + 1) * group] = landed[n, k].reshape(both, group)
            save(mix.at[n], mix_o.at[n])
            sums = partial_sums(n, 0, mix.at[n], wo.at[n])
            forward(d_of[n])
            base = tok[...].astype(F32) if n == 0 else stream[...]
            sums.arrived()
            total = base + part[...] + got[n, 0].astype(F32)
            mid[n] = total
            n2[n, :local] = rms(total, gain_row(2 * n + 1))
            norm_now = norm_link(n2, n).start()
            save(mid.at[n], mid_o.at[n])
            finish(g_of[n])
            save(wg.at[n], wg_o.at[n])
            for number in held:
                saved(number)
            norm_now.arrived()
            save(n2.at[n], n2_o.at[n])
            gate_up(n)
            held = [save(act, act_o.at[n]), save(kept, kept_o.at[n])]
            if n == 0:
                forward(q_of[1])
                begin(o_of[1])
            finish(d_of[n])
            save(wd.at[n], wd_o.at[n])
            sums = partial_sums(n, 1, act, wd.at[n])
            sums.arrived()
            total = mid[n] + part[...] + got[n, 1].astype(F32)
            if n + 1 < layers:
                stream[...] = total
                n1[n + 1, :local] = rms(total, gain_row(2 * n + 2))
                norm_now = norm_link(n1, n + 1).start()
                save(stream, stream_o)
            else:
                final_o[...] = total.astype(BF)
        for one in flights:
            one.sent()
        for number in range(len(saves)):
            saved(number)

    def stacked(*dims):
        return (layers, *dims)

    outs = [
        shape(stacked(width, 3 * half), BF),
        shape(stacked(half, width), BF),
        shape(stacked(width, 2 * hid), BF),
        shape(stacked(hid, width), BF),
        shape(stacked(both, width), BF),
        shape(stacked(both, width), BF),
        shape(stacked(3, 2, span, group), BF),
        shape(stacked(both, half), BF),
        shape(stacked(local, width), F32),
        shape((local, width), F32),
        shape(stacked(both, hid), BF),
        shape(stacked(both, 2 * hid), BF),
        shape((2 * layers, width), F32),
        shape((2, span, 128), F32),
        shape((2, span, 128), F32),
        shape((2, 8, 128), jnp.int32),
        shape((local, width), BF),
    ]
    out_specs = [ANY] * 17
    out_specs[12] = out_specs[16] = VM
    scratch = [
        pltpu.VMEM(stacked(width, 3 * half), BF),
        pltpu.VMEM(stacked(half, width), BF),
        pltpu.VMEM(stacked(width, 2 * hid), BF),
        pltpu.VMEM(stacked(hid, width), BF),
        pltpu.VMEM((block, 3 * width), BF),
        pltpu.VMEM((2, block, hidden), BF),
        pltpu.VMEM(stacked(block, 3 * half), BF),
        pltpu.VMEM(stacked(block, 2 * hid), BF),
        pltpu.VMEM(stacked(both, width), BF),
        pltpu.VMEM(stacked(both, width), BF),
        pltpu.VMEM(stacked(3, 2, span, group), BF),
        pltpu.VMEM((ctx, 3, 2, local, group), BF),
        pltpu.VMEM(stacked(ctx, 2, local, group), BF),
        pltpu.VMEM(stacked(ctx, 2, local, group), BF),
        pltpu.VMEM((both, half), BF),
        pltpu.VMEM(stacked(both, half), BF),
        pltpu.VMEM(stacked(local, width), F32),
        pltpu.VMEM((local, width), F32),
        pltpu.VMEM((both, hid), BF),
        pltpu.VMEM((both, 2 * hid), BF),
        pltpu.VMEM((local, width), F32),
        pltpu.VMEM((local, width), BF),
        pltpu.VMEM(stacked(2, local, width), BF),
        pltpu.VMEM((shards, 8, block), F32),
        pltpu.VMEM((2, 8, 128), jnp.int32),
        pltpu.VMEM((2, span, 128), F32),
        pltpu.VMEM((2, span, 128), F32),
        pltpu.VMEM((2, span, 128), jnp.int32),
        pltpu.SemaphoreType.DMA((2, 80)),
        pltpu.SemaphoreType.DMA((8,)),
        pltpu.SemaphoreType.DMA((32,)),
    ]
    return pl.pallas_call(
        kernel,
        out_shape=outs,
        in_specs=[VM] * 3 + [ANY] * 5,
        out_specs=out_specs,
        scratch_shapes=scratch,
        compiler_params=pltpu.CompilerParams(
            vmem_limit_bytes=62 * MIB, collective_id=0, has_side_effects=True
        ),
        cost_estimate=pl.CostEstimate(
            flops=14 * 10**9, bytes_accessed=60 * MIB, transcendentals=0
        ),
    )(tokens, lengths, gain_rows, w_qkv, w_out, w_gate, w_up, w_down)


def backward_pass(saved, tokens, cotangent):
    local, width = tokens.shape
    wq_s, wo_s, wg_s, wd_s = saved[:4]
    layers = wq_s.shape[0]
    half = width // 2
    hid = wd_s.shape[1]
    shards, ctx = lax.axis_size("fsdp"), lax.axis_size("ctx")
    chips = shards // 2
    block = width // shards
    hid_block = hid // chips
    group = half // ctx
    span = ctx * local
    heads = group // HD
    both = 2 * local
    documents = 4
    sizes = {
        "d": (hid_block, width),
        "g": (2 * block, 2 * hid),
        "o": (block, width),
        "q": (2 * block, 3 * half),
    }
    names = ("d", "g", "o", "q")

    def kernel(*refs):
        refs = list(refs)

        def take(count):
            out = refs[:count]
            del refs[:count]
            return out

        cot_i, tok_i, lens, gain = take(4)
        wq_i, wo_i, wg_i, wd_i, n1_i, n2_i, whole_i, mix_i, mid_i, stream_i = take(10)
        act_i, kept_i, cos_i, sin_i = take(4)
        grad_o, gain_o, q_o, o_o, gate_o, up_o, d_o = take(7)
        lands = {}
        for name in names:
            lands[name] = dict(zip(("x1", "y1", "x2", "y2", "z"), take(5)))
        swap_land = dict(zip(("g", "q"), take(2)))
        wq, wo, wg, wd, act, kept, norm, whole, mix, wide = take(10)
        flow, fgrad, got, do_in, dq_in, part, other, grad, middle = take(9)
        do_out, dq_out, key_sum, value_sum, carry, joined, cos, sin = take(8)
        blocks = dict(zip(names, take(4)))
        finals = dict(zip(names, take(4)))
        tmp, stage, gain_rows, gain_send, gain_land, gain_sum, gain_line = take(7)
        sems, load_sems, tmp_sems, out_sems = take(4)
        f = lax.axis_index("fsdp")
        z = lax.axis_index("ctx")
        core = lax.rem(f, 2)
        chip = f // 2
        inner = (z == 1) | (z == 2)
        outer = (z == 0) | (z == 3)
        flights = []

        def link(source, target, arriving, axis, bit):
            made = Link(source, target, arriving, sems, len(flights), axis, bit)
            flights.append(made)
            return made

        def rows(index, count):
            return pl.ds(pl.multiple_of(index * count, 16), count)

        def cx(bit):
            return lax.bitwise_xor(chip, bit)

        loading = {}
        slots = {}

        def load(name, source, target):
            slot = slots.setdefault(name, len(slots))
            copy = pltpu.make_async_copy(source, target, load_sems.at[slot])
            copy.start()
            loading[name] = copy

        def loaded(*wanted):
            for name in wanted:
                if name in loading:
                    loading.pop(name).wait()

        top = layers - 1
        load("cot", cot_i, flow.at[pl.ds(0, local), :])
        load("act", act_i.at[top], act)
        load("wd", wd_i.at[top], wd)
        load("kept", kept_i.at[top], kept)
        load("wg", wg_i.at[top], wg)
        load("wide", mid_i.at[top], wide)
        load("wo", wo_i.at[top], wo)
        load("norm", n2_i.at[top], norm)
        load("mix", mix_i.at[top], mix)
        load("whole", whole_i.at[top], whole)
        load("wq", wq_i.at[top], wq)
        load("cos", cos_i, cos)
        load("sin", sin_i, sin)
        enter(list(range(1, shards)), list(range(1, ctx)))

        def pair_link(buffer):
            upper = buffer.at[pl.ds(local, local), :]
            return link(buffer.at[pl.ds(0, local), :], upper, upper, "fsdp", 1)

        loaded("cot")
        e_link = pair_link(flow).start()
        grad[...] = flow[:local].astype(F32)

        class Reduce:
            def __init__(self, name, n):
                self.name, self.n = name, n
                self.count, self.columns = sizes[name]
                self.side = self.columns // 2
                self.blocks, self.final = blocks[name], finals[name]
                self.land = lands[name]
                left, right = pl.ds(0, self.side), pl.ds(self.side, self.side)
                self.halves = (left, right)

                def piece(k, columns):
                    return self.blocks.at[rows(cx(k), self.count), columns]

                def into(where, slot=None):
                    ref = self.land[where]
                    return ref.at[n] if slot is None else ref.at[n, slot]

                def hop(source, target, bit):
                    return link(source, target, target, "fsdp", bit)

                self.x_own = hop(piece(1, left), into("x1", 0), 2)
                self.x_far = hop(piece(3, left), into("x1", 1), 2)
                self.y_own = hop(piece(2, right), into("y1", 0), 4)
                self.y_far = hop(piece(3, right), into("y1", 1), 4)
                self.y_next = hop(piece(2, left), into("y2"), 4)
                self.x_next = hop(piece(1, right), into("x2"), 2)
                self.line = []
                for side in self.halves:
                    steps = []
                    for step, bit in ((0, 1), (1, 3), (2, 1)):
                        target = self.land["z"].at[n, step, :, side]
                        steps.append(link(self.final.at[:, side], target, target, "ctx", bit))
                    self.line.append(steps)
                self.swap = None
                if name in swap_land:
                    out = rows(1 - core, block)
                    to = swap_land[name].at[n]
                    self.swap = link(self.final.at[out, :], to, to, "fsdp", 1)

            def fetch(self, *sources):
                copies = []
                for slot, source in enumerate(sources):
                    copy = pltpu.make_async_copy(
                        source,
                        tmp.at[slot, pl.ds(0, self.count), pl.ds(0, self.side)],
                        tmp_sems.at[slot],
                    )
                    copy.start()
                    copies.append(copy)
                for copy in copies:
                    copy.wait()

            def add(self, source, source_row, columns, target, target_row, slots_used):
                def step(tile, carry):
                    at = pl.ds(pl.multiple_of(source_row + tile * 32, 16), 32)
                    total = source[at, columns].astype(F32)
                    here = pl.ds(pl.multiple_of(tile * 32, 16), 32)
                    for slot in slots_used:
                        total = total + tmp[slot, here, : self.side].astype(F32)
                    to = pl.ds(pl.multiple_of(target_row + tile * 32, 16), 32)
                    target[to, columns] = total.astype(BF)
                    return carry

                lax.fori_loop(0, self.count // 32, step, 0)

            def first(self):
                self.x_far.arrived()
                self.y_far.arrived()
                self.fetch(self.land["x1"].at[self.n, 1], self.land["y1"].at[self.n, 1])
                at = cx(2) * self.count
                self.add(self.blocks, at, self.halves[0], self.blocks, at, (0,))
                self.y_next.start()
                at = cx(1) * self.count
                self.add(self.blocks, at, self.halves[1], self.blocks, at, (1,))
                self.x_next.start()

            def second(self):
                at = chip * self.count
                self.x_own.arrived()
                self.y_next.arrived()
                self.fetch(self.land["x1"].at[self.n, 0], self.land["y2"].at[self.n])
                self.add(self.blocks, at, self.halves[0], self.final, 0, (0, 1))
                pl.when(outer)(self.line[0][0].out.start)
                self.y_own.arrived()
                self.x_next.arrived()
                self.fetch(self.land["y1"].at[self.n, 0], self.land["x2"].at[self.n])
                self.add(self.blocks, at, self.halves[1], self.final, 0, (0, 1))
                pl.when(outer)(self.line[1][0].out.start)
                for one in (self.x_own, self.x_far, self.y_own, self.y_far, self.x_next, self.y_next):
                    one.sent()

            def inward(self):
                @pl.when(inner)
                def _():
                    for which, steps in enumerate(self.line):
                        steps[0].into.wait_recv()
                        self.fetch(self.land["z"].at[self.n, 0, :, self.halves[which]])
                        self.add(self.final, 0, self.halves[which], self.final, 0, (0,))
                        steps[1].out.start()

            def across(self):
                @pl.when(inner)
                def _():
                    for which, steps in enumerate(self.line):
                        steps[1].into.wait_recv()
                        self.fetch(self.land["z"].at[self.n, 1, :, self.halves[which]])
                        steps[1].out.wait_send()
                        self.add(self.final, 0, self.halves[which], self.final, 0, (0,))
                        steps[2].out.start()

            def outward(self):
                @pl.when(outer)
                def _():
                    for which, steps in enumerate(self.line):
                        steps[2].into.wait_recv()
                        steps[0].out.wait_send()
                        copy = pltpu.make_async_copy(
                            self.land["z"].at[self.n, 2, :, self.halves[which]],
                            self.final.at[:, self.halves[which]],
                            tmp_sems.at[0],
                        )
                        copy.start()
                        copy.wait()

                @pl.when(inner)
                def _():
                    for steps in self.line:
                        steps[2].out.wait_send()

                if self.swap is not None:
                    self.swap.start()

            def write(self):
                n = self.n
                if self.name in ("d", "o"):
                    target = d_o if self.name == "d" else o_o
                    run_copies([pltpu.make_async_copy(self.final, target.at[n], out_sems.at[0])])
                    return
                self.swap.arrived()
                parts_now = 3 if self.name == "q" else 2
                wide_now = self.columns // parts_now
                places = [
                    (k // 2, pl.ds((k % 2) * block, block), pl.ds(0, wide_now)) for k in range(3)
                ]
                if self.name == "g":
                    places[1] = (1, pl.ds(0, block), pl.ds(0, wide_now))
                run_copies(
                    [
                        pltpu.make_async_copy(
                            swap_land[self.name].at[n, :, pl.ds(k * wide_now, wide_now)],
                            tmp.at[places[k]],
                            out_sems.at[2 + k],
                        )
                        for k in range(parts_now)
                    ]
                )
                mine = rows(core, block)

                def sets(part_now, start_now, count_now):
                    first_at = part_now * wide_now + start_now
                    own = self.final[mine, first_at : first_at + count_now]
                    slot, row_at, _ = places[part_now]
                    theirs = tmp[slot, row_at, start_now : start_now + count_now]
                    return (
                        lax.select(core == 0, own, theirs),
                        lax.select(core == 0, theirs, own),
                    )

                if self.name == "q":
                    for kind in range(3):
                        for j in range(chips):
                            even, odd = sets(kind, j * block, block)
                            to = kind * width + 2 * j * block
                            stage[:, to : to + block] = even
                            stage[:, to + block : to + 2 * block] = odd
                    run_copies([pltpu.make_async_copy(stage, q_o.at[n], out_sems.at[0])])
                else:
                    for which, target in enumerate((gate_o, up_o)):
                        even, odd = sets(which, 0, hid)
                        parts = []
                        for j in range(chips):
                            at = slice(j * hid_block, (j + 1) * hid_block)
                            parts += [even[:, at], odd[:, at]]
                        stage[:, : 2 * hid] = jnp.concatenate(parts, axis=1)
                        run_copies(
                            [
                                pltpu.make_async_copy(
                                    stage.at[:, pl.ds(0, 2 * hid)], target.at[n], out_sems.at[0]
                                )
                            ]
                        )
                self.swap.sent()

        def grad_tile(target, row, count, left, columns, right, wide_count):
            turned = left[:, columns]
            for begin in range(0, wide_count, 512):
                end = min(begin + 512, wide_count)
                target[pl.ds(row, count), begin:end] = dot_tn(turned, right[:, begin:end]).astype(BF)

        def compute_blocks(job, left, right):
            for k in (3, 1, 2, 0):
                row = pl.multiple_of(cx(k) * job.count, 128)
                grad_tile(job.blocks, row, job.count, left, pl.ds(row, job.count), right, job.columns)
                if k == 3:
                    job.x_far.start()
                    job.y_far.start()
                elif k == 1:
                    job.x_own.start()
                elif k == 2:
                    job.y_own.start()

        def compute_down(job):
            def step(tile, carry):
                row = pl.multiple_of(tile * 256, 128)
                grad_tile(job.blocks, row, 256, act, pl.ds(row, 256), flow, width)
                return carry

            lax.fori_loop(0, hid // 256, step, 0)
            if hid % 256:
                row = hid // 256 * 256
                grad_tile(job.blocks, row, hid % 256, act, pl.ds(row, hid % 256), flow, width)
            for one in (job.x_far, job.y_far, job.x_own, job.y_own):
                one.start()

        last_sum = [None]

        def partial_sums(which, product):
            if last_sum[0] is not None:
                last_sum[0].sent()

            def step(tile, carry):
                columns = rows(tile, 256)
                value = product(columns)
                part[:, columns] = value[:local]
                other[:, columns] = value[local:].astype(BF)
                return carry

            lax.fori_loop(0, width // 256, step, 0)
            last_sum[0] = link(other, got.at[which], got.at[which], "fsdp", 1).start()
            return last_sum[0]

        def norm_step(x, gain_now, gain_row, which, target, low_target):
            factor = lax.rsqrt(jnp.mean(x * x, axis=1, keepdims=True) + EPSILON)
            back = part[...] + got[which].astype(F32)
            scaled = back * gain_now
            gain_rows[gain_row : gain_row + 1, :] = jnp.sum(back * x * factor, axis=0, keepdims=True)
            mean_term = jnp.mean(scaled * x, axis=1, keepdims=True)
            base = grad[...] if target is middle else middle[...]
            result = base + factor * scaled - x * (factor * factor * factor * mean_term)
            target[...] = result
            if low_target is not None:
                low_target[:local] = result.astype(BF)

        def mlp_back():
            def span_step(base, count):
                here, there = pl.ds(base, count), pl.ds(hid + base, count)
                back = dot_nt(flow[...], wd[here, :])
                gate = kept[:, here].astype(F32)
                up = kept[:, there].astype(F32)
                sig = jax.nn.sigmoid(gate)
                kept[:, here] = (back * up * sig * (1.0 + gate * (1.0 - sig))).astype(BF)
                kept[:, there] = (back * gate * sig).astype(BF)

            def step(tile, carry):
                span_step(pl.multiple_of(tile * 256, 128), 256)
                return carry

            lax.fori_loop(0, hid // 256, step, 0)
            if hid % 256:
                span_step(hid // 256 * 256, hid % 256)

        lane_head = lax.broadcasted_iota(jnp.int32, (1, group), 1) // HD
        line_head = lax.broadcasted_iota(jnp.int32, (group, 1), 0) // HD

        def start_row(r):
            at = lax.broadcasted_iota(jnp.int32, (1, span), 1)
            first = jnp.zeros((1, span), jnp.int32)
            end = jnp.zeros((1, 1), jnp.int32)
            for j in range(documents):
                end = end + lens[r, j : j + 1, 0:1]
                first = jnp.where(at >= end, end, first)
            return first

        def attend_step(n):
            def row_step(r, nothing):
                key_sum[...] = jnp.zeros_like(key_sum)
                value_sum[...] = jnp.zeros_like(value_sum)
                key_turned = whole[1, r].astype(F32).T.astype(BF)
                starts = start_row(r)
                for piece in range(ctx):
                    keys = (piece + 1) * local
                    here = slice(piece * local, keys)
                    query = whole[0, r, here, :] * SCORE_SCALE
                    back = do_in[r, here, :]
                    key = whole[1, r, :keys, :]
                    value = whole[2, r, :keys, :]
                    k_at = lax.broadcasted_iota(jnp.int32, (keys, local), 0)
                    q_at = lax.broadcasted_iota(jnp.int32, (keys, local), 1) + piece * local
                    allowed = (k_at <= q_at) & (k_at >= starts[:, here])
                    turned = None
                    for head in range(heads):
                        q_head = jnp.where(lane_head == head, query, jnp.zeros_like(query))
                        b_head = jnp.where(lane_head == head, back, jnp.zeros_like(back))
                        scores = jnp.where(allowed, dot_nt(key, q_head), MASK_FILL)
                        peak = jnp.max(scores, axis=0, keepdims=True)
                        powers = jnp.exp(scores - peak)
                        total = jnp.sum(powers, axis=0, keepdims=True)
                        probs = powers * (1.0 / total)
                        back_probs = dot_nt(value, b_head)
                        delta = jnp.sum(probs * back_probs, axis=0, keepdims=True)
                        back_scores = (probs * (back_probs - delta)).astype(BF)
                        value_sum[:keys] += dot(probs.astype(BF), b_head)
                        key_sum[:keys] += dot(back_scores, q_head)
                        sub = dot(key_turned[:, :keys], back_scores)
                        turned = sub if head == 0 else jnp.where(line_head == head, sub, turned)
                    back_query = turned.T * SCORE_SCALE
                    dq_out[piece, 0, r] = turn(
                        back_query, cos[r, here, :], sin[r, here, :], -1
                    ).astype(BF)
                for piece in range(ctx):
                    here = slice(piece * local, (piece + 1) * local)
                    dq_out[piece, 1, r] = turn(
                        key_sum[here, :], cos[r, here, :], sin[r, here, :], -1
                    ).astype(BF)
                    if n == top:
                        back_value = 0.5 * value_sum[here, :]
                        carry[r, here, :] = back_value
                    else:
                        back_value = value_sum[here, :] + carry[r, here, :]
                    dq_out[piece, 2, r] = back_value.astype(BF)
                return nothing

            lax.fori_loop(0, 2, row_step, 0)

        def spread(buffer, landing, target_of):
            made = []
            for bit in range(1, ctx):
                to = lax.bitwise_xor(z, bit)
                made.append(
                    link(buffer.at[to], target_of(landing, z), target_of(landing, to), "ctx", bit)
                )
            return made

        def own_copy(source, target):
            copy = pltpu.make_async_copy(source, target, out_sems.at[1])
            copy.start()
            return copy

        def token_rows(ref, index):
            return ref.at[:, rows(index, local), :]

        def slab_of(ref, index):
            return ref.at[index]

        jobs = {}
        gain_value = lambda n: gain[n : n + 1, :]
        f_link = None
        do_links, dq_links = [], []
        for n in (1, 0):
            job = {name: Reduce(name, n) for name in names}
            jobs[n] = job
            loaded("act")
            e_link.arrived()
            compute_down(job["d"])
            if n:
                load("act", act_i.at[0], act)
            loaded("wd", "kept")
            mlp_back()
            if n:
                load("wd", wd_i.at[0], wd)
            loaded("wg")
            sums = partial_sums(0, lambda columns: dot_nt(kept[...], wg[columns, :]))
            if n:
                load("wg", wg_i.at[0], wg)
            loaded("wide")
            if f_link is not None:
                f_link.sent()
            sums.arrived()
            norm_step(wide[...], gain_value(2 * n + 1), 2 * n + 1, 0, middle, fgrad)
            f_link = pair_link(fgrad).start()
            if n:
                load("wide", stream_i, wide)
            loaded("wo")
            for one in do_links:
                one.sent()
            f_link.arrived()
            for tile in range(half // 256):
                back = dot_nt(fgrad[...], wo[tile * 256 : (tile + 1) * 256, :]).astype(BF)
                for sub in range(256 // group):
                    do_out[tile * 256 // group + sub] = back[
                        :, sub * group : (sub + 1) * group
                    ].reshape(2, local, group)
            if n:
                load("wo", wo_i.at[0], wo)
            do_links = spread(do_out, do_in, token_rows)
            for one in do_links:
                one.start()
            own = own_copy(do_out.at[z], token_rows(do_in, z))
            loaded("norm")
            compute_blocks(job["g"], norm, kept)
            load("norm", n1_i.at[n], norm)
            if n:
                load("kept", kept_i.at[0], kept)
            loaded("mix")
            compute_blocks(job["o"], mix, fgrad)
            if not n:
                f_link.sent()
                load("tok", tok_i, fgrad.at[pl.ds(0, local), :])
            if n:
                load("mix", mix_i.at[0], mix)
                job["d"].first()
                job["d"].second()
            else:
                jobs[1]["d"].across()
                jobs[1]["g"].inward()
                jobs[1]["q"].first()
                job["d"].first()
            loaded("whole", "cos", "sin")
            own.wait()
            for one in do_links:
                one.arrived()
            for one in dq_links:
                one.sent()
            attend_step(n)
            if n:
                load("whole", whole_i.at[0], whole)
            dq_links = spread(dq_out, dq_in, slab_of)
            for one in dq_links:
                one.start()
            own = own_copy(dq_out.at[z], dq_in.at[z])
            if n:
                job["g"].first()
                job["o"].first()
                job["d"].inward()
                job["g"].second()
                job["o"].second()
            else:
                jobs[1]["o"].inward()
                jobs[1]["q"].second()
                jobs[1]["d"].outward()
                jobs[1]["d"].write()
                job["d"].second()
                jobs[1]["g"].across()
                jobs[1]["o"].across()
                job["g"].first()
                job["o"].first()
                jobs[1]["q"].inward()
            loaded("wq")
            own.wait()
            for one in dq_links:
                one.arrived()
            for k in range(ctx):
                for kind in range(3):
                    base = kind * half + k * group
                    joined[:, base : base + group] = dq_in[k, kind].reshape(both, group)
            sums = partial_sums(1, lambda columns: dot_nt(joined[...], wq[columns, :]))
            if n:
                load("wq", wq_i.at[0], wq)
            loaded("norm")
            compute_blocks(job["q"], norm, joined)
            if n:
                load("norm", n2_i.at[0], norm)
            loaded("wide")
            e_link.sent()
            sums.arrived()
            if n:
                norm_step(wide[...], gain_value(2 * n), 2 * n, 1, grad, flow)
                e_link = pair_link(flow).start()
                load("wide", mid_i.at[0], wide)
            else:
                loaded("tok")
                norm_step(fgrad[:local].astype(F32), gain_value(0), 0, 1, grad_o, None)

        for s in range(shards):
            gain_send[s] = jnp.concatenate(
                [gain_rows[:4, s * block : (s + 1) * block], jnp.zeros((4, block), F32)]
            )
        gain_links = []
        for bit in range(1, shards):
            to = lax.bitwise_xor(f, bit)
            gain_links.append(
                link(gain_send.at[to], gain_land.at[f], gain_land.at[to], "fsdp", bit).start()
            )
        gain_land[f] = gain_send[f]

        upper, lower = jobs[1], jobs[0]
        lower["q"].first()
        for one in gain_links:
            one.arrived()
        total = gain_land[0]
        for s in range(1, shards):
            total = total + gain_land[s]
        gain_sum[...] = total
        line_links = []
        for bit in range(1, ctx):
            to = lax.bitwise_xor(z, bit)
            line_links.append(
                link(gain_sum, gain_line.at[z], gain_line.at[to], "ctx", bit).start()
            )
        gain_line[z] = total
        upper["g"].outward()
        upper["o"].outward()
        upper["o"].write()
        upper["g"].write()
        lower["g"].second()
        lower["o"].second()
        upper["q"].across()
        lower["d"].inward()
        lower["g"].inward()
        lower["o"].inward()
        upper["q"].outward()
        upper["q"].write()
        lower["q"].second()
        lower["d"].across()
        lower["q"].inward()
        lower["g"].across()
        lower["o"].across()
        lower["q"].across()
        lower["d"].outward()
        lower["d"].write()
        lower["g"].outward()
        lower["o"].outward()
        lower["o"].write()
        lower["q"].outward()
        lower["g"].write()
        lower["q"].write()
        for one in line_links:
            one.arrived()
        total = gain_line[0]
        for k in range(1, ctx):
            total = total + gain_line[k]
        gain_o[...] = total
        for one in flights:
            one.sent()

    def vm(*dims, kind=BF):
        return pltpu.VMEM(dims, kind)

    outs = [
        shape((local, width), F32),
        shape((8, block), F32),
        shape((layers, block, 3 * width), BF),
        shape((layers, block, width), BF),
        shape((layers, block, 2 * hid), BF),
        shape((layers, block, 2 * hid), BF),
        shape((layers, hid_block, width), BF),
    ]
    for name in names:
        count, columns = sizes[name]
        outs += [
            shape((layers, 2, count, columns // 2), BF),
            shape((layers, 2, count, columns // 2), BF),
            shape((layers, count, columns // 2), BF),
            shape((layers, count, columns // 2), BF),
            shape((layers, 3, count, columns), BF),
        ]
    outs += [shape((layers, block, sizes[name][1]), BF) for name in ("g", "q")]
    scratch = [
        vm(width, 3 * half),
        vm(half, width),
        vm(width, 2 * hid),
        vm(hid, width),
        vm(both, hid),
        vm(both, 2 * hid),
        vm(both, width),
        vm(3, 2, span, group),
        vm(both, half),
        vm(local, width, kind=F32),
        vm(both, width),
        vm(both, width),
        vm(2, local, width),
        vm(2, span, group),
        vm(ctx, 3, 2, local, group),
        vm(local, width, kind=F32),
        vm(local, width),
        vm(local, width, kind=F32),
        vm(local, width, kind=F32),
        vm(ctx, 2, local, group),
        vm(ctx, 3, 2, local, group),
        vm(span, group, kind=F32),
        vm(span, group, kind=F32),
        vm(2, span, group, kind=F32),
        vm(both, 3 * half),
        vm(2, span, 128, kind=F32),
        vm(2, span, 128, kind=F32),
    ]
    scratch += [vm(chips * sizes[name][0], sizes[name][1]) for name in names]
    scratch += [vm(*sizes[name]) for name in names]
    scratch += [
        vm(2, max(hid_block, 2 * block), hid),
        vm(block, 3 * width),
        vm(8, width, kind=F32),
        vm(shards, 8, block, kind=F32),
        vm(shards, 8, block, kind=F32),
        vm(8, block, kind=F32),
        vm(ctx, 8, block, kind=F32),
        pltpu.SemaphoreType.DMA((2, 144)),
        pltpu.SemaphoreType.DMA((20,)),
        pltpu.SemaphoreType.DMA((2,)),
        pltpu.SemaphoreType.DMA((6,)),
    ]
    (wq, wo, wg, wd, n1, n2, whole, mix, mid, stream, act, kept) = saved[:12]
    gain_all, cosines, sines, lens_all = saved[12:16]
    return pl.pallas_call(
        kernel,
        out_shape=outs,
        in_specs=[ANY] * 2 + [VM] * 2 + [ANY] * 14,
        out_specs=[VM] * 2 + [ANY] * (len(outs) - 2),
        scratch_shapes=scratch,
        compiler_params=pltpu.CompilerParams(
            vmem_limit_bytes=63 * MIB, collective_id=1, has_side_effects=True
        ),
        cost_estimate=pl.CostEstimate(
            flops=28 * 10**9, bytes_accessed=100 * MIB, transcendentals=0
        ),
    )(
        cotangent, tokens, lens_all, gain_all, wq, wo, wg, wd, n1, n2, whole, mix, mid, stream,
        act, kept, cosines, sines,
    )


def add_low(left, right):
    return (left.astype(F32) + right.astype(F32)).astype(BF)


def reduce_chips(blocks, chips):
    if chips != 4:
        total = blocks[0].astype(F32)
        for k in range(1, chips):
            total = total + swap(blocks[k], "fsdp", 2 * k).astype(F32)
        return total.astype(BF)
    send_x, keep_x, send_y, keep_y = blocks
    got_x = swap(send_x, "fsdp", 2)
    got_y = swap(send_y, "fsdp", 4)
    on_x = swap(add_low(keep_x[1], got_x[1]), "fsdp", 4)
    on_y = swap(add_low(keep_y[1], got_y[1]), "fsdp", 2)
    first = add_low(add_low(keep_x[0], got_x[0]), on_x)
    second = add_low(add_low(keep_y[0], got_y[0]), on_y)
    return jnp.concatenate([first, second], axis=1)


def reduce_line(block):
    if lax.axis_size("ctx") != 4:
        return lax.psum(block, "ctx")
    z = lax.axis_index("ctx")
    inner = (z == 1) | (z == 2)
    inward = lax.ppermute(block, "ctx", [(0, 1), (3, 2)])
    pair = jnp.where(inner, add_low(block, inward), block)
    across = lax.ppermute(pair, "ctx", [(1, 2), (2, 1)])
    total = add_low(pair, across)
    outward = lax.ppermute(total, "ctx", [(1, 0), (2, 3)])
    return jnp.where(inner, total, outward)


def own_rows(block):
    core = lax.axis_index("fsdp") % 2
    rows = block.shape[0] // 2
    mine = lax.dynamic_slice_in_dim(block, core * rows, rows)
    theirs = swap(lax.dynamic_slice_in_dim(block, (1 - core) * rows, rows), "fsdp", 1)
    low = jnp.where(core == 0, mine, theirs)
    high = jnp.where(core == 0, theirs, mine)
    return jnp.stack([low, high])


def chip_piece(mine, other):
    core = lax.axis_index("fsdp") % 2
    got = swap(other, "fsdp", 1)
    return jnp.where(
        core == 0, jnp.concatenate([mine, got]), jnp.concatenate([got, mine])
    )


def document_starts(lengths, index):
    ends = []
    total = jnp.int32(0)
    for j in range(lengths.shape[0]):
        total = total + lengths[j]
        ends.append(total)
    start = jnp.zeros_like(index)
    for end in ends:
        start = jnp.where(index >= end, end, start)
    return start


def rotary(positions):
    pairs = HD // 2
    lane = jnp.arange(128, dtype=jnp.int32)
    frequency = jnp.exp(-math.log(10000.0) * jnp.arange(pairs, dtype=F32) / pairs)
    angles = positions.astype(F32)[..., None] * frequency
    cosines = jnp.tile(jnp.cos(angles), 128 // pairs)
    sines = jnp.tile(jnp.sin(angles), 128 // pairs)
    low = jnp.where(lane % HD < pairs, -sines, 0.0)
    high = jnp.where(lane % HD >= pairs, sines, 0.0)
    return [cosines, low, high]


def body(tokens, doc_lengths, cotangent, gains, w_qkv, w_out, w_gate, w_up, w_down):
    _, local, width = tokens.shape
    layers = gains.shape[0]
    shards = lax.axis_size("fsdp")
    ctx = lax.axis_size("ctx")
    chips = shards // 2
    block = width // shards
    hidden = w_gate.shape[2]
    hidden_half = hidden // 2
    hidden_block = hidden // shards
    core = lax.axis_index("fsdp") % 2
    z = lax.axis_index("ctx")
    span = local * ctx

    def pick(array, axis, which):
        return lax.dynamic_index_in_dim(array, which, axis, keepdims=False)

    if chips == 4 and ctx == 4 and layers == 2:
        saved = forward_pass(
            tokens[0], doc_lengths, gains, w_qkv, w_out, w_gate, w_up, w_down
        )
        made = backward_pass(saved, tokens[0], cotangent[0])
        grad, gain_sum, qkv_sum, out_sum, gate_sum, up_sum, down_sum = made[:7]
        sums = [s.astype(F32) for s in (qkv_sum, out_sum, gate_sum, up_sum, down_sum)]
        gain_sum = gain_sum[: 2 * layers].reshape(layers, 2, block)
        return (saved[16][None], grad[None], gain_sum, *sums)

    qkv_weights, out_weights, gu_weights, down_weights = [], [], [], []
    for layer in range(layers):
        qkv = w_qkv[layer].reshape(block, 3, chips, 2, block)
        sides = [pick(qkv, 3, which).reshape(block, -1) for which in (core, 1 - core)]
        qkv_weights.append(gather(chip_piece(*sides), chips))
        out_weights.append(gather(w_out[layer], chips))
        sides = []
        for which in (core, 1 - core):
            both = [
                pick(w[layer].reshape(block, chips, 2, hidden_block), 2, which).reshape(
                    block, hidden_half
                )
                for w in (w_gate, w_up)
            ]
            sides.append(jnp.concatenate(both, axis=1))
        gu_weights.append(gather(chip_piece(*sides), chips))
        down_weights.append(gather(w_down[layer], chips))

    all_gains = lax.all_gather(gains, "fsdp", axis=2, tiled=True)
    gain_rows = [[all_gains[layer, n][None] for n in range(2)] for layer in range(layers)]

    index = jnp.arange(span, dtype=jnp.int32)
    lengths = [doc_lengths[0], swap(doc_lengths, "fsdp", 1)[0]]
    starts = jnp.stack([document_starts(row, index) for row in lengths])
    row_tables = rotary(index[None] - starts)
    here_tables = [lax.dynamic_slice_in_dim(t, z * local, local, axis=1) for t in row_tables]
    head_lanes = min(128, width // 2 // ctx)
    head_tables = [t[:, :, :head_lanes] for t in row_tables]
    start_column = starts[:, :, None]
    start_row = starts[:, None, :]

    def pair(array):
        return (array, swap(array, "fsdp", 1))

    stream = tokens[0]
    kept = []
    first_value = None
    (low,) = join_norm(stream, None, None, gain_rows[0][0])
    for layer in range(layers):
        normed = pair(low)
        slabs, first_value = project(
            *normed, here_tables, first_value, qkv_weights[layer], ctx, layer == layers - 1
        )
        slabs = exchange(slabs)
        mixed = exchange(attend(slabs, start_column))
        own, other, joined = mix_out(mixed, out_weights[layer])
        middle, low = join_norm(stream, own, swap(other, "fsdp", 1), gain_rows[layer][1])
        normed_two = pair(low)
        active, gu_kept = gate_up(*normed_two, gu_weights[layer])
        own, other = down(active, down_weights[layer])
        after = gain_rows[min(layer + 1, layers - 1)][0]
        kept.append((stream, normed, slabs, joined, middle, normed_two, active, gu_kept))
        stream, low = join_norm(middle, own, swap(other, "fsdp", 1), after)
    out_tokens = stream.astype(BF)[None]

    grad = cotangent[0]
    low = cotangent[0]
    carried = None
    gain_grads = [[None, None] for _ in range(layers)]
    done = [None] * layers
    for layer in reversed(range(layers)):
        stream, normed, slabs, joined, middle, normed_two, active, gu_kept = kept[layer]
        sent = pair(low)
        down_blocks = weight_grad([active], sent, chips)
        gu_grads, own, other = mlp_back(
            *sent, gu_kept, gu_weights[layer], down_weights[layer]
        )
        grad, low, gain_grads[layer][1] = norm_back(
            middle, own, swap(other, "fsdp", 1), gain_rows[layer][1], grad
        )
        gu_blocks = weight_grad(normed_two, [gu_grads], chips)
        mixed_back = pair(low)
        grad_slabs = exchange(mix_back(*mixed_back, out_weights[layer], ctx))
        out_blocks = weight_grad([joined], mixed_back, chips)
        grad_slabs, carry_out = attend_back(slabs, grad_slabs, start_row, head_tables, carried)
        carried = carry_out
        own, other, qkv_grads = project_back(exchange(grad_slabs), qkv_weights[layer])
        qkv_blocks = weight_grad(normed, [qkv_grads], chips)
        grad, low, gain_grads[layer][0] = norm_back(
            stream, own, swap(other, "fsdp", 1), gain_rows[layer][0], grad
        )
        down_sum = reduce_line(reduce_chips(down_blocks, chips)).astype(F32)
        gu_sum = own_rows(reduce_line(reduce_chips(gu_blocks, chips)))
        out_sum = reduce_line(reduce_chips(out_blocks, chips)).astype(F32)
        qkv_sum = own_rows(reduce_line(reduce_chips(qkv_blocks, chips)))
        qkv_sum = qkv_sum.reshape(2, block, 3, chips, block).transpose(1, 2, 3, 0, 4)
        qkv_sum = qkv_sum.reshape(block, 3 * width).astype(F32)
        gu_sum = gu_sum.reshape(2, block, 2, chips, hidden_block).transpose(2, 1, 3, 0, 4)
        gu_sum = gu_sum.reshape(2, block, hidden).astype(F32)
        done[layer] = (qkv_sum, out_sum, gu_sum[0], gu_sum[1], down_sum)

    gain_sum = jnp.stack([jnp.concatenate(rows) for rows in gain_grads])
    gain_sum = lax.psum_scatter(gain_sum, "fsdp", scatter_dimension=2, tiled=True)
    gain_sum = lax.psum(gain_sum, "ctx")
    stacked = [jnp.stack([done[layer][n] for layer in range(layers)]) for n in range(5)]
    return (out_tokens, grad[None], gain_sum, *stacked)


def solution(mesh):
    rows = P(None, "fsdp", None)
    tokens = P("fsdp", "ctx", None)
    gains = P(None, None, "fsdp")
    return jax.shard_map(
        body,
        mesh=mesh,
        in_specs=(tokens, P("fsdp", None), tokens, gains, rows, rows, rows, rows, rows),
        out_specs=(tokens, tokens, gains, rows, rows, rows, rows, rows),
        check_vma=False,
    )
```

```python
import math

import jax
import jax.numpy as jnp
from jax import lax
from jax.experimental import pallas as pl
from jax.experimental.pallas import tpu as pltpu
from jax.sharding import PartitionSpec as P

HEADS = 16
HD = 64
EPSILON = 1e-06
SCORE_SCALE = 0.125
MASK_FILL = -1e30
BF = jnp.bfloat16
F32 = jnp.float32
MIB = 1024 * 1024
ANY = pl.BlockSpec(memory_space=pl.ANY)
VM = pl.BlockSpec(memory_space=pltpu.VMEM)
NT = (((1,), (1,)), ((), ()))
TN = (((0,), (0,)), ((), ()))


def dot(left, right):
    return jnp.dot(left, right, preferred_element_type=F32)


def dot_nt(left, right):
    return lax.dot_general(left, right, NT, preferred_element_type=F32)


def dot_tn(left, right):
    return lax.dot_general(left, right, TN, preferred_element_type=F32)


def swap(array, axis, bit):
    size = lax.axis_size(axis)
    return lax.ppermute(array, axis, [(i, i ^ bit) for i in range(size)])


def call(kernel, outs, out_specs, scratch, args, in_specs, flops, vmem):
    nbytes = sum(a.size * a.dtype.itemsize for a in args)
    nbytes += sum(math.prod(o.shape) * o.dtype.itemsize for o in outs)
    return pl.pallas_call(
        kernel,
        out_shape=outs,
        in_specs=in_specs,
        out_specs=out_specs,
        scratch_shapes=scratch,
        compiler_params=pltpu.CompilerParams(vmem_limit_bytes=vmem * MIB),
        cost_estimate=pl.CostEstimate(flops=flops, bytes_accessed=nbytes, transcendentals=0),
    )(*args)


def shape(dims, kind):
    return jax.ShapeDtypeStruct(tuple(dims), kind)


def chip_index():
    return lax.axis_index("fsdp") // 2


def run_copies(copies):
    for copy in copies:
        copy.start()
    for copy in copies:
        copy.wait()


def weight_copies(plan, refs, buffer, sems, first):
    chip = chip_index()
    rows = plan[0][2]
    copies = []
    for number, ((k, offset, count), ref) in enumerate(zip(plan[1], refs)):
        start = pl.multiple_of(lax.bitwise_xor(chip, k) * rows + offset, 16)
        copies.append(
            pltpu.make_async_copy(
                ref, buffer.at[pl.ds(start, count), :], sems.at[first + number]
            )
        )
    return copies


class Pieces:
    def __init__(self, arrays, where, rows):
        self.arrays = arrays
        self.where = where
        self.rows = rows

    @property
    def plan(self):
        return ((0, 0, self.rows), self.where)


def gather(piece, chips):
    rows = piece.shape[0]
    if chips == 4:
        half = rows // 2
        from_x = swap(piece, "fsdp", 2)
        from_y = swap(piece, "fsdp", 4)
        far_one = swap(from_x[:half], "fsdp", 4)
        far_two = swap(from_y[half:], "fsdp", 2)
        return Pieces(
            [piece, from_x, from_y, far_one, far_two],
            [(0, 0, rows), (1, 0, rows), (2, 0, rows), (3, 0, half), (3, half, rows - half)],
            rows,
        )
    arrays = [piece] + [swap(piece, "fsdp", 2 * k) for k in range(1, chips)]
    return Pieces(arrays, [(k, 0, rows) for k in range(chips)], rows)


def rope(x, cosines, low_sine, high_sine):
    width = x.shape[-1]
    return (
        x * cosines
        + pltpu.roll(x, width - HD // 2, 1) * low_sine
        + pltpu.roll(x, HD // 2, 1) * high_sine
    )


def project(n_own, n_other, tables, first_value, weight, ctx, last):
    local, width = n_own.shape
    half = width // 2
    group = half // ctx
    pieces = len(weight.arrays)
    plan = weight.plan

    def kernel(*refs):
        own, other, cos, low, high = refs[:5]
        at = 5
        v_in = None
        if first_value is not None:
            v_in = refs[at]
            at += 1
        w_refs = refs[at : at + pieces]
        at += pieces
        slabs = refs[at : at + ctx]
        at += ctx
        v_out = None
        if first_value is None:
            v_out = refs[at]
            at += 1
        buffer, tokens, slab, sems, out_sems = refs[at:]
        copies = weight_copies(plan, w_refs, buffer, sems, 0)
        for copy in copies:
            copy.start()
        tokens[:local] = own[...]
        tokens[local:] = other[...]
        tables_now = [t[...].reshape(2 * local, 128) for t in (cos, low, high)]
        for copy in copies:
            copy.wait()
        for tile in range(3 * half // 256):
            acc = dot(tokens[...], buffer[:, tile * 256 : (tile + 1) * 256])
            kind = tile * 256 // half
            base = tile * 256 - kind * half
            for sub in range(2):
                x = acc[:, sub * 128 : (sub + 1) * 128]
                column = base + sub * 128
                if kind < 2:
                    x = rope(x, *tables_now)
                elif first_value is not None:
                    x = 0.5 * x + 0.5 * v_in[:, column : column + 128].astype(F32)
                x = x.astype(BF)
                if kind == 2 and v_out is not None:
                    v_out[:, column : column + 128] = x
                for part in range(128 // group):
                    slab[column // group + part, kind] = x[
                        :, part * group : (part + 1) * group
                    ].reshape(2, local, group)
        z = lax.axis_index("ctx")
        run_copies(
            [
                pltpu.make_async_copy(slab.at[lax.bitwise_xor(z, k)], slabs[k], out_sems.at[k])
                for k in range(ctx)
            ]
        )

    args = [n_own, n_other, *tables]
    specs = [VM] * 5
    outs = [shape((3, 2, local, group), BF)] * ctx
    out_specs = [ANY] * ctx
    if first_value is not None:
        args.append(first_value)
        specs.append(VM)
    else:
        outs.append(shape((2 * local, half), BF))
        out_specs.append(VM)
    args += weight.arrays
    specs += [ANY] * pieces
    got = call(
        kernel,
        outs,
        out_specs,
        [
            pltpu.VMEM((width, 3 * half), BF),
            pltpu.VMEM((2 * local, width), BF),
            pltpu.VMEM((ctx, 3, 2, local, group), BF),
            pltpu.SemaphoreType.DMA((pieces,)),
            pltpu.SemaphoreType.DMA((ctx,)),
        ],
        args,
        specs,
        2 * 2 * local * width * 3 * half,
        40,
    )
    return got[:ctx], (first_value if first_value is not None else got[ctx])


def exchange(slabs):
    return [slabs[0]] + [swap(slabs[k], "ctx", k) for k in range(1, len(slabs))]


def attend(slabs, start_column):
    ctx = len(slabs)
    _, _, local, group = slabs[0].shape
    span = ctx * local
    heads = group // HD

    def kernel(*refs):
        starts = refs[0]
        ins = refs[1 : 1 + ctx]
        outs = refs[1 + ctx : 1 + 2 * ctx]
        whole, mixed, sems, out_sems = refs[1 + 2 * ctx :]
        z = lax.axis_index("ctx")
        copies = []
        for k in range(ctx):
            at = pl.multiple_of(lax.bitwise_xor(z, k) * local, 16)
            copies.append(
                pltpu.make_async_copy(
                    ins[k], whole.at[:, :, pl.ds(at, local), :], sems.at[k]
                )
            )
        run_copies(copies)
        lane = lax.broadcasted_iota(jnp.int32, (1, group), 1) // HD

        def row_step(row, carry):
            for block in range(ctx):
                keys = (block + 1) * local
                here = slice(block * local, keys)
                query = whole[0, row, here, :] * SCORE_SCALE
                key = whole[1, row, :keys, :]
                value = whole[2, row, :keys, :]
                k_at = lax.broadcasted_iota(jnp.int32, (local, keys), 1)
                q_at = lax.broadcasted_iota(jnp.int32, (local, keys), 0) + block * local
                allowed = (k_at <= q_at) & (k_at >= starts[row, here, :])
                result = None
                for head in range(heads):
                    q_head = jnp.where(lane == head, query, jnp.zeros_like(query))
                    scores = jnp.where(allowed, dot_nt(q_head, key), MASK_FILL)
                    top = jnp.max(scores, axis=1, keepdims=True)
                    powers = jnp.exp(scores - top)
                    total = jnp.sum(powers, axis=1, keepdims=True)
                    probs = (powers * (1.0 / total)).astype(BF)
                    out = dot(probs, value)
                    result = out if result is None else jnp.where(lane == head, out, result)
                mixed[block, row] = result.astype(BF)
            return carry

        lax.fori_loop(0, 2, row_step, 0)
        run_copies(
            [
                pltpu.make_async_copy(mixed.at[lax.bitwise_xor(z, k)], outs[k], out_sems.at[k])
                for k in range(ctx)
            ]
        )

    return call(
        kernel,
        [shape((2, local, group), BF)] * ctx,
        [ANY] * ctx,
        [
            pltpu.VMEM((3, 2, span, group), BF),
            pltpu.VMEM((ctx, 2, local, group), BF),
            pltpu.SemaphoreType.DMA((ctx,)),
            pltpu.SemaphoreType.DMA((ctx,)),
        ],
        [start_column, *slabs],
        [VM] + [ANY] * ctx,
        2 * 2 * 2 * heads * span * span * 128,
        40,
    )


def halves_out(product, own_ref, other_ref, columns, local):
    own_ref[:, columns] = product[:local]
    other_ref[:, columns] = product[local:].astype(BF)


def mix_out(slabs, weight):
    ctx = len(slabs)
    _, local, group = slabs[0].shape
    half = ctx * group
    width = weight.arrays[0].shape[1]
    pieces = len(weight.arrays)
    plan = weight.plan

    def kernel(*refs):
        ins = refs[:ctx]
        w_refs = refs[ctx : ctx + pieces]
        own, other, joined, buffer, landed, sems = refs[ctx + pieces :]
        z = lax.axis_index("ctx")
        copies = weight_copies(plan, w_refs, buffer, sems, ctx)
        for k in range(ctx):
            copies.append(
                pltpu.make_async_copy(ins[k], landed.at[lax.bitwise_xor(z, k)], sems.at[k])
            )
        run_copies(copies)
        for k in range(ctx):
            joined[:, k * group : (k + 1) * group] = landed[k].reshape(2 * local, group)
        for tile in range(width // 256):
            columns = slice(tile * 256, (tile + 1) * 256)
            halves_out(dot(joined[...], buffer[:, columns]), own, other, columns, local)

    return call(
        kernel,
        [shape((local, width), F32), shape((local, width), BF), shape((2 * local, half), BF)],
        [VM] * 3,
        [
            pltpu.VMEM((half, width), BF),
            pltpu.VMEM((ctx, 2, local, group), BF),
            pltpu.SemaphoreType.DMA((ctx + pieces,)),
        ],
        [*slabs, *weight.arrays],
        [ANY] * (ctx + pieces),
        2 * 2 * local * half * width,
        24,
    )


def join_norm(base, own, other, gain):
    local, width = base.shape
    fresh = own is not None

    def kernel(*refs):
        if fresh:
            base_ref, own_ref, other_ref, gain_ref, sum_ref, low_ref = refs
            total = base_ref[...].astype(F32) + own_ref[...] + other_ref[...].astype(F32)
            sum_ref[...] = total
        else:
            base_ref, gain_ref, low_ref = refs
            total = base_ref[...].astype(F32)
        factor = lax.rsqrt(jnp.mean(total * total, axis=1, keepdims=True) + EPSILON)
        low_ref[...] = (total * factor * gain_ref[...].astype(F32)).astype(BF)

    outs = [shape((local, width), BF)]
    args = [base, gain]
    if fresh:
        outs = [shape((local, width), F32)] + outs
        args = [base, own, other, gain]
    return call(
        kernel, outs, [VM] * len(outs), [], args, [VM] * len(args), 8 * local * width, 16
    )


def gate_up(n_own, n_other, weight):
    local, width = n_own.shape
    hidden2 = weight.arrays[0].shape[1]
    hidden = hidden2 // 2
    pieces = len(weight.arrays)
    plan = weight.plan

    def kernel(*refs):
        own, other = refs[:2]
        w_refs = refs[2 : 2 + pieces]
        active, kept, buffer, tokens, sems = refs[2 + pieces :]
        copies = weight_copies(plan, w_refs, buffer, sems, 0)
        for copy in copies:
            copy.start()
        tokens[:local] = own[...]
        tokens[local:] = other[...]
        for copy in copies:
            copy.wait()

        def span_step(base, count):
            here, there = pl.ds(base, count), pl.ds(hidden + base, count)
            gate = dot(tokens[...], buffer[:, here])
            up = dot(tokens[...], buffer[:, there])
            kept[:, here] = gate.astype(BF)
            kept[:, there] = up.astype(BF)
            active[:, here] = (gate * jax.nn.sigmoid(gate) * up).astype(BF)

        def step(tile, carry):
            span_step(pl.multiple_of(tile * 256, 128), 256)
            return carry

        lax.fori_loop(0, hidden // 256, step, 0)
        if hidden % 256:
            span_step(hidden // 256 * 256, hidden % 256)

    return call(
        kernel,
        [shape((2 * local, hidden), BF), shape((2 * local, hidden2), BF)],
        [VM] * 2,
        [
            pltpu.VMEM((width, hidden2), BF),
            pltpu.VMEM((2 * local, width), BF),
            pltpu.SemaphoreType.DMA((pieces,)),
        ],
        [n_own, n_other, *weight.arrays],
        [VM] * 2 + [ANY] * pieces,
        2 * 2 * local * width * hidden2,
        40,
    )


def down(active, weight):
    tokens, hidden = active.shape
    local = tokens // 2
    width = weight.arrays[0].shape[1]
    pieces = len(weight.arrays)
    plan = weight.plan

    def kernel(*refs):
        left = refs[0]
        w_refs = refs[1 : 1 + pieces]
        own, other, buffer, sems = refs[1 + pieces :]
        run_copies(weight_copies(plan, w_refs, buffer, sems, 0))

        def step(tile, carry):
            columns = pl.ds(pl.multiple_of(tile * 256, 256), 256)
            halves_out(dot(left[...], buffer[:, columns]), own, other, columns, local)
            return carry

        lax.fori_loop(0, width // 256, step, 0)

    return call(
        kernel,
        [shape((local, width), F32), shape((local, width), BF)],
        [VM] * 2,
        [pltpu.VMEM((hidden, width), BF), pltpu.SemaphoreType.DMA((pieces,))],
        [active, *weight.arrays],
        [VM] + [ANY] * pieces,
        2 * tokens * hidden * width,
        24,
    )


def mlp_back(e_own, e_other, kept, gu_weight, down_weight):
    local, width = e_own.shape
    hidden2 = kept.shape[1]
    hidden = hidden2 // 2
    pieces = len(gu_weight.arrays)
    more = len(down_weight.arrays)
    gu_plan, down_plan = gu_weight.plan, down_weight.plan

    def kernel(*refs):
        e_one, e_two, kept_ref = refs[:3]
        gu_refs = refs[3 : 3 + pieces]
        down_refs = refs[3 + pieces : 3 + pieces + more]
        grads, own, other, gu, wd, tokens, sems = refs[3 + pieces + more :]
        first = weight_copies(down_plan, down_refs, wd, sems, pieces)
        second = weight_copies(gu_plan, gu_refs, gu, sems, 0)
        for copy in first + second:
            copy.start()
        tokens[:local] = e_one[...]
        tokens[local:] = e_two[...]
        for copy in first:
            copy.wait()

        def span_step(base, count):
            here, there = pl.ds(base, count), pl.ds(hidden + base, count)
            flow = dot_nt(tokens[...], wd[here, :])
            gate = kept_ref[:, here].astype(F32)
            up = kept_ref[:, there].astype(F32)
            sig = jax.nn.sigmoid(gate)
            grads[:, here] = (flow * up * sig * (1.0 + gate * (1.0 - sig))).astype(BF)
            grads[:, there] = (flow * gate * sig).astype(BF)

        def step(tile, carry):
            span_step(pl.multiple_of(tile * 256, 128), 256)
            return carry

        lax.fori_loop(0, hidden // 256, step, 0)
        if hidden % 256:
            span_step(hidden // 256 * 256, hidden % 256)
        for copy in second:
            copy.wait()

        def back_step(tile, carry):
            rows = pl.ds(pl.multiple_of(tile * 256, 256), 256)
            halves_out(dot_nt(grads[...], gu[rows, :]), own, other, rows, local)
            return carry

        lax.fori_loop(0, width // 256, back_step, 0)

    return call(
        kernel,
        [
            shape((2 * local, hidden2), BF),
            shape((local, width), F32),
            shape((local, width), BF),
        ],
        [VM] * 3,
        [
            pltpu.VMEM((width, hidden2), BF),
            pltpu.VMEM((hidden, width), BF),
            pltpu.VMEM((2 * local, width), BF),
            pltpu.SemaphoreType.DMA((pieces + more,)),
        ],
        [e_own, e_other, kept, *gu_weight.arrays, *down_weight.arrays],
        [VM] * 3 + [ANY] * (pieces + more),
        2 * 2 * local * width * hidden * 3,
        48,
    )


def norm_back(stream, own, other, gain, grad):
    local, width = stream.shape

    def kernel(x_ref, own_ref, other_ref, gain_ref, grad_ref, out_ref, low_ref, gain_out):
        x = x_ref[...].astype(F32)
        factor = lax.rsqrt(jnp.mean(x * x, axis=1, keepdims=True) + EPSILON)
        flow = own_ref[...] + other_ref[...].astype(F32)
        scaled = flow * gain_ref[...].astype(F32)
        gain_out[...] = jnp.sum(flow * x * factor, axis=0, keepdims=True)
        mean_term = jnp.mean(scaled * x, axis=1, keepdims=True)
        result = (
            grad_ref[...].astype(F32)
            + factor * scaled
            - x * (factor * factor * factor * mean_term)
        )
        out_ref[...] = result
        low_ref[...] = result.astype(BF)

    return call(
        kernel,
        [shape((local, width), F32), shape((local, width), BF), shape((1, width), F32)],
        [VM] * 3,
        [],
        [stream, own, other, gain, grad],
        [VM] * 5,
        12 * local * width,
        24,
    )


def mix_back(f_own, f_other, weight, ctx):
    local, width = f_own.shape
    half = width // 2
    group = half // ctx
    pieces = len(weight.arrays)
    plan = weight.plan

    def kernel(*refs):
        own, other = refs[:2]
        w_refs = refs[2 : 2 + pieces]
        slabs = refs[2 + pieces : 2 + pieces + ctx]
        buffer, tokens, slab, sems, out_sems = refs[2 + pieces + ctx :]
        copies = weight_copies(plan, w_refs, buffer, sems, 0)
        for copy in copies:
            copy.start()
        tokens[:local] = own[...]
        tokens[local:] = other[...]
        for copy in copies:
            copy.wait()
        for tile in range(half // 256):
            flow = dot_nt(tokens[...], buffer[tile * 256 : (tile + 1) * 256, :]).astype(BF)
            for part in range(256 // group):
                slab[tile * 256 // group + part] = flow[
                    :, part * group : (part + 1) * group
                ].reshape(2, local, group)
        z = lax.axis_index("ctx")
        run_copies(
            [
                pltpu.make_async_copy(slab.at[lax.bitwise_xor(z, k)], slabs[k], out_sems.at[k])
                for k in range(ctx)
            ]
        )

    return call(
        kernel,
        [shape((2, local, group), BF)] * ctx,
        [ANY] * ctx,
        [
            pltpu.VMEM((half, width), BF),
            pltpu.VMEM((2 * local, width), BF),
            pltpu.VMEM((ctx, 2, local, group), BF),
            pltpu.SemaphoreType.DMA((pieces,)),
            pltpu.SemaphoreType.DMA((ctx,)),
        ],
        [f_own, f_other, *weight.arrays],
        [VM] * 2 + [ANY] * pieces,
        2 * 2 * local * half * width,
        24,
    )


def attend_back(slabs, grad_slabs, start_row, tables, carried):
    ctx = len(grad_slabs)
    _, local, group = grad_slabs[0].shape
    span = ctx * local
    parts = len(slabs)
    heads = group // HD
    first = carried is not None

    def kernel(*refs):
        starts, cos, low, high = refs[:4]
        at = 4
        carry_in = None
        if first:
            carry_in = refs[at]
            at += 1
        ins = refs[at : at + parts]
        at += parts
        grads = refs[at : at + ctx]
        outs = refs[at + ctx : at + 2 * ctx]
        at += 2 * ctx
        carry_out = None
        if not first:
            carry_out = refs[at]
            at += 1
        whole, flow_in, slab, key_sum, value_sum, sems, out_sems = refs[at:]
        z = lax.axis_index("ctx")
        copies = []
        if parts == 1:
            copies.append(pltpu.make_async_copy(ins[0], whole, sems.at[0]))
        for k in range(ctx):
            to = pl.ds(pl.multiple_of(lax.bitwise_xor(z, k) * local, 16), local)
            if parts > 1:
                copies.append(
                    pltpu.make_async_copy(ins[k], whole.at[:, :, to, :], sems.at[k])
                )
            copies.append(
                pltpu.make_async_copy(grads[k], flow_in.at[:, to, :], sems.at[ctx + k])
            )
        run_copies(copies)
        lane = lax.broadcasted_iota(jnp.int32, (1, group), 1) // HD
        line = lax.broadcasted_iota(jnp.int32, (group, 1), 0) // HD

        def row_step(row, carry):
            key_sum[...] = jnp.zeros_like(key_sum)
            value_sum[...] = jnp.zeros_like(value_sum)
            key_turned = whole[1, row].astype(F32).T.astype(BF)
            for block in range(ctx):
                keys = (block + 1) * local
                here = slice(block * local, keys)
                query = whole[0, row, here, :] * SCORE_SCALE
                grad = flow_in[row, here, :]
                key = whole[1, row, :keys, :]
                value = whole[2, row, :keys, :]
                k_at = lax.broadcasted_iota(jnp.int32, (keys, local), 0)
                q_at = lax.broadcasted_iota(jnp.int32, (keys, local), 1) + block * local
                allowed = (k_at <= q_at) & (k_at >= starts[row, :, here])
                turned = None
                for head in range(heads):
                    mine = lane == head
                    q_head = jnp.where(mine, query, jnp.zeros_like(query))
                    g_head = jnp.where(mine, grad, jnp.zeros_like(grad))
                    scores = jnp.where(allowed, dot_nt(key, q_head), MASK_FILL)
                    top = jnp.max(scores, axis=0, keepdims=True)
                    powers = jnp.exp(scores - top)
                    total = jnp.sum(powers, axis=0, keepdims=True)
                    probs = powers * (1.0 / total)
                    grad_probs = dot_nt(value, g_head)
                    delta = jnp.sum(probs * grad_probs, axis=0, keepdims=True)
                    grad_scores = (probs * (grad_probs - delta)).astype(BF)
                    value_sum[:keys] += dot(probs.astype(BF), g_head)
                    key_sum[:keys] += dot(grad_scores, q_head)
                    part = dot(key_turned[:, :keys], grad_scores)
                    turned = part if turned is None else jnp.where(line == head, part, turned)
                grad_query = turned.T * SCORE_SCALE
                slab[block, 0, row] = rope(
                    grad_query, cos[row, here, :], -low[row, here, :], -high[row, here, :]
                ).astype(BF)
            for block in range(ctx):
                here = slice(block * local, (block + 1) * local)
                slab[block, 1, row] = rope(
                    key_sum[here, :], cos[row, here, :], -low[row, here, :], -high[row, here, :]
                ).astype(BF)
                if first:
                    total_value = value_sum[here, :] + carry_in[row, here, :]
                else:
                    total_value = 0.5 * value_sum[here, :]
                    carry_out[row, here, :] = total_value
                slab[block, 2, row] = total_value.astype(BF)
            return carry

        lax.fori_loop(0, 2, row_step, 0)
        run_copies(
            [
                pltpu.make_async_copy(slab.at[lax.bitwise_xor(z, k)], outs[k], out_sems.at[k])
                for k in range(ctx)
            ]
        )

    args = [start_row, *tables]
    specs = [VM] * 4
    outs = [shape((3, 2, local, group), BF)] * ctx
    out_specs = [ANY] * ctx
    if first:
        args.append(carried)
        specs.append(VM)
    else:
        outs.append(shape((2, span, group), F32))
        out_specs.append(VM)
    got = call(
        kernel,
        outs,
        out_specs,
        [
            pltpu.VMEM((3, 2, span, group), BF),
            pltpu.VMEM((2, span, group), BF),
            pltpu.VMEM((ctx, 3, 2, local, group), BF),
            pltpu.VMEM((span, group), F32),
            pltpu.VMEM((span, group), F32),
            pltpu.SemaphoreType.DMA((2 * ctx,)),
            pltpu.SemaphoreType.DMA((ctx,)),
        ],
        [*args, *slabs, *grad_slabs],
        specs + [ANY] * (parts + ctx),
        2 * 5 * 2 * heads * span * span * 128,
        48,
    )
    return got[:ctx], (None if first else got[ctx])


def project_back(slabs, weight):
    ctx = len(slabs)
    _, _, local, group = slabs[0].shape
    half = ctx * group
    width = 2 * half
    pieces = len(weight.arrays)
    plan = weight.plan

    def kernel(*refs):
        ins = refs[:ctx]
        w_refs = refs[ctx : ctx + pieces]
        own, other, joined, buffer, landed, sems = refs[ctx + pieces :]
        z = lax.axis_index("ctx")
        copies = weight_copies(plan, w_refs, buffer, sems, ctx)
        for k in range(ctx):
            copies.append(
                pltpu.make_async_copy(ins[k], landed.at[lax.bitwise_xor(z, k)], sems.at[k])
            )
        run_copies(copies)
        for k in range(ctx):
            for kind in range(3):
                base = kind * half + k * group
                joined[:, base : base + group] = landed[k, kind].reshape(2 * local, group)

        def step(tile, carry):
            rows = pl.ds(pl.multiple_of(tile * 256, 256), 256)
            halves_out(dot_nt(joined[...], buffer[rows, :]), own, other, rows, local)
            return carry

        lax.fori_loop(0, width // 256, step, 0)

    return call(
        kernel,
        [
            shape((local, width), F32),
            shape((local, width), BF),
            shape((2 * local, 3 * half), BF),
        ],
        [VM] * 3,
        [
            pltpu.VMEM((width, 3 * half), BF),
            pltpu.VMEM((ctx, 3, 2, local, group), BF),
            pltpu.SemaphoreType.DMA((ctx + pieces,)),
        ],
        [*slabs, *weight.arrays],
        [ANY] * (ctx + pieces),
        2 * 2 * local * 3 * half * width,
        40,
    )


def weight_grad(left, right, chips):
    lefts, rights = list(left), list(right)
    tall = lefts[0].shape[1]
    wide = rights[0].shape[1]
    tokens = lefts[0].shape[0] * len(lefts)
    rows = tall // chips
    halved = wide // 2
    split = chips == 4

    def kernel(*refs):
        l_refs = refs[: len(lefts)]
        r_refs = refs[len(lefts) : len(lefts) + len(rights)]
        at = len(lefts) + len(rights)
        count = 4 if split else chips
        outs = refs[at : at + count]
        grads, l_buf, r_buf, sems = refs[at + count :]
        if len(lefts) == 2:
            l_buf[: tokens // 2] = l_refs[0][...]
            l_buf[tokens // 2 :] = l_refs[1][...]
            l_now = l_buf
        else:
            l_now = l_refs[0]
        if len(rights) == 2:
            r_buf[: tokens // 2] = r_refs[0][...]
            r_buf[tokens // 2 :] = r_refs[1][...]
            r_now = r_buf
        else:
            r_now = r_refs[0]

        def tile_step(base, size):
            turned = l_now[:, pl.ds(base, size)]
            for start in range(0, wide, 512):
                stop = min(start + 512, wide)
                grads[pl.ds(base, size), start:stop] = dot_tn(
                    turned, r_now[:, start:stop]
                ).astype(BF)

        def step(tile, carry):
            tile_step(pl.multiple_of(tile * 256, 256), 256)
            return carry

        lax.fori_loop(0, tall // 256, step, 0)
        if tall % 256:
            tile_step(tall // 256 * 256, tall % 256)
        chip = chip_index()

        def block(k):
            return pl.ds(pl.multiple_of(lax.bitwise_xor(chip, k) * rows, 16), rows)

        copies = []
        if split:
            for which, order in enumerate(((1, 3), (0, 2), (2, 3), (0, 1))):
                columns = pl.ds((which // 2) * halved, halved)
                for slot, k in enumerate(order):
                    copies.append(
                        pltpu.make_async_copy(
                            grads.at[block(k), columns],
                            outs[which].at[slot],
                            sems.at[2 * which + slot],
                        )
                    )
        else:
            for k in range(chips):
                copies.append(
                    pltpu.make_async_copy(grads.at[block(k), :], outs[k], sems.at[k])
                )
        run_copies(copies)

    if split:
        outs = [shape((2, rows, halved), BF)] * 4
    else:
        outs = [shape((rows, wide), BF)] * chips
    small = (16, 128)
    return call(
        kernel,
        outs,
        [ANY] * len(outs),
        [
            pltpu.VMEM((tall, wide), BF),
            pltpu.VMEM((tokens, tall) if len(lefts) == 2 else small, BF),
            pltpu.VMEM((tokens, wide) if len(rights) == 2 else small, BF),
            pltpu.SemaphoreType.DMA((8 if split else chips,)),
        ],
        [*lefts, *rights],
        [VM] * (len(lefts) + len(rights)),
        2 * tokens * tall * wide,
        48,
    )


class Link:
    def __init__(self, source, target, arriving, sems, slot, axis, bit):
        device = {axis: lax.bitwise_xor(lax.axis_index(axis), bit)}

        def make(to):
            return pltpu.make_async_remote_copy(
                src_ref=source,
                dst_ref=to,
                send_sem=sems.at[0, slot],
                recv_sem=sems.at[1, slot],
                device_id=device,
                device_id_type=pl.DeviceIdType.MESH,
            )

        self.out = make(target)
        self.into = make(arriving)
        self.flying = False

    def start(self):
        self.out.start()
        self.flying = True
        return self

    def arrived(self):
        self.into.wait_recv()

    def sent(self):
        if self.flying:
            self.out.wait_send()
        self.flying = False


def enter(fsdp_bits, ctx_bits):
    barrier = pltpu.get_barrier_semaphore()
    for axis, bits in (("fsdp", fsdp_bits), ("ctx", ctx_bits)):
        for bit in bits:
            pl.semaphore_signal(
                barrier,
                inc=1,
                device_id={axis: lax.bitwise_xor(lax.axis_index(axis), bit)},
                device_id_type=pl.DeviceIdType.MESH,
            )
    pl.semaphore_wait(barrier, len(fsdp_bits) + len(ctx_bits))


def turn(x, cosines, sines, direction):
    width, pairs = x.shape[-1], HD // 2
    lane = lax.broadcasted_iota(jnp.int32, (1, width), 1)
    ahead = pltpu.roll(x, width - pairs, 1)
    behind = pltpu.roll(x, pairs, 1)
    other = jnp.where(lax.rem(lane, HD) < pairs, -ahead, behind)
    return x * cosines + other * (sines if direction > 0 else -sines)


def rms(total, gain):
    factor = lax.rsqrt(jnp.mean(total * total, axis=1, keepdims=True) + EPSILON)
    return (total * factor * gain).astype(BF)


def forward_pass(tokens, doc_lengths, gains, w_qkv, w_out, w_gate, w_up, w_down):
    local, width = tokens.shape
    layers, block, _ = w_qkv.shape
    hidden = w_gate.shape[2]
    hid = hidden // 2
    hid_block = w_down.shape[1]
    half = width // 2
    shards, ctx = lax.axis_size("fsdp"), lax.axis_size("ctx")
    chips = shards // 2
    group = half // ctx
    span = ctx * local
    heads = group // HD
    both = 2 * local
    documents = doc_lengths.shape[1]
    lengths = jnp.zeros((8, 128), jnp.int32).at[:documents].set(doc_lengths[0][:, None])
    gain_rows = jnp.zeros((8, block), F32).at[: 2 * layers].set(
        gains.reshape(2 * layers, block).astype(F32)
    )

    def kernel(*refs):
        (tok, lens, gain_in, qkv_in, out_in, gate_in, up_in, down_in) = refs[:8]
        (wq_o, wo_o, wg_o, wd_o, n1_o, n2_o, whole_o, mix_o, mid_o, stream_o) = refs[8:18]
        (act_o, kept_o, gain_o, cos_o, sin_o, start_o, final_o) = refs[18:25]
        (wq, wo, wg, wd, qkv_raw, gu_raw, q_stage, g_stage) = refs[25:33]
        (n1, n2, whole, slab, mixed, landed, value, mix, mid, stream) = refs[33:43]
        (act, kept, part, other, got, gbuf, lens_all, cos, sin, start) = refs[43:53]
        (sems, local_sems, save_sems) = refs[53:]
        f = lax.axis_index("fsdp")
        z = lax.axis_index("ctx")
        core = lax.rem(f, 2)
        chip = f // 2
        flights = []
        saves = []

        def link(source, target, arriving, axis, bit):
            made = Link(source, target, arriving, sems, len(flights), axis, bit)
            flights.append(made)
            return made

        def save(source, target):
            copy = pltpu.make_async_copy(source, target, save_sems.at[len(saves)])
            copy.start()
            saves.append(copy)
            return len(saves) - 1

        def saved(number):
            if saves[number] is not None:
                saves[number].wait()
            saves[number] = None

        def rows(index, count):
            return pl.ds(pl.multiple_of(index * count, 16), count)

        def fx(bit):
            return lax.bitwise_xor(f, bit)

        def cx(bit):
            return lax.bitwise_xor(chip, bit)

        class Halved:
            def __init__(self, buffer, stage):
                def at(index):
                    return buffer.at[rows(index, block), :]

                self.first = [
                    link(stage, at(f), at(fx(bit)), "fsdp", bit) for bit in (1, 3, 5)
                ] + [link(at(f), at(f), at(fx(bit)), "fsdp", bit) for bit in (2, 4)]
                over_y, over_x, far = 2 * cx(1), 2 * cx(2) + 1, 2 * cx(3)
                self.second = [
                    link(at(over_y), at(over_y), at(far), "fsdp", 4),
                    link(at(over_x), at(over_x), at(far + 1), "fsdp", 2),
                ]

        class Rowed:
            def __init__(self, buffer, source, count):
                small = count // 2

                def at(index):
                    return buffer.at[rows(index, count), :]

                def side(index, which):
                    begin = pl.multiple_of(index * count + which * small, 16)
                    return buffer.at[pl.ds(begin, small), :]

                self.first = [
                    link(source, at(chip), at(cx(bit // 2)), "fsdp", bit) for bit in (2, 4)
                ]
                self.second = [
                    link(side(cx(1), 0), side(cx(1), 0), side(cx(3), 0), "fsdp", 4),
                    link(side(cx(2), 1), side(cx(2), 1), side(cx(3), 1), "fsdp", 2),
                ]

        def begin(weight):
            for one in weight.first:
                one.start()

        def forward(weight):
            for one in weight.first:
                one.arrived()
            for one in weight.second:
                one.start()

        def finish(weight):
            for one in weight.second:
                one.arrived()

        q_of = [Halved(wq.at[n], q_stage.at[n]) for n in range(layers)]
        g_of = [Halved(wg.at[n], g_stage.at[n]) for n in range(layers)]
        o_of = [Rowed(wo.at[n], out_in.at[n], block) for n in range(layers)]
        d_of = [Rowed(wd.at[n], down_in.at[n], hid_block) for n in range(layers)]

        def local_copy(source, target, slot):
            copy = pltpu.make_async_copy(source, target, local_sems.at[slot])
            copy.start()
            return copy

        def choose(first, second):
            return lax.select(core == 0, first, second)

        def stage_qkv(n):
            for kind in range(3):
                for j in range(chips):
                    at = kind * width + 2 * j * block
                    even = qkv_raw[:, at : at + block]
                    odd = qkv_raw[:, at + block : at + 2 * block]
                    to = kind * half + j * block
                    wq[n, rows(f, block), to : to + block] = choose(even, odd)
                    q_stage[n, :, to : to + block] = choose(odd, even)

        def stage_gu(n):
            for which in range(2):
                sets = []
                for lane_core in range(2):
                    parts = []
                    for j in range(chips):
                        at = (2 * j + lane_core) * hid_block
                        parts.append(gu_raw[which, :, at : at + hid_block])
                    sets.append(jnp.concatenate(parts, axis=1))
                to = slice(which * hid, (which + 1) * hid)
                wg[n, rows(f, block), to] = choose(sets[0], sets[1])
                g_stage[n, :, to] = choose(sets[1], sets[0])

        def load(n):
            return [
                local_copy(qkv_in.at[n], qkv_raw, 0),
                local_copy(gate_in.at[n], gu_raw.at[0], 1),
                local_copy(up_in.at[n], gu_raw.at[1], 2),
            ]

        loads = load(0)
        mine = []
        for n in range(layers):
            mine.append(local_copy(out_in.at[n], wo.at[n, rows(chip, block), :], 3 + n))
            mine.append(
                local_copy(down_in.at[n], wd.at[n, rows(chip, hid_block), :], 3 + layers + n)
            )
        spare = 3 + 2 * layers
        loads[0].wait()
        stage_qkv(0)
        gain_links = [
            link(gain_in, gbuf.at[f], gbuf.at[fx(bit)], "fsdp", bit) for bit in range(1, shards)
        ]
        lens_link = link(lens, lens_all.at[1], lens_all.at[1], "fsdp", 1)
        enter(list(range(1, shards)), list(range(1, ctx)))
        for one in gain_links:
            one.start()
        lens_link.start()
        begin(q_of[0])
        gbuf[f] = gain_in[...]
        lens_all[0] = lens[...]
        for copy in mine + loads[1:]:
            copy.wait()
        stage_gu(0)
        loads = load(1)
        for one in gain_links:
            one.arrived()

        def gain_row(n):
            return jnp.concatenate([gbuf[s, n : n + 1, :] for s in range(shards)], axis=1)

        for n in range(2 * layers):
            gain_o[n : n + 1, :] = gain_row(n)

        def norm_link(buffer, n):
            upper = buffer.at[n, pl.ds(local, local), :]
            return link(buffer.at[n, pl.ds(0, local), :], upper, upper, "fsdp", 1)

        n1[0, :local] = rms(tok[...].astype(F32), gain_row(0))
        norm_now = norm_link(n1, 0).start()

        lens_link.arrived()
        pairs = HD // 2
        lane = lax.broadcasted_iota(jnp.int32, (1, 128), 1)
        frequency = jnp.exp((-math.log(10000.0) / pairs) * lax.rem(lane, pairs).astype(F32))

        def table_step(index, carry):
            r = index // ctx
            piece = lax.rem(index, ctx)
            to = rows(piece, local)
            at = lax.broadcasted_iota(jnp.int32, (local, 128), 0) + piece * local
            first = jnp.zeros((local, 128), jnp.int32)
            end = jnp.zeros((1, 128), jnp.int32)
            for j in range(documents):
                end = end + lens_all[r, j : j + 1, :]
                first = jnp.where(at >= end, end, first)
            start[r, to, :] = first
            angle = (at - first).astype(F32) * frequency
            sin[r, to, :] = jnp.sin(angle)
            cos[r, to, :] = jnp.cos(angle)
            return carry

        lax.fori_loop(0, 2 * ctx, table_step, 0)
        here_rows = rows(z, local)
        for source, target in ((cos, cos_o), (sin, sin_o), (lens_all, start_o)):
            save(source, target)
        lane_head = lax.broadcasted_iota(jnp.int32, (1, group), 1) // HD

        def do_project(n):
            for tile in range(3 * half // 256):
                acc = dot(n1[n], wq[n, :, tile * 256 : (tile + 1) * 256])
                kind = tile * 256 // half
                for sub in range(256 // group):
                    column = tile * 256 - kind * half + sub * group
                    for r in range(2):
                        x = acc[r * local : (r + 1) * local, sub * group : (sub + 1) * group]
                        at = (slice(r * local, (r + 1) * local), slice(column, column + group))
                        if kind < 2:
                            x = turn(x, cos[r, here_rows, :], sin[r, here_rows, :], 1)
                        elif n > 0:
                            x = 0.5 * x + 0.5 * value[at].astype(F32)
                        x = x.astype(BF)
                        if kind == 2 and n == 0:
                            value[at] = x
                        slab[column // group, kind, r] = x

        def slab_links(n):
            made = []
            for bit in range(1, ctx):
                to = lax.bitwise_xor(z, bit)
                made.append(
                    link(
                        slab.at[to],
                        whole.at[n, :, :, rows(z, local), :],
                        whole.at[n, :, :, rows(to, local), :],
                        "ctx",
                        bit,
                    )
                )
            return made

        def mixed_links(n):
            made = []
            for bit in range(1, ctx):
                to = lax.bitwise_xor(z, bit)
                made.append(link(mixed.at[n, to], landed.at[n, z], landed.at[n, to], "ctx", bit))
            return made

        def do_attend(n):
            def row_step(r, carry):
                for piece in range(ctx):
                    keys = (piece + 1) * local
                    here = slice(piece * local, keys)
                    query = whole[n, 0, r, here, :] * SCORE_SCALE
                    key = whole[n, 1, r, :keys, :]
                    val = whole[n, 2, r, :keys, :]
                    k_at = lax.broadcasted_iota(jnp.int32, (local, keys), 1)
                    q_at = lax.broadcasted_iota(jnp.int32, (local, keys), 0) + piece * local
                    allowed = (k_at <= q_at) & (k_at >= start[r, here, 0:1])
                    result = None
                    for head in range(heads):
                        q_head = jnp.where(lane_head == head, query, jnp.zeros_like(query))
                        scores = jnp.where(allowed, dot_nt(q_head, key), MASK_FILL)
                        top = jnp.max(scores, axis=1, keepdims=True)
                        powers = jnp.exp(scores - top)
                        total = jnp.sum(powers, axis=1, keepdims=True)
                        probs = (powers * (1.0 / total)).astype(BF)
                        out = dot(probs, val)
                        result = out if head == 0 else jnp.where(lane_head == head, out, result)
                    mixed[n, piece, r] = result.astype(BF)
                return carry

            lax.fori_loop(0, 2, row_step, 0)

        last_sum = [None]

        def partial_sums(n, which, left, weight):
            if last_sum[0] is not None:
                last_sum[0].sent()

            def step(tile, carry):
                columns = rows(tile, 256)
                product = dot(left[...], weight[:, columns])
                part[:, columns] = product[:local]
                other[:, columns] = product[local:].astype(BF)
                return carry

            lax.fori_loop(0, width // 256, step, 0)
            to = got.at[n, which]
            last_sum[0] = link(other, to, to, "fsdp", 1).start()
            return last_sum[0]

        def gate_up(n):
            def span_step(base, count):
                here, there = pl.ds(base, count), pl.ds(hid + base, count)
                gate = dot(n2[n], wg[n, :, here])
                up = dot(n2[n], wg[n, :, there])
                kept[:, here] = gate.astype(BF)
                kept[:, there] = up.astype(BF)
                act[:, here] = (gate * jax.nn.sigmoid(gate) * up).astype(BF)

            def step(tile, carry):
                span_step(pl.multiple_of(tile * 256, 128), 256)
                return carry

            lax.fori_loop(0, hid // 256, step, 0)
            if hid % 256:
                span_step(hid // 256 * 256, hid % 256)

        slab_flights = []
        held = []
        for n in range(layers):
            if n == 0:
                forward(q_of[0])
                begin(o_of[0])
            finish(q_of[n])
            save(wq.at[n], wq_o.at[n])
            begin(g_of[n])
            norm_now.arrived()
            save(n1.at[n], n1_o.at[n])
            for one in slab_flights:
                one.sent()
            do_project(n)
            slab_flights = slab_links(n)
            for one in slab_flights:
                one.start()
            own = local_copy(slab.at[z], whole.at[n, :, :, here_rows, :], spare)
            if n == 0:
                for copy in loads:
                    copy.wait()
                stage_qkv(1)
                stage_gu(1)
            forward(o_of[n])
            finish(o_of[n])
            save(wo.at[n], wo_o.at[n])
            if n > 0:
                forward(g_of[n])
                begin(d_of[n])
            own.wait()
            for one in slab_flights:
                one.arrived()
            save(whole.at[n], whole_o.at[n])
            if n == 0:
                forward(g_of[n])
                begin(d_of[n])
            do_attend(n)
            back = mixed_links(n)
            for one in back:
                one.start()
            own = local_copy(mixed.at[n, z], landed.at[n, z], spare)
            if n == 0:
                begin(q_of[1])
            own.wait()
            for one in back:
                one.arrived()
            for k in range(ctx):
                mix[n, :, k * group : (k + 1) * group] = landed[n, k].reshape(both, group)
            save(mix.at[n], mix_o.at[n])
            sums = partial_sums(n, 0, mix.at[n], wo.at[n])
            forward(d_of[n])
            base = tok[...].astype(F32) if n == 0 else stream[...]
            sums.arrived()
            total = base + part[...] + got[n, 0].astype(F32)
            mid[n] = total
            n2[n, :local] = rms(total, gain_row(2 * n + 1))
            norm_now = norm_link(n2, n).start()
            save(mid.at[n], mid_o.at[n])
            finish(g_of[n])
            save(wg.at[n], wg_o.at[n])
            for number in held:
                saved(number)
            norm_now.arrived()
            save(n2.at[n], n2_o.at[n])
            gate_up(n)
            held = [save(act, act_o.at[n]), save(kept, kept_o.at[n])]
            if n == 0:
                forward(q_of[1])
                begin(o_of[1])
            finish(d_of[n])
            save(wd.at[n], wd_o.at[n])
            sums = partial_sums(n, 1, act, wd.at[n])
            sums.arrived()
            total = mid[n] + part[...] + got[n, 1].astype(F32)
            if n + 1 < layers:
                stream[...] = total
                n1[n + 1, :local] = rms(total, gain_row(2 * n + 2))
                norm_now = norm_link(n1, n + 1).start()
                save(stream, stream_o)
            else:
                final_o[...] = total.astype(BF)
        for one in flights:
            one.sent()
        for number in range(len(saves)):
            saved(number)

    def stacked(*dims):
        return (layers, *dims)

    outs = [
        shape(stacked(width, 3 * half), BF),
        shape(stacked(half, width), BF),
        shape(stacked(width, 2 * hid), BF),
        shape(stacked(hid, width), BF),
        shape(stacked(both, width), BF),
        shape(stacked(both, width), BF),
        shape(stacked(3, 2, span, group), BF),
        shape(stacked(both, half), BF),
        shape(stacked(local, width), F32),
        shape((local, width), F32),
        shape(stacked(both, hid), BF),
        shape(stacked(both, 2 * hid), BF),
        shape((2 * layers, width), F32),
        shape((2, span, 128), F32),
        shape((2, span, 128), F32),
        shape((2, 8, 128), jnp.int32),
        shape((local, width), BF),
    ]
    out_specs = [ANY] * 17
    out_specs[12] = out_specs[16] = VM
    scratch = [
        pltpu.VMEM(stacked(width, 3 * half), BF),
        pltpu.VMEM(stacked(half, width), BF),
        pltpu.VMEM(stacked(width, 2 * hid), BF),
        pltpu.VMEM(stacked(hid, width), BF),
        pltpu.VMEM((block, 3 * width), BF),
        pltpu.VMEM((2, block, hidden), BF),
        pltpu.VMEM(stacked(block, 3 * half), BF),
        pltpu.VMEM(stacked(block, 2 * hid), BF),
        pltpu.VMEM(stacked(both, width), BF),
        pltpu.VMEM(stacked(both, width), BF),
        pltpu.VMEM(stacked(3, 2, span, group), BF),
        pltpu.VMEM((ctx, 3, 2, local, group), BF),
        pltpu.VMEM(stacked(ctx, 2, local, group), BF),
        pltpu.VMEM(stacked(ctx, 2, local, group), BF),
        pltpu.VMEM((both, half), BF),
        pltpu.VMEM(stacked(both, half), BF),
        pltpu.VMEM(stacked(local, width), F32),
        pltpu.VMEM((local, width), F32),
        pltpu.VMEM((both, hid), BF),
        pltpu.VMEM((both, 2 * hid), BF),
        pltpu.VMEM((local, width), F32),
        pltpu.VMEM((local, width), BF),
        pltpu.VMEM(stacked(2, local, width), BF),
        pltpu.VMEM((shards, 8, block), F32),
        pltpu.VMEM((2, 8, 128), jnp.int32),
        pltpu.VMEM((2, span, 128), F32),
        pltpu.VMEM((2, span, 128), F32),
        pltpu.VMEM((2, span, 128), jnp.int32),
        pltpu.SemaphoreType.DMA((2, 80)),
        pltpu.SemaphoreType.DMA((8,)),
        pltpu.SemaphoreType.DMA((32,)),
    ]
    return pl.pallas_call(
        kernel,
        out_shape=outs,
        in_specs=[VM] * 3 + [ANY] * 5,
        out_specs=out_specs,
        scratch_shapes=scratch,
        compiler_params=pltpu.CompilerParams(
            vmem_limit_bytes=62 * MIB, collective_id=0, has_side_effects=True
        ),
        cost_estimate=pl.CostEstimate(
            flops=14 * 10**9, bytes_accessed=60 * MIB, transcendentals=0
        ),
    )(tokens, lengths, gain_rows, w_qkv, w_out, w_gate, w_up, w_down)


BACK_ORDER = (
    ("mlp", 1), ("dW", 1), ("nrm2", 1), ("mixb", 1), ("gW", 1),
    ("oW", 1), ("T", "o", 1), ("F", "d", 1, 0), ("F", "d", 1, 1), ("att", 1),
    ("F", "o", 1, 0), ("F", "o", 1, 1), ("F", "gb", 1, 0), ("F", "gb", 1, 1), ("S", "d", 1, 0),
    ("S", "d", 1, 1), ("T", "ga", 1), ("S", "gb", 1, 0), ("S", "gb", 1, 1), ("F", "ga", 1, 0),
    ("F", "ga", 1, 1), ("pb", 1), ("qW", 1), ("nrm1", 1), ("I", "d", 1, 0),
    ("I", "d", 1, 1), ("mlp", 0), ("dW", 0), ("F", "q", 1, 0), ("nrm2", 0),
    ("F", "q", 1, 1), ("S", "o", 1, 0), ("mixb", 0), ("X", "d", 1, 0), ("X", "d", 1, 1),
    ("S", "o", 1, 1), ("oW", 0), ("S", "ga", 1, 0), ("S", "ga", 1, 1), ("gW", 0),
    ("T", "ga", 0), ("I", "o", 1, 0), ("I", "gb", 1, 0), ("I", "gb", 1, 1), ("T", "o", 0),
    ("F", "d", 0, 0), ("F", "d", 0, 1), ("att", 0), ("S", "q", 1, 0), ("O", "d", 1, 0),
    ("O", "d", 1, 1), ("X", "o", 1, 0), ("F", "o", 0, 0), ("S", "q", 1, 1), ("W", "d", 1),
    ("F", "o", 0, 1), ("I", "o", 1, 1), ("X", "gb", 1, 0), ("X", "gb", 1, 1), ("I", "ga", 1, 0),
    ("I", "ga", 1, 1), ("O", "o", 1, 0), ("X", "o", 1, 1), ("F", "gb", 0, 0), ("F", "gb", 0, 1),
    ("S", "d", 0, 0), ("S", "d", 0, 1), ("F", "ga", 0, 0), ("F", "ga", 0, 1), ("O", "o", 1, 1),
    ("W", "o", 1), ("I", "q", 1, 0), ("X", "ga", 1, 0), ("X", "ga", 1, 1), ("O", "gb", 1, 0),
    ("I", "q", 1, 1), ("O", "gb", 1, 1), ("pb", 0), ("qW", 0), ("nrm1", 0),
    ("G1", 0), ("I", "d", 0, 0), ("I", "d", 0, 1), ("S", "o", 0, 0), ("S", "o", 0, 1),
    ("T", "q", 0), ("G2", 0), ("W", "gb", 1), ("S", "gb", 0, 0), ("X", "q", 1, 0),
    ("S", "gb", 0, 1), ("I", "o", 0, 0), ("O", "ga", 1, 0), ("I", "o", 0, 1), ("O", "ga", 1, 1),
    ("X", "q", 1, 1), ("F", "q", 0, 0), ("W", "ga", 1), ("F", "q", 0, 1), ("S", "ga", 0, 0),
    ("O", "q", 1, 0), ("S", "ga", 0, 1), ("X", "o", 0, 0), ("I", "gb", 0, 0), ("X", "o", 0, 1),
    ("X", "d", 0, 0), ("O", "q", 1, 1), ("I", "gb", 0, 1), ("X", "d", 0, 1), ("W", "q", 1),
    ("O", "o", 0, 0), ("S", "q", 0, 0), ("O", "o", 0, 1), ("S", "q", 0, 1), ("X", "gb", 0, 0),
    ("W", "o", 0), ("I", "ga", 0, 0), ("X", "gb", 0, 1), ("I", "ga", 0, 1), ("O", "d", 0, 0),
    ("O", "d", 0, 1), ("I", "q", 0, 0), ("W", "d", 0), ("X", "ga", 0, 0), ("X", "ga", 0, 1),
    ("O", "gb", 0, 0), ("O", "gb", 0, 1), ("I", "q", 0, 1), ("W", "gb", 0), ("X", "q", 0, 0),
    ("X", "q", 0, 1), ("O", "ga", 0, 0), ("O", "ga", 0, 1), ("W", "ga", 0), ("O", "q", 0, 0),
    ("O", "q", 0, 1), ("W", "q", 0), ("G3", 0),
)
HELD = (("o", 1), ("ga", 1), ("ga", 0), ("o", 0), ("q", 0),)
DEFER = True


def backward_pass(saved, tokens, cotangent):
    local, width = tokens.shape
    wq_s, wo_s, wg_s, wd_s = saved[:4]
    layers = wq_s.shape[0]
    half = width // 2
    hid = wd_s.shape[1]
    shards, ctx = lax.axis_size("fsdp"), lax.axis_size("ctx")
    chips = shards // 2
    block = width // shards
    hid_block = hid // chips
    group = half // ctx
    span = ctx * local
    heads = group // HD
    both = 2 * local
    documents = 4
    sizes = {
        "d": (hid_block, width),
        "g": (2 * block, 2 * hid),
        "o": (block, width),
        "q": (2 * block, 3 * half),
    }
    names = ("d", "g", "o", "q")
    pieces_of = {"d": ("d",), "g": ("ga", "gb"), "o": ("o",), "q": ("q",)}
    units = [unit for name in names for unit in pieces_of[name]]
    counts = {unit: sizes[unit[0]][0] // len(pieces_of[unit[0]]) for unit in units}

    def kernel(*refs):
        refs = list(refs)

        def take(count):
            out = refs[:count]
            del refs[:count]
            return out

        cot_i, tok_i, lens, gain = take(4)
        wq_i, wo_i, wg_i, wd_i, n1_i, n2_i, whole_i, mix_i, mid_i, stream_i = take(10)
        act_i, kept_i, cos_i, sin_i = take(4)
        grad_o, gain_o, q_o, o_o, gate_o, up_o, d_o = take(7)
        lands = {}
        for unit in units:
            lands[unit] = dict(zip(("x1", "y1", "x2", "y2", "z"), take(5)))
        swap_land = dict(zip(("g", "q"), take(2)))
        wq, wo, wg, wd, act, kept, norm, whole, mix, wide = take(10)
        flow, fgrad, got, do_in, dq_in, part, other, grad, middle = take(9)
        do_out, dq_out, key_sum, value_sum, carry, joined, cos, sin = take(8)
        blocks = dict(zip(names, take(4)))
        finals = dict(zip(names, take(4)))
        tmp, stage, gain_rows, gain_send, gain_land, gain_sum, gain_line = take(7)
        sems, load_sems, tmp_sems, out_sems = take(4)
        f = lax.axis_index("fsdp")
        z = lax.axis_index("ctx")
        core = lax.rem(f, 2)
        chip = f // 2
        inner = (z == 1) | (z == 2)
        outer = (z == 0) | (z == 3)
        flights = []

        def link(source, target, arriving, axis, bit):
            made = Link(source, target, arriving, sems, len(flights), axis, bit)
            flights.append(made)
            return made

        def rows(index, count):
            return pl.ds(pl.multiple_of(index * count, 16), count)

        def cx(bit):
            return lax.bitwise_xor(chip, bit)

        loading = {}
        slots = {}

        def load(name, source, target):
            slot = slots.setdefault(name, len(slots))
            copy = pltpu.make_async_copy(source, target, load_sems.at[slot])
            copy.start()
            loading[name] = copy

        def loaded(*wanted):
            for name in wanted:
                if name in loading:
                    loading.pop(name).wait()

        top = layers - 1
        load("cot", cot_i, flow.at[pl.ds(0, local), :])
        load("act", act_i.at[top], act)
        load("wd", wd_i.at[top], wd)
        load("kept", kept_i.at[top], kept)
        load("wg", wg_i.at[top], wg)
        load("wide", mid_i.at[top], wide)
        load("wo", wo_i.at[top], wo)
        load("norm", n2_i.at[top], norm)
        load("mix", mix_i.at[top], mix)
        load("whole", whole_i.at[top], whole)
        load("wq", wq_i.at[top], wq)
        load("cos", cos_i, cos)
        load("sin", sin_i, sin)
        enter(list(range(1, shards)), list(range(1, ctx)))

        def pair_link(buffer):
            upper = buffer.at[pl.ds(local, local), :]
            return link(buffer.at[pl.ds(0, local), :], upper, upper, "fsdp", 1)

        loaded("cot")
        e_link = pair_link(flow).start()
        grad[...] = flow[:local].astype(F32)

        class Reduce:
            def __init__(self, unit, n):
                name = unit[0]
                self.name, self.n = name, n
                whole_rows, self.columns = sizes[name]
                self.count = counts[unit]
                self.chunk = pieces_of[name].index(unit) if len(pieces_of[name]) > 1 else None
                self.offset = self.count * (self.chunk or 0)
                self.side = self.columns // 2
                self.blocks, self.final = blocks[name], finals[name]
                self.land = lands[unit]
                left, right = pl.ds(0, self.side), pl.ds(self.side, self.side)
                self.halves = (left, right)

                def row(k):
                    return cx(k) * whole_rows + self.offset

                self.row = row

                def piece(k, columns):
                    at = pl.ds(pl.multiple_of(row(k), 16), self.count)
                    return self.blocks.at[at, columns]

                def into(where, slot=None):
                    ref = self.land[where]
                    return ref.at[n] if slot is None else ref.at[n, slot]

                def hop(source, target, bit):
                    return link(source, target, target, "fsdp", bit)

                self.far = (hop(piece(3, left), into("x1", 1), 2), hop(piece(3, right), into("y1", 1), 4))
                self.near = (hop(piece(1, left), into("x1", 0), 2), hop(piece(2, right), into("y1", 0), 4))
                self.next = (hop(piece(2, left), into("y2"), 4), hop(piece(1, right), into("x2"), 2))
                self.line = []
                for side in self.halves:
                    steps = []
                    source = self.final.at[pl.ds(self.offset, self.count), side]
                    for step, bit in ((0, 1), (1, 3), (2, 1)):
                        target = self.land["z"].at[n, step, :, side]
                        steps.append(link(source, target, target, "ctx", bit))
                    self.line.append(steps)
                self.swap = None
                if name in swap_land:
                    out = rows(1 - core, block)
                    to = swap_land[name].at[n]
                    self.swap = link(self.final.at[out, :], to, to, "fsdp", 1)
                self.complete = 0
                self.held = (unit, n) in HELD

            def fetch(self, *sources):
                copies = []
                for slot, source in enumerate(sources):
                    copy = pltpu.make_async_copy(
                        source,
                        tmp.at[slot, pl.ds(0, self.count), pl.ds(0, self.side)],
                        tmp_sems.at[slot],
                    )
                    copy.start()
                    copies.append(copy)
                for copy in copies:
                    copy.wait()

            def add(self, source, source_row, columns, target, target_row, slots_used):
                def step(tile, carry):
                    at = pl.ds(pl.multiple_of(source_row + tile * 32, 16), 32)
                    total = source[at, columns].astype(F32)
                    here = pl.ds(pl.multiple_of(tile * 32, 16), 32)
                    for slot in slots_used:
                        total = total + tmp[slot, here, : self.side].astype(F32)
                    to = pl.ds(pl.multiple_of(target_row + tile * 32, 16), 32)
                    target[to, columns] = total.astype(BF)
                    return carry

                lax.fori_loop(0, self.count // 32, step, 0)

            def T(self):
                self.far[0].start()
                self.far[1].start()

            def settled(self):
                for one in (*self.far, *self.near, *self.next):
                    one.sent()

            def F(self, h):
                self.far[h].arrived()
                self.fetch(self.land[("x1", "y1")[h]].at[self.n, 1])
                at = self.row(2 - h)
                self.add(self.blocks, at, self.halves[h], self.blocks, at, (0,))
                self.next[h].start()
                if DEFER:
                    self.near[h].start()

            def S(self, h):
                self.near[h].arrived()
                self.next[h].arrived()
                self.fetch(
                    self.land[("x1", "y1")[h]].at[self.n, 0], self.land[("y2", "x2")[h]].at[self.n]
                )
                self.add(self.blocks, self.row(0), self.halves[h], self.final, self.offset, (0, 1))
                pl.when(outer)(self.line[h][0].out.start)

            def I(self, h):
                @pl.when(inner)
                def _():
                    steps = self.line[h]
                    steps[0].into.wait_recv()
                    self.fetch(self.land["z"].at[self.n, 0, :, self.halves[h]])
                    self.add(self.final, self.offset, self.halves[h], self.final, self.offset, (0,))
                    steps[1].out.start()

            def X(self, h):
                @pl.when(inner)
                def _():
                    steps = self.line[h]
                    steps[1].into.wait_recv()
                    self.fetch(self.land["z"].at[self.n, 1, :, self.halves[h]])
                    steps[1].out.wait_send()
                    self.add(self.final, self.offset, self.halves[h], self.final, self.offset, (0,))
                    steps[2].out.start()

            def O(self, h):
                steps = self.line[h]

                @pl.when(outer)
                def _():
                    steps[2].into.wait_recv()
                    steps[0].out.wait_send()
                    copy = pltpu.make_async_copy(
                        self.land["z"].at[self.n, 2, :, self.halves[h]],
                        self.final.at[pl.ds(self.offset, self.count), self.halves[h]],
                        tmp_sems.at[0],
                    )
                    copy.start()
                    copy.wait()

                pl.when(inner)(steps[2].out.wait_send)
                self.complete += 1
                if self.complete == 2 and self.swap is not None:
                    if self.chunk is None:
                        self.swap.out.start()
                    else:
                        pl.when(core != self.chunk)(self.swap.out.start)

            def W(self):
                if self.chunk is None:
                    self.write()
                else:
                    pl.when(core == self.chunk)(self.write)
                    pl.when(core != self.chunk)(self.swap.out.wait_send)

            def write(self):
                n = self.n
                if self.name in ("d", "o"):
                    target = d_o if self.name == "d" else o_o
                    run_copies([pltpu.make_async_copy(self.final, target.at[n], out_sems.at[0])])
                    return
                self.swap.into.wait_recv()
                parts_now = 3 if self.name == "q" else 2
                wide_now = self.columns // parts_now
                places = [
                    (k // 2, pl.ds((k % 2) * block, block), pl.ds(0, wide_now)) for k in range(3)
                ]
                if self.name == "g":
                    places[1] = (1, pl.ds(0, block), pl.ds(0, wide_now))
                run_copies(
                    [
                        pltpu.make_async_copy(
                            swap_land[self.name].at[n, :, pl.ds(k * wide_now, wide_now)],
                            tmp.at[places[k]],
                            out_sems.at[2 + k],
                        )
                        for k in range(parts_now)
                    ]
                )
                mine = rows(core, block)

                def sets(part_now, start_now, count_now):
                    first_at = part_now * wide_now + start_now
                    own = self.final[mine, first_at : first_at + count_now]
                    slot, row_at, _ = places[part_now]
                    theirs = tmp[slot, row_at, start_now : start_now + count_now]
                    return (
                        lax.select(core == 0, own, theirs),
                        lax.select(core == 0, theirs, own),
                    )

                if self.name == "q":
                    for kind in range(3):
                        for j in range(chips):
                            even, odd = sets(kind, j * block, block)
                            to = kind * width + 2 * j * block
                            stage[:, to : to + block] = even
                            stage[:, to + block : to + 2 * block] = odd
                    run_copies([pltpu.make_async_copy(stage, q_o.at[n], out_sems.at[0])])
                else:
                    for which, target in enumerate((gate_o, up_o)):
                        even, odd = sets(which, 0, hid)
                        parts = []
                        for j in range(chips):
                            at = slice(j * hid_block, (j + 1) * hid_block)
                            parts += [even[:, at], odd[:, at]]
                        stage[:, : 2 * hid] = jnp.concatenate(parts, axis=1)
                        run_copies(
                            [
                                pltpu.make_async_copy(
                                    stage.at[:, pl.ds(0, 2 * hid)], target.at[n], out_sems.at[0]
                                )
                            ]
                        )
                if self.chunk is None:
                    self.swap.out.wait_send()

        def grad_tile(target, row, count, left, columns, right, wide_count):
            turned = left[:, columns]
            for begin in range(0, wide_count, 512):
                end = min(begin + 512, wide_count)
                target[pl.ds(row, count), begin:end] = dot_tn(turned, right[:, begin:end]).astype(BF)

        def begin(job, k):
            if k == 3 and not job.held:
                job.T()
            elif k and not DEFER:
                job.near[k - 1].start()

        def compute_blocks(name, n, left, right):
            if not n:
                for unit in pieces_of[name]:
                    jobs[unit, 1].settled()
            count, columns = sizes[name]
            for k in (3, 1, 2, 0):
                row = pl.multiple_of(cx(k) * count, 128)
                grad_tile(blocks[name], row, count, left, pl.ds(row, count), right, columns)
                for unit in pieces_of[name]:
                    begin(jobs[unit, n], k)

        def compute_down(n):
            if not n:
                jobs["d", 1].settled()

            def step(tile, carry):
                row = pl.multiple_of(tile * 256, 128)
                grad_tile(blocks["d"], row, 256, act, pl.ds(row, 256), flow, width)
                return carry

            lax.fori_loop(0, hid // 256, step, 0)
            if hid % 256:
                row = hid // 256 * 256
                grad_tile(blocks["d"], row, hid % 256, act, pl.ds(row, hid % 256), flow, width)
            for k in (3, 1, 2):
                begin(jobs["d", n], k)

        last_sum = [None]

        def partial_sums(which, product):
            if last_sum[0] is not None:
                last_sum[0].sent()

            def step(tile, carry):
                columns = rows(tile, 256)
                value = product(columns)
                part[:, columns] = value[:local]
                other[:, columns] = value[local:].astype(BF)
                return carry

            lax.fori_loop(0, width // 256, step, 0)
            last_sum[0] = link(other, got.at[which], got.at[which], "fsdp", 1).start()
            return last_sum[0]

        def norm_step(x, gain_now, gain_row, which, target, low_target):
            factor = lax.rsqrt(jnp.mean(x * x, axis=1, keepdims=True) + EPSILON)
            back = part[...] + got[which].astype(F32)
            scaled = back * gain_now
            gain_rows[gain_row : gain_row + 1, :] = jnp.sum(back * x * factor, axis=0, keepdims=True)
            mean_term = jnp.mean(scaled * x, axis=1, keepdims=True)
            base = grad[...] if target is middle else middle[...]
            result = base + factor * scaled - x * (factor * factor * factor * mean_term)
            target[...] = result
            if low_target is not None:
                low_target[:local] = result.astype(BF)

        def mlp_back():
            def span_step(base, count):
                here, there = pl.ds(base, count), pl.ds(hid + base, count)
                back = dot_nt(flow[...], wd[here, :])
                gate = kept[:, here].astype(F32)
                up = kept[:, there].astype(F32)
                sig = jax.nn.sigmoid(gate)
                kept[:, here] = (back * up * sig * (1.0 + gate * (1.0 - sig))).astype(BF)
                kept[:, there] = (back * gate * sig).astype(BF)

            def step(tile, carry):
                span_step(pl.multiple_of(tile * 256, 128), 256)
                return carry

            lax.fori_loop(0, hid // 256, step, 0)
            if hid % 256:
                span_step(hid // 256 * 256, hid % 256)

        lane_head = lax.broadcasted_iota(jnp.int32, (1, group), 1) // HD
        line_head = lax.broadcasted_iota(jnp.int32, (group, 1), 0) // HD

        def start_row(r):
            at = lax.broadcasted_iota(jnp.int32, (1, span), 1)
            first = jnp.zeros((1, span), jnp.int32)
            end = jnp.zeros((1, 1), jnp.int32)
            for j in range(documents):
                end = end + lens[r, j : j + 1, 0:1]
                first = jnp.where(at >= end, end, first)
            return first

        def attend_step(n):
            def row_step(r, nothing):
                key_sum[...] = jnp.zeros_like(key_sum)
                value_sum[...] = jnp.zeros_like(value_sum)
                key_turned = whole[1, r].astype(F32).T.astype(BF)
                starts = start_row(r)
                for piece in range(ctx):
                    keys = (piece + 1) * local
                    here = slice(piece * local, keys)
                    query = whole[0, r, here, :] * SCORE_SCALE
                    back = do_in[r, here, :]
                    key = whole[1, r, :keys, :]
                    value = whole[2, r, :keys, :]
                    k_at = lax.broadcasted_iota(jnp.int32, (keys, local), 0)
                    q_at = lax.broadcasted_iota(jnp.int32, (keys, local), 1) + piece * local
                    allowed = (k_at <= q_at) & (k_at >= starts[:, here])
                    turned = None
                    for head in range(heads):
                        q_head = jnp.where(lane_head == head, query, jnp.zeros_like(query))
                        b_head = jnp.where(lane_head == head, back, jnp.zeros_like(back))
                        scores = jnp.where(allowed, dot_nt(key, q_head), MASK_FILL)
                        peak = jnp.max(scores, axis=0, keepdims=True)
                        powers = jnp.exp(scores - peak)
                        total = jnp.sum(powers, axis=0, keepdims=True)
                        probs = powers * (1.0 / total)
                        back_probs = dot_nt(value, b_head)
                        delta = jnp.sum(probs * back_probs, axis=0, keepdims=True)
                        back_scores = (probs * (back_probs - delta)).astype(BF)
                        value_sum[:keys] += dot(probs.astype(BF), b_head)
                        key_sum[:keys] += dot(back_scores, q_head)
                        sub = dot(key_turned[:, :keys], back_scores)
                        turned = sub if head == 0 else jnp.where(line_head == head, sub, turned)
                    back_query = turned.T * SCORE_SCALE
                    dq_out[piece, 0, r] = turn(
                        back_query, cos[r, here, :], sin[r, here, :], -1
                    ).astype(BF)
                for piece in range(ctx):
                    here = slice(piece * local, (piece + 1) * local)
                    dq_out[piece, 1, r] = turn(
                        key_sum[here, :], cos[r, here, :], sin[r, here, :], -1
                    ).astype(BF)
                    if n == top:
                        back_value = 0.5 * value_sum[here, :]
                        carry[r, here, :] = back_value
                    else:
                        back_value = value_sum[here, :] + carry[r, here, :]
                    dq_out[piece, 2, r] = back_value.astype(BF)
                return nothing

            lax.fori_loop(0, 2, row_step, 0)

        def spread(buffer, landing, target_of):
            made = []
            for bit in range(1, ctx):
                to = lax.bitwise_xor(z, bit)
                made.append(
                    link(buffer.at[to], target_of(landing, z), target_of(landing, to), "ctx", bit)
                )
            return made

        def own_copy(source, target):
            copy = pltpu.make_async_copy(source, target, out_sems.at[1])
            copy.start()
            return copy

        def token_rows(ref, index):
            return ref.at[:, rows(index, local), :]

        def slab_of(ref, index):
            return ref.at[index]

        jobs = {(unit, n): Reduce(unit, n) for n in (1, 0) for unit in units}
        state = {"e": e_link, "f": None, "do": [], "dq": []}

        def gain_value(n):
            return gain[n : n + 1, :]

        def await_flow(n):
            if state["e"] is not None:
                state["e"].arrived()
                state["sent"] = state["e"]
                state["e"] = None

        def op_dW(n):
            loaded("act")
            await_flow(n)
            compute_down(n)
            if n:
                load("act", act_i.at[0], act)

        def op_mlp(n):
            loaded("wd", "kept")
            await_flow(n)
            mlp_back()
            if n:
                load("wd", wd_i.at[0], wd)
            loaded("wg")
            state["sums"] = partial_sums(0, lambda columns: dot_nt(kept[...], wg[columns, :]))
            if n:
                load("wg", wg_i.at[0], wg)

        def op_nrm2(n):
            loaded("wide")
            if state["f"] is not None:
                state["f"].sent()
            state["sums"].arrived()
            norm_step(wide[...], gain_value(2 * n + 1), 2 * n + 1, 0, middle, fgrad)
            state["f"] = pair_link(fgrad).start()
            state["fresh"] = True
            if n:
                load("wide", stream_i, wide)

        def await_fgrad():
            if state["fresh"]:
                state["f"].arrived()
            state["fresh"] = False

        def op_mixb(n):
            loaded("wo")
            for one in state["do"]:
                one.sent()
            await_fgrad()
            for tile in range(half // 256):
                back = dot_nt(fgrad[...], wo[tile * 256 : (tile + 1) * 256, :]).astype(BF)
                for sub in range(256 // group):
                    do_out[tile * 256 // group + sub] = back[
                        :, sub * group : (sub + 1) * group
                    ].reshape(2, local, group)
            if n:
                load("wo", wo_i.at[0], wo)
            state["do"] = spread(do_out, do_in, token_rows)
            for one in state["do"]:
                one.start()
            state["own"] = own_copy(do_out.at[z], token_rows(do_in, z))

        def op_gW(n):
            loaded("norm")
            compute_blocks("g", n, norm, kept)
            load("norm", n1_i.at[n], norm)
            if n:
                load("kept", kept_i.at[0], kept)

        def op_oW(n):
            loaded("mix")
            await_fgrad()
            compute_blocks("o", n, mix, fgrad)
            if n:
                load("mix", mix_i.at[0], mix)

        def op_att(n):
            loaded("whole", "cos", "sin")
            state["own"].wait()
            for one in state["do"]:
                one.arrived()
            for one in state["dq"]:
                one.sent()
            attend_step(n)
            if n:
                load("whole", whole_i.at[0], whole)
            state["dq"] = spread(dq_out, dq_in, slab_of)
            for one in state["dq"]:
                one.start()
            state["own"] = own_copy(dq_out.at[z], dq_in.at[z])

        def op_pb(n):
            loaded("wq")
            state["own"].wait()
            for one in state["dq"]:
                one.arrived()
            for k in range(ctx):
                for kind in range(3):
                    base = kind * half + k * group
                    joined[:, base : base + group] = dq_in[k, kind].reshape(both, group)
            state["sums"] = partial_sums(1, lambda columns: dot_nt(joined[...], wq[columns, :]))
            if n:
                load("wq", wq_i.at[0], wq)

        def op_qW(n):
            loaded("norm")
            compute_blocks("q", n, norm, joined)
            if n:
                load("norm", n2_i.at[0], norm)

        def op_nrm1(n):
            if not n:
                state["f"].sent()
                load("tok", tok_i, fgrad.at[pl.ds(0, local), :])
                loaded("tok")
            loaded("wide")
            state["sent"].sent()
            state["sums"].arrived()
            if n:
                norm_step(wide[...], gain_value(2 * n), 2 * n, 1, grad, flow)
                state["e"] = pair_link(flow).start()
                load("wide", mid_i.at[0], wide)
            else:
                norm_step(fgrad[:local].astype(F32), gain_value(0), 0, 1, grad_o, None)

        def op_G1(n):
            for s in range(shards):
                gain_send[s] = jnp.concatenate(
                    [gain_rows[:4, s * block : (s + 1) * block], jnp.zeros((4, block), F32)]
                )
            state["gain"] = []
            for bit in range(1, shards):
                to = lax.bitwise_xor(f, bit)
                state["gain"].append(
                    link(gain_send.at[to], gain_land.at[f], gain_land.at[to], "fsdp", bit).start()
                )
            gain_land[f] = gain_send[f]

        def op_G2(n):
            for one in state["gain"]:
                one.arrived()
            total = gain_land[0]
            for s in range(1, shards):
                total = total + gain_land[s]
            gain_sum[...] = total
            state["line"] = []
            for bit in range(1, ctx):
                to = lax.bitwise_xor(z, bit)
                state["line"].append(
                    link(gain_sum, gain_line.at[z], gain_line.at[to], "ctx", bit).start()
                )
            gain_line[z] = total

        def op_G3(n):
            for one in state["line"]:
                one.arrived()
            total = gain_line[0]
            for k in range(1, ctx):
                total = total + gain_line[k]
            gain_o[...] = total

        chain = {
            "dW": op_dW, "mlp": op_mlp, "nrm2": op_nrm2, "mixb": op_mixb, "gW": op_gW,
            "oW": op_oW, "att": op_att, "pb": op_pb, "qW": op_qW, "nrm1": op_nrm1,
            "G1": op_G1, "G2": op_G2, "G3": op_G3,
        }
        for step in BACK_ORDER:
            if step[0] in chain:
                chain[step[0]](step[1])
            elif step[0] in ("W", "T"):
                getattr(jobs[step[1], step[2]], step[0])()
            else:
                getattr(jobs[step[1], step[2]], step[0])(step[3])
        for one in flights:
            one.sent()

    def vm(*dims, kind=BF):
        return pltpu.VMEM(dims, kind)

    outs = [
        shape((local, width), F32),
        shape((8, block), F32),
        shape((layers, block, 3 * width), BF),
        shape((layers, block, width), BF),
        shape((layers, block, 2 * hid), BF),
        shape((layers, block, 2 * hid), BF),
        shape((layers, hid_block, width), BF),
    ]
    for unit in units:
        count, columns = counts[unit], sizes[unit[0]][1]
        outs += [
            shape((layers, 2, count, columns // 2), BF),
            shape((layers, 2, count, columns // 2), BF),
            shape((layers, count, columns // 2), BF),
            shape((layers, count, columns // 2), BF),
            shape((layers, 3, count, columns), BF),
        ]
    outs += [shape((layers, block, sizes[name][1]), BF) for name in ("g", "q")]
    scratch = [
        vm(width, 3 * half),
        vm(half, width),
        vm(width, 2 * hid),
        vm(hid, width),
        vm(both, hid),
        vm(both, 2 * hid),
        vm(both, width),
        vm(3, 2, span, group),
        vm(both, half),
        vm(local, width, kind=F32),
        vm(both, width),
        vm(both, width),
        vm(2, local, width),
        vm(2, span, group),
        vm(ctx, 3, 2, local, group),
        vm(local, width, kind=F32),
        vm(local, width),
        vm(local, width, kind=F32),
        vm(local, width, kind=F32),
        vm(ctx, 2, local, group),
        vm(ctx, 3, 2, local, group),
        vm(span, group, kind=F32),
        vm(span, group, kind=F32),
        vm(2, span, group, kind=F32),
        vm(both, 3 * half),
        vm(2, span, 128, kind=F32),
        vm(2, span, 128, kind=F32),
    ]
    scratch += [vm(chips * sizes[name][0], sizes[name][1]) for name in names]
    scratch += [vm(*sizes[name]) for name in names]
    scratch += [
        vm(2, max(hid_block, 2 * block), hid),
        vm(block, 3 * width),
        vm(8, width, kind=F32),
        vm(shards, 8, block, kind=F32),
        vm(shards, 8, block, kind=F32),
        vm(8, block, kind=F32),
        vm(ctx, 8, block, kind=F32),
        pltpu.SemaphoreType.DMA((2, 176)),
        pltpu.SemaphoreType.DMA((20,)),
        pltpu.SemaphoreType.DMA((2,)),
        pltpu.SemaphoreType.DMA((6,)),
    ]
    (wq, wo, wg, wd, n1, n2, whole, mix, mid, stream, act, kept) = saved[:12]
    gain_all, cosines, sines, lens_all = saved[12:16]
    return pl.pallas_call(
        kernel,
        out_shape=outs,
        in_specs=[ANY] * 2 + [VM] * 2 + [ANY] * 14,
        out_specs=[VM] * 2 + [ANY] * (len(outs) - 2),
        scratch_shapes=scratch,
        compiler_params=pltpu.CompilerParams(
            vmem_limit_bytes=63 * MIB, collective_id=1, has_side_effects=True
        ),
        cost_estimate=pl.CostEstimate(
            flops=28 * 10**9, bytes_accessed=100 * MIB, transcendentals=0
        ),
    )(
        cotangent, tokens, lens_all, gain_all, wq, wo, wg, wd, n1, n2, whole, mix, mid, stream,
        act, kept, cosines, sines,
    )


def add_low(left, right):
    return (left.astype(F32) + right.astype(F32)).astype(BF)


def reduce_chips(blocks, chips):
    if chips != 4:
        total = blocks[0].astype(F32)
        for k in range(1, chips):
            total = total + swap(blocks[k], "fsdp", 2 * k).astype(F32)
        return total.astype(BF)
    send_x, keep_x, send_y, keep_y = blocks
    got_x = swap(send_x, "fsdp", 2)
    got_y = swap(send_y, "fsdp", 4)
    on_x = swap(add_low(keep_x[1], got_x[1]), "fsdp", 4)
    on_y = swap(add_low(keep_y[1], got_y[1]), "fsdp", 2)
    first = add_low(add_low(keep_x[0], got_x[0]), on_x)
    second = add_low(add_low(keep_y[0], got_y[0]), on_y)
    return jnp.concatenate([first, second], axis=1)


def reduce_line(block):
    if lax.axis_size("ctx") != 4:
        return lax.psum(block, "ctx")
    z = lax.axis_index("ctx")
    inner = (z == 1) | (z == 2)
    inward = lax.ppermute(block, "ctx", [(0, 1), (3, 2)])
    pair = jnp.where(inner, add_low(block, inward), block)
    across = lax.ppermute(pair, "ctx", [(1, 2), (2, 1)])
    total = add_low(pair, across)
    outward = lax.ppermute(total, "ctx", [(1, 0), (2, 3)])
    return jnp.where(inner, total, outward)


def own_rows(block):
    core = lax.axis_index("fsdp") % 2
    rows = block.shape[0] // 2
    mine = lax.dynamic_slice_in_dim(block, core * rows, rows)
    theirs = swap(lax.dynamic_slice_in_dim(block, (1 - core) * rows, rows), "fsdp", 1)
    low = jnp.where(core == 0, mine, theirs)
    high = jnp.where(core == 0, theirs, mine)
    return jnp.stack([low, high])


def chip_piece(mine, other):
    core = lax.axis_index("fsdp") % 2
    got = swap(other, "fsdp", 1)
    return jnp.where(
        core == 0, jnp.concatenate([mine, got]), jnp.concatenate([got, mine])
    )


def document_starts(lengths, index):
    ends = []
    total = jnp.int32(0)
    for j in range(lengths.shape[0]):
        total = total + lengths[j]
        ends.append(total)
    start = jnp.zeros_like(index)
    for end in ends:
        start = jnp.where(index >= end, end, start)
    return start


def rotary(positions):
    pairs = HD // 2
    lane = jnp.arange(128, dtype=jnp.int32)
    frequency = jnp.exp(-math.log(10000.0) * jnp.arange(pairs, dtype=F32) / pairs)
    angles = positions.astype(F32)[..., None] * frequency
    cosines = jnp.tile(jnp.cos(angles), 128 // pairs)
    sines = jnp.tile(jnp.sin(angles), 128 // pairs)
    low = jnp.where(lane % HD < pairs, -sines, 0.0)
    high = jnp.where(lane % HD >= pairs, sines, 0.0)
    return [cosines, low, high]


def body(tokens, doc_lengths, cotangent, gains, w_qkv, w_out, w_gate, w_up, w_down):
    _, local, width = tokens.shape
    layers = gains.shape[0]
    shards = lax.axis_size("fsdp")
    ctx = lax.axis_size("ctx")
    chips = shards // 2
    block = width // shards
    hidden = w_gate.shape[2]
    hidden_half = hidden // 2
    hidden_block = hidden // shards
    core = lax.axis_index("fsdp") % 2
    z = lax.axis_index("ctx")
    span = local * ctx

    def pick(array, axis, which):
        return lax.dynamic_index_in_dim(array, which, axis, keepdims=False)

    if chips == 4 and ctx == 4 and layers == 2:
        saved = forward_pass(
            tokens[0], doc_lengths, gains, w_qkv, w_out, w_gate, w_up, w_down
        )
        made = backward_pass(saved, tokens[0], cotangent[0])
        grad, gain_sum, qkv_sum, out_sum, gate_sum, up_sum, down_sum = made[:7]
        sums = [s.astype(F32) for s in (qkv_sum, out_sum, gate_sum, up_sum, down_sum)]
        gain_sum = gain_sum[: 2 * layers].reshape(layers, 2, block)
        return (saved[16][None], grad[None], gain_sum, *sums)

    qkv_weights, out_weights, gu_weights, down_weights = [], [], [], []
    for layer in range(layers):
        qkv = w_qkv[layer].reshape(block, 3, chips, 2, block)
        sides = [pick(qkv, 3, which).reshape(block, -1) for which in (core, 1 - core)]
        qkv_weights.append(gather(chip_piece(*sides), chips))
        out_weights.append(gather(w_out[layer], chips))
        sides = []
        for which in (core, 1 - core):
            both = [
                pick(w[layer].reshape(block, chips, 2, hidden_block), 2, which).reshape(
                    block, hidden_half
                )
                for w in (w_gate, w_up)
            ]
            sides.append(jnp.concatenate(both, axis=1))
        gu_weights.append(gather(chip_piece(*sides), chips))
        down_weights.append(gather(w_down[layer], chips))

    all_gains = lax.all_gather(gains, "fsdp", axis=2, tiled=True)
    gain_rows = [[all_gains[layer, n][None] for n in range(2)] for layer in range(layers)]

    index = jnp.arange(span, dtype=jnp.int32)
    lengths = [doc_lengths[0], swap(doc_lengths, "fsdp", 1)[0]]
    starts = jnp.stack([document_starts(row, index) for row in lengths])
    row_tables = rotary(index[None] - starts)
    here_tables = [lax.dynamic_slice_in_dim(t, z * local, local, axis=1) for t in row_tables]
    head_lanes = min(128, width // 2 // ctx)
    head_tables = [t[:, :, :head_lanes] for t in row_tables]
    start_column = starts[:, :, None]
    start_row = starts[:, None, :]

    def pair(array):
        return (array, swap(array, "fsdp", 1))

    stream = tokens[0]
    kept = []
    first_value = None
    (low,) = join_norm(stream, None, None, gain_rows[0][0])
    for layer in range(layers):
        normed = pair(low)
        slabs, first_value = project(
            *normed, here_tables, first_value, qkv_weights[layer], ctx, layer == layers - 1
        )
        slabs = exchange(slabs)
        mixed = exchange(attend(slabs, start_column))
        own, other, joined = mix_out(mixed, out_weights[layer])
        middle, low = join_norm(stream, own, swap(other, "fsdp", 1), gain_rows[layer][1])
        normed_two = pair(low)
        active, gu_kept = gate_up(*normed_two, gu_weights[layer])
        own, other = down(active, down_weights[layer])
        after = gain_rows[min(layer + 1, layers - 1)][0]
        kept.append((stream, normed, slabs, joined, middle, normed_two, active, gu_kept))
        stream, low = join_norm(middle, own, swap(other, "fsdp", 1), after)
    out_tokens = stream.astype(BF)[None]

    grad = cotangent[0]
    low = cotangent[0]
    carried = None
    gain_grads = [[None, None] for _ in range(layers)]
    done = [None] * layers
    for layer in reversed(range(layers)):
        stream, normed, slabs, joined, middle, normed_two, active, gu_kept = kept[layer]
        sent = pair(low)
        down_blocks = weight_grad([active], sent, chips)
        gu_grads, own, other = mlp_back(
            *sent, gu_kept, gu_weights[layer], down_weights[layer]
        )
        grad, low, gain_grads[layer][1] = norm_back(
            middle, own, swap(other, "fsdp", 1), gain_rows[layer][1], grad
        )
        gu_blocks = weight_grad(normed_two, [gu_grads], chips)
        mixed_back = pair(low)
        grad_slabs = exchange(mix_back(*mixed_back, out_weights[layer], ctx))
        out_blocks = weight_grad([joined], mixed_back, chips)
        grad_slabs, carry_out = attend_back(slabs, grad_slabs, start_row, head_tables, carried)
        carried = carry_out
        own, other, qkv_grads = project_back(exchange(grad_slabs), qkv_weights[layer])
        qkv_blocks = weight_grad(normed, [qkv_grads], chips)
        grad, low, gain_grads[layer][0] = norm_back(
            stream, own, swap(other, "fsdp", 1), gain_rows[layer][0], grad
        )
        down_sum = reduce_line(reduce_chips(down_blocks, chips)).astype(F32)
        gu_sum = own_rows(reduce_line(reduce_chips(gu_blocks, chips)))
        out_sum = reduce_line(reduce_chips(out_blocks, chips)).astype(F32)
        qkv_sum = own_rows(reduce_line(reduce_chips(qkv_blocks, chips)))
        qkv_sum = qkv_sum.reshape(2, block, 3, chips, block).transpose(1, 2, 3, 0, 4)
        qkv_sum = qkv_sum.reshape(block, 3 * width).astype(F32)
        gu_sum = gu_sum.reshape(2, block, 2, chips, hidden_block).transpose(2, 1, 3, 0, 4)
        gu_sum = gu_sum.reshape(2, block, hidden).astype(F32)
        done[layer] = (qkv_sum, out_sum, gu_sum[0], gu_sum[1], down_sum)

    gain_sum = jnp.stack([jnp.concatenate(rows) for rows in gain_grads])
    gain_sum = lax.psum_scatter(gain_sum, "fsdp", scatter_dimension=2, tiled=True)
    gain_sum = lax.psum(gain_sum, "ctx")
    stacked = [jnp.stack([done[layer][n] for layer in range(layers)]) for n in range(5)]
    return (out_tokens, grad[None], gain_sum, *stacked)


def solution(mesh):
    rows = P(None, "fsdp", None)
    tokens = P("fsdp", "ctx", None)
    gains = P(None, None, "fsdp")
    return jax.shard_map(
        body,
        mesh=mesh,
        in_specs=(tokens, P("fsdp", None), tokens, gains, rows, rows, rows, rows, rows),
        out_specs=(tokens, tokens, gains, rows, rows, rows, rows, rows),
        check_vma=False,
    )
```

```python
import math

import jax
import jax.numpy as jnp
from jax import lax
from jax.experimental import pallas as pl
from jax.experimental.pallas import tpu as pltpu
from jax.sharding import PartitionSpec as P

HEADS = 16
HD = 64
EPSILON = 1e-06
SCORE_SCALE = 0.125
MASK_FILL = -1e30
BF = jnp.bfloat16
F32 = jnp.float32
MIB = 1024 * 1024
ANY = pl.BlockSpec(memory_space=pl.ANY)
VM = pl.BlockSpec(memory_space=pltpu.VMEM)
NT = (((1,), (1,)), ((), ()))
TN = (((0,), (0,)), ((), ()))


def dot(left, right):
    return jnp.dot(left, right, preferred_element_type=F32)


def dot_nt(left, right):
    return lax.dot_general(left, right, NT, preferred_element_type=F32)


def dot_tn(left, right):
    return lax.dot_general(left, right, TN, preferred_element_type=F32)


def swap(array, axis, bit):
    size = lax.axis_size(axis)
    return lax.ppermute(array, axis, [(i, i ^ bit) for i in range(size)])


def call(kernel, outs, out_specs, scratch, args, in_specs, flops, vmem):
    nbytes = sum(a.size * a.dtype.itemsize for a in args)
    nbytes += sum(math.prod(o.shape) * o.dtype.itemsize for o in outs)
    return pl.pallas_call(
        kernel,
        out_shape=outs,
        in_specs=in_specs,
        out_specs=out_specs,
        scratch_shapes=scratch,
        compiler_params=pltpu.CompilerParams(vmem_limit_bytes=vmem * MIB),
        cost_estimate=pl.CostEstimate(flops=flops, bytes_accessed=nbytes, transcendentals=0),
    )(*args)


def shape(dims, kind):
    return jax.ShapeDtypeStruct(tuple(dims), kind)


def chip_index():
    return lax.axis_index("fsdp") // 2


def run_copies(copies):
    for copy in copies:
        copy.start()
    for copy in copies:
        copy.wait()


def weight_copies(plan, refs, buffer, sems, first):
    chip = chip_index()
    rows = plan[0][2]
    copies = []
    for number, ((k, offset, count), ref) in enumerate(zip(plan[1], refs)):
        start = pl.multiple_of(lax.bitwise_xor(chip, k) * rows + offset, 16)
        copies.append(
            pltpu.make_async_copy(
                ref, buffer.at[pl.ds(start, count), :], sems.at[first + number]
            )
        )
    return copies


class Pieces:
    def __init__(self, arrays, where, rows):
        self.arrays = arrays
        self.where = where
        self.rows = rows

    @property
    def plan(self):
        return ((0, 0, self.rows), self.where)


def gather(piece, chips):
    rows = piece.shape[0]
    if chips == 4:
        half = rows // 2
        from_x = swap(piece, "fsdp", 2)
        from_y = swap(piece, "fsdp", 4)
        far_one = swap(from_x[:half], "fsdp", 4)
        far_two = swap(from_y[half:], "fsdp", 2)
        return Pieces(
            [piece, from_x, from_y, far_one, far_two],
            [(0, 0, rows), (1, 0, rows), (2, 0, rows), (3, 0, half), (3, half, rows - half)],
            rows,
        )
    arrays = [piece] + [swap(piece, "fsdp", 2 * k) for k in range(1, chips)]
    return Pieces(arrays, [(k, 0, rows) for k in range(chips)], rows)


def rope(x, cosines, low_sine, high_sine):
    width = x.shape[-1]
    return (
        x * cosines
        + pltpu.roll(x, width - HD // 2, 1) * low_sine
        + pltpu.roll(x, HD // 2, 1) * high_sine
    )


def project(n_own, n_other, tables, first_value, weight, ctx, last):
    local, width = n_own.shape
    half = width // 2
    group = half // ctx
    pieces = len(weight.arrays)
    plan = weight.plan

    def kernel(*refs):
        own, other, cos, low, high = refs[:5]
        at = 5
        v_in = None
        if first_value is not None:
            v_in = refs[at]
            at += 1
        w_refs = refs[at : at + pieces]
        at += pieces
        slabs = refs[at : at + ctx]
        at += ctx
        v_out = None
        if first_value is None:
            v_out = refs[at]
            at += 1
        buffer, tokens, slab, sems, out_sems = refs[at:]
        copies = weight_copies(plan, w_refs, buffer, sems, 0)
        for copy in copies:
            copy.start()
        tokens[:local] = own[...]
        tokens[local:] = other[...]
        tables_now = [t[...].reshape(2 * local, 128) for t in (cos, low, high)]
        for copy in copies:
            copy.wait()
        for tile in range(3 * half // 256):
            acc = dot(tokens[...], buffer[:, tile * 256 : (tile + 1) * 256])
            kind = tile * 256 // half
            base = tile * 256 - kind * half
            for sub in range(2):
                x = acc[:, sub * 128 : (sub + 1) * 128]
                column = base + sub * 128
                if kind < 2:
                    x = rope(x, *tables_now)
                elif first_value is not None:
                    x = 0.5 * x + 0.5 * v_in[:, column : column + 128].astype(F32)
                x = x.astype(BF)
                if kind == 2 and v_out is not None:
                    v_out[:, column : column + 128] = x
                for part in range(128 // group):
                    slab[column // group + part, kind] = x[
                        :, part * group : (part + 1) * group
                    ].reshape(2, local, group)
        z = lax.axis_index("ctx")
        run_copies(
            [
                pltpu.make_async_copy(slab.at[lax.bitwise_xor(z, k)], slabs[k], out_sems.at[k])
                for k in range(ctx)
            ]
        )

    args = [n_own, n_other, *tables]
    specs = [VM] * 5
    outs = [shape((3, 2, local, group), BF)] * ctx
    out_specs = [ANY] * ctx
    if first_value is not None:
        args.append(first_value)
        specs.append(VM)
    else:
        outs.append(shape((2 * local, half), BF))
        out_specs.append(VM)
    args += weight.arrays
    specs += [ANY] * pieces
    got = call(
        kernel,
        outs,
        out_specs,
        [
            pltpu.VMEM((width, 3 * half), BF),
            pltpu.VMEM((2 * local, width), BF),
            pltpu.VMEM((ctx, 3, 2, local, group), BF),
            pltpu.SemaphoreType.DMA((pieces,)),
            pltpu.SemaphoreType.DMA((ctx,)),
        ],
        args,
        specs,
        2 * 2 * local * width * 3 * half,
        40,
    )
    return got[:ctx], (first_value if first_value is not None else got[ctx])


def exchange(slabs):
    return [slabs[0]] + [swap(slabs[k], "ctx", k) for k in range(1, len(slabs))]


def attend(slabs, start_column):
    ctx = len(slabs)
    _, _, local, group = slabs[0].shape
    span = ctx * local
    heads = group // HD

    def kernel(*refs):
        starts = refs[0]
        ins = refs[1 : 1 + ctx]
        outs = refs[1 + ctx : 1 + 2 * ctx]
        whole, mixed, sems, out_sems = refs[1 + 2 * ctx :]
        z = lax.axis_index("ctx")
        copies = []
        for k in range(ctx):
            at = pl.multiple_of(lax.bitwise_xor(z, k) * local, 16)
            copies.append(
                pltpu.make_async_copy(
                    ins[k], whole.at[:, :, pl.ds(at, local), :], sems.at[k]
                )
            )
        run_copies(copies)
        lane = lax.broadcasted_iota(jnp.int32, (1, group), 1) // HD

        def row_step(row, carry):
            for block in range(ctx):
                keys = (block + 1) * local
                here = slice(block * local, keys)
                query = whole[0, row, here, :] * SCORE_SCALE
                key = whole[1, row, :keys, :]
                value = whole[2, row, :keys, :]
                k_at = lax.broadcasted_iota(jnp.int32, (local, keys), 1)
                q_at = lax.broadcasted_iota(jnp.int32, (local, keys), 0) + block * local
                allowed = (k_at <= q_at) & (k_at >= starts[row, here, :])
                result = None
                for head in range(heads):
                    q_head = jnp.where(lane == head, query, jnp.zeros_like(query))
                    scores = jnp.where(allowed, dot_nt(q_head, key), MASK_FILL)
                    top = jnp.max(scores, axis=1, keepdims=True)
                    powers = jnp.exp(scores - top)
                    total = jnp.sum(powers, axis=1, keepdims=True)
                    probs = (powers * (1.0 / total)).astype(BF)
                    out = dot(probs, value)
                    result = out if result is None else jnp.where(lane == head, out, result)
                mixed[block, row] = result.astype(BF)
            return carry

        lax.fori_loop(0, 2, row_step, 0)
        run_copies(
            [
                pltpu.make_async_copy(mixed.at[lax.bitwise_xor(z, k)], outs[k], out_sems.at[k])
                for k in range(ctx)
            ]
        )

    return call(
        kernel,
        [shape((2, local, group), BF)] * ctx,
        [ANY] * ctx,
        [
            pltpu.VMEM((3, 2, span, group), BF),
            pltpu.VMEM((ctx, 2, local, group), BF),
            pltpu.SemaphoreType.DMA((ctx,)),
            pltpu.SemaphoreType.DMA((ctx,)),
        ],
        [start_column, *slabs],
        [VM] + [ANY] * ctx,
        2 * 2 * 2 * heads * span * span * 128,
        40,
    )


def halves_out(product, own_ref, other_ref, columns, local):
    own_ref[:, columns] = product[:local]
    other_ref[:, columns] = product[local:].astype(BF)


def mix_out(slabs, weight):
    ctx = len(slabs)
    _, local, group = slabs[0].shape
    half = ctx * group
    width = weight.arrays[0].shape[1]
    pieces = len(weight.arrays)
    plan = weight.plan

    def kernel(*refs):
        ins = refs[:ctx]
        w_refs = refs[ctx : ctx + pieces]
        own, other, joined, buffer, landed, sems = refs[ctx + pieces :]
        z = lax.axis_index("ctx")
        copies = weight_copies(plan, w_refs, buffer, sems, ctx)
        for k in range(ctx):
            copies.append(
                pltpu.make_async_copy(ins[k], landed.at[lax.bitwise_xor(z, k)], sems.at[k])
            )
        run_copies(copies)
        for k in range(ctx):
            joined[:, k * group : (k + 1) * group] = landed[k].reshape(2 * local, group)
        for tile in range(width // 256):
            columns = slice(tile * 256, (tile + 1) * 256)
            halves_out(dot(joined[...], buffer[:, columns]), own, other, columns, local)

    return call(
        kernel,
        [shape((local, width), F32), shape((local, width), BF), shape((2 * local, half), BF)],
        [VM] * 3,
        [
            pltpu.VMEM((half, width), BF),
            pltpu.VMEM((ctx, 2, local, group), BF),
            pltpu.SemaphoreType.DMA((ctx + pieces,)),
        ],
        [*slabs, *weight.arrays],
        [ANY] * (ctx + pieces),
        2 * 2 * local * half * width,
        24,
    )


def join_norm(base, own, other, gain):
    local, width = base.shape
    fresh = own is not None

    def kernel(*refs):
        if fresh:
            base_ref, own_ref, other_ref, gain_ref, sum_ref, low_ref = refs
            total = base_ref[...].astype(F32) + own_ref[...] + other_ref[...].astype(F32)
            sum_ref[...] = total
        else:
            base_ref, gain_ref, low_ref = refs
            total = base_ref[...].astype(F32)
        factor = lax.rsqrt(jnp.mean(total * total, axis=1, keepdims=True) + EPSILON)
        low_ref[...] = (total * factor * gain_ref[...].astype(F32)).astype(BF)

    outs = [shape((local, width), BF)]
    args = [base, gain]
    if fresh:
        outs = [shape((local, width), F32)] + outs
        args = [base, own, other, gain]
    return call(
        kernel, outs, [VM] * len(outs), [], args, [VM] * len(args), 8 * local * width, 16
    )


def gate_up(n_own, n_other, weight):
    local, width = n_own.shape
    hidden2 = weight.arrays[0].shape[1]
    hidden = hidden2 // 2
    pieces = len(weight.arrays)
    plan = weight.plan

    def kernel(*refs):
        own, other = refs[:2]
        w_refs = refs[2 : 2 + pieces]
        active, kept, buffer, tokens, sems = refs[2 + pieces :]
        copies = weight_copies(plan, w_refs, buffer, sems, 0)
        for copy in copies:
            copy.start()
        tokens[:local] = own[...]
        tokens[local:] = other[...]
        for copy in copies:
            copy.wait()

        def span_step(base, count):
            here, there = pl.ds(base, count), pl.ds(hidden + base, count)
            gate = dot(tokens[...], buffer[:, here])
            up = dot(tokens[...], buffer[:, there])
            kept[:, here] = gate.astype(BF)
            kept[:, there] = up.astype(BF)
            active[:, here] = (gate * jax.nn.sigmoid(gate) * up).astype(BF)

        def step(tile, carry):
            span_step(pl.multiple_of(tile * 256, 128), 256)
            return carry

        lax.fori_loop(0, hidden // 256, step, 0)
        if hidden % 256:
            span_step(hidden // 256 * 256, hidden % 256)

    return call(
        kernel,
        [shape((2 * local, hidden), BF), shape((2 * local, hidden2), BF)],
        [VM] * 2,
        [
            pltpu.VMEM((width, hidden2), BF),
            pltpu.VMEM((2 * local, width), BF),
            pltpu.SemaphoreType.DMA((pieces,)),
        ],
        [n_own, n_other, *weight.arrays],
        [VM] * 2 + [ANY] * pieces,
        2 * 2 * local * width * hidden2,
        40,
    )


def down(active, weight):
    tokens, hidden = active.shape
    local = tokens // 2
    width = weight.arrays[0].shape[1]
    pieces = len(weight.arrays)
    plan = weight.plan

    def kernel(*refs):
        left = refs[0]
        w_refs = refs[1 : 1 + pieces]
        own, other, buffer, sems = refs[1 + pieces :]
        run_copies(weight_copies(plan, w_refs, buffer, sems, 0))

        def step(tile, carry):
            columns = pl.ds(pl.multiple_of(tile * 256, 256), 256)
            halves_out(dot(left[...], buffer[:, columns]), own, other, columns, local)
            return carry

        lax.fori_loop(0, width // 256, step, 0)

    return call(
        kernel,
        [shape((local, width), F32), shape((local, width), BF)],
        [VM] * 2,
        [pltpu.VMEM((hidden, width), BF), pltpu.SemaphoreType.DMA((pieces,))],
        [active, *weight.arrays],
        [VM] + [ANY] * pieces,
        2 * tokens * hidden * width,
        24,
    )


def mlp_back(e_own, e_other, kept, gu_weight, down_weight):
    local, width = e_own.shape
    hidden2 = kept.shape[1]
    hidden = hidden2 // 2
    pieces = len(gu_weight.arrays)
    more = len(down_weight.arrays)
    gu_plan, down_plan = gu_weight.plan, down_weight.plan

    def kernel(*refs):
        e_one, e_two, kept_ref = refs[:3]
        gu_refs = refs[3 : 3 + pieces]
        down_refs = refs[3 + pieces : 3 + pieces + more]
        grads, own, other, gu, wd, tokens, sems = refs[3 + pieces + more :]
        first = weight_copies(down_plan, down_refs, wd, sems, pieces)
        second = weight_copies(gu_plan, gu_refs, gu, sems, 0)
        for copy in first + second:
            copy.start()
        tokens[:local] = e_one[...]
        tokens[local:] = e_two[...]
        for copy in first:
            copy.wait()

        def span_step(base, count):
            here, there = pl.ds(base, count), pl.ds(hidden + base, count)
            flow = dot_nt(tokens[...], wd[here, :])
            gate = kept_ref[:, here].astype(F32)
            up = kept_ref[:, there].astype(F32)
            sig = jax.nn.sigmoid(gate)
            grads[:, here] = (flow * up * sig * (1.0 + gate * (1.0 - sig))).astype(BF)
            grads[:, there] = (flow * gate * sig).astype(BF)

        def step(tile, carry):
            span_step(pl.multiple_of(tile * 256, 128), 256)
            return carry

        lax.fori_loop(0, hidden // 256, step, 0)
        if hidden % 256:
            span_step(hidden // 256 * 256, hidden % 256)
        for copy in second:
            copy.wait()

        def back_step(tile, carry):
            rows = pl.ds(pl.multiple_of(tile * 256, 256), 256)
            halves_out(dot_nt(grads[...], gu[rows, :]), own, other, rows, local)
            return carry

        lax.fori_loop(0, width // 256, back_step, 0)

    return call(
        kernel,
        [
            shape((2 * local, hidden2), BF),
            shape((local, width), F32),
            shape((local, width), BF),
        ],
        [VM] * 3,
        [
            pltpu.VMEM((width, hidden2), BF),
            pltpu.VMEM((hidden, width), BF),
            pltpu.VMEM((2 * local, width), BF),
            pltpu.SemaphoreType.DMA((pieces + more,)),
        ],
        [e_own, e_other, kept, *gu_weight.arrays, *down_weight.arrays],
        [VM] * 3 + [ANY] * (pieces + more),
        2 * 2 * local * width * hidden * 3,
        48,
    )


def norm_back(stream, own, other, gain, grad):
    local, width = stream.shape

    def kernel(x_ref, own_ref, other_ref, gain_ref, grad_ref, out_ref, low_ref, gain_out):
        x = x_ref[...].astype(F32)
        factor = lax.rsqrt(jnp.mean(x * x, axis=1, keepdims=True) + EPSILON)
        flow = own_ref[...] + other_ref[...].astype(F32)
        scaled = flow * gain_ref[...].astype(F32)
        gain_out[...] = jnp.sum(flow * x * factor, axis=0, keepdims=True)
        mean_term = jnp.mean(scaled * x, axis=1, keepdims=True)
        result = (
            grad_ref[...].astype(F32)
            + factor * scaled
            - x * (factor * factor * factor * mean_term)
        )
        out_ref[...] = result
        low_ref[...] = result.astype(BF)

    return call(
        kernel,
        [shape((local, width), F32), shape((local, width), BF), shape((1, width), F32)],
        [VM] * 3,
        [],
        [stream, own, other, gain, grad],
        [VM] * 5,
        12 * local * width,
        24,
    )


def mix_back(f_own, f_other, weight, ctx):
    local, width = f_own.shape
    half = width // 2
    group = half // ctx
    pieces = len(weight.arrays)
    plan = weight.plan

    def kernel(*refs):
        own, other = refs[:2]
        w_refs = refs[2 : 2 + pieces]
        slabs = refs[2 + pieces : 2 + pieces + ctx]
        buffer, tokens, slab, sems, out_sems = refs[2 + pieces + ctx :]
        copies = weight_copies(plan, w_refs, buffer, sems, 0)
        for copy in copies:
            copy.start()
        tokens[:local] = own[...]
        tokens[local:] = other[...]
        for copy in copies:
            copy.wait()
        for tile in range(half // 256):
            flow = dot_nt(tokens[...], buffer[tile * 256 : (tile + 1) * 256, :]).astype(BF)
            for part in range(256 // group):
                slab[tile * 256 // group + part] = flow[
                    :, part * group : (part + 1) * group
                ].reshape(2, local, group)
        z = lax.axis_index("ctx")
        run_copies(
            [
                pltpu.make_async_copy(slab.at[lax.bitwise_xor(z, k)], slabs[k], out_sems.at[k])
                for k in range(ctx)
            ]
        )

    return call(
        kernel,
        [shape((2, local, group), BF)] * ctx,
        [ANY] * ctx,
        [
            pltpu.VMEM((half, width), BF),
            pltpu.VMEM((2 * local, width), BF),
            pltpu.VMEM((ctx, 2, local, group), BF),
            pltpu.SemaphoreType.DMA((pieces,)),
            pltpu.SemaphoreType.DMA((ctx,)),
        ],
        [f_own, f_other, *weight.arrays],
        [VM] * 2 + [ANY] * pieces,
        2 * 2 * local * half * width,
        24,
    )


def attend_back(slabs, grad_slabs, start_row, tables, carried):
    ctx = len(grad_slabs)
    _, local, group = grad_slabs[0].shape
    span = ctx * local
    parts = len(slabs)
    heads = group // HD
    first = carried is not None

    def kernel(*refs):
        starts, cos, low, high = refs[:4]
        at = 4
        carry_in = None
        if first:
            carry_in = refs[at]
            at += 1
        ins = refs[at : at + parts]
        at += parts
        grads = refs[at : at + ctx]
        outs = refs[at + ctx : at + 2 * ctx]
        at += 2 * ctx
        carry_out = None
        if not first:
            carry_out = refs[at]
            at += 1
        whole, flow_in, slab, key_sum, value_sum, sems, out_sems = refs[at:]
        z = lax.axis_index("ctx")
        copies = []
        if parts == 1:
            copies.append(pltpu.make_async_copy(ins[0], whole, sems.at[0]))
        for k in range(ctx):
            to = pl.ds(pl.multiple_of(lax.bitwise_xor(z, k) * local, 16), local)
            if parts > 1:
                copies.append(
                    pltpu.make_async_copy(ins[k], whole.at[:, :, to, :], sems.at[k])
                )
            copies.append(
                pltpu.make_async_copy(grads[k], flow_in.at[:, to, :], sems.at[ctx + k])
            )
        run_copies(copies)
        lane = lax.broadcasted_iota(jnp.int32, (1, group), 1) // HD
        line = lax.broadcasted_iota(jnp.int32, (group, 1), 0) // HD

        def row_step(row, carry):
            key_sum[...] = jnp.zeros_like(key_sum)
            value_sum[...] = jnp.zeros_like(value_sum)
            key_turned = whole[1, row].astype(F32).T.astype(BF)
            for block in range(ctx):
                keys = (block + 1) * local
                here = slice(block * local, keys)
                query = whole[0, row, here, :] * SCORE_SCALE
                grad = flow_in[row, here, :]
                key = whole[1, row, :keys, :]
                value = whole[2, row, :keys, :]
                k_at = lax.broadcasted_iota(jnp.int32, (keys, local), 0)
                q_at = lax.broadcasted_iota(jnp.int32, (keys, local), 1) + block * local
                allowed = (k_at <= q_at) & (k_at >= starts[row, :, here])
                turned = None
                for head in range(heads):
                    mine = lane == head
                    q_head = jnp.where(mine, query, jnp.zeros_like(query))
                    g_head = jnp.where(mine, grad, jnp.zeros_like(grad))
                    scores = jnp.where(allowed, dot_nt(key, q_head), MASK_FILL)
                    top = jnp.max(scores, axis=0, keepdims=True)
                    powers = jnp.exp(scores - top)
                    total = jnp.sum(powers, axis=0, keepdims=True)
                    probs = powers * (1.0 / total)
                    grad_probs = dot_nt(value, g_head)
                    delta = jnp.sum(probs * grad_probs, axis=0, keepdims=True)
                    grad_scores = (probs * (grad_probs - delta)).astype(BF)
                    value_sum[:keys] += dot(probs.astype(BF), g_head)
                    key_sum[:keys] += dot(grad_scores, q_head)
                    part = dot(key_turned[:, :keys], grad_scores)
                    turned = part if turned is None else jnp.where(line == head, part, turned)
                grad_query = turned.T * SCORE_SCALE
                slab[block, 0, row] = rope(
                    grad_query, cos[row, here, :], -low[row, here, :], -high[row, here, :]
                ).astype(BF)
            for block in range(ctx):
                here = slice(block * local, (block + 1) * local)
                slab[block, 1, row] = rope(
                    key_sum[here, :], cos[row, here, :], -low[row, here, :], -high[row, here, :]
                ).astype(BF)
                if first:
                    total_value = value_sum[here, :] + carry_in[row, here, :]
                else:
                    total_value = 0.5 * value_sum[here, :]
                    carry_out[row, here, :] = total_value
                slab[block, 2, row] = total_value.astype(BF)
            return carry

        lax.fori_loop(0, 2, row_step, 0)
        run_copies(
            [
                pltpu.make_async_copy(slab.at[lax.bitwise_xor(z, k)], outs[k], out_sems.at[k])
                for k in range(ctx)
            ]
        )

    args = [start_row, *tables]
    specs = [VM] * 4
    outs = [shape((3, 2, local, group), BF)] * ctx
    out_specs = [ANY] * ctx
    if first:
        args.append(carried)
        specs.append(VM)
    else:
        outs.append(shape((2, span, group), F32))
        out_specs.append(VM)
    got = call(
        kernel,
        outs,
        out_specs,
        [
            pltpu.VMEM((3, 2, span, group), BF),
            pltpu.VMEM((2, span, group), BF),
            pltpu.VMEM((ctx, 3, 2, local, group), BF),
            pltpu.VMEM((span, group), F32),
            pltpu.VMEM((span, group), F32),
            pltpu.SemaphoreType.DMA((2 * ctx,)),
            pltpu.SemaphoreType.DMA((ctx,)),
        ],
        [*args, *slabs, *grad_slabs],
        specs + [ANY] * (parts + ctx),
        2 * 5 * 2 * heads * span * span * 128,
        48,
    )
    return got[:ctx], (None if first else got[ctx])


def project_back(slabs, weight):
    ctx = len(slabs)
    _, _, local, group = slabs[0].shape
    half = ctx * group
    width = 2 * half
    pieces = len(weight.arrays)
    plan = weight.plan

    def kernel(*refs):
        ins = refs[:ctx]
        w_refs = refs[ctx : ctx + pieces]
        own, other, joined, buffer, landed, sems = refs[ctx + pieces :]
        z = lax.axis_index("ctx")
        copies = weight_copies(plan, w_refs, buffer, sems, ctx)
        for k in range(ctx):
            copies.append(
                pltpu.make_async_copy(ins[k], landed.at[lax.bitwise_xor(z, k)], sems.at[k])
            )
        run_copies(copies)
        for k in range(ctx):
            for kind in range(3):
                base = kind * half + k * group
                joined[:, base : base + group] = landed[k, kind].reshape(2 * local, group)

        def step(tile, carry):
            rows = pl.ds(pl.multiple_of(tile * 256, 256), 256)
            halves_out(dot_nt(joined[...], buffer[rows, :]), own, other, rows, local)
            return carry

        lax.fori_loop(0, width // 256, step, 0)

    return call(
        kernel,
        [
            shape((local, width), F32),
            shape((local, width), BF),
            shape((2 * local, 3 * half), BF),
        ],
        [VM] * 3,
        [
            pltpu.VMEM((width, 3 * half), BF),
            pltpu.VMEM((ctx, 3, 2, local, group), BF),
            pltpu.SemaphoreType.DMA((ctx + pieces,)),
        ],
        [*slabs, *weight.arrays],
        [ANY] * (ctx + pieces),
        2 * 2 * local * 3 * half * width,
        40,
    )


def weight_grad(left, right, chips):
    lefts, rights = list(left), list(right)
    tall = lefts[0].shape[1]
    wide = rights[0].shape[1]
    tokens = lefts[0].shape[0] * len(lefts)
    rows = tall // chips
    halved = wide // 2
    split = chips == 4

    def kernel(*refs):
        l_refs = refs[: len(lefts)]
        r_refs = refs[len(lefts) : len(lefts) + len(rights)]
        at = len(lefts) + len(rights)
        count = 4 if split else chips
        outs = refs[at : at + count]
        grads, l_buf, r_buf, sems = refs[at + count :]
        if len(lefts) == 2:
            l_buf[: tokens // 2] = l_refs[0][...]
            l_buf[tokens // 2 :] = l_refs[1][...]
            l_now = l_buf
        else:
            l_now = l_refs[0]
        if len(rights) == 2:
            r_buf[: tokens // 2] = r_refs[0][...]
            r_buf[tokens // 2 :] = r_refs[1][...]
            r_now = r_buf
        else:
            r_now = r_refs[0]

        def tile_step(base, size):
            turned = l_now[:, pl.ds(base, size)]
            for start in range(0, wide, 512):
                stop = min(start + 512, wide)
                grads[pl.ds(base, size), start:stop] = dot_tn(
                    turned, r_now[:, start:stop]
                ).astype(BF)

        def step(tile, carry):
            tile_step(pl.multiple_of(tile * 256, 256), 256)
            return carry

        lax.fori_loop(0, tall // 256, step, 0)
        if tall % 256:
            tile_step(tall // 256 * 256, tall % 256)
        chip = chip_index()

        def block(k):
            return pl.ds(pl.multiple_of(lax.bitwise_xor(chip, k) * rows, 16), rows)

        copies = []
        if split:
            for which, order in enumerate(((1, 3), (0, 2), (2, 3), (0, 1))):
                columns = pl.ds((which // 2) * halved, halved)
                for slot, k in enumerate(order):
                    copies.append(
                        pltpu.make_async_copy(
                            grads.at[block(k), columns],
                            outs[which].at[slot],
                            sems.at[2 * which + slot],
                        )
                    )
        else:
            for k in range(chips):
                copies.append(
                    pltpu.make_async_copy(grads.at[block(k), :], outs[k], sems.at[k])
                )
        run_copies(copies)

    if split:
        outs = [shape((2, rows, halved), BF)] * 4
    else:
        outs = [shape((rows, wide), BF)] * chips
    small = (16, 128)
    return call(
        kernel,
        outs,
        [ANY] * len(outs),
        [
            pltpu.VMEM((tall, wide), BF),
            pltpu.VMEM((tokens, tall) if len(lefts) == 2 else small, BF),
            pltpu.VMEM((tokens, wide) if len(rights) == 2 else small, BF),
            pltpu.SemaphoreType.DMA((8 if split else chips,)),
        ],
        [*lefts, *rights],
        [VM] * (len(lefts) + len(rights)),
        2 * tokens * tall * wide,
        48,
    )


class Link:
    def __init__(self, source, target, arriving, sems, slot, axis, bit):
        device = {axis: lax.bitwise_xor(lax.axis_index(axis), bit)}

        def make(to):
            return pltpu.make_async_remote_copy(
                src_ref=source,
                dst_ref=to,
                send_sem=sems.at[0, slot],
                recv_sem=sems.at[1, slot],
                device_id=device,
                device_id_type=pl.DeviceIdType.MESH,
            )

        self.out = make(target)
        self.into = make(arriving)
        self.flying = False

    def start(self):
        self.out.start()
        self.flying = True
        return self

    def arrived(self):
        self.into.wait_recv()

    def sent(self):
        if self.flying:
            self.out.wait_send()
        self.flying = False


def enter(fsdp_bits, ctx_bits):
    barrier = pltpu.get_barrier_semaphore()
    for axis, bits in (("fsdp", fsdp_bits), ("ctx", ctx_bits)):
        for bit in bits:
            pl.semaphore_signal(
                barrier,
                inc=1,
                device_id={axis: lax.bitwise_xor(lax.axis_index(axis), bit)},
                device_id_type=pl.DeviceIdType.MESH,
            )
    pl.semaphore_wait(barrier, len(fsdp_bits) + len(ctx_bits))


def turn(x, cosines, sines, direction):
    width, pairs = x.shape[-1], HD // 2
    lane = lax.broadcasted_iota(jnp.int32, (1, width), 1)
    ahead = pltpu.roll(x, width - pairs, 1)
    behind = pltpu.roll(x, pairs, 1)
    other = jnp.where(lax.rem(lane, HD) < pairs, -ahead, behind)
    return x * cosines + other * (sines if direction > 0 else -sines)


def rms(total, gain):
    factor = lax.rsqrt(jnp.mean(total * total, axis=1, keepdims=True) + EPSILON)
    return (total * factor * gain).astype(BF)


def forward_pass(tokens, doc_lengths, gains, w_qkv, w_out, w_gate, w_up, w_down):
    local, width = tokens.shape
    layers, block, _ = w_qkv.shape
    hidden = w_gate.shape[2]
    hid = hidden // 2
    hid_block = w_down.shape[1]
    half = width // 2
    shards, ctx = lax.axis_size("fsdp"), lax.axis_size("ctx")
    chips = shards // 2
    group = half // ctx
    span = ctx * local
    heads = group // HD
    both = 2 * local
    documents = doc_lengths.shape[1]
    lengths = jnp.zeros((8, 128), jnp.int32).at[:documents].set(doc_lengths[0][:, None])
    gain_rows = jnp.zeros((8, block), F32).at[: 2 * layers].set(
        gains.reshape(2 * layers, block).astype(F32)
    )

    def kernel(*refs):
        (tok, lens, gain_in, qkv_in, out_in, gate_in, up_in, down_in) = refs[:8]
        (wq_o, wo_o, wg_o, wd_o, n1_o, n2_o, whole_o, mix_o, mid_o, stream_o) = refs[8:18]
        (act_o, kept_o, gain_o, cos_o, sin_o, start_o, final_o) = refs[18:25]
        (wq, wo, wg, wd, qkv_raw, gu_raw, q_stage, g_stage) = refs[25:33]
        (n1, n2, whole, slab, mixed, landed, value, mix, mid, stream) = refs[33:43]
        (act, kept, part, other, got, gbuf, lens_all, cos, sin, start) = refs[43:53]
        (sems, local_sems, save_sems) = refs[53:]
        f = lax.axis_index("fsdp")
        z = lax.axis_index("ctx")
        core = lax.rem(f, 2)
        chip = f // 2
        flights = []
        saves = []

        def link(source, target, arriving, axis, bit):
            made = Link(source, target, arriving, sems, len(flights), axis, bit)
            flights.append(made)
            return made

        def save(source, target):
            copy = pltpu.make_async_copy(source, target, save_sems.at[len(saves)])
            copy.start()
            saves.append(copy)
            return len(saves) - 1

        def saved(number):
            if saves[number] is not None:
                saves[number].wait()
            saves[number] = None

        def rows(index, count):
            return pl.ds(pl.multiple_of(index * count, 16), count)

        def fx(bit):
            return lax.bitwise_xor(f, bit)

        def cx(bit):
            return lax.bitwise_xor(chip, bit)

        class Halved:
            def __init__(self, buffer, stage):
                def at(index):
                    return buffer.at[rows(index, block), :]

                self.first = [
                    link(stage, at(f), at(fx(bit)), "fsdp", bit) for bit in (1, 3, 5)
                ] + [link(at(f), at(f), at(fx(bit)), "fsdp", bit) for bit in (2, 4)]
                over_y, over_x, far = 2 * cx(1), 2 * cx(2) + 1, 2 * cx(3)
                self.second = [
                    link(at(over_y), at(over_y), at(far), "fsdp", 4),
                    link(at(over_x), at(over_x), at(far + 1), "fsdp", 2),
                ]

        class Rowed:
            def __init__(self, buffer, source, count):
                small = count // 2

                def at(index):
                    return buffer.at[rows(index, count), :]

                def side(index, which):
                    begin = pl.multiple_of(index * count + which * small, 16)
                    return buffer.at[pl.ds(begin, small), :]

                self.first = [
                    link(source, at(chip), at(cx(bit // 2)), "fsdp", bit) for bit in (2, 4)
                ]
                self.second = [
                    link(side(cx(1), 0), side(cx(1), 0), side(cx(3), 0), "fsdp", 4),
                    link(side(cx(2), 1), side(cx(2), 1), side(cx(3), 1), "fsdp", 2),
                ]

        def begin(weight):
            for one in weight.first:
                one.start()

        def forward(weight):
            for one in weight.first:
                one.arrived()
            for one in weight.second:
                one.start()

        def finish(weight):
            for one in weight.second:
                one.arrived()

        q_of = [Halved(wq.at[n], q_stage.at[n]) for n in range(layers)]
        g_of = [Halved(wg.at[n], g_stage.at[n]) for n in range(layers)]
        o_of = [Rowed(wo.at[n], out_in.at[n], block) for n in range(layers)]
        d_of = [Rowed(wd.at[n], down_in.at[n], hid_block) for n in range(layers)]

        def local_copy(source, target, slot):
            copy = pltpu.make_async_copy(source, target, local_sems.at[slot])
            copy.start()
            return copy

        def choose(first, second):
            return lax.select(core == 0, first, second)

        def stage_qkv(n):
            for kind in range(3):
                for j in range(chips):
                    at = kind * width + 2 * j * block
                    even = qkv_raw[:, at : at + block]
                    odd = qkv_raw[:, at + block : at + 2 * block]
                    to = kind * half + j * block
                    wq[n, rows(f, block), to : to + block] = choose(even, odd)
                    q_stage[n, :, to : to + block] = choose(odd, even)

        def stage_gu(n):
            for which in range(2):
                sets = []
                for lane_core in range(2):
                    parts = []
                    for j in range(chips):
                        at = (2 * j + lane_core) * hid_block
                        parts.append(gu_raw[which, :, at : at + hid_block])
                    sets.append(jnp.concatenate(parts, axis=1))
                to = slice(which * hid, (which + 1) * hid)
                wg[n, rows(f, block), to] = choose(sets[0], sets[1])
                g_stage[n, :, to] = choose(sets[1], sets[0])

        def load(n):
            return [
                local_copy(qkv_in.at[n], qkv_raw, 0),
                local_copy(gate_in.at[n], gu_raw.at[0], 1),
                local_copy(up_in.at[n], gu_raw.at[1], 2),
            ]

        loads = load(0)
        mine = []
        for n in range(layers):
            mine.append(local_copy(out_in.at[n], wo.at[n, rows(chip, block), :], 3 + n))
            mine.append(
                local_copy(down_in.at[n], wd.at[n, rows(chip, hid_block), :], 3 + layers + n)
            )
        spare = 3 + 2 * layers
        loads[0].wait()
        stage_qkv(0)
        gain_links = [
            link(gain_in, gbuf.at[f], gbuf.at[fx(bit)], "fsdp", bit) for bit in range(1, shards)
        ]
        lens_link = link(lens, lens_all.at[1], lens_all.at[1], "fsdp", 1)
        enter(list(range(1, shards)), list(range(1, ctx)))
        for one in gain_links:
            one.start()
        lens_link.start()
        begin(q_of[0])
        gbuf[f] = gain_in[...]
        lens_all[0] = lens[...]
        for copy in mine + loads[1:]:
            copy.wait()
        stage_gu(0)
        loads = load(1)
        for one in gain_links:
            one.arrived()

        def gain_row(n):
            return jnp.concatenate([gbuf[s, n : n + 1, :] for s in range(shards)], axis=1)

        for n in range(2 * layers):
            gain_o[n : n + 1, :] = gain_row(n)

        def norm_link(buffer, n):
            upper = buffer.at[n, pl.ds(local, local), :]
            return link(buffer.at[n, pl.ds(0, local), :], upper, upper, "fsdp", 1)

        n1[0, :local] = rms(tok[...].astype(F32), gain_row(0))
        norm_now = norm_link(n1, 0).start()

        lens_link.arrived()
        pairs = HD // 2
        lane = lax.broadcasted_iota(jnp.int32, (1, 128), 1)
        frequency = jnp.exp((-math.log(10000.0) / pairs) * lax.rem(lane, pairs).astype(F32))

        def table_step(index, carry):
            r = index // ctx
            piece = lax.rem(index, ctx)
            to = rows(piece, local)
            at = lax.broadcasted_iota(jnp.int32, (local, 128), 0) + piece * local
            first = jnp.zeros((local, 128), jnp.int32)
            end = jnp.zeros((1, 128), jnp.int32)
            for j in range(documents):
                end = end + lens_all[r, j : j + 1, :]
                first = jnp.where(at >= end, end, first)
            start[r, to, :] = first
            angle = (at - first).astype(F32) * frequency
            sin[r, to, :] = jnp.sin(angle)
            cos[r, to, :] = jnp.cos(angle)
            return carry

        lax.fori_loop(0, 2 * ctx, table_step, 0)
        here_rows = rows(z, local)
        for source, target in ((cos, cos_o), (sin, sin_o), (lens_all, start_o)):
            save(source, target)
        lane_head = lax.broadcasted_iota(jnp.int32, (1, group), 1) // HD

        def do_project(n):
            for tile in range(3 * half // 256):
                acc = dot(n1[n], wq[n, :, tile * 256 : (tile + 1) * 256])
                kind = tile * 256 // half
                for sub in range(256 // group):
                    column = tile * 256 - kind * half + sub * group
                    for r in range(2):
                        x = acc[r * local : (r + 1) * local, sub * group : (sub + 1) * group]
                        at = (slice(r * local, (r + 1) * local), slice(column, column + group))
                        if kind < 2:
                            x = turn(x, cos[r, here_rows, :], sin[r, here_rows, :], 1)
                        elif n > 0:
                            x = 0.5 * x + 0.5 * value[at].astype(F32)
                        x = x.astype(BF)
                        if kind == 2 and n == 0:
                            value[at] = x
                        slab[column // group, kind, r] = x

        def slab_links(n):
            made = []
            for bit in range(1, ctx):
                to = lax.bitwise_xor(z, bit)
                made.append(
                    link(
                        slab.at[to],
                        whole.at[n, :, :, rows(z, local), :],
                        whole.at[n, :, :, rows(to, local), :],
                        "ctx",
                        bit,
                    )
                )
            return made

        def mixed_links(n):
            made = []
            for bit in range(1, ctx):
                to = lax.bitwise_xor(z, bit)
                made.append(link(mixed.at[n, to], landed.at[n, z], landed.at[n, to], "ctx", bit))
            return made

        def do_attend(n):
            def row_step(r, carry):
                for piece in range(ctx):
                    keys = (piece + 1) * local
                    here = slice(piece * local, keys)
                    query = whole[n, 0, r, here, :] * SCORE_SCALE
                    key = whole[n, 1, r, :keys, :]
                    val = whole[n, 2, r, :keys, :]
                    k_at = lax.broadcasted_iota(jnp.int32, (local, keys), 1)
                    q_at = lax.broadcasted_iota(jnp.int32, (local, keys), 0) + piece * local
                    allowed = (k_at <= q_at) & (k_at >= start[r, here, 0:1])
                    result = None
                    for head in range(heads):
                        q_head = jnp.where(lane_head == head, query, jnp.zeros_like(query))
                        scores = jnp.where(allowed, dot_nt(q_head, key), MASK_FILL)
                        top = jnp.max(scores, axis=1, keepdims=True)
                        powers = jnp.exp(scores - top)
                        total = jnp.sum(powers, axis=1, keepdims=True)
                        probs = (powers * (1.0 / total)).astype(BF)
                        out = dot(probs, val)
                        result = out if head == 0 else jnp.where(lane_head == head, out, result)
                    mixed[n, piece, r] = result.astype(BF)
                return carry

            lax.fori_loop(0, 2, row_step, 0)

        last_sum = [None]

        def partial_sums(n, which, left, weight):
            if last_sum[0] is not None:
                last_sum[0].sent()

            def step(tile, carry):
                columns = rows(tile, 256)
                product = dot(left[...], weight[:, columns])
                part[:, columns] = product[:local]
                other[:, columns] = product[local:].astype(BF)
                return carry

            lax.fori_loop(0, width // 256, step, 0)
            to = got.at[n, which]
            last_sum[0] = link(other, to, to, "fsdp", 1).start()
            return last_sum[0]

        def gate_up(n):
            def span_step(base, count):
                here, there = pl.ds(base, count), pl.ds(hid + base, count)
                gate = dot(n2[n], wg[n, :, here])
                up = dot(n2[n], wg[n, :, there])
                kept[:, here] = gate.astype(BF)
                kept[:, there] = up.astype(BF)
                act[:, here] = (gate * jax.nn.sigmoid(gate) * up).astype(BF)

            def step(tile, carry):
                span_step(pl.multiple_of(tile * 256, 128), 256)
                return carry

            lax.fori_loop(0, hid // 256, step, 0)
            if hid % 256:
                span_step(hid // 256 * 256, hid % 256)

        slab_flights = []
        held = []
        for n in range(layers):
            if n == 0:
                forward(q_of[0])
                begin(o_of[0])
            finish(q_of[n])
            save(wq.at[n], wq_o.at[n])
            begin(g_of[n])
            norm_now.arrived()
            save(n1.at[n], n1_o.at[n])
            for one in slab_flights:
                one.sent()
            do_project(n)
            slab_flights = slab_links(n)
            for one in slab_flights:
                one.start()
            own = local_copy(slab.at[z], whole.at[n, :, :, here_rows, :], spare)
            if n == 0:
                for copy in loads:
                    copy.wait()
                stage_qkv(1)
                stage_gu(1)
            forward(o_of[n])
            finish(o_of[n])
            save(wo.at[n], wo_o.at[n])
            if n > 0:
                forward(g_of[n])
                begin(d_of[n])
            own.wait()
            for one in slab_flights:
                one.arrived()
            save(whole.at[n], whole_o.at[n])
            if n == 0:
                forward(g_of[n])
                begin(d_of[n])
            do_attend(n)
            back = mixed_links(n)
            for one in back:
                one.start()
            own = local_copy(mixed.at[n, z], landed.at[n, z], spare)
            if n == 0:
                begin(q_of[1])
            own.wait()
            for one in back:
                one.arrived()
            for k in range(ctx):
                mix[n, :, k * group : (k + 1) * group] = landed[n, k].reshape(both, group)
            save(mix.at[n], mix_o.at[n])
            sums = partial_sums(n, 0, mix.at[n], wo.at[n])
            forward(d_of[n])
            base = tok[...].astype(F32) if n == 0 else stream[...]
            sums.arrived()
            total = base + part[...] + got[n, 0].astype(F32)
            mid[n] = total
            n2[n, :local] = rms(total, gain_row(2 * n + 1))
            norm_now = norm_link(n2, n).start()
            save(mid.at[n], mid_o.at[n])
            finish(g_of[n])
            save(wg.at[n], wg_o.at[n])
            for number in held:
                saved(number)
            norm_now.arrived()
            save(n2.at[n], n2_o.at[n])
            gate_up(n)
            held = [save(act, act_o.at[n]), save(kept, kept_o.at[n])]
            if n == 0:
                forward(q_of[1])
                begin(o_of[1])
            finish(d_of[n])
            save(wd.at[n], wd_o.at[n])
            sums = partial_sums(n, 1, act, wd.at[n])
            sums.arrived()
            total = mid[n] + part[...] + got[n, 1].astype(F32)
            if n + 1 < layers:
                stream[...] = total
                n1[n + 1, :local] = rms(total, gain_row(2 * n + 2))
                norm_now = norm_link(n1, n + 1).start()
                save(stream, stream_o)
            else:
                final_o[...] = total.astype(BF)
        for one in flights:
            one.sent()
        for number in range(len(saves)):
            saved(number)

    def stacked(*dims):
        return (layers, *dims)

    outs = [
        shape(stacked(width, 3 * half), BF),
        shape(stacked(half, width), BF),
        shape(stacked(width, 2 * hid), BF),
        shape(stacked(hid, width), BF),
        shape(stacked(both, width), BF),
        shape(stacked(both, width), BF),
        shape(stacked(3, 2, span, group), BF),
        shape(stacked(both, half), BF),
        shape(stacked(local, width), F32),
        shape((local, width), F32),
        shape(stacked(both, hid), BF),
        shape(stacked(both, 2 * hid), BF),
        shape((2 * layers, width), F32),
        shape((2, span, 128), F32),
        shape((2, span, 128), F32),
        shape((2, 8, 128), jnp.int32),
        shape((local, width), BF),
    ]
    out_specs = [ANY] * 17
    out_specs[12] = out_specs[16] = VM
    scratch = [
        pltpu.VMEM(stacked(width, 3 * half), BF),
        pltpu.VMEM(stacked(half, width), BF),
        pltpu.VMEM(stacked(width, 2 * hid), BF),
        pltpu.VMEM(stacked(hid, width), BF),
        pltpu.VMEM((block, 3 * width), BF),
        pltpu.VMEM((2, block, hidden), BF),
        pltpu.VMEM(stacked(block, 3 * half), BF),
        pltpu.VMEM(stacked(block, 2 * hid), BF),
        pltpu.VMEM(stacked(both, width), BF),
        pltpu.VMEM(stacked(both, width), BF),
        pltpu.VMEM(stacked(3, 2, span, group), BF),
        pltpu.VMEM((ctx, 3, 2, local, group), BF),
        pltpu.VMEM(stacked(ctx, 2, local, group), BF),
        pltpu.VMEM(stacked(ctx, 2, local, group), BF),
        pltpu.VMEM((both, half), BF),
        pltpu.VMEM(stacked(both, half), BF),
        pltpu.VMEM(stacked(local, width), F32),
        pltpu.VMEM((local, width), F32),
        pltpu.VMEM((both, hid), BF),
        pltpu.VMEM((both, 2 * hid), BF),
        pltpu.VMEM((local, width), F32),
        pltpu.VMEM((local, width), BF),
        pltpu.VMEM(stacked(2, local, width), BF),
        pltpu.VMEM((shards, 8, block), F32),
        pltpu.VMEM((2, 8, 128), jnp.int32),
        pltpu.VMEM((2, span, 128), F32),
        pltpu.VMEM((2, span, 128), F32),
        pltpu.VMEM((2, span, 128), jnp.int32),
        pltpu.SemaphoreType.DMA((2, 80)),
        pltpu.SemaphoreType.DMA((8,)),
        pltpu.SemaphoreType.DMA((32,)),
    ]
    return pl.pallas_call(
        kernel,
        out_shape=outs,
        in_specs=[VM] * 3 + [ANY] * 5,
        out_specs=out_specs,
        scratch_shapes=scratch,
        compiler_params=pltpu.CompilerParams(
            vmem_limit_bytes=62 * MIB, collective_id=0, has_side_effects=True
        ),
        cost_estimate=pl.CostEstimate(
            flops=14 * 10**9, bytes_accessed=60 * MIB, transcendentals=0
        ),
    )(tokens, lengths, gain_rows, w_qkv, w_out, w_gate, w_up, w_down)


BACK_ORDER = (
    ("dW", 1), ("mlp", 1), ("F", "d", 1, 0), ("nrm2", 1), ("F", "d", 1, 1),
    ("mixb", 1), ("oW", 1), ("gW", 1), ("dos", 1), ("att", 1, 0),
    ("S", "d", 1, 0), ("att", 1, 1), ("S", "d", 1, 1), ("T", "gb", 1), ("F", "ga", 1, 0),
    ("F", "ga", 1, 1), ("F", "o", 1, 0), ("F", "o", 1, 1), ("S", "o", 1, 0), ("S", "o", 1, 1),
    ("F", "gb", 1, 0), ("F", "gb", 1, 1), ("pb", 1), ("qW", 1), ("nrm1", 1),
    ("S", "ga", 1, 0), ("I", "d", 1, 0), ("I", "d", 1, 1), ("S", "ga", 1, 1), ("I", "o", 1, 0),
    ("I", "o", 1, 1), ("dW", 0), ("T", "d", 0), ("mlp", 0), ("I", "ga", 1, 0),
    ("S", "gb", 1, 0), ("nrm2", 0), ("X", "o", 1, 0), ("F", "q", 1, 0), ("mixb", 0),
    ("F", "q", 1, 1), ("X", "d", 1, 0), ("oW", 0), ("X", "o", 1, 1), ("X", "d", 1, 1),
    ("F", "d", 0, 0), ("F", "d", 0, 1), ("I", "ga", 1, 1), ("S", "gb", 1, 1), ("O", "o", 1, 0),
    ("dos", 0), ("att", 0, 0), ("X", "ga", 1, 0), ("S", "q", 1, 0), ("O", "o", 1, 1),
    ("I", "gb", 1, 0), ("W", "o", 1), ("att", 0, 1), ("S", "q", 1, 1), ("gW", 0),
    ("T", "ga", 0), ("X", "ga", 1, 1), ("O", "d", 1, 0), ("F", "ga", 0, 0), ("F", "ga", 0, 1),
    ("F", "gb", 0, 0), ("F", "gb", 0, 1), ("O", "d", 1, 1), ("I", "gb", 1, 1), ("X", "gb", 1, 0),
    ("W", "d", 1), ("S", "d", 0, 0), ("S", "d", 0, 1), ("pb", 0), ("qW", 0),
    ("nrm1", 0), ("G1", 0), ("I", "q", 1, 0), ("O", "ga", 1, 0), ("O", "ga", 1, 1),
    ("X", "gb", 1, 1), ("I", "q", 1, 1), ("G2", 0), ("W", "ga", 1), ("S", "ga", 0, 0),
    ("T", "o", 0), ("O", "gb", 1, 0), ("S", "ga", 0, 1), ("I", "d", 0, 0), ("I", "d", 0, 1),
    ("T", "q", 0), ("X", "q", 1, 0), ("O", "gb", 1, 1), ("F", "o", 0, 0), ("F", "o", 0, 1),
    ("W", "gb", 1), ("S", "gb", 0, 0), ("S", "gb", 0, 1), ("X", "q", 1, 1), ("O", "q", 1, 0),
    ("I", "ga", 0, 0), ("S", "o", 0, 0), ("S", "o", 0, 1), ("F", "q", 0, 0), ("F", "q", 0, 1),
    ("I", "ga", 0, 1), ("X", "d", 0, 0), ("X", "d", 0, 1), ("O", "q", 1, 1), ("W", "q", 1),
    ("I", "o", 0, 0), ("I", "o", 0, 1), ("X", "ga", 0, 0), ("I", "gb", 0, 0), ("S", "q", 0, 0),
    ("S", "q", 0, 1), ("I", "gb", 0, 1), ("O", "d", 0, 0), ("X", "o", 0, 0), ("O", "d", 0, 1),
    ("X", "ga", 0, 1), ("X", "o", 0, 1), ("W", "d", 0), ("O", "o", 0, 0), ("O", "ga", 0, 0),
    ("I", "q", 0, 0), ("I", "q", 0, 1), ("X", "gb", 0, 0), ("X", "gb", 0, 1), ("O", "o", 0, 1),
    ("O", "ga", 0, 1), ("W", "o", 0), ("W", "ga", 0), ("X", "q", 0, 0), ("X", "q", 0, 1),
    ("O", "gb", 0, 0), ("O", "gb", 0, 1), ("W", "gb", 0), ("O", "q", 0, 0), ("O", "q", 0, 1),
    ("W", "q", 0), ("G3", 0),
)
HELD = (("gb", 1), ("d", 0), ("ga", 0), ("o", 0), ("q", 0),)
DEFER = True


def backward_pass(saved, tokens, cotangent):
    local, width = tokens.shape
    wq_s, wo_s, wg_s, wd_s = saved[:4]
    layers = wq_s.shape[0]
    half = width // 2
    hid = wd_s.shape[1]
    shards, ctx = lax.axis_size("fsdp"), lax.axis_size("ctx")
    chips = shards // 2
    block = width // shards
    hid_block = hid // chips
    group = half // ctx
    span = ctx * local
    heads = group // HD
    both = 2 * local
    documents = 4
    sizes = {
        "d": (hid_block, width),
        "g": (2 * block, 2 * hid),
        "o": (block, width),
        "q": (2 * block, 3 * half),
    }
    names = ("d", "g", "o", "q")
    pieces_of = {"d": ("d",), "g": ("ga", "gb"), "o": ("o",), "q": ("q",)}
    units = [unit for name in names for unit in pieces_of[name]]
    counts = {unit: sizes[unit[0]][0] // len(pieces_of[unit[0]]) for unit in units}

    def kernel(*refs):
        refs = list(refs)

        def take(count):
            out = refs[:count]
            del refs[:count]
            return out

        cot_i, tok_i, lens, gain = take(4)
        wq_i, wo_i, wg_i, wd_i, n1_i, n2_i, whole_i, mix_i, mid_i, stream_i = take(10)
        act_i, kept_i, cos_i, sin_i = take(4)
        grad_o, gain_o, q_o, o_o, gate_o, up_o, d_o = take(7)
        lands = {}
        for unit in units:
            lands[unit] = dict(zip(("x1", "y1", "x2", "y2", "z"), take(5)))
        swap_land = dict(zip(("g", "q"), take(2)))
        wq, wo, wg, wd, act, kept, norm, whole, mix, wide = take(10)
        flow, fgrad, got, do_in, dq_in, part, other, grad, middle = take(9)
        do_out, dq_out, key_sum, value_sum, carry, joined, cos, sin = take(8)
        blocks = dict(zip(names, take(4)))
        finals = dict(zip(names, take(4)))
        tmp, stage, gain_rows, gain_send, gain_land, gain_sum, gain_line = take(7)
        sems, load_sems, tmp_sems, out_sems, own_sems = take(5)
        f = lax.axis_index("fsdp")
        z = lax.axis_index("ctx")
        core = lax.rem(f, 2)
        chip = f // 2
        inner = (z == 1) | (z == 2)
        outer = (z == 0) | (z == 3)
        flights = []

        def link(source, target, arriving, axis, bit):
            made = Link(source, target, arriving, sems, len(flights), axis, bit)
            flights.append(made)
            return made

        def rows(index, count):
            return pl.ds(pl.multiple_of(index * count, 16), count)

        def cx(bit):
            return lax.bitwise_xor(chip, bit)

        loading = {}
        slots = {}

        def load(name, source, target):
            slot = slots.setdefault(name, len(slots))
            copy = pltpu.make_async_copy(source, target, load_sems.at[slot])
            copy.start()
            loading[name] = copy

        def loaded(*wanted):
            for name in wanted:
                if name in loading:
                    loading.pop(name).wait()

        top = layers - 1
        load("cot", cot_i, flow.at[pl.ds(0, local), :])
        load("act", act_i.at[top], act)
        load("wd", wd_i.at[top], wd)
        load("kept", kept_i.at[top], kept)
        load("wg", wg_i.at[top], wg)
        load("wide", mid_i.at[top], wide)
        load("wo", wo_i.at[top], wo)
        load("norm", n2_i.at[top], norm)
        load("mix", mix_i.at[top], mix)
        load("whole", whole_i.at[top], whole)
        load("wq", wq_i.at[top], wq)
        load("cos", cos_i, cos)
        load("sin", sin_i, sin)
        enter(list(range(1, shards)), list(range(1, ctx)))

        def pair_link(buffer):
            upper = buffer.at[pl.ds(local, local), :]
            return link(buffer.at[pl.ds(0, local), :], upper, upper, "fsdp", 1)

        loaded("cot")
        e_link = pair_link(flow).start()
        grad[...] = flow[:local].astype(F32)

        class Reduce:
            def __init__(self, unit, n):
                name = unit[0]
                self.name, self.n = name, n
                whole_rows, self.columns = sizes[name]
                self.count = counts[unit]
                self.chunk = pieces_of[name].index(unit) if len(pieces_of[name]) > 1 else None
                self.offset = self.count * (self.chunk or 0)
                self.side = self.columns // 2
                self.blocks, self.final = blocks[name], finals[name]
                self.land = lands[unit]
                left, right = pl.ds(0, self.side), pl.ds(self.side, self.side)
                self.halves = (left, right)

                def row(k):
                    return cx(k) * whole_rows + self.offset

                self.row = row

                def piece(k, columns):
                    at = pl.ds(pl.multiple_of(row(k), 16), self.count)
                    return self.blocks.at[at, columns]

                def into(where, slot=None):
                    ref = self.land[where]
                    return ref.at[n] if slot is None else ref.at[n, slot]

                def hop(source, target, bit):
                    return link(source, target, target, "fsdp", bit)

                self.far = (hop(piece(3, left), into("x1", 1), 2), hop(piece(3, right), into("y1", 1), 4))
                self.near = (hop(piece(1, left), into("x1", 0), 2), hop(piece(2, right), into("y1", 0), 4))
                self.next = (hop(piece(2, left), into("y2"), 4), hop(piece(1, right), into("x2"), 2))
                self.line = []
                for side in self.halves:
                    steps = []
                    source = self.final.at[pl.ds(self.offset, self.count), side]
                    for step, bit in ((0, 1), (1, 3), (2, 1)):
                        target = self.land["z"].at[n, step, :, side]
                        steps.append(link(source, target, target, "ctx", bit))
                    self.line.append(steps)
                self.swap = None
                if name in swap_land:
                    out = rows(1 - core, block)
                    to = swap_land[name].at[n]
                    self.swap = link(self.final.at[out, :], to, to, "fsdp", 1)
                self.complete = 0
                self.held = (unit, n) in HELD

            def fetch(self, *sources):
                copies = []
                for slot, source in enumerate(sources):
                    copy = pltpu.make_async_copy(
                        source,
                        tmp.at[slot, pl.ds(0, self.count), pl.ds(0, self.side)],
                        tmp_sems.at[slot],
                    )
                    copy.start()
                    copies.append(copy)
                for copy in copies:
                    copy.wait()

            def add(self, source, source_row, columns, target, target_row, slots_used):
                def step(tile, carry):
                    at = pl.ds(pl.multiple_of(source_row + tile * 32, 16), 32)
                    total = source[at, columns].astype(F32)
                    here = pl.ds(pl.multiple_of(tile * 32, 16), 32)
                    for slot in slots_used:
                        total = total + tmp[slot, here, : self.side].astype(F32)
                    to = pl.ds(pl.multiple_of(target_row + tile * 32, 16), 32)
                    target[to, columns] = total.astype(BF)
                    return carry

                lax.fori_loop(0, self.count // 32, step, 0)

            def T(self):
                self.far[0].start()
                self.far[1].start()

            def settled(self):
                for one in (*self.far, *self.near, *self.next):
                    one.sent()

            def F(self, h):
                self.far[h].arrived()
                self.fetch(self.land[("x1", "y1")[h]].at[self.n, 1])
                at = self.row(2 - h)
                self.add(self.blocks, at, self.halves[h], self.blocks, at, (0,))
                self.next[h].start()
                if DEFER:
                    self.near[h].start()

            def S(self, h):
                self.near[h].arrived()
                self.next[h].arrived()
                self.fetch(
                    self.land[("x1", "y1")[h]].at[self.n, 0], self.land[("y2", "x2")[h]].at[self.n]
                )
                self.add(self.blocks, self.row(0), self.halves[h], self.final, self.offset, (0, 1))
                pl.when(outer)(self.line[h][0].out.start)

            def I(self, h):
                @pl.when(inner)
                def _():
                    steps = self.line[h]
                    steps[0].into.wait_recv()
                    self.fetch(self.land["z"].at[self.n, 0, :, self.halves[h]])
                    self.add(self.final, self.offset, self.halves[h], self.final, self.offset, (0,))
                    steps[1].out.start()

            def X(self, h):
                @pl.when(inner)
                def _():
                    steps = self.line[h]
                    steps[1].into.wait_recv()
                    self.fetch(self.land["z"].at[self.n, 1, :, self.halves[h]])
                    steps[1].out.wait_send()
                    self.add(self.final, self.offset, self.halves[h], self.final, self.offset, (0,))
                    steps[2].out.start()

            def O(self, h):
                steps = self.line[h]

                @pl.when(outer)
                def _():
                    steps[2].into.wait_recv()
                    steps[0].out.wait_send()
                    copy = pltpu.make_async_copy(
                        self.land["z"].at[self.n, 2, :, self.halves[h]],
                        self.final.at[pl.ds(self.offset, self.count), self.halves[h]],
                        tmp_sems.at[0],
                    )
                    copy.start()
                    copy.wait()

                pl.when(inner)(steps[2].out.wait_send)
                self.complete += 1
                if self.complete == 2 and self.swap is not None:
                    if self.chunk is None:
                        self.swap.out.start()
                    else:
                        pl.when(core != self.chunk)(self.swap.out.start)

            def W(self):
                if self.chunk is None:
                    self.write()
                else:
                    pl.when(core == self.chunk)(self.write)
                    pl.when(core != self.chunk)(self.swap.out.wait_send)

            def write(self):
                n = self.n
                if self.name in ("d", "o"):
                    target = d_o if self.name == "d" else o_o
                    run_copies([pltpu.make_async_copy(self.final, target.at[n], out_sems.at[0])])
                    return
                self.swap.into.wait_recv()
                parts_now = 3 if self.name == "q" else 2
                wide_now = self.columns // parts_now
                places = [
                    (k // 2, pl.ds((k % 2) * block, block), pl.ds(0, wide_now)) for k in range(3)
                ]
                if self.name == "g":
                    places[1] = (1, pl.ds(0, block), pl.ds(0, wide_now))
                run_copies(
                    [
                        pltpu.make_async_copy(
                            swap_land[self.name].at[n, :, pl.ds(k * wide_now, wide_now)],
                            tmp.at[places[k]],
                            out_sems.at[2 + k],
                        )
                        for k in range(parts_now)
                    ]
                )
                mine = rows(core, block)

                def sets(part_now, start_now, count_now):
                    first_at = part_now * wide_now + start_now
                    own = self.final[mine, first_at : first_at + count_now]
                    slot, row_at, _ = places[part_now]
                    theirs = tmp[slot, row_at, start_now : start_now + count_now]
                    return (
                        lax.select(core == 0, own, theirs),
                        lax.select(core == 0, theirs, own),
                    )

                if self.name == "q":
                    for kind in range(3):
                        for j in range(chips):
                            even, odd = sets(kind, j * block, block)
                            to = kind * width + 2 * j * block
                            stage[:, to : to + block] = even
                            stage[:, to + block : to + 2 * block] = odd
                    run_copies([pltpu.make_async_copy(stage, q_o.at[n], out_sems.at[0])])
                else:
                    for which, target in enumerate((gate_o, up_o)):
                        even, odd = sets(which, 0, hid)
                        parts = []
                        for j in range(chips):
                            at = slice(j * hid_block, (j + 1) * hid_block)
                            parts += [even[:, at], odd[:, at]]
                        stage[:, : 2 * hid] = jnp.concatenate(parts, axis=1)
                        run_copies(
                            [
                                pltpu.make_async_copy(
                                    stage.at[:, pl.ds(0, 2 * hid)], target.at[n], out_sems.at[0]
                                )
                            ]
                        )
                if self.chunk is None:
                    self.swap.out.wait_send()

        def grad_tile(target, row, count, left, columns, right, wide_count):
            turned = left[:, columns]
            for begin in range(0, wide_count, 512):
                end = min(begin + 512, wide_count)
                target[pl.ds(row, count), begin:end] = dot_tn(turned, right[:, begin:end]).astype(BF)

        def begin(job, k):
            if k == 3 and not job.held:
                job.T()
            elif k and not DEFER:
                job.near[k - 1].start()

        def compute_blocks(name, n, left, right):
            if not n:
                for unit in pieces_of[name]:
                    jobs[unit, 1].settled()
            count, columns = sizes[name]
            for k in (3, 1, 2, 0):
                row = pl.multiple_of(cx(k) * count, 128)
                grad_tile(blocks[name], row, count, left, pl.ds(row, count), right, columns)
                for unit in pieces_of[name]:
                    begin(jobs[unit, n], k)

        def compute_down(n):
            if not n:
                jobs["d", 1].settled()

            def step(tile, carry):
                row = pl.multiple_of(tile * 256, 128)
                grad_tile(blocks["d"], row, 256, act, pl.ds(row, 256), flow, width)
                return carry

            lax.fori_loop(0, hid // 256, step, 0)
            if hid % 256:
                row = hid // 256 * 256
                grad_tile(blocks["d"], row, hid % 256, act, pl.ds(row, hid % 256), flow, width)
            for k in (3, 1, 2):
                begin(jobs["d", n], k)

        last_sum = [None]

        def partial_sums(which, product):
            if last_sum[0] is not None:
                last_sum[0].sent()

            def step(tile, carry):
                columns = rows(tile, 256)
                value = product(columns)
                part[:, columns] = value[:local]
                other[:, columns] = value[local:].astype(BF)
                return carry

            lax.fori_loop(0, width // 256, step, 0)
            last_sum[0] = link(other, got.at[which], got.at[which], "fsdp", 1).start()
            return last_sum[0]

        def norm_step(x, gain_now, gain_row, which, target, low_target):
            factor = lax.rsqrt(jnp.mean(x * x, axis=1, keepdims=True) + EPSILON)
            back = part[...] + got[which].astype(F32)
            scaled = back * gain_now
            gain_rows[gain_row : gain_row + 1, :] = jnp.sum(back * x * factor, axis=0, keepdims=True)
            mean_term = jnp.mean(scaled * x, axis=1, keepdims=True)
            base = grad[...] if target is middle else middle[...]
            result = base + factor * scaled - x * (factor * factor * factor * mean_term)
            target[...] = result
            if low_target is not None:
                low_target[:local] = result.astype(BF)

        def mlp_back():
            def span_step(base, count):
                here, there = pl.ds(base, count), pl.ds(hid + base, count)
                back = dot_nt(flow[...], wd[here, :])
                gate = kept[:, here].astype(F32)
                up = kept[:, there].astype(F32)
                sig = jax.nn.sigmoid(gate)
                kept[:, here] = (back * up * sig * (1.0 + gate * (1.0 - sig))).astype(BF)
                kept[:, there] = (back * gate * sig).astype(BF)

            def step(tile, carry):
                span_step(pl.multiple_of(tile * 256, 128), 256)
                return carry

            lax.fori_loop(0, hid // 256, step, 0)
            if hid % 256:
                span_step(hid // 256 * 256, hid % 256)

        lane_head = lax.broadcasted_iota(jnp.int32, (1, group), 1) // HD
        line_head = lax.broadcasted_iota(jnp.int32, (group, 1), 0) // HD

        def start_row(r):
            at = lax.broadcasted_iota(jnp.int32, (1, span), 1)
            first = jnp.zeros((1, span), jnp.int32)
            end = jnp.zeros((1, 1), jnp.int32)
            for j in range(documents):
                end = end + lens[r, j : j + 1, 0:1]
                first = jnp.where(at >= end, end, first)
            return first

        def attend_row(n, r):
            if True:
                key_sum[...] = jnp.zeros_like(key_sum)
                value_sum[...] = jnp.zeros_like(value_sum)
                key_turned = whole[1, r].astype(F32).T.astype(BF)
                starts = start_row(r)
                for piece in range(ctx):
                    keys = (piece + 1) * local
                    here = slice(piece * local, keys)
                    query = whole[0, r, here, :] * SCORE_SCALE
                    back = do_in[r, here, :]
                    key = whole[1, r, :keys, :]
                    value = whole[2, r, :keys, :]
                    k_at = lax.broadcasted_iota(jnp.int32, (keys, local), 0)
                    q_at = lax.broadcasted_iota(jnp.int32, (keys, local), 1) + piece * local
                    allowed = (k_at <= q_at) & (k_at >= starts[:, here])
                    turned = None
                    for head in range(heads):
                        q_head = jnp.where(lane_head == head, query, jnp.zeros_like(query))
                        b_head = jnp.where(lane_head == head, back, jnp.zeros_like(back))
                        scores = jnp.where(allowed, dot_nt(key, q_head), MASK_FILL)
                        peak = jnp.max(scores, axis=0, keepdims=True)
                        powers = jnp.exp(scores - peak)
                        total = jnp.sum(powers, axis=0, keepdims=True)
                        probs = powers * (1.0 / total)
                        back_probs = dot_nt(value, b_head)
                        delta = jnp.sum(probs * back_probs, axis=0, keepdims=True)
                        back_scores = (probs * (back_probs - delta)).astype(BF)
                        value_sum[:keys] += dot(probs.astype(BF), b_head)
                        key_sum[:keys] += dot(back_scores, q_head)
                        sub = dot(key_turned[:, :keys], back_scores)
                        turned = sub if head == 0 else jnp.where(line_head == head, sub, turned)
                    back_query = turned.T * SCORE_SCALE
                    dq_out[piece, 0, r] = turn(
                        back_query, cos[r, here, :], sin[r, here, :], -1
                    ).astype(BF)
                for piece in range(ctx):
                    here = slice(piece * local, (piece + 1) * local)
                    dq_out[piece, 1, r] = turn(
                        key_sum[here, :], cos[r, here, :], sin[r, here, :], -1
                    ).astype(BF)
                    if n == top:
                        back_value = 0.5 * value_sum[here, :]
                        carry[r, here, :] = back_value
                    else:
                        back_value = value_sum[here, :] + carry[r, here, :]
                    dq_out[piece, 2, r] = back_value.astype(BF)

        def spread(source_of, target_of):
            made = []
            for bit in range(1, ctx):
                to = lax.bitwise_xor(z, bit)
                made.append(link(source_of(to), target_of(z), target_of(to), "ctx", bit))
            return made

        def own_copy(r, source, target):
            copy = pltpu.make_async_copy(source, target, own_sems.at[r])
            copy.start()
            return copy

        def do_links(r):
            return spread(lambda to: do_out.at[to, r], lambda at: do_in.at[r, rows(at, local), :])

        def dq_links(r):
            return spread(lambda to: dq_out.at[to, :, r], lambda at: dq_in.at[at, :, r])

        jobs = {(unit, n): Reduce(unit, n) for n in (1, 0) for unit in units}
        state = {"e": e_link, "f": None, "do": [[], []], "dq": [[], []], "own": [None, None]}

        def gain_value(n):
            return gain[n : n + 1, :]

        def await_flow(n):
            if state["e"] is not None:
                state["e"].arrived()
                state["sent"] = state["e"]
                state["e"] = None

        def op_dW(n):
            loaded("act")
            await_flow(n)
            compute_down(n)
            if n:
                load("act", act_i.at[0], act)

        def op_mlp(n):
            loaded("wd", "kept")
            await_flow(n)
            mlp_back()
            if n:
                load("wd", wd_i.at[0], wd)
            loaded("wg")
            state["sums"] = partial_sums(0, lambda columns: dot_nt(kept[...], wg[columns, :]))
            if n:
                load("wg", wg_i.at[0], wg)

        def op_nrm2(n):
            loaded("wide")
            if state["f"] is not None:
                state["f"].sent()
            state["sums"].arrived()
            norm_step(wide[...], gain_value(2 * n + 1), 2 * n + 1, 0, middle, fgrad)
            state["f"] = pair_link(fgrad).start()
            state["fresh"] = True
            if n:
                load("wide", stream_i, wide)

        def await_fgrad():
            if state["fresh"]:
                state["f"].arrived()
            state["fresh"] = False

        def op_mixb(n):
            loaded("wo")
            for one in state["do"][0] + state["do"][1]:
                one.sent()
            await_fgrad()
            for tile in range(half // 256):
                back = dot_nt(fgrad[...], wo[tile * 256 : (tile + 1) * 256, :]).astype(BF)
                for sub in range(256 // group):
                    do_out[tile * 256 // group + sub] = back[
                        :, sub * group : (sub + 1) * group
                    ].reshape(2, local, group)
            if n:
                load("wo", wo_i.at[0], wo)
            state["do"] = [do_links(0), do_links(1)]
            for one in state["do"][0]:
                one.start()
            for r in range(2):
                state["own"][r] = own_copy(r, do_out.at[z, r], do_in.at[r, rows(z, local), :])

        def op_dos(n):
            for one in state["do"][0]:
                one.arrived()
            for one in state["do"][1]:
                one.start()

        def op_gW(n):
            loaded("norm")
            compute_blocks("g", n, norm, kept)
            load("norm", n1_i.at[n], norm)
            if n:
                load("kept", kept_i.at[0], kept)

        def op_oW(n):
            loaded("mix")
            await_fgrad()
            compute_blocks("o", n, mix, fgrad)
            if n:
                load("mix", mix_i.at[0], mix)

        def op_att(n, r):
            loaded("whole", "cos", "sin")
            state["own"][r].wait()
            if r:
                for one in state["do"][r]:
                    one.arrived()
            for one in state["dq"][r]:
                one.sent()
            attend_row(n, r)
            if n and r:
                load("whole", whole_i.at[0], whole)
            state["dq"][r] = dq_links(r)
            for one in state["dq"][r]:
                one.start()
            state["own"][r] = own_copy(r, dq_out.at[z, :, r], dq_in.at[z, :, r])

        def op_pb(n):
            loaded("wq")
            for r in range(2):
                state["own"][r].wait()
                for one in state["dq"][r]:
                    one.arrived()
            for k in range(ctx):
                for kind in range(3):
                    base = kind * half + k * group
                    joined[:, base : base + group] = dq_in[k, kind].reshape(both, group)
            state["sums"] = partial_sums(1, lambda columns: dot_nt(joined[...], wq[columns, :]))
            if n:
                load("wq", wq_i.at[0], wq)

        def op_qW(n):
            loaded("norm")
            compute_blocks("q", n, norm, joined)
            if n:
                load("norm", n2_i.at[0], norm)

        def op_nrm1(n):
            if not n:
                state["f"].sent()
                load("tok", tok_i, fgrad.at[pl.ds(0, local), :])
                loaded("tok")
            loaded("wide")
            state["sent"].sent()
            state["sums"].arrived()
            if n:
                norm_step(wide[...], gain_value(2 * n), 2 * n, 1, grad, flow)
                state["e"] = pair_link(flow).start()
                load("wide", mid_i.at[0], wide)
            else:
                norm_step(fgrad[:local].astype(F32), gain_value(0), 0, 1, grad_o, None)

        def op_G1(n):
            for s in range(shards):
                gain_send[s] = jnp.concatenate(
                    [gain_rows[:4, s * block : (s + 1) * block], jnp.zeros((4, block), F32)]
                )
            state["gain"] = []
            for bit in range(1, shards):
                to = lax.bitwise_xor(f, bit)
                state["gain"].append(
                    link(gain_send.at[to], gain_land.at[f], gain_land.at[to], "fsdp", bit).start()
                )
            gain_land[f] = gain_send[f]

        def op_G2(n):
            for one in state["gain"]:
                one.arrived()
            total = gain_land[0]
            for s in range(1, shards):
                total = total + gain_land[s]
            gain_sum[...] = total
            state["line"] = []
            for bit in range(1, ctx):
                to = lax.bitwise_xor(z, bit)
                state["line"].append(
                    link(gain_sum, gain_line.at[z], gain_line.at[to], "ctx", bit).start()
                )
            gain_line[z] = total

        def op_G3(n):
            for one in state["line"]:
                one.arrived()
            total = gain_line[0]
            for k in range(1, ctx):
                total = total + gain_line[k]
            gain_o[...] = total

        chain = {
            "dW": op_dW, "mlp": op_mlp, "nrm2": op_nrm2, "mixb": op_mixb, "gW": op_gW,
            "oW": op_oW, "att": op_att, "dos": op_dos, "pb": op_pb, "qW": op_qW, "nrm1": op_nrm1,
            "G1": op_G1, "G2": op_G2, "G3": op_G3,
        }
        for step in BACK_ORDER:
            if step[0] in chain:
                chain[step[0]](*step[1:])
            elif step[0] in ("W", "T"):
                getattr(jobs[step[1], step[2]], step[0])()
            else:
                getattr(jobs[step[1], step[2]], step[0])(step[3])
        for one in flights:
            one.sent()

    def vm(*dims, kind=BF):
        return pltpu.VMEM(dims, kind)

    outs = [
        shape((local, width), F32),
        shape((8, block), F32),
        shape((layers, block, 3 * width), BF),
        shape((layers, block, width), BF),
        shape((layers, block, 2 * hid), BF),
        shape((layers, block, 2 * hid), BF),
        shape((layers, hid_block, width), BF),
    ]
    for unit in units:
        count, columns = counts[unit], sizes[unit[0]][1]
        outs += [
            shape((layers, 2, count, columns // 2), BF),
            shape((layers, 2, count, columns // 2), BF),
            shape((layers, count, columns // 2), BF),
            shape((layers, count, columns // 2), BF),
            shape((layers, 3, count, columns), BF),
        ]
    outs += [shape((layers, block, sizes[name][1]), BF) for name in ("g", "q")]
    scratch = [
        vm(width, 3 * half),
        vm(half, width),
        vm(width, 2 * hid),
        vm(hid, width),
        vm(both, hid),
        vm(both, 2 * hid),
        vm(both, width),
        vm(3, 2, span, group),
        vm(both, half),
        vm(local, width, kind=F32),
        vm(both, width),
        vm(both, width),
        vm(2, local, width),
        vm(2, span, group),
        vm(ctx, 3, 2, local, group),
        vm(local, width, kind=F32),
        vm(local, width),
        vm(local, width, kind=F32),
        vm(local, width, kind=F32),
        vm(ctx, 2, local, group),
        vm(ctx, 3, 2, local, group),
        vm(span, group, kind=F32),
        vm(span, group, kind=F32),
        vm(2, span, group, kind=F32),
        vm(both, 3 * half),
        vm(2, span, 128, kind=F32),
        vm(2, span, 128, kind=F32),
    ]
    scratch += [vm(chips * sizes[name][0], sizes[name][1]) for name in names]
    scratch += [vm(*sizes[name]) for name in names]
    scratch += [
        vm(2, max(hid_block, 2 * block), hid),
        vm(block, 3 * width),
        vm(8, width, kind=F32),
        vm(shards, 8, block, kind=F32),
        vm(shards, 8, block, kind=F32),
        vm(8, block, kind=F32),
        vm(ctx, 8, block, kind=F32),
        pltpu.SemaphoreType.DMA((2, 192)),
        pltpu.SemaphoreType.DMA((20,)),
        pltpu.SemaphoreType.DMA((2,)),
        pltpu.SemaphoreType.DMA((6,)),
        pltpu.SemaphoreType.DMA((2,)),
    ]
    (wq, wo, wg, wd, n1, n2, whole, mix, mid, stream, act, kept) = saved[:12]
    gain_all, cosines, sines, lens_all = saved[12:16]
    return pl.pallas_call(
        kernel,
        out_shape=outs,
        in_specs=[ANY] * 2 + [VM] * 2 + [ANY] * 14,
        out_specs=[VM] * 2 + [ANY] * (len(outs) - 2),
        scratch_shapes=scratch,
        compiler_params=pltpu.CompilerParams(
            vmem_limit_bytes=63 * MIB, collective_id=1, has_side_effects=True
        ),
        cost_estimate=pl.CostEstimate(
            flops=28 * 10**9, bytes_accessed=100 * MIB, transcendentals=0
        ),
    )(
        cotangent, tokens, lens_all, gain_all, wq, wo, wg, wd, n1, n2, whole, mix, mid, stream,
        act, kept, cosines, sines,
    )


def add_low(left, right):
    return (left.astype(F32) + right.astype(F32)).astype(BF)


def reduce_chips(blocks, chips):
    if chips != 4:
        total = blocks[0].astype(F32)
        for k in range(1, chips):
            total = total + swap(blocks[k], "fsdp", 2 * k).astype(F32)
        return total.astype(BF)
    send_x, keep_x, send_y, keep_y = blocks
    got_x = swap(send_x, "fsdp", 2)
    got_y = swap(send_y, "fsdp", 4)
    on_x = swap(add_low(keep_x[1], got_x[1]), "fsdp", 4)
    on_y = swap(add_low(keep_y[1], got_y[1]), "fsdp", 2)
    first = add_low(add_low(keep_x[0], got_x[0]), on_x)
    second = add_low(add_low(keep_y[0], got_y[0]), on_y)
    return jnp.concatenate([first, second], axis=1)


def reduce_line(block):
    if lax.axis_size("ctx") != 4:
        return lax.psum(block, "ctx")
    z = lax.axis_index("ctx")
    inner = (z == 1) | (z == 2)
    inward = lax.ppermute(block, "ctx", [(0, 1), (3, 2)])
    pair = jnp.where(inner, add_low(block, inward), block)
    across = lax.ppermute(pair, "ctx", [(1, 2), (2, 1)])
    total = add_low(pair, across)
    outward = lax.ppermute(total, "ctx", [(1, 0), (2, 3)])
    return jnp.where(inner, total, outward)


def own_rows(block):
    core = lax.axis_index("fsdp") % 2
    rows = block.shape[0] // 2
    mine = lax.dynamic_slice_in_dim(block, core * rows, rows)
    theirs = swap(lax.dynamic_slice_in_dim(block, (1 - core) * rows, rows), "fsdp", 1)
    low = jnp.where(core == 0, mine, theirs)
    high = jnp.where(core == 0, theirs, mine)
    return jnp.stack([low, high])


def chip_piece(mine, other):
    core = lax.axis_index("fsdp") % 2
    got = swap(other, "fsdp", 1)
    return jnp.where(
        core == 0, jnp.concatenate([mine, got]), jnp.concatenate([got, mine])
    )


def document_starts(lengths, index):
    ends = []
    total = jnp.int32(0)
    for j in range(lengths.shape[0]):
        total = total + lengths[j]
        ends.append(total)
    start = jnp.zeros_like(index)
    for end in ends:
        start = jnp.where(index >= end, end, start)
    return start


def rotary(positions):
    pairs = HD // 2
    lane = jnp.arange(128, dtype=jnp.int32)
    frequency = jnp.exp(-math.log(10000.0) * jnp.arange(pairs, dtype=F32) / pairs)
    angles = positions.astype(F32)[..., None] * frequency
    cosines = jnp.tile(jnp.cos(angles), 128 // pairs)
    sines = jnp.tile(jnp.sin(angles), 128 // pairs)
    low = jnp.where(lane % HD < pairs, -sines, 0.0)
    high = jnp.where(lane % HD >= pairs, sines, 0.0)
    return [cosines, low, high]


def body(tokens, doc_lengths, cotangent, gains, w_qkv, w_out, w_gate, w_up, w_down):
    _, local, width = tokens.shape
    layers = gains.shape[0]
    shards = lax.axis_size("fsdp")
    ctx = lax.axis_size("ctx")
    chips = shards // 2
    block = width // shards
    hidden = w_gate.shape[2]
    hidden_half = hidden // 2
    hidden_block = hidden // shards
    core = lax.axis_index("fsdp") % 2
    z = lax.axis_index("ctx")
    span = local * ctx

    def pick(array, axis, which):
        return lax.dynamic_index_in_dim(array, which, axis, keepdims=False)

    if chips == 4 and ctx == 4 and layers == 2:
        saved = forward_pass(
            tokens[0], doc_lengths, gains, w_qkv, w_out, w_gate, w_up, w_down
        )
        made = backward_pass(saved, tokens[0], cotangent[0])
        grad, gain_sum, qkv_sum, out_sum, gate_sum, up_sum, down_sum = made[:7]
        sums = [s.astype(F32) for s in (qkv_sum, out_sum, gate_sum, up_sum, down_sum)]
        gain_sum = gain_sum[: 2 * layers].reshape(layers, 2, block)
        return (saved[16][None], grad[None], gain_sum, *sums)

    qkv_weights, out_weights, gu_weights, down_weights = [], [], [], []
    for layer in range(layers):
        qkv = w_qkv[layer].reshape(block, 3, chips, 2, block)
        sides = [pick(qkv, 3, which).reshape(block, -1) for which in (core, 1 - core)]
        qkv_weights.append(gather(chip_piece(*sides), chips))
        out_weights.append(gather(w_out[layer], chips))
        sides = []
        for which in (core, 1 - core):
            both = [
                pick(w[layer].reshape(block, chips, 2, hidden_block), 2, which).reshape(
                    block, hidden_half
                )
                for w in (w_gate, w_up)
            ]
            sides.append(jnp.concatenate(both, axis=1))
        gu_weights.append(gather(chip_piece(*sides), chips))
        down_weights.append(gather(w_down[layer], chips))

    all_gains = lax.all_gather(gains, "fsdp", axis=2, tiled=True)
    gain_rows = [[all_gains[layer, n][None] for n in range(2)] for layer in range(layers)]

    index = jnp.arange(span, dtype=jnp.int32)
    lengths = [doc_lengths[0], swap(doc_lengths, "fsdp", 1)[0]]
    starts = jnp.stack([document_starts(row, index) for row in lengths])
    row_tables = rotary(index[None] - starts)
    here_tables = [lax.dynamic_slice_in_dim(t, z * local, local, axis=1) for t in row_tables]
    head_lanes = min(128, width // 2 // ctx)
    head_tables = [t[:, :, :head_lanes] for t in row_tables]
    start_column = starts[:, :, None]
    start_row = starts[:, None, :]

    def pair(array):
        return (array, swap(array, "fsdp", 1))

    stream = tokens[0]
    kept = []
    first_value = None
    (low,) = join_norm(stream, None, None, gain_rows[0][0])
    for layer in range(layers):
        normed = pair(low)
        slabs, first_value = project(
            *normed, here_tables, first_value, qkv_weights[layer], ctx, layer == layers - 1
        )
        slabs = exchange(slabs)
        mixed = exchange(attend(slabs, start_column))
        own, other, joined = mix_out(mixed, out_weights[layer])
        middle, low = join_norm(stream, own, swap(other, "fsdp", 1), gain_rows[layer][1])
        normed_two = pair(low)
        active, gu_kept = gate_up(*normed_two, gu_weights[layer])
        own, other = down(active, down_weights[layer])
        after = gain_rows[min(layer + 1, layers - 1)][0]
        kept.append((stream, normed, slabs, joined, middle, normed_two, active, gu_kept))
        stream, low = join_norm(middle, own, swap(other, "fsdp", 1), after)
    out_tokens = stream.astype(BF)[None]

    grad = cotangent[0]
    low = cotangent[0]
    carried = None
    gain_grads = [[None, None] for _ in range(layers)]
    done = [None] * layers
    for layer in reversed(range(layers)):
        stream, normed, slabs, joined, middle, normed_two, active, gu_kept = kept[layer]
        sent = pair(low)
        down_blocks = weight_grad([active], sent, chips)
        gu_grads, own, other = mlp_back(
            *sent, gu_kept, gu_weights[layer], down_weights[layer]
        )
        grad, low, gain_grads[layer][1] = norm_back(
            middle, own, swap(other, "fsdp", 1), gain_rows[layer][1], grad
        )
        gu_blocks = weight_grad(normed_two, [gu_grads], chips)
        mixed_back = pair(low)
        grad_slabs = exchange(mix_back(*mixed_back, out_weights[layer], ctx))
        out_blocks = weight_grad([joined], mixed_back, chips)
        grad_slabs, carry_out = attend_back(slabs, grad_slabs, start_row, head_tables, carried)
        carried = carry_out
        own, other, qkv_grads = project_back(exchange(grad_slabs), qkv_weights[layer])
        qkv_blocks = weight_grad(normed, [qkv_grads], chips)
        grad, low, gain_grads[layer][0] = norm_back(
            stream, own, swap(other, "fsdp", 1), gain_rows[layer][0], grad
        )
        down_sum = reduce_line(reduce_chips(down_blocks, chips)).astype(F32)
        gu_sum = own_rows(reduce_line(reduce_chips(gu_blocks, chips)))
        out_sum = reduce_line(reduce_chips(out_blocks, chips)).astype(F32)
        qkv_sum = own_rows(reduce_line(reduce_chips(qkv_blocks, chips)))
        qkv_sum = qkv_sum.reshape(2, block, 3, chips, block).transpose(1, 2, 3, 0, 4)
        qkv_sum = qkv_sum.reshape(block, 3 * width).astype(F32)
        gu_sum = gu_sum.reshape(2, block, 2, chips, hidden_block).transpose(2, 1, 3, 0, 4)
        gu_sum = gu_sum.reshape(2, block, hidden).astype(F32)
        done[layer] = (qkv_sum, out_sum, gu_sum[0], gu_sum[1], down_sum)

    gain_sum = jnp.stack([jnp.concatenate(rows) for rows in gain_grads])
    gain_sum = lax.psum_scatter(gain_sum, "fsdp", scatter_dimension=2, tiled=True)
    gain_sum = lax.psum(gain_sum, "ctx")
    stacked = [jnp.stack([done[layer][n] for layer in range(layers)]) for n in range(5)]
    return (out_tokens, grad[None], gain_sum, *stacked)


def solution(mesh):
    rows = P(None, "fsdp", None)
    tokens = P("fsdp", "ctx", None)
    gains = P(None, None, "fsdp")
    return jax.shard_map(
        body,
        mesh=mesh,
        in_specs=(tokens, P("fsdp", None), tokens, gains, rows, rows, rows, rows, rows),
        out_specs=(tokens, tokens, gains, rows, rows, rows, rows, rows),
        check_vma=False,
    )
```

```python
import math

import jax
import jax.numpy as jnp
from jax import lax
from jax.experimental import pallas as pl
from jax.experimental.pallas import tpu as pltpu
from jax.sharding import PartitionSpec as P

HEADS = 16
HD = 64
EPSILON = 1e-06
SCORE_SCALE = 0.125
MASK_FILL = -1e30
BF = jnp.bfloat16
F32 = jnp.float32
MIB = 1024 * 1024
ANY = pl.BlockSpec(memory_space=pl.ANY)
VM = pl.BlockSpec(memory_space=pltpu.VMEM)
NT = (((1,), (1,)), ((), ()))
TN = (((0,), (0,)), ((), ()))


def dot(left, right):
    return jnp.dot(left, right, preferred_element_type=F32)


def dot_nt(left, right):
    return lax.dot_general(left, right, NT, preferred_element_type=F32)


def dot_tn(left, right):
    return lax.dot_general(left, right, TN, preferred_element_type=F32)


def swap(array, axis, bit):
    size = lax.axis_size(axis)
    return lax.ppermute(array, axis, [(i, i ^ bit) for i in range(size)])


def call(kernel, outs, out_specs, scratch, args, in_specs, flops, vmem):
    nbytes = sum(a.size * a.dtype.itemsize for a in args)
    nbytes += sum(math.prod(o.shape) * o.dtype.itemsize for o in outs)
    return pl.pallas_call(
        kernel,
        out_shape=outs,
        in_specs=in_specs,
        out_specs=out_specs,
        scratch_shapes=scratch,
        compiler_params=pltpu.CompilerParams(vmem_limit_bytes=vmem * MIB),
        cost_estimate=pl.CostEstimate(flops=flops, bytes_accessed=nbytes, transcendentals=0),
    )(*args)


def shape(dims, kind):
    return jax.ShapeDtypeStruct(tuple(dims), kind)


def chip_index():
    return lax.axis_index("fsdp") // 2


def run_copies(copies):
    for copy in copies:
        copy.start()
    for copy in copies:
        copy.wait()


def weight_copies(plan, refs, buffer, sems, first):
    chip = chip_index()
    rows = plan[0][2]
    copies = []
    for number, ((k, offset, count), ref) in enumerate(zip(plan[1], refs)):
        start = pl.multiple_of(lax.bitwise_xor(chip, k) * rows + offset, 16)
        copies.append(
            pltpu.make_async_copy(
                ref, buffer.at[pl.ds(start, count), :], sems.at[first + number]
            )
        )
    return copies


class Pieces:
    def __init__(self, arrays, where, rows):
        self.arrays = arrays
        self.where = where
        self.rows = rows

    @property
    def plan(self):
        return ((0, 0, self.rows), self.where)


def gather(piece, chips):
    rows = piece.shape[0]
    if chips == 4:
        half = rows // 2
        from_x = swap(piece, "fsdp", 2)
        from_y = swap(piece, "fsdp", 4)
        far_one = swap(from_x[:half], "fsdp", 4)
        far_two = swap(from_y[half:], "fsdp", 2)
        return Pieces(
            [piece, from_x, from_y, far_one, far_two],
            [(0, 0, rows), (1, 0, rows), (2, 0, rows), (3, 0, half), (3, half, rows - half)],
            rows,
        )
    arrays = [piece] + [swap(piece, "fsdp", 2 * k) for k in range(1, chips)]
    return Pieces(arrays, [(k, 0, rows) for k in range(chips)], rows)


def rope(x, cosines, low_sine, high_sine):
    width = x.shape[-1]
    return (
        x * cosines
        + pltpu.roll(x, width - HD // 2, 1) * low_sine
        + pltpu.roll(x, HD // 2, 1) * high_sine
    )


def project(n_own, n_other, tables, first_value, weight, ctx, last):
    local, width = n_own.shape
    half = width // 2
    group = half // ctx
    pieces = len(weight.arrays)
    plan = weight.plan

    def kernel(*refs):
        own, other, cos, low, high = refs[:5]
        at = 5
        v_in = None
        if first_value is not None:
            v_in = refs[at]
            at += 1
        w_refs = refs[at : at + pieces]
        at += pieces
        slabs = refs[at : at + ctx]
        at += ctx
        v_out = None
        if first_value is None:
            v_out = refs[at]
            at += 1
        buffer, tokens, slab, sems, out_sems = refs[at:]
        copies = weight_copies(plan, w_refs, buffer, sems, 0)
        for copy in copies:
            copy.start()
        tokens[:local] = own[...]
        tokens[local:] = other[...]
        tables_now = [t[...].reshape(2 * local, 128) for t in (cos, low, high)]
        for copy in copies:
            copy.wait()
        for tile in range(3 * half // 256):
            acc = dot(tokens[...], buffer[:, tile * 256 : (tile + 1) * 256])
            kind = tile * 256 // half
            base = tile * 256 - kind * half
            for sub in range(2):
                x = acc[:, sub * 128 : (sub + 1) * 128]
                column = base + sub * 128
                if kind < 2:
                    x = rope(x, *tables_now)
                elif first_value is not None:
                    x = 0.5 * x + 0.5 * v_in[:, column : column + 128].astype(F32)
                x = x.astype(BF)
                if kind == 2 and v_out is not None:
                    v_out[:, column : column + 128] = x
                for part in range(128 // group):
                    slab[column // group + part, kind] = x[
                        :, part * group : (part + 1) * group
                    ].reshape(2, local, group)
        z = lax.axis_index("ctx")
        run_copies(
            [
                pltpu.make_async_copy(slab.at[lax.bitwise_xor(z, k)], slabs[k], out_sems.at[k])
                for k in range(ctx)
            ]
        )

    args = [n_own, n_other, *tables]
    specs = [VM] * 5
    outs = [shape((3, 2, local, group), BF)] * ctx
    out_specs = [ANY] * ctx
    if first_value is not None:
        args.append(first_value)
        specs.append(VM)
    else:
        outs.append(shape((2 * local, half), BF))
        out_specs.append(VM)
    args += weight.arrays
    specs += [ANY] * pieces
    got = call(
        kernel,
        outs,
        out_specs,
        [
            pltpu.VMEM((width, 3 * half), BF),
            pltpu.VMEM((2 * local, width), BF),
            pltpu.VMEM((ctx, 3, 2, local, group), BF),
            pltpu.SemaphoreType.DMA((pieces,)),
            pltpu.SemaphoreType.DMA((ctx,)),
        ],
        args,
        specs,
        2 * 2 * local * width * 3 * half,
        40,
    )
    return got[:ctx], (first_value if first_value is not None else got[ctx])


def exchange(slabs):
    return [slabs[0]] + [swap(slabs[k], "ctx", k) for k in range(1, len(slabs))]


def attend(slabs, start_column):
    ctx = len(slabs)
    _, _, local, group = slabs[0].shape
    span = ctx * local
    heads = group // HD

    def kernel(*refs):
        starts = refs[0]
        ins = refs[1 : 1 + ctx]
        outs = refs[1 + ctx : 1 + 2 * ctx]
        whole, mixed, sems, out_sems = refs[1 + 2 * ctx :]
        z = lax.axis_index("ctx")
        copies = []
        for k in range(ctx):
            at = pl.multiple_of(lax.bitwise_xor(z, k) * local, 16)
            copies.append(
                pltpu.make_async_copy(
                    ins[k], whole.at[:, :, pl.ds(at, local), :], sems.at[k]
                )
            )
        run_copies(copies)
        lane = lax.broadcasted_iota(jnp.int32, (1, group), 1) // HD

        def row_step(row, carry):
            for block in range(ctx):
                keys = (block + 1) * local
                here = slice(block * local, keys)
                query = whole[0, row, here, :] * SCORE_SCALE
                key = whole[1, row, :keys, :]
                value = whole[2, row, :keys, :]
                k_at = lax.broadcasted_iota(jnp.int32, (local, keys), 1)
                q_at = lax.broadcasted_iota(jnp.int32, (local, keys), 0) + block * local
                allowed = (k_at <= q_at) & (k_at >= starts[row, here, :])
                result = None
                for head in range(heads):
                    q_head = jnp.where(lane == head, query, jnp.zeros_like(query))
                    scores = jnp.where(allowed, dot_nt(q_head, key), MASK_FILL)
                    top = jnp.max(scores, axis=1, keepdims=True)
                    powers = jnp.exp(scores - top)
                    total = jnp.sum(powers, axis=1, keepdims=True)
                    probs = (powers * (1.0 / total)).astype(BF)
                    out = dot(probs, value)
                    result = out if result is None else jnp.where(lane == head, out, result)
                mixed[block, row] = result.astype(BF)
            return carry

        lax.fori_loop(0, 2, row_step, 0)
        run_copies(
            [
                pltpu.make_async_copy(mixed.at[lax.bitwise_xor(z, k)], outs[k], out_sems.at[k])
                for k in range(ctx)
            ]
        )

    return call(
        kernel,
        [shape((2, local, group), BF)] * ctx,
        [ANY] * ctx,
        [
            pltpu.VMEM((3, 2, span, group), BF),
            pltpu.VMEM((ctx, 2, local, group), BF),
            pltpu.SemaphoreType.DMA((ctx,)),
            pltpu.SemaphoreType.DMA((ctx,)),
        ],
        [start_column, *slabs],
        [VM] + [ANY] * ctx,
        2 * 2 * 2 * heads * span * span * 128,
        40,
    )


def halves_out(product, own_ref, other_ref, columns, local):
    own_ref[:, columns] = product[:local]
    other_ref[:, columns] = product[local:].astype(BF)


def mix_out(slabs, weight):
    ctx = len(slabs)
    _, local, group = slabs[0].shape
    half = ctx * group
    width = weight.arrays[0].shape[1]
    pieces = len(weight.arrays)
    plan = weight.plan

    def kernel(*refs):
        ins = refs[:ctx]
        w_refs = refs[ctx : ctx + pieces]
        own, other, joined, buffer, landed, sems = refs[ctx + pieces :]
        z = lax.axis_index("ctx")
        copies = weight_copies(plan, w_refs, buffer, sems, ctx)
        for k in range(ctx):
            copies.append(
                pltpu.make_async_copy(ins[k], landed.at[lax.bitwise_xor(z, k)], sems.at[k])
            )
        run_copies(copies)
        for k in range(ctx):
            joined[:, k * group : (k + 1) * group] = landed[k].reshape(2 * local, group)
        for tile in range(width // 256):
            columns = slice(tile * 256, (tile + 1) * 256)
            halves_out(dot(joined[...], buffer[:, columns]), own, other, columns, local)

    return call(
        kernel,
        [shape((local, width), F32), shape((local, width), BF), shape((2 * local, half), BF)],
        [VM] * 3,
        [
            pltpu.VMEM((half, width), BF),
            pltpu.VMEM((ctx, 2, local, group), BF),
            pltpu.SemaphoreType.DMA((ctx + pieces,)),
        ],
        [*slabs, *weight.arrays],
        [ANY] * (ctx + pieces),
        2 * 2 * local * half * width,
        24,
    )


def join_norm(base, own, other, gain):
    local, width = base.shape
    fresh = own is not None

    def kernel(*refs):
        if fresh:
            base_ref, own_ref, other_ref, gain_ref, sum_ref, low_ref = refs
            total = base_ref[...].astype(F32) + own_ref[...] + other_ref[...].astype(F32)
            sum_ref[...] = total
        else:
            base_ref, gain_ref, low_ref = refs
            total = base_ref[...].astype(F32)
        factor = lax.rsqrt(jnp.mean(total * total, axis=1, keepdims=True) + EPSILON)
        low_ref[...] = (total * factor * gain_ref[...].astype(F32)).astype(BF)

    outs = [shape((local, width), BF)]
    args = [base, gain]
    if fresh:
        outs = [shape((local, width), F32)] + outs
        args = [base, own, other, gain]
    return call(
        kernel, outs, [VM] * len(outs), [], args, [VM] * len(args), 8 * local * width, 16
    )


def gate_up(n_own, n_other, weight):
    local, width = n_own.shape
    hidden2 = weight.arrays[0].shape[1]
    hidden = hidden2 // 2
    pieces = len(weight.arrays)
    plan = weight.plan

    def kernel(*refs):
        own, other = refs[:2]
        w_refs = refs[2 : 2 + pieces]
        active, kept, buffer, tokens, sems = refs[2 + pieces :]
        copies = weight_copies(plan, w_refs, buffer, sems, 0)
        for copy in copies:
            copy.start()
        tokens[:local] = own[...]
        tokens[local:] = other[...]
        for copy in copies:
            copy.wait()

        def span_step(base, count):
            here, there = pl.ds(base, count), pl.ds(hidden + base, count)
            gate = dot(tokens[...], buffer[:, here])
            up = dot(tokens[...], buffer[:, there])
            kept[:, here] = gate.astype(BF)
            kept[:, there] = up.astype(BF)
            active[:, here] = (gate * jax.nn.sigmoid(gate) * up).astype(BF)

        def step(tile, carry):
            span_step(pl.multiple_of(tile * 256, 128), 256)
            return carry

        lax.fori_loop(0, hidden // 256, step, 0)
        if hidden % 256:
            span_step(hidden // 256 * 256, hidden % 256)

    return call(
        kernel,
        [shape((2 * local, hidden), BF), shape((2 * local, hidden2), BF)],
        [VM] * 2,
        [
            pltpu.VMEM((width, hidden2), BF),
            pltpu.VMEM((2 * local, width), BF),
            pltpu.SemaphoreType.DMA((pieces,)),
        ],
        [n_own, n_other, *weight.arrays],
        [VM] * 2 + [ANY] * pieces,
        2 * 2 * local * width * hidden2,
        40,
    )


def down(active, weight):
    tokens, hidden = active.shape
    local = tokens // 2
    width = weight.arrays[0].shape[1]
    pieces = len(weight.arrays)
    plan = weight.plan

    def kernel(*refs):
        left = refs[0]
        w_refs = refs[1 : 1 + pieces]
        own, other, buffer, sems = refs[1 + pieces :]
        run_copies(weight_copies(plan, w_refs, buffer, sems, 0))

        def step(tile, carry):
            columns = pl.ds(pl.multiple_of(tile * 256, 256), 256)
            halves_out(dot(left[...], buffer[:, columns]), own, other, columns, local)
            return carry

        lax.fori_loop(0, width // 256, step, 0)

    return call(
        kernel,
        [shape((local, width), F32), shape((local, width), BF)],
        [VM] * 2,
        [pltpu.VMEM((hidden, width), BF), pltpu.SemaphoreType.DMA((pieces,))],
        [active, *weight.arrays],
        [VM] + [ANY] * pieces,
        2 * tokens * hidden * width,
        24,
    )


def mlp_back(e_own, e_other, kept, gu_weight, down_weight):
    local, width = e_own.shape
    hidden2 = kept.shape[1]
    hidden = hidden2 // 2
    pieces = len(gu_weight.arrays)
    more = len(down_weight.arrays)
    gu_plan, down_plan = gu_weight.plan, down_weight.plan

    def kernel(*refs):
        e_one, e_two, kept_ref = refs[:3]
        gu_refs = refs[3 : 3 + pieces]
        down_refs = refs[3 + pieces : 3 + pieces + more]
        grads, own, other, gu, wd, tokens, sems = refs[3 + pieces + more :]
        first = weight_copies(down_plan, down_refs, wd, sems, pieces)
        second = weight_copies(gu_plan, gu_refs, gu, sems, 0)
        for copy in first + second:
            copy.start()
        tokens[:local] = e_one[...]
        tokens[local:] = e_two[...]
        for copy in first:
            copy.wait()

        def span_step(base, count):
            here, there = pl.ds(base, count), pl.ds(hidden + base, count)
            flow = dot_nt(tokens[...], wd[here, :])
            gate = kept_ref[:, here].astype(F32)
            up = kept_ref[:, there].astype(F32)
            sig = jax.nn.sigmoid(gate)
            grads[:, here] = (flow * up * sig * (1.0 + gate * (1.0 - sig))).astype(BF)
            grads[:, there] = (flow * gate * sig).astype(BF)

        def step(tile, carry):
            span_step(pl.multiple_of(tile * 256, 128), 256)
            return carry

        lax.fori_loop(0, hidden // 256, step, 0)
        if hidden % 256:
            span_step(hidden // 256 * 256, hidden % 256)
        for copy in second:
            copy.wait()

        def back_step(tile, carry):
            rows = pl.ds(pl.multiple_of(tile * 256, 256), 256)
            halves_out(dot_nt(grads[...], gu[rows, :]), own, other, rows, local)
            return carry

        lax.fori_loop(0, width // 256, back_step, 0)

    return call(
        kernel,
        [
            shape((2 * local, hidden2), BF),
            shape((local, width), F32),
            shape((local, width), BF),
        ],
        [VM] * 3,
        [
            pltpu.VMEM((width, hidden2), BF),
            pltpu.VMEM((hidden, width), BF),
            pltpu.VMEM((2 * local, width), BF),
            pltpu.SemaphoreType.DMA((pieces + more,)),
        ],
        [e_own, e_other, kept, *gu_weight.arrays, *down_weight.arrays],
        [VM] * 3 + [ANY] * (pieces + more),
        2 * 2 * local * width * hidden * 3,
        48,
    )


def norm_back(stream, own, other, gain, grad):
    local, width = stream.shape

    def kernel(x_ref, own_ref, other_ref, gain_ref, grad_ref, out_ref, low_ref, gain_out):
        x = x_ref[...].astype(F32)
        factor = lax.rsqrt(jnp.mean(x * x, axis=1, keepdims=True) + EPSILON)
        flow = own_ref[...] + other_ref[...].astype(F32)
        scaled = flow * gain_ref[...].astype(F32)
        gain_out[...] = jnp.sum(flow * x * factor, axis=0, keepdims=True)
        mean_term = jnp.mean(scaled * x, axis=1, keepdims=True)
        result = (
            grad_ref[...].astype(F32)
            + factor * scaled
            - x * (factor * factor * factor * mean_term)
        )
        out_ref[...] = result
        low_ref[...] = result.astype(BF)

    return call(
        kernel,
        [shape((local, width), F32), shape((local, width), BF), shape((1, width), F32)],
        [VM] * 3,
        [],
        [stream, own, other, gain, grad],
        [VM] * 5,
        12 * local * width,
        24,
    )


def mix_back(f_own, f_other, weight, ctx):
    local, width = f_own.shape
    half = width // 2
    group = half // ctx
    pieces = len(weight.arrays)
    plan = weight.plan

    def kernel(*refs):
        own, other = refs[:2]
        w_refs = refs[2 : 2 + pieces]
        slabs = refs[2 + pieces : 2 + pieces + ctx]
        buffer, tokens, slab, sems, out_sems = refs[2 + pieces + ctx :]
        copies = weight_copies(plan, w_refs, buffer, sems, 0)
        for copy in copies:
            copy.start()
        tokens[:local] = own[...]
        tokens[local:] = other[...]
        for copy in copies:
            copy.wait()
        for tile in range(half // 256):
            flow = dot_nt(tokens[...], buffer[tile * 256 : (tile + 1) * 256, :]).astype(BF)
            for part in range(256 // group):
                slab[tile * 256 // group + part] = flow[
                    :, part * group : (part + 1) * group
                ].reshape(2, local, group)
        z = lax.axis_index("ctx")
        run_copies(
            [
                pltpu.make_async_copy(slab.at[lax.bitwise_xor(z, k)], slabs[k], out_sems.at[k])
                for k in range(ctx)
            ]
        )

    return call(
        kernel,
        [shape((2, local, group), BF)] * ctx,
        [ANY] * ctx,
        [
            pltpu.VMEM((half, width), BF),
            pltpu.VMEM((2 * local, width), BF),
            pltpu.VMEM((ctx, 2, local, group), BF),
            pltpu.SemaphoreType.DMA((pieces,)),
            pltpu.SemaphoreType.DMA((ctx,)),
        ],
        [f_own, f_other, *weight.arrays],
        [VM] * 2 + [ANY] * pieces,
        2 * 2 * local * half * width,
        24,
    )


def attend_back(slabs, grad_slabs, start_row, tables, carried):
    ctx = len(grad_slabs)
    _, local, group = grad_slabs[0].shape
    span = ctx * local
    parts = len(slabs)
    heads = group // HD
    first = carried is not None

    def kernel(*refs):
        starts, cos, low, high = refs[:4]
        at = 4
        carry_in = None
        if first:
            carry_in = refs[at]
            at += 1
        ins = refs[at : at + parts]
        at += parts
        grads = refs[at : at + ctx]
        outs = refs[at + ctx : at + 2 * ctx]
        at += 2 * ctx
        carry_out = None
        if not first:
            carry_out = refs[at]
            at += 1
        whole, flow_in, slab, key_sum, value_sum, sems, out_sems = refs[at:]
        z = lax.axis_index("ctx")
        copies = []
        if parts == 1:
            copies.append(pltpu.make_async_copy(ins[0], whole, sems.at[0]))
        for k in range(ctx):
            to = pl.ds(pl.multiple_of(lax.bitwise_xor(z, k) * local, 16), local)
            if parts > 1:
                copies.append(
                    pltpu.make_async_copy(ins[k], whole.at[:, :, to, :], sems.at[k])
                )
            copies.append(
                pltpu.make_async_copy(grads[k], flow_in.at[:, to, :], sems.at[ctx + k])
            )
        run_copies(copies)
        lane = lax.broadcasted_iota(jnp.int32, (1, group), 1) // HD
        line = lax.broadcasted_iota(jnp.int32, (group, 1), 0) // HD

        def row_step(row, carry):
            key_sum[...] = jnp.zeros_like(key_sum)
            value_sum[...] = jnp.zeros_like(value_sum)
            key_turned = whole[1, row].astype(F32).T.astype(BF)
            for block in range(ctx):
                keys = (block + 1) * local
                here = slice(block * local, keys)
                query = whole[0, row, here, :] * SCORE_SCALE
                grad = flow_in[row, here, :]
                key = whole[1, row, :keys, :]
                value = whole[2, row, :keys, :]
                k_at = lax.broadcasted_iota(jnp.int32, (keys, local), 0)
                q_at = lax.broadcasted_iota(jnp.int32, (keys, local), 1) + block * local
                allowed = (k_at <= q_at) & (k_at >= starts[row, :, here])
                turned = None
                for head in range(heads):
                    mine = lane == head
                    q_head = jnp.where(mine, query, jnp.zeros_like(query))
                    g_head = jnp.where(mine, grad, jnp.zeros_like(grad))
                    scores = jnp.where(allowed, dot_nt(key, q_head), MASK_FILL)
                    top = jnp.max(scores, axis=0, keepdims=True)
                    powers = jnp.exp(scores - top)
                    total = jnp.sum(powers, axis=0, keepdims=True)
                    probs = powers * (1.0 / total)
                    grad_probs = dot_nt(value, g_head)
                    delta = jnp.sum(probs * grad_probs, axis=0, keepdims=True)
                    grad_scores = (probs * (grad_probs - delta)).astype(BF)
                    value_sum[:keys] += dot(probs.astype(BF), g_head)
                    key_sum[:keys] += dot(grad_scores, q_head)
                    part = dot(key_turned[:, :keys], grad_scores)
                    turned = part if turned is None else jnp.where(line == head, part, turned)
                grad_query = turned.T * SCORE_SCALE
                slab[block, 0, row] = rope(
                    grad_query, cos[row, here, :], -low[row, here, :], -high[row, here, :]
                ).astype(BF)
            for block in range(ctx):
                here = slice(block * local, (block + 1) * local)
                slab[block, 1, row] = rope(
                    key_sum[here, :], cos[row, here, :], -low[row, here, :], -high[row, here, :]
                ).astype(BF)
                if first:
                    total_value = value_sum[here, :] + carry_in[row, here, :]
                else:
                    total_value = 0.5 * value_sum[here, :]
                    carry_out[row, here, :] = total_value
                slab[block, 2, row] = total_value.astype(BF)
            return carry

        lax.fori_loop(0, 2, row_step, 0)
        run_copies(
            [
                pltpu.make_async_copy(slab.at[lax.bitwise_xor(z, k)], outs[k], out_sems.at[k])
                for k in range(ctx)
            ]
        )

    args = [start_row, *tables]
    specs = [VM] * 4
    outs = [shape((3, 2, local, group), BF)] * ctx
    out_specs = [ANY] * ctx
    if first:
        args.append(carried)
        specs.append(VM)
    else:
        outs.append(shape((2, span, group), F32))
        out_specs.append(VM)
    got = call(
        kernel,
        outs,
        out_specs,
        [
            pltpu.VMEM((3, 2, span, group), BF),
            pltpu.VMEM((2, span, group), BF),
            pltpu.VMEM((ctx, 3, 2, local, group), BF),
            pltpu.VMEM((span, group), F32),
            pltpu.VMEM((span, group), F32),
            pltpu.SemaphoreType.DMA((2 * ctx,)),
            pltpu.SemaphoreType.DMA((ctx,)),
        ],
        [*args, *slabs, *grad_slabs],
        specs + [ANY] * (parts + ctx),
        2 * 5 * 2 * heads * span * span * 128,
        48,
    )
    return got[:ctx], (None if first else got[ctx])


def project_back(slabs, weight):
    ctx = len(slabs)
    _, _, local, group = slabs[0].shape
    half = ctx * group
    width = 2 * half
    pieces = len(weight.arrays)
    plan = weight.plan

    def kernel(*refs):
        ins = refs[:ctx]
        w_refs = refs[ctx : ctx + pieces]
        own, other, joined, buffer, landed, sems = refs[ctx + pieces :]
        z = lax.axis_index("ctx")
        copies = weight_copies(plan, w_refs, buffer, sems, ctx)
        for k in range(ctx):
            copies.append(
                pltpu.make_async_copy(ins[k], landed.at[lax.bitwise_xor(z, k)], sems.at[k])
            )
        run_copies(copies)
        for k in range(ctx):
            for kind in range(3):
                base = kind * half + k * group
                joined[:, base : base + group] = landed[k, kind].reshape(2 * local, group)

        def step(tile, carry):
            rows = pl.ds(pl.multiple_of(tile * 256, 256), 256)
            halves_out(dot_nt(joined[...], buffer[rows, :]), own, other, rows, local)
            return carry

        lax.fori_loop(0, width // 256, step, 0)

    return call(
        kernel,
        [
            shape((local, width), F32),
            shape((local, width), BF),
            shape((2 * local, 3 * half), BF),
        ],
        [VM] * 3,
        [
            pltpu.VMEM((width, 3 * half), BF),
            pltpu.VMEM((ctx, 3, 2, local, group), BF),
            pltpu.SemaphoreType.DMA((ctx + pieces,)),
        ],
        [*slabs, *weight.arrays],
        [ANY] * (ctx + pieces),
        2 * 2 * local * 3 * half * width,
        40,
    )


def weight_grad(left, right, chips):
    lefts, rights = list(left), list(right)
    tall = lefts[0].shape[1]
    wide = rights[0].shape[1]
    tokens = lefts[0].shape[0] * len(lefts)
    rows = tall // chips
    halved = wide // 2
    split = chips == 4

    def kernel(*refs):
        l_refs = refs[: len(lefts)]
        r_refs = refs[len(lefts) : len(lefts) + len(rights)]
        at = len(lefts) + len(rights)
        count = 4 if split else chips
        outs = refs[at : at + count]
        grads, l_buf, r_buf, sems = refs[at + count :]
        if len(lefts) == 2:
            l_buf[: tokens // 2] = l_refs[0][...]
            l_buf[tokens // 2 :] = l_refs[1][...]
            l_now = l_buf
        else:
            l_now = l_refs[0]
        if len(rights) == 2:
            r_buf[: tokens // 2] = r_refs[0][...]
            r_buf[tokens // 2 :] = r_refs[1][...]
            r_now = r_buf
        else:
            r_now = r_refs[0]

        def tile_step(base, size):
            turned = l_now[:, pl.ds(base, size)]
            for start in range(0, wide, 512):
                stop = min(start + 512, wide)
                grads[pl.ds(base, size), start:stop] = dot_tn(
                    turned, r_now[:, start:stop]
                ).astype(BF)

        def step(tile, carry):
            tile_step(pl.multiple_of(tile * 256, 256), 256)
            return carry

        lax.fori_loop(0, tall // 256, step, 0)
        if tall % 256:
            tile_step(tall // 256 * 256, tall % 256)
        chip = chip_index()

        def block(k):
            return pl.ds(pl.multiple_of(lax.bitwise_xor(chip, k) * rows, 16), rows)

        copies = []
        if split:
            for which, order in enumerate(((1, 3), (0, 2), (2, 3), (0, 1))):
                columns = pl.ds((which // 2) * halved, halved)
                for slot, k in enumerate(order):
                    copies.append(
                        pltpu.make_async_copy(
                            grads.at[block(k), columns],
                            outs[which].at[slot],
                            sems.at[2 * which + slot],
                        )
                    )
        else:
            for k in range(chips):
                copies.append(
                    pltpu.make_async_copy(grads.at[block(k), :], outs[k], sems.at[k])
                )
        run_copies(copies)

    if split:
        outs = [shape((2, rows, halved), BF)] * 4
    else:
        outs = [shape((rows, wide), BF)] * chips
    small = (16, 128)
    return call(
        kernel,
        outs,
        [ANY] * len(outs),
        [
            pltpu.VMEM((tall, wide), BF),
            pltpu.VMEM((tokens, tall) if len(lefts) == 2 else small, BF),
            pltpu.VMEM((tokens, wide) if len(rights) == 2 else small, BF),
            pltpu.SemaphoreType.DMA((8 if split else chips,)),
        ],
        [*lefts, *rights],
        [VM] * (len(lefts) + len(rights)),
        2 * tokens * tall * wide,
        48,
    )


FORE_ORDER = (
    ("B", "q", 0), ("stg0", 0), ("n1", 0), ("tab", 0), ("F", "q", 0),
    ("B", "o", 0), ("R", "q", 0), ("B", "g", 0), ("prj", 0), ("stg1", 0),
    ("F", "o", 0), ("qss", 0), ("att", 0, 0), ("F", "g", 0), ("B", "d", 0),
    ("att", 0, 1), ("B", "q", 1), ("R", "g", 0), ("out", 0), ("F", "d", 0),
    ("nrm", 0), ("gu", 0), ("F", "q", 1), ("B", "o", 1), ("R", "d", 0),
    ("dn", 0), ("R", "q", 1), ("end", 0), ("B", "g", 1), ("prj", 1),
    ("F", "o", 1), ("qss", 1), ("att", 1, 0), ("F", "g", 1), ("B", "d", 1),
    ("att", 1, 1), ("R", "g", 1), ("out", 1), ("F", "d", 1), ("nrm", 1),
    ("R", "d", 1), ("gu", 1), ("dn", 1), ("end", 1),
)
AIDED = (("q", 0), ("g", 0), ("d", 0), ("q", 1), ("g", 1), ("d", 1),)


class Link:
    def __init__(self, source, target, arriving, sems, slot, axis, bit):
        device = {axis: lax.bitwise_xor(lax.axis_index(axis), bit)}

        def make(to):
            return pltpu.make_async_remote_copy(
                src_ref=source,
                dst_ref=to,
                send_sem=sems.at[0, slot],
                recv_sem=sems.at[1, slot],
                device_id=device,
                device_id_type=pl.DeviceIdType.MESH,
            )

        self.out = make(target)
        self.into = make(arriving)
        self.flying = False

    def start(self):
        self.out.start()
        self.flying = True
        return self

    def arrived(self):
        self.into.wait_recv()

    def sent(self):
        if self.flying:
            self.out.wait_send()
        self.flying = False


def enter(fsdp_bits, ctx_bits):
    barrier = pltpu.get_barrier_semaphore()
    for axis, bits in (("fsdp", fsdp_bits), ("ctx", ctx_bits)):
        for bit in bits:
            pl.semaphore_signal(
                barrier,
                inc=1,
                device_id={axis: lax.bitwise_xor(lax.axis_index(axis), bit)},
                device_id_type=pl.DeviceIdType.MESH,
            )
    pl.semaphore_wait(barrier, len(fsdp_bits) + len(ctx_bits))


def turn(x, cosines, sines, direction):
    width, pairs = x.shape[-1], HD // 2
    lane = lax.broadcasted_iota(jnp.int32, (1, width), 1)
    ahead = pltpu.roll(x, width - pairs, 1)
    behind = pltpu.roll(x, pairs, 1)
    other = jnp.where(lax.rem(lane, HD) < pairs, -ahead, behind)
    return x * cosines + other * (sines if direction > 0 else -sines)


def rms(total, gain):
    factor = lax.rsqrt(jnp.mean(total * total, axis=1, keepdims=True) + EPSILON)
    return (total * factor * gain).astype(BF)


def forward_pass(tokens, doc_lengths, gains, w_qkv, w_out, w_gate, w_up, w_down):
    local, width = tokens.shape
    layers, block, _ = w_qkv.shape
    hidden = w_gate.shape[2]
    hid = hidden // 2
    hid_block = w_down.shape[1]
    half = width // 2
    shards, ctx = lax.axis_size("fsdp"), lax.axis_size("ctx")
    chips = shards // 2
    group = half // ctx
    span = ctx * local
    heads = group // HD
    both = 2 * local
    documents = doc_lengths.shape[1]
    def kernel(*refs):
        (tok, lens, gain_in, qkv_in, out_in, gate_in, up_in, down_in) = refs[:8]
        (wq_o, wo_o, wg_o, wd_o, n1_o, n2_o, whole_o, mix_o, mid_o, stream_o) = refs[8:18]
        (act_o, kept_o, gain_o, cos_o, sin_o, start_o, final_o) = refs[18:25]
        (wq, wo, wg, wd, qkv_raw, gu_raw, q_stage, g_stage) = refs[25:33]
        (n1, n2, whole, slab, mixed, landed, value, mix, mid, stream) = refs[33:43]
        (act, kept, part, other, got, gbuf, lens_all, cos, sin, start) = refs[43:53]
        (sems, local_sems, save_sems) = refs[53:]
        f = lax.axis_index("fsdp")
        z = lax.axis_index("ctx")
        core = lax.rem(f, 2)
        chip = f // 2
        flights = []
        saves = []

        def link(source, target, arriving, axis, bit):
            made = Link(source, target, arriving, sems, len(flights), axis, bit)
            flights.append(made)
            return made

        def save(source, target):
            copy = pltpu.make_async_copy(source, target, save_sems.at[len(saves)])
            copy.start()
            saves.append(copy)
            return len(saves) - 1

        def saved(number):
            if saves[number] is not None:
                saves[number].wait()
            saves[number] = None

        def rows(index, count):
            return pl.ds(pl.multiple_of(index * count, 16), count)

        def fx(bit):
            return lax.bitwise_xor(f, bit)

        def cx(bit):
            return lax.bitwise_xor(chip, bit)

        odd = lax.rem(z, 2)

        def spread_far(weight, at, passed_on, far, columns, aided):
            weight.third = []
            if not aided:
                weight.second = [
                    link(at(one), at(one), at(to), "fsdp", bit)
                    for one, to, bit in zip(passed_on, far, (4, 2))
                ]
                return
            some = pl.ds(pl.multiple_of(odd * (columns // 2), 128), columns // 2)
            rest = pl.ds(pl.multiple_of((1 - odd) * (columns // 2), 128), columns // 2)
            weight.second = []
            for one, to, bit in zip(passed_on, far, (4, 2)):
                source = at(one).at[:, some]
                weight.second.append(link(source, source, at(to).at[:, some], "fsdp", bit))
                mine = at(to).at[:, some]
                weight.third.append(link(mine, mine, at(to).at[:, rest], "ctx", 1))

        class Halved:
            def __init__(self, buffer, stage, aided):
                def at(index):
                    return buffer.at[rows(index, block), :]

                self.first = [
                    link(stage, at(f), at(fx(bit)), "fsdp", bit) for bit in (1, 3, 5)
                ] + [link(at(f), at(f), at(fx(bit)), "fsdp", bit) for bit in (2, 4)]
                far = 2 * cx(3)
                spread_far(self, at, (2 * cx(1), 2 * cx(2) + 1), (far, far + 1), buffer.shape[1], aided)

        class Rowed:
            def __init__(self, buffer, source, count, aided):
                small = count // 2

                def at(index):
                    return buffer.at[rows(index, count), :]

                def side(index, which):
                    begin = pl.multiple_of(index * count + which * small, 16)
                    return buffer.at[pl.ds(begin, small), :]

                self.first = [
                    link(source, at(chip), at(cx(bit // 2)), "fsdp", bit) for bit in (2, 4)
                ]
                far = cx(3)
                spread_far(
                    self,
                    lambda spot: side(*spot),
                    ((cx(1), 0), (cx(2), 1)),
                    ((far, 0), (far, 1)),
                    buffer.shape[1],
                    aided,
                )

        def begin(weight):
            for one in weight.first:
                one.start()

        def forward(weight):
            for one in weight.first:
                one.arrived()
            for one in weight.second:
                one.start()

        def relay(weight):
            for one in weight.second:
                one.arrived()
            for one in weight.third:
                one.start()

        def finish(weight):
            for one in weight.third or weight.second:
                one.arrived()

        def aided(name, n):
            return (name, n) in AIDED

        weights = {}
        for n in range(layers):
            weights["q", n] = Halved(wq.at[n], q_stage.at[n], aided("q", n))
            weights["g", n] = Halved(wg.at[n], g_stage.at[n], aided("g", n))
            weights["o", n] = Rowed(wo.at[n], out_in.at[n], block, aided("o", n))
            weights["d", n] = Rowed(wd.at[n], down_in.at[n], hid_block, aided("d", n))

        def local_copy(source, target, slot):
            copy = pltpu.make_async_copy(source, target, local_sems.at[slot])
            copy.start()
            return copy

        def choose(first, second):
            return lax.select(core == 0, first, second)

        def stage_qkv(n):
            for kind in range(3):
                for j in range(chips):
                    at = kind * width + 2 * j * block
                    even = qkv_raw[:, at : at + block]
                    odd = qkv_raw[:, at + block : at + 2 * block]
                    to = kind * half + j * block
                    wq[n, rows(f, block), to : to + block] = choose(even, odd)
                    q_stage[n, :, to : to + block] = choose(odd, even)

        def stage_gu(n):
            for which in range(2):
                sets = []
                for lane_core in range(2):
                    parts = []
                    for j in range(chips):
                        at = (2 * j + lane_core) * hid_block
                        parts.append(gu_raw[which, :, at : at + hid_block])
                    sets.append(jnp.concatenate(parts, axis=1))
                to = slice(which * hid, (which + 1) * hid)
                wg[n, rows(f, block), to] = choose(sets[0], sets[1])
                g_stage[n, :, to] = choose(sets[1], sets[0])

        def load(n):
            return [
                local_copy(qkv_in.at[n], qkv_raw, 0),
                local_copy(gate_in.at[n], gu_raw.at[0], 1),
                local_copy(up_in.at[n], gu_raw.at[1], 2),
            ]

        loads = load(0)
        mine = []
        for n in range(layers):
            mine.append(local_copy(out_in.at[n], wo.at[n, rows(chip, block), :], 3 + n))
            mine.append(
                local_copy(down_in.at[n], wd.at[n, rows(chip, hid_block), :], 3 + layers + n)
            )
        spare = 3 + 2 * layers
        loads[0].wait()
        stage_qkv(0)
        gbuf[f] = jnp.concatenate(
            [gain_in[n].astype(F32) for n in range(layers)]
            + [jnp.zeros((8 - 2 * layers, block), F32)]
        )
        lens_all[0] = jnp.concatenate(
            [jnp.broadcast_to(lens[0:1, n : n + 1], (1, 128)) for n in range(documents)]
            + [jnp.zeros((8 - documents, 128), jnp.int32)]
        )
        gain_links = [
            link(gbuf.at[f], gbuf.at[f], gbuf.at[fx(bit)], "fsdp", bit) for bit in range(1, shards)
        ]
        lens_link = link(lens_all.at[0], lens_all.at[1], lens_all.at[1], "fsdp", 1)
        enter(list(range(1, shards)), list(range(1, ctx)))
        for one in gain_links:
            one.start()
        lens_link.start()
        state = {"loads": loads, "mine": mine, "slab": [[], []], "mix": [[], []], "held": []}

        def op_stg0(n):
            for copy in state["loads"][1:]:
                copy.wait()
            stage_gu(0)
            state["loads"] = load(1)

        def op_stg1(n):
            for copy in state["loads"]:
                copy.wait()
            stage_qkv(1)
            stage_gu(1)

        def gain_row(n):
            return jnp.concatenate([gbuf[s, n : n + 1, :] for s in range(shards)], axis=1)

        def norm_link(buffer, n):
            upper = buffer.at[n, pl.ds(local, local), :]
            return link(buffer.at[n, pl.ds(0, local), :], upper, upper, "fsdp", 1)

        def op_n1(n):
            for one in gain_links:
                one.arrived()
            for row in range(2 * layers):
                gain_o[row : row + 1, :] = gain_row(row)
            n1[0, :local] = rms(tok[...].astype(F32), gain_row(0))
            state["norm"] = norm_link(n1, 0).start()

        pairs = HD // 2
        lane = lax.broadcasted_iota(jnp.int32, (1, 128), 1)
        frequency = jnp.exp((-math.log(10000.0) / pairs) * lax.rem(lane, pairs).astype(F32))

        def table_step(index, carry):
            r = index // ctx
            piece = lax.rem(index, ctx)
            to = rows(piece, local)
            at = lax.broadcasted_iota(jnp.int32, (local, 128), 0) + piece * local
            first = jnp.zeros((local, 128), jnp.int32)
            end = jnp.zeros((1, 128), jnp.int32)
            for j in range(documents):
                end = end + lens_all[r, j : j + 1, :]
                first = jnp.where(at >= end, end, first)
            start[r, to, :] = first
            angle = (at - first).astype(F32) * frequency
            sin[r, to, :] = jnp.sin(angle)
            cos[r, to, :] = jnp.cos(angle)
            return carry

        def op_tab(n):
            lens_link.arrived()
            lax.fori_loop(0, 2 * ctx, table_step, 0)
            for source, target in ((cos, cos_o), (sin, sin_o), (lens_all, start_o)):
                save(source, target)

        here_rows = rows(z, local)
        lane_head = lax.broadcasted_iota(jnp.int32, (1, group), 1) // HD

        def do_project(n):
            for tile in range(3 * half // 256):
                acc = dot(n1[n], wq[n, :, tile * 256 : (tile + 1) * 256])
                kind = tile * 256 // half
                for sub in range(256 // group):
                    column = tile * 256 - kind * half + sub * group
                    for r in range(2):
                        x = acc[r * local : (r + 1) * local, sub * group : (sub + 1) * group]
                        at = (slice(r * local, (r + 1) * local), slice(column, column + group))
                        if kind < 2:
                            x = turn(x, cos[r, here_rows, :], sin[r, here_rows, :], 1)
                        elif n > 0:
                            x = 0.5 * x + 0.5 * value[at].astype(F32)
                        x = x.astype(BF)
                        if kind == 2 and n == 0:
                            value[at] = x
                        slab[column // group, kind, r] = x

        def slab_links(n, r):
            made = []
            for bit in range(1, ctx):
                to = lax.bitwise_xor(z, bit)
                made.append(
                    link(
                        slab.at[to, :, r],
                        whole.at[n, :, r, rows(z, local), :],
                        whole.at[n, :, r, rows(to, local), :],
                        "ctx",
                        bit,
                    )
                )
            return made

        def mixed_links(n, r):
            made = []
            for bit in range(1, ctx):
                to = lax.bitwise_xor(z, bit)
                made.append(
                    link(mixed.at[n, to, r], landed.at[n, z, r], landed.at[n, to, r], "ctx", bit)
                )
            return made

        def do_attend(n, r):
            if True:
                for piece in range(ctx):
                    keys = (piece + 1) * local
                    here = slice(piece * local, keys)
                    query = whole[n, 0, r, here, :] * SCORE_SCALE
                    key = whole[n, 1, r, :keys, :]
                    val = whole[n, 2, r, :keys, :]
                    k_at = lax.broadcasted_iota(jnp.int32, (local, keys), 1)
                    q_at = lax.broadcasted_iota(jnp.int32, (local, keys), 0) + piece * local
                    allowed = (k_at <= q_at) & (k_at >= start[r, here, 0:1])
                    result = None
                    for head in range(heads):
                        q_head = jnp.where(lane_head == head, query, jnp.zeros_like(query))
                        scores = jnp.where(allowed, dot_nt(q_head, key), MASK_FILL)
                        top = jnp.max(scores, axis=1, keepdims=True)
                        powers = jnp.exp(scores - top)
                        total = jnp.sum(powers, axis=1, keepdims=True)
                        probs = (powers * (1.0 / total)).astype(BF)
                        out = dot(probs, val)
                        result = out if head == 0 else jnp.where(lane_head == head, out, result)
                    mixed[n, piece, r] = result.astype(BF)

        last_sum = [None]

        def partial_sums(n, which, left, weight):
            if last_sum[0] is not None:
                last_sum[0].sent()

            def step(tile, carry):
                columns = rows(tile, 256)
                product = dot(left[...], weight[:, columns])
                part[:, columns] = product[:local]
                other[:, columns] = product[local:].astype(BF)
                return carry

            lax.fori_loop(0, width // 256, step, 0)
            to = got.at[n, which]
            last_sum[0] = link(other, to, to, "fsdp", 1).start()
            return last_sum[0]

        def gate_up(n):
            def span_step(base, count):
                here, there = pl.ds(base, count), pl.ds(hid + base, count)
                gate = dot(n2[n], wg[n, :, here])
                up = dot(n2[n], wg[n, :, there])
                kept[:, here] = gate.astype(BF)
                kept[:, there] = up.astype(BF)
                act[:, here] = (gate * jax.nn.sigmoid(gate) * up).astype(BF)

            def step(tile, carry):
                span_step(pl.multiple_of(tile * 256, 128), 256)
                return carry

            lax.fori_loop(0, hid // 256, step, 0)
            if hid % 256:
                span_step(hid // 256 * 256, hid % 256)

        def op_prj(n):
            finish(weights["q", n])
            save(wq.at[n], wq_o.at[n])
            state["norm"].arrived()
            save(n1.at[n], n1_o.at[n])
            for one in state["slab"][0] + state["slab"][1]:
                one.sent()
            do_project(n)
            state["slab"] = [slab_links(n, 0), slab_links(n, 1)]
            for one in state["slab"][0]:
                one.start()
            state["own"] = local_copy(slab.at[z], whole.at[n, :, :, here_rows, :], spare)

        def op_qss(n):
            for one in state["slab"][0]:
                one.arrived()
            for one in state["slab"][1]:
                one.start()

        def op_att(n, r):
            if r:
                for one in state["slab"][1]:
                    one.arrived()
                save(whole.at[n], whole_o.at[n])
            else:
                state["own"].wait()
            do_attend(n, r)
            state["mix"][r] = mixed_links(n, r)
            for one in state["mix"][r]:
                one.start()
            if r:
                state["own"] = local_copy(mixed.at[n, z], landed.at[n, z], spare)

        def op_out(n):
            finish(weights["o", n])
            for copy in state["mine"]:
                copy.wait()
            state["mine"] = []
            save(wo.at[n], wo_o.at[n])
            state["own"].wait()
            for one in state["mix"][0] + state["mix"][1]:
                one.arrived()
            for k in range(ctx):
                mix[n, :, k * group : (k + 1) * group] = landed[n, k].reshape(both, group)
            save(mix.at[n], mix_o.at[n])
            state["sums"] = partial_sums(n, 0, mix.at[n], wo.at[n])

        def op_nrm(n):
            base = tok[...].astype(F32) if n == 0 else stream[...]
            state["sums"].arrived()
            total = base + part[...] + got[n, 0].astype(F32)
            mid[n] = total
            n2[n, :local] = rms(total, gain_row(2 * n + 1))
            state["norm"] = norm_link(n2, n).start()
            save(mid.at[n], mid_o.at[n])

        def op_gu(n):
            finish(weights["g", n])
            save(wg.at[n], wg_o.at[n])
            for number in state["held"]:
                saved(number)
            state["norm"].arrived()
            save(n2.at[n], n2_o.at[n])
            gate_up(n)
            state["held"] = [save(act, act_o.at[n]), save(kept, kept_o.at[n])]

        def op_dn(n):
            finish(weights["d", n])
            save(wd.at[n], wd_o.at[n])
            state["sums"] = partial_sums(n, 1, act, wd.at[n])

        def op_end(n):
            state["sums"].arrived()
            total = mid[n] + part[...] + got[n, 1].astype(F32)
            if n + 1 < layers:
                stream[...] = total
                n1[n + 1, :local] = rms(total, gain_row(2 * n + 2))
                state["norm"] = norm_link(n1, n + 1).start()
                save(stream, stream_o)
            else:
                final_o[...] = total.astype(BF)

        chain = {
            "stg0": op_stg0, "stg1": op_stg1, "n1": op_n1, "tab": op_tab, "prj": op_prj,
            "qss": op_qss, "att": op_att, "out": op_out, "nrm": op_nrm, "gu": op_gu,
            "dn": op_dn, "end": op_end,
        }
        moves = {"B": begin, "F": forward, "R": relay}
        for step in FORE_ORDER:
            if step[0] in chain:
                chain[step[0]](*step[1:])
            else:
                moves[step[0]](weights[step[1], step[2]])
        for one in flights:
            one.sent()
        for number in range(len(saves)):
            saved(number)

    def stacked(*dims):
        return (layers, *dims)

    outs = [
        shape(stacked(width, 3 * half), BF),
        shape(stacked(half, width), BF),
        shape(stacked(width, 2 * hid), BF),
        shape(stacked(hid, width), BF),
        shape(stacked(both, width), BF),
        shape(stacked(both, width), BF),
        shape(stacked(3, 2, span, group), BF),
        shape(stacked(both, half), BF),
        shape(stacked(local, width), F32),
        shape((local, width), F32),
        shape(stacked(both, hid), BF),
        shape(stacked(both, 2 * hid), BF),
        shape((2 * layers, width), F32),
        shape((2, span, 128), F32),
        shape((2, span, 128), F32),
        shape((2, 8, 128), jnp.int32),
        shape((local, width), BF),
    ]
    out_specs = [ANY] * 17
    out_specs[12] = out_specs[16] = VM
    scratch = [
        pltpu.VMEM(stacked(width, 3 * half), BF),
        pltpu.VMEM(stacked(half, width), BF),
        pltpu.VMEM(stacked(width, 2 * hid), BF),
        pltpu.VMEM(stacked(hid, width), BF),
        pltpu.VMEM((block, 3 * width), BF),
        pltpu.VMEM((2, block, hidden), BF),
        pltpu.VMEM(stacked(block, 3 * half), BF),
        pltpu.VMEM(stacked(block, 2 * hid), BF),
        pltpu.VMEM(stacked(both, width), BF),
        pltpu.VMEM(stacked(both, width), BF),
        pltpu.VMEM(stacked(3, 2, span, group), BF),
        pltpu.VMEM((ctx, 3, 2, local, group), BF),
        pltpu.VMEM(stacked(ctx, 2, local, group), BF),
        pltpu.VMEM(stacked(ctx, 2, local, group), BF),
        pltpu.VMEM((both, half), BF),
        pltpu.VMEM(stacked(both, half), BF),
        pltpu.VMEM(stacked(local, width), F32),
        pltpu.VMEM((local, width), F32),
        pltpu.VMEM((both, hid), BF),
        pltpu.VMEM((both, 2 * hid), BF),
        pltpu.VMEM((local, width), F32),
        pltpu.VMEM((local, width), BF),
        pltpu.VMEM(stacked(2, local, width), BF),
        pltpu.VMEM((shards, 8, block), F32),
        pltpu.VMEM((2, 8, 128), jnp.int32),
        pltpu.VMEM((2, span, 128), F32),
        pltpu.VMEM((2, span, 128), F32),
        pltpu.VMEM((2, span, 128), jnp.int32),
        pltpu.SemaphoreType.DMA((2, 112)),
        pltpu.SemaphoreType.DMA((8,)),
        pltpu.SemaphoreType.DMA((32,)),
    ]
    return pl.pallas_call(
        kernel,
        out_shape=outs,
        in_specs=[VM] * 3 + [ANY] * 5,
        out_specs=out_specs,
        scratch_shapes=scratch,
        compiler_params=pltpu.CompilerParams(
            vmem_limit_bytes=62 * MIB, collective_id=0, has_side_effects=True
        ),
        cost_estimate=pl.CostEstimate(
            flops=14 * 10**9, bytes_accessed=60 * MIB, transcendentals=0
        ),
    )(tokens, doc_lengths, gains, w_qkv, w_out, w_gate, w_up, w_down)


BACK_ORDER = (
    ("dW", 1), ("mlp", 1), ("F", "d", 1, 0), ("nrm2", 1), ("F", "d", 1, 1),
    ("mixb", 1), ("gW", 1), ("oW", 1), ("T", "o", 1), ("dos", 1),
    ("att", 1, 0), ("S", "d", 1, 0), ("att", 1, 1), ("T", "gb", 1), ("S", "d", 1, 1),
    ("F", "o", 1, 0), ("F", "o", 1, 1), ("F", "ga", 1, 0), ("F", "ga", 1, 1), ("F", "gb", 1, 0),
    ("F", "gb", 1, 1), ("pb", 1), ("qW", 1), ("nrm1", 1), ("I", "d", 1, 0),
    ("I", "d", 1, 1), ("S", "o", 1, 0), ("S", "o", 1, 1), ("S", "ga", 1, 0), ("S", "ga", 1, 1),
    ("dW", 0), ("T", "d", 0), ("mlp", 0), ("I", "o", 1, 0), ("X", "d", 1, 0),
    ("nrm2", 0), ("X", "d", 1, 1), ("I", "o", 1, 1), ("mixb", 0), ("X", "o", 1, 0),
    ("I", "ga", 1, 0), ("I", "ga", 1, 1), ("F", "q", 1, 0), ("F", "q", 1, 1), ("X", "o", 1, 1),
    ("F", "d", 0, 0), ("F", "d", 0, 1), ("S", "gb", 1, 0), ("S", "gb", 1, 1), ("dos", 0),
    ("att", 0, 0), ("gW", 0), ("O", "d", 1, 0), ("O", "o", 1, 0), ("oW", 0),
    ("T", "o", 0), ("O", "o", 1, 1), ("att", 0, 1), ("W", "o", 1), ("O", "d", 1, 1),
    ("X", "ga", 1, 0), ("X", "ga", 1, 1), ("W", "d", 1), ("S", "q", 1, 0), ("F", "o", 0, 0),
    ("F", "o", 0, 1), ("S", "q", 1, 1), ("I", "gb", 1, 0), ("F", "ga", 0, 0), ("F", "ga", 0, 1),
    ("I", "gb", 1, 1), ("F", "gb", 0, 0), ("pb", 0), ("qW", 0), ("T", "q", 0),
    ("nrm1", 0), ("G1", 0), ("S", "d", 0, 0), ("S", "d", 0, 1), ("I", "q", 1, 0),
    ("I", "q", 1, 1), ("X", "gb", 1, 0), ("G2", 0), ("X", "gb", 1, 1), ("O", "ga", 1, 0),
    ("O", "ga", 1, 1), ("F", "gb", 0, 1), ("S", "o", 0, 0), ("W", "ga", 1), ("S", "ga", 0, 0),
    ("S", "o", 0, 1), ("S", "ga", 0, 1), ("I", "d", 0, 0), ("X", "q", 1, 0), ("X", "q", 1, 1),
    ("O", "gb", 1, 0), ("O", "gb", 1, 1), ("I", "d", 0, 1), ("I", "o", 0, 0), ("F", "q", 0, 0),
    ("F", "q", 0, 1), ("I", "o", 0, 1), ("W", "gb", 1), ("X", "d", 0, 0), ("S", "gb", 0, 0),
    ("S", "gb", 0, 1), ("X", "o", 0, 0), ("I", "ga", 0, 0), ("X", "o", 0, 1), ("I", "ga", 0, 1),
    ("O", "q", 1, 0), ("X", "d", 0, 1), ("O", "q", 1, 1), ("W", "q", 1), ("S", "q", 0, 0),
    ("S", "q", 0, 1), ("O", "o", 0, 0), ("O", "o", 0, 1), ("I", "gb", 0, 0), ("I", "gb", 0, 1),
    ("X", "ga", 0, 0), ("O", "d", 0, 0), ("X", "ga", 0, 1), ("W", "o", 0), ("O", "d", 0, 1),
    ("W", "d", 0), ("I", "q", 0, 0), ("I", "q", 0, 1), ("X", "gb", 0, 0), ("X", "gb", 0, 1),
    ("O", "ga", 0, 0), ("O", "ga", 0, 1), ("W", "ga", 0), ("X", "q", 0, 0), ("X", "q", 0, 1),
    ("O", "gb", 0, 0), ("O", "gb", 0, 1), ("W", "gb", 0), ("O", "q", 0, 0), ("O", "q", 0, 1),
    ("W", "q", 0), ("G3", 0),
)
HELD = (("o", 1), ("gb", 1), ("d", 0), ("o", 0), ("q", 0),)
DEFER = True


def backward_pass(saved, tokens, cotangent):
    local, width = tokens.shape
    wq_s, wo_s, wg_s, wd_s = saved[:4]
    layers = wq_s.shape[0]
    half = width // 2
    hid = wd_s.shape[1]
    shards, ctx = lax.axis_size("fsdp"), lax.axis_size("ctx")
    chips = shards // 2
    block = width // shards
    hid_block = hid // chips
    group = half // ctx
    span = ctx * local
    heads = group // HD
    both = 2 * local
    documents = 4
    sizes = {
        "d": (hid_block, width),
        "g": (2 * block, 2 * hid),
        "o": (block, width),
        "q": (2 * block, 3 * half),
    }
    names = ("d", "g", "o", "q")
    pieces_of = {"d": ("d",), "g": ("ga", "gb"), "o": ("o",), "q": ("q",)}
    units = [unit for name in names for unit in pieces_of[name]]
    counts = {unit: sizes[unit[0]][0] // len(pieces_of[unit[0]]) for unit in units}

    def kernel(*refs):
        refs = list(refs)

        def take(count):
            out = refs[:count]
            del refs[:count]
            return out

        cot_i, tok_i, lens, gain = take(4)
        wq_i, wo_i, wg_i, wd_i, n1_i, n2_i, whole_i, mix_i, mid_i, stream_i = take(10)
        act_i, kept_i, cos_i, sin_i = take(4)
        grad_o, gain_o, q_o, o_o, gate_o, up_o, d_o = take(7)
        lands = {}
        for unit in units:
            lands[unit] = dict(zip(("x1", "y1", "x2", "y2", "z"), take(5)))
        swap_land = dict(zip(("g", "q"), take(2)))
        wq, wo, wg, wd, act, kept, norm, whole, mix, wide = take(10)
        flow, fgrad, got, do_in, dq_in, part, other, grad, middle = take(9)
        do_out, dq_out, key_sum, value_sum, carry, joined, cos, sin = take(8)
        blocks = dict(zip(names, take(4)))
        finals = dict(zip(names, take(4)))
        tmp, stage, gain_rows, gain_send, gain_land, gain_sum, gain_line = take(7)
        sems, load_sems, tmp_sems, out_sems, own_sems = take(5)
        f = lax.axis_index("fsdp")
        z = lax.axis_index("ctx")
        core = lax.rem(f, 2)
        chip = f // 2
        inner = (z == 1) | (z == 2)
        outer = (z == 0) | (z == 3)
        flights = []

        def link(source, target, arriving, axis, bit):
            made = Link(source, target, arriving, sems, len(flights), axis, bit)
            flights.append(made)
            return made

        def rows(index, count):
            return pl.ds(pl.multiple_of(index * count, 16), count)

        def cx(bit):
            return lax.bitwise_xor(chip, bit)

        loading = {}
        slots = {}

        def load(name, source, target):
            slot = slots.setdefault(name, len(slots))
            copy = pltpu.make_async_copy(source, target, load_sems.at[slot])
            copy.start()
            loading[name] = copy

        def loaded(*wanted):
            for name in wanted:
                if name in loading:
                    loading.pop(name).wait()

        top = layers - 1
        load("cot", cot_i, flow.at[pl.ds(0, local), :])
        load("act", act_i.at[top], act)
        load("wd", wd_i.at[top], wd)
        load("kept", kept_i.at[top], kept)
        load("wg", wg_i.at[top], wg)
        load("wide", mid_i.at[top], wide)
        load("wo", wo_i.at[top], wo)
        load("norm", n2_i.at[top], norm)
        load("mix", mix_i.at[top], mix)
        load("whole", whole_i.at[top], whole)
        load("wq", wq_i.at[top], wq)
        load("cos", cos_i, cos)
        load("sin", sin_i, sin)
        enter(list(range(1, shards)), list(range(1, ctx)))

        def pair_link(buffer):
            upper = buffer.at[pl.ds(local, local), :]
            return link(buffer.at[pl.ds(0, local), :], upper, upper, "fsdp", 1)

        loaded("cot")
        e_link = pair_link(flow).start()
        grad[...] = flow[:local].astype(F32)

        class Reduce:
            def __init__(self, unit, n):
                name = unit[0]
                self.name, self.n = name, n
                whole_rows, self.columns = sizes[name]
                self.count = counts[unit]
                self.chunk = pieces_of[name].index(unit) if len(pieces_of[name]) > 1 else None
                self.offset = self.count * (self.chunk or 0)
                self.side = self.columns // 2
                self.blocks, self.final = blocks[name], finals[name]
                self.land = lands[unit]
                left, right = pl.ds(0, self.side), pl.ds(self.side, self.side)
                self.halves = (left, right)

                def row(k):
                    return cx(k) * whole_rows + self.offset

                self.row = row

                def piece(k, columns):
                    at = pl.ds(pl.multiple_of(row(k), 16), self.count)
                    return self.blocks.at[at, columns]

                def into(where, slot=None):
                    ref = self.land[where]
                    return ref.at[n] if slot is None else ref.at[n, slot]

                def hop(source, target, bit):
                    return link(source, target, target, "fsdp", bit)

                self.far = (hop(piece(3, left), into("x1", 1), 2), hop(piece(3, right), into("y1", 1), 4))
                self.near = (hop(piece(1, left), into("x1", 0), 2), hop(piece(2, right), into("y1", 0), 4))
                self.next = (hop(piece(2, left), into("y2"), 4), hop(piece(1, right), into("x2"), 2))
                self.line = []
                for side in self.halves:
                    steps = []
                    source = self.final.at[pl.ds(self.offset, self.count), side]
                    for step, bit in ((0, 1), (1, 3), (2, 1)):
                        target = self.land["z"].at[n, step, :, side]
                        steps.append(link(source, target, target, "ctx", bit))
                    self.line.append(steps)
                self.swap = None
                if name in swap_land:
                    out = rows(1 - core, block)
                    to = swap_land[name].at[n]
                    self.swap = link(self.final.at[out, :], to, to, "fsdp", 1)
                self.complete = 0
                self.held = (unit, n) in HELD

            def fetch(self, *sources):
                copies = []
                for slot, source in enumerate(sources):
                    copy = pltpu.make_async_copy(
                        source,
                        tmp.at[slot, pl.ds(0, self.count), pl.ds(0, self.side)],
                        tmp_sems.at[slot],
                    )
                    copy.start()
                    copies.append(copy)
                for copy in copies:
                    copy.wait()

            def add(self, source, source_row, columns, target, target_row, slots_used):
                def step(tile, carry):
                    at = pl.ds(pl.multiple_of(source_row + tile * 32, 16), 32)
                    total = source[at, columns].astype(F32)
                    here = pl.ds(pl.multiple_of(tile * 32, 16), 32)
                    for slot in slots_used:
                        total = total + tmp[slot, here, : self.side].astype(F32)
                    to = pl.ds(pl.multiple_of(target_row + tile * 32, 16), 32)
                    target[to, columns] = total.astype(BF)
                    return carry

                lax.fori_loop(0, self.count // 32, step, 0)

            def T(self):
                self.far[0].start()
                self.far[1].start()

            def settled(self):
                for one in (*self.far, *self.near, *self.next):
                    one.sent()

            def F(self, h):
                self.far[h].arrived()
                self.fetch(self.land[("x1", "y1")[h]].at[self.n, 1])
                at = self.row(2 - h)
                self.add(self.blocks, at, self.halves[h], self.blocks, at, (0,))
                self.next[h].start()
                if DEFER:
                    self.near[h].start()

            def S(self, h):
                self.near[h].arrived()
                self.next[h].arrived()
                self.fetch(
                    self.land[("x1", "y1")[h]].at[self.n, 0], self.land[("y2", "x2")[h]].at[self.n]
                )
                self.add(self.blocks, self.row(0), self.halves[h], self.final, self.offset, (0, 1))
                pl.when(outer)(self.line[h][0].out.start)

            def I(self, h):
                @pl.when(inner)
                def _():
                    steps = self.line[h]
                    steps[0].into.wait_recv()
                    self.fetch(self.land["z"].at[self.n, 0, :, self.halves[h]])
                    self.add(self.final, self.offset, self.halves[h], self.final, self.offset, (0,))
                    steps[1].out.start()

            def X(self, h):
                @pl.when(inner)
                def _():
                    steps = self.line[h]
                    steps[1].into.wait_recv()
                    self.fetch(self.land["z"].at[self.n, 1, :, self.halves[h]])
                    steps[1].out.wait_send()
                    self.add(self.final, self.offset, self.halves[h], self.final, self.offset, (0,))
                    steps[2].out.start()

            def O(self, h):
                steps = self.line[h]

                @pl.when(outer)
                def _():
                    steps[2].into.wait_recv()
                    steps[0].out.wait_send()
                    copy = pltpu.make_async_copy(
                        self.land["z"].at[self.n, 2, :, self.halves[h]],
                        self.final.at[pl.ds(self.offset, self.count), self.halves[h]],
                        tmp_sems.at[0],
                    )
                    copy.start()
                    copy.wait()

                pl.when(inner)(steps[2].out.wait_send)
                self.complete += 1
                if self.complete == 2 and self.swap is not None:
                    if self.chunk is None:
                        self.swap.out.start()
                    else:
                        pl.when(core != self.chunk)(self.swap.out.start)

            def W(self):
                if self.chunk is None:
                    self.write()
                else:
                    pl.when(core == self.chunk)(self.write)
                    pl.when(core != self.chunk)(self.swap.out.wait_send)

            def write(self):
                n = self.n
                if self.name in ("d", "o"):
                    target = d_o if self.name == "d" else o_o
                    run_copies([pltpu.make_async_copy(self.final, target.at[n], out_sems.at[0])])
                    return
                self.swap.into.wait_recv()
                parts_now = 3 if self.name == "q" else 2
                wide_now = self.columns // parts_now
                places = [
                    (k // 2, pl.ds((k % 2) * block, block), pl.ds(0, wide_now)) for k in range(3)
                ]
                if self.name == "g":
                    places[1] = (1, pl.ds(0, block), pl.ds(0, wide_now))
                run_copies(
                    [
                        pltpu.make_async_copy(
                            swap_land[self.name].at[n, :, pl.ds(k * wide_now, wide_now)],
                            tmp.at[places[k]],
                            out_sems.at[2 + k],
                        )
                        for k in range(parts_now)
                    ]
                )
                mine = rows(core, block)

                def sets(part_now, start_now, count_now):
                    first_at = part_now * wide_now + start_now
                    own = self.final[mine, first_at : first_at + count_now]
                    slot, row_at, _ = places[part_now]
                    theirs = tmp[slot, row_at, start_now : start_now + count_now]
                    return (
                        lax.select(core == 0, own, theirs),
                        lax.select(core == 0, theirs, own),
                    )

                if self.name == "q":
                    for kind in range(3):
                        for j in range(chips):
                            even, odd = sets(kind, j * block, block)
                            to = kind * width + 2 * j * block
                            stage[:, to : to + block] = even
                            stage[:, to + block : to + 2 * block] = odd
                    run_copies([pltpu.make_async_copy(stage, q_o.at[n], out_sems.at[0])])
                else:
                    for which, target in enumerate((gate_o, up_o)):
                        even, odd = sets(which, 0, hid)
                        parts = []
                        for j in range(chips):
                            at = slice(j * hid_block, (j + 1) * hid_block)
                            parts += [even[:, at], odd[:, at]]
                        stage[:, : 2 * hid] = jnp.concatenate(parts, axis=1)
                        run_copies(
                            [
                                pltpu.make_async_copy(
                                    stage.at[:, pl.ds(0, 2 * hid)], target.at[n], out_sems.at[0]
                                )
                            ]
                        )
                if self.chunk is None:
                    self.swap.out.wait_send()

        def grad_tile(target, row, count, left, columns, right, wide_count):
            turned = left[:, columns]
            for begin in range(0, wide_count, 512):
                end = min(begin + 512, wide_count)
                target[pl.ds(row, count), begin:end] = dot_tn(turned, right[:, begin:end]).astype(BF)

        def begin(job, k):
            if k == 3 and not job.held:
                job.T()
            elif k and not DEFER:
                job.near[k - 1].start()

        def compute_blocks(name, n, left, right):
            if not n:
                for unit in pieces_of[name]:
                    jobs[unit, 1].settled()
            count, columns = sizes[name]
            for k in (3, 1, 2, 0):
                row = pl.multiple_of(cx(k) * count, 128)
                grad_tile(blocks[name], row, count, left, pl.ds(row, count), right, columns)
                for unit in pieces_of[name]:
                    begin(jobs[unit, n], k)

        def compute_down(n):
            if not n:
                jobs["d", 1].settled()

            def step(tile, carry):
                row = pl.multiple_of(tile * 256, 128)
                grad_tile(blocks["d"], row, 256, act, pl.ds(row, 256), flow, width)
                return carry

            lax.fori_loop(0, hid // 256, step, 0)
            if hid % 256:
                row = hid // 256 * 256
                grad_tile(blocks["d"], row, hid % 256, act, pl.ds(row, hid % 256), flow, width)
            for k in (3, 1, 2):
                begin(jobs["d", n], k)

        last_sum = [None]

        def partial_sums(which, product):
            if last_sum[0] is not None:
                last_sum[0].sent()

            def step(tile, carry):
                columns = rows(tile, 256)
                value = product(columns)
                part[:, columns] = value[:local]
                other[:, columns] = value[local:].astype(BF)
                return carry

            lax.fori_loop(0, width // 256, step, 0)
            last_sum[0] = link(other, got.at[which], got.at[which], "fsdp", 1).start()
            return last_sum[0]

        def norm_step(x, gain_now, gain_row, which, target, low_target):
            factor = lax.rsqrt(jnp.mean(x * x, axis=1, keepdims=True) + EPSILON)
            back = part[...] + got[which].astype(F32)
            scaled = back * gain_now
            gain_rows[gain_row : gain_row + 1, :] = jnp.sum(back * x * factor, axis=0, keepdims=True)
            mean_term = jnp.mean(scaled * x, axis=1, keepdims=True)
            base = grad[...] if target is middle else middle[...]
            result = base + factor * scaled - x * (factor * factor * factor * mean_term)
            target[...] = result
            if low_target is not None:
                low_target[:local] = result.astype(BF)

        def mlp_back():
            def span_step(base, count):
                here, there = pl.ds(base, count), pl.ds(hid + base, count)
                back = dot_nt(flow[...], wd[here, :])
                gate = kept[:, here].astype(F32)
                up = kept[:, there].astype(F32)
                sig = jax.nn.sigmoid(gate)
                kept[:, here] = (back * up * sig * (1.0 + gate * (1.0 - sig))).astype(BF)
                kept[:, there] = (back * gate * sig).astype(BF)

            def step(tile, carry):
                span_step(pl.multiple_of(tile * 256, 128), 256)
                return carry

            lax.fori_loop(0, hid // 256, step, 0)
            if hid % 256:
                span_step(hid // 256 * 256, hid % 256)

        lane_head = lax.broadcasted_iota(jnp.int32, (1, group), 1) // HD
        line_head = lax.broadcasted_iota(jnp.int32, (group, 1), 0) // HD

        def start_row(r):
            at = lax.broadcasted_iota(jnp.int32, (1, span), 1)
            first = jnp.zeros((1, span), jnp.int32)
            end = jnp.zeros((1, 1), jnp.int32)
            for j in range(documents):
                end = end + lens[r, j : j + 1, 0:1]
                first = jnp.where(at >= end, end, first)
            return first

        def attend_row(n, r):
            if True:
                key_sum[...] = jnp.zeros_like(key_sum)
                value_sum[...] = jnp.zeros_like(value_sum)
                key_turned = whole[1, r].astype(F32).T.astype(BF)
                starts = start_row(r)
                for piece in range(ctx):
                    keys = (piece + 1) * local
                    here = slice(piece * local, keys)
                    query = whole[0, r, here, :] * SCORE_SCALE
                    back = do_in[r, here, :]
                    key = whole[1, r, :keys, :]
                    value = whole[2, r, :keys, :]
                    k_at = lax.broadcasted_iota(jnp.int32, (keys, local), 0)
                    q_at = lax.broadcasted_iota(jnp.int32, (keys, local), 1) + piece * local
                    allowed = (k_at <= q_at) & (k_at >= starts[:, here])
                    turned = None
                    for head in range(heads):
                        q_head = jnp.where(lane_head == head, query, jnp.zeros_like(query))
                        b_head = jnp.where(lane_head == head, back, jnp.zeros_like(back))
                        scores = jnp.where(allowed, dot_nt(key, q_head), MASK_FILL)
                        peak = jnp.max(scores, axis=0, keepdims=True)
                        powers = jnp.exp(scores - peak)
                        total = jnp.sum(powers, axis=0, keepdims=True)
                        probs = powers * (1.0 / total)
                        back_probs = dot_nt(value, b_head)
                        delta = jnp.sum(probs * back_probs, axis=0, keepdims=True)
                        back_scores = (probs * (back_probs - delta)).astype(BF)
                        value_sum[:keys] += dot(probs.astype(BF), b_head)
                        key_sum[:keys] += dot(back_scores, q_head)
                        sub = dot(key_turned[:, :keys], back_scores)
                        turned = sub if head == 0 else jnp.where(line_head == head, sub, turned)
                    back_query = turned.T * SCORE_SCALE
                    dq_out[piece, 0, r] = turn(
                        back_query, cos[r, here, :], sin[r, here, :], -1
                    ).astype(BF)
                for piece in range(ctx):
                    here = slice(piece * local, (piece + 1) * local)
                    dq_out[piece, 1, r] = turn(
                        key_sum[here, :], cos[r, here, :], sin[r, here, :], -1
                    ).astype(BF)
                    if n == top:
                        back_value = 0.5 * value_sum[here, :]
                        carry[r, here, :] = back_value
                    else:
                        back_value = value_sum[here, :] + carry[r, here, :]
                    dq_out[piece, 2, r] = back_value.astype(BF)

        def spread(source_of, target_of):
            made = []
            for bit in range(1, ctx):
                to = lax.bitwise_xor(z, bit)
                made.append(link(source_of(to), target_of(z), target_of(to), "ctx", bit))
            return made

        def own_copy(r, source, target):
            copy = pltpu.make_async_copy(source, target, own_sems.at[r])
            copy.start()
            return copy

        def do_links(r):
            return spread(lambda to: do_out.at[to, r], lambda at: do_in.at[r, rows(at, local), :])

        def dq_links(r):
            return spread(lambda to: dq_out.at[to, :, r], lambda at: dq_in.at[at, :, r])

        jobs = {(unit, n): Reduce(unit, n) for n in (1, 0) for unit in units}
        state = {"e": e_link, "f": None, "do": [[], []], "dq": [[], []], "own": [None, None]}

        def gain_value(n):
            return gain[n : n + 1, :]

        def await_flow(n):
            if state["e"] is not None:
                state["e"].arrived()
                state["sent"] = state["e"]
                state["e"] = None

        def op_dW(n):
            loaded("act")
            await_flow(n)
            compute_down(n)
            if n:
                load("act", act_i.at[0], act)

        def op_mlp(n):
            loaded("wd", "kept")
            await_flow(n)
            mlp_back()
            if n:
                load("wd", wd_i.at[0], wd)
            loaded("wg")
            state["sums"] = partial_sums(0, lambda columns: dot_nt(kept[...], wg[columns, :]))
            if n:
                load("wg", wg_i.at[0], wg)

        def op_nrm2(n):
            loaded("wide")
            if state["f"] is not None:
                state["f"].sent()
            state["sums"].arrived()
            norm_step(wide[...], gain_value(2 * n + 1), 2 * n + 1, 0, middle, fgrad)
            state["f"] = pair_link(fgrad).start()
            state["fresh"] = True
            if n:
                load("wide", stream_i, wide)

        def await_fgrad():
            if state["fresh"]:
                state["f"].arrived()
            state["fresh"] = False

        def op_mixb(n):
            loaded("wo")
            for one in state["do"][0] + state["do"][1]:
                one.sent()
            await_fgrad()
            for tile in range(half // 256):
                back = dot_nt(fgrad[...], wo[tile * 256 : (tile + 1) * 256, :]).astype(BF)
                for sub in range(256 // group):
                    do_out[tile * 256 // group + sub] = back[
                        :, sub * group : (sub + 1) * group
                    ].reshape(2, local, group)
            if n:
                load("wo", wo_i.at[0], wo)
            state["do"] = [do_links(0), do_links(1)]
            for one in state["do"][0]:
                one.start()
            for r in range(2):
                state["own"][r] = own_copy(r, do_out.at[z, r], do_in.at[r, rows(z, local), :])

        def op_dos(n):
            for one in state["do"][0]:
                one.arrived()
            for one in state["do"][1]:
                one.start()

        def op_gW(n):
            loaded("norm")
            compute_blocks("g", n, norm, kept)
            load("norm", n1_i.at[n], norm)
            if n:
                load("kept", kept_i.at[0], kept)

        def op_oW(n):
            loaded("mix")
            await_fgrad()
            compute_blocks("o", n, mix, fgrad)
            if n:
                load("mix", mix_i.at[0], mix)

        def op_att(n, r):
            loaded("whole", "cos", "sin")
            state["own"][r].wait()
            if r:
                for one in state["do"][r]:
                    one.arrived()
            for one in state["dq"][r]:
                one.sent()
            attend_row(n, r)
            if n and r:
                load("whole", whole_i.at[0], whole)
            state["dq"][r] = dq_links(r)
            for one in state["dq"][r]:
                one.start()
            state["own"][r] = own_copy(r, dq_out.at[z, :, r], dq_in.at[z, :, r])

        def op_pb(n):
            loaded("wq")
            for r in range(2):
                state["own"][r].wait()
                for one in state["dq"][r]:
                    one.arrived()
            for k in range(ctx):
                for kind in range(3):
                    base = kind * half + k * group
                    joined[:, base : base + group] = dq_in[k, kind].reshape(both, group)
            state["sums"] = partial_sums(1, lambda columns: dot_nt(joined[...], wq[columns, :]))
            if n:
                load("wq", wq_i.at[0], wq)

        def op_qW(n):
            loaded("norm")
            compute_blocks("q", n, norm, joined)
            if n:
                load("norm", n2_i.at[0], norm)

        def op_nrm1(n):
            if not n:
                state["f"].sent()
                load("tok", tok_i, fgrad.at[pl.ds(0, local), :])
                loaded("tok")
            loaded("wide")
            state["sent"].sent()
            state["sums"].arrived()
            if n:
                norm_step(wide[...], gain_value(2 * n), 2 * n, 1, grad, flow)
                state["e"] = pair_link(flow).start()
                load("wide", mid_i.at[0], wide)
            else:
                norm_step(fgrad[:local].astype(F32), gain_value(0), 0, 1, grad_o, None)

        def op_G1(n):
            for s in range(shards):
                gain_send[s] = jnp.concatenate(
                    [gain_rows[:4, s * block : (s + 1) * block], jnp.zeros((4, block), F32)]
                )
            state["gain"] = []
            for bit in range(1, shards):
                to = lax.bitwise_xor(f, bit)
                state["gain"].append(
                    link(gain_send.at[to], gain_land.at[f], gain_land.at[to], "fsdp", bit).start()
                )
            gain_land[f] = gain_send[f]

        def op_G2(n):
            for one in state["gain"]:
                one.arrived()
            total = gain_land[0]
            for s in range(1, shards):
                total = total + gain_land[s]
            gain_sum[...] = total
            state["line"] = []
            for bit in range(1, ctx):
                to = lax.bitwise_xor(z, bit)
                state["line"].append(
                    link(gain_sum, gain_line.at[z], gain_line.at[to], "ctx", bit).start()
                )
            gain_line[z] = total

        def op_G3(n):
            for one in state["line"]:
                one.arrived()
            total = gain_line[0]
            for k in range(1, ctx):
                total = total + gain_line[k]
            gain_o[...] = total[: 2 * layers]

        chain = {
            "dW": op_dW, "mlp": op_mlp, "nrm2": op_nrm2, "mixb": op_mixb, "gW": op_gW,
            "oW": op_oW, "att": op_att, "dos": op_dos, "pb": op_pb, "qW": op_qW, "nrm1": op_nrm1,
            "G1": op_G1, "G2": op_G2, "G3": op_G3,
        }
        for step in BACK_ORDER:
            if step[0] in chain:
                chain[step[0]](*step[1:])
            elif step[0] in ("W", "T"):
                getattr(jobs[step[1], step[2]], step[0])()
            else:
                getattr(jobs[step[1], step[2]], step[0])(step[3])
        for one in flights:
            one.sent()

    def vm(*dims, kind=BF):
        return pltpu.VMEM(dims, kind)

    outs = [
        shape((local, width), F32),
        shape((2 * layers, block), F32),
        shape((layers, block, 3 * width), BF),
        shape((layers, block, width), BF),
        shape((layers, block, 2 * hid), BF),
        shape((layers, block, 2 * hid), BF),
        shape((layers, hid_block, width), BF),
    ]
    for unit in units:
        count, columns = counts[unit], sizes[unit[0]][1]
        outs += [
            shape((layers, 2, count, columns // 2), BF),
            shape((layers, 2, count, columns // 2), BF),
            shape((layers, count, columns // 2), BF),
            shape((layers, count, columns // 2), BF),
            shape((layers, 3, count, columns), BF),
        ]
    outs += [shape((layers, block, sizes[name][1]), BF) for name in ("g", "q")]
    scratch = [
        vm(width, 3 * half),
        vm(half, width),
        vm(width, 2 * hid),
        vm(hid, width),
        vm(both, hid),
        vm(both, 2 * hid),
        vm(both, width),
        vm(3, 2, span, group),
        vm(both, half),
        vm(local, width, kind=F32),
        vm(both, width),
        vm(both, width),
        vm(2, local, width),
        vm(2, span, group),
        vm(ctx, 3, 2, local, group),
        vm(local, width, kind=F32),
        vm(local, width),
        vm(local, width, kind=F32),
        vm(local, width, kind=F32),
        vm(ctx, 2, local, group),
        vm(ctx, 3, 2, local, group),
        vm(span, group, kind=F32),
        vm(span, group, kind=F32),
        vm(2, span, group, kind=F32),
        vm(both, 3 * half),
        vm(2, span, 128, kind=F32),
        vm(2, span, 128, kind=F32),
    ]
    scratch += [vm(chips * sizes[name][0], sizes[name][1]) for name in names]
    scratch += [vm(*sizes[name]) for name in names]
    scratch += [
        vm(2, max(hid_block, 2 * block), hid),
        vm(block, 3 * width),
        vm(8, width, kind=F32),
        vm(shards, 8, block, kind=F32),
        vm(shards, 8, block, kind=F32),
        vm(8, block, kind=F32),
        vm(ctx, 8, block, kind=F32),
        pltpu.SemaphoreType.DMA((2, 192)),
        pltpu.SemaphoreType.DMA((20,)),
        pltpu.SemaphoreType.DMA((2,)),
        pltpu.SemaphoreType.DMA((6,)),
        pltpu.SemaphoreType.DMA((2,)),
    ]
    (wq, wo, wg, wd, n1, n2, whole, mix, mid, stream, act, kept) = saved[:12]
    gain_all, cosines, sines, lens_all = saved[12:16]
    return pl.pallas_call(
        kernel,
        out_shape=outs,
        in_specs=[ANY] * 2 + [VM] * 2 + [ANY] * 14,
        out_specs=[VM] * 2 + [ANY] * (len(outs) - 2),
        scratch_shapes=scratch,
        compiler_params=pltpu.CompilerParams(
            vmem_limit_bytes=63 * MIB, collective_id=1, has_side_effects=True
        ),
        cost_estimate=pl.CostEstimate(
            flops=28 * 10**9, bytes_accessed=100 * MIB, transcendentals=0
        ),
    )(
        cotangent, tokens, lens_all, gain_all, wq, wo, wg, wd, n1, n2, whole, mix, mid, stream,
        act, kept, cosines, sines,
    )


def add_low(left, right):
    return (left.astype(F32) + right.astype(F32)).astype(BF)


def reduce_chips(blocks, chips):
    if chips != 4:
        total = blocks[0].astype(F32)
        for k in range(1, chips):
            total = total + swap(blocks[k], "fsdp", 2 * k).astype(F32)
        return total.astype(BF)
    send_x, keep_x, send_y, keep_y = blocks
    got_x = swap(send_x, "fsdp", 2)
    got_y = swap(send_y, "fsdp", 4)
    on_x = swap(add_low(keep_x[1], got_x[1]), "fsdp", 4)
    on_y = swap(add_low(keep_y[1], got_y[1]), "fsdp", 2)
    first = add_low(add_low(keep_x[0], got_x[0]), on_x)
    second = add_low(add_low(keep_y[0], got_y[0]), on_y)
    return jnp.concatenate([first, second], axis=1)


def reduce_line(block):
    if lax.axis_size("ctx") != 4:
        return lax.psum(block, "ctx")
    z = lax.axis_index("ctx")
    inner = (z == 1) | (z == 2)
    inward = lax.ppermute(block, "ctx", [(0, 1), (3, 2)])
    pair = jnp.where(inner, add_low(block, inward), block)
    across = lax.ppermute(pair, "ctx", [(1, 2), (2, 1)])
    total = add_low(pair, across)
    outward = lax.ppermute(total, "ctx", [(1, 0), (2, 3)])
    return jnp.where(inner, total, outward)


def own_rows(block):
    core = lax.axis_index("fsdp") % 2
    rows = block.shape[0] // 2
    mine = lax.dynamic_slice_in_dim(block, core * rows, rows)
    theirs = swap(lax.dynamic_slice_in_dim(block, (1 - core) * rows, rows), "fsdp", 1)
    low = jnp.where(core == 0, mine, theirs)
    high = jnp.where(core == 0, theirs, mine)
    return jnp.stack([low, high])


def chip_piece(mine, other):
    core = lax.axis_index("fsdp") % 2
    got = swap(other, "fsdp", 1)
    return jnp.where(
        core == 0, jnp.concatenate([mine, got]), jnp.concatenate([got, mine])
    )


def document_starts(lengths, index):
    ends = []
    total = jnp.int32(0)
    for j in range(lengths.shape[0]):
        total = total + lengths[j]
        ends.append(total)
    start = jnp.zeros_like(index)
    for end in ends:
        start = jnp.where(index >= end, end, start)
    return start


def rotary(positions):
    pairs = HD // 2
    lane = jnp.arange(128, dtype=jnp.int32)
    frequency = jnp.exp(-math.log(10000.0) * jnp.arange(pairs, dtype=F32) / pairs)
    angles = positions.astype(F32)[..., None] * frequency
    cosines = jnp.tile(jnp.cos(angles), 128 // pairs)
    sines = jnp.tile(jnp.sin(angles), 128 // pairs)
    low = jnp.where(lane % HD < pairs, -sines, 0.0)
    high = jnp.where(lane % HD >= pairs, sines, 0.0)
    return [cosines, low, high]


def body(tokens, doc_lengths, cotangent, gains, w_qkv, w_out, w_gate, w_up, w_down):
    _, local, width = tokens.shape
    layers = gains.shape[0]
    shards = lax.axis_size("fsdp")
    ctx = lax.axis_size("ctx")
    chips = shards // 2
    block = width // shards
    hidden = w_gate.shape[2]
    hidden_half = hidden // 2
    hidden_block = hidden // shards
    core = lax.axis_index("fsdp") % 2
    z = lax.axis_index("ctx")
    span = local * ctx

    def pick(array, axis, which):
        return lax.dynamic_index_in_dim(array, which, axis, keepdims=False)

    if chips == 4 and ctx == 4 and layers == 2:
        saved = forward_pass(
            tokens[0], doc_lengths, gains, w_qkv, w_out, w_gate, w_up, w_down
        )
        made = backward_pass(saved, tokens[0], cotangent[0])
        grad, gain_sum, qkv_sum, out_sum, gate_sum, up_sum, down_sum = made[:7]
        sums = [s.astype(F32) for s in (qkv_sum, out_sum, gate_sum, up_sum, down_sum)]
        gain_sum = gain_sum.reshape(layers, 2, block)
        return (saved[16][None], grad[None], gain_sum, *sums)

    qkv_weights, out_weights, gu_weights, down_weights = [], [], [], []
    for layer in range(layers):
        qkv = w_qkv[layer].reshape(block, 3, chips, 2, block)
        sides = [pick(qkv, 3, which).reshape(block, -1) for which in (core, 1 - core)]
        qkv_weights.append(gather(chip_piece(*sides), chips))
        out_weights.append(gather(w_out[layer], chips))
        sides = []
        for which in (core, 1 - core):
            both = [
                pick(w[layer].reshape(block, chips, 2, hidden_block), 2, which).reshape(
                    block, hidden_half
                )
                for w in (w_gate, w_up)
            ]
            sides.append(jnp.concatenate(both, axis=1))
        gu_weights.append(gather(chip_piece(*sides), chips))
        down_weights.append(gather(w_down[layer], chips))

    all_gains = lax.all_gather(gains, "fsdp", axis=2, tiled=True)
    gain_rows = [[all_gains[layer, n][None] for n in range(2)] for layer in range(layers)]

    index = jnp.arange(span, dtype=jnp.int32)
    lengths = [doc_lengths[0], swap(doc_lengths, "fsdp", 1)[0]]
    starts = jnp.stack([document_starts(row, index) for row in lengths])
    row_tables = rotary(index[None] - starts)
    here_tables = [lax.dynamic_slice_in_dim(t, z * local, local, axis=1) for t in row_tables]
    head_lanes = min(128, width // 2 // ctx)
    head_tables = [t[:, :, :head_lanes] for t in row_tables]
    start_column = starts[:, :, None]
    start_row = starts[:, None, :]

    def pair(array):
        return (array, swap(array, "fsdp", 1))

    stream = tokens[0]
    kept = []
    first_value = None
    (low,) = join_norm(stream, None, None, gain_rows[0][0])
    for layer in range(layers):
        normed = pair(low)
        slabs, first_value = project(
            *normed, here_tables, first_value, qkv_weights[layer], ctx, layer == layers - 1
        )
        slabs = exchange(slabs)
        mixed = exchange(attend(slabs, start_column))
        own, other, joined = mix_out(mixed, out_weights[layer])
        middle, low = join_norm(stream, own, swap(other, "fsdp", 1), gain_rows[layer][1])
        normed_two = pair(low)
        active, gu_kept = gate_up(*normed_two, gu_weights[layer])
        own, other = down(active, down_weights[layer])
        after = gain_rows[min(layer + 1, layers - 1)][0]
        kept.append((stream, normed, slabs, joined, middle, normed_two, active, gu_kept))
        stream, low = join_norm(middle, own, swap(other, "fsdp", 1), after)
    out_tokens = stream.astype(BF)[None]

    grad = cotangent[0]
    low = cotangent[0]
    carried = None
    gain_grads = [[None, None] for _ in range(layers)]
    done = [None] * layers
    for layer in reversed(range(layers)):
        stream, normed, slabs, joined, middle, normed_two, active, gu_kept = kept[layer]
        sent = pair(low)
        down_blocks = weight_grad([active], sent, chips)
        gu_grads, own, other = mlp_back(
            *sent, gu_kept, gu_weights[layer], down_weights[layer]
        )
        grad, low, gain_grads[layer][1] = norm_back(
            middle, own, swap(other, "fsdp", 1), gain_rows[layer][1], grad
        )
        gu_blocks = weight_grad(normed_two, [gu_grads], chips)
        mixed_back = pair(low)
        grad_slabs = exchange(mix_back(*mixed_back, out_weights[layer], ctx))
        out_blocks = weight_grad([joined], mixed_back, chips)
        grad_slabs, carry_out = attend_back(slabs, grad_slabs, start_row, head_tables, carried)
        carried = carry_out
        own, other, qkv_grads = project_back(exchange(grad_slabs), qkv_weights[layer])
        qkv_blocks = weight_grad(normed, [qkv_grads], chips)
        grad, low, gain_grads[layer][0] = norm_back(
            stream, own, swap(other, "fsdp", 1), gain_rows[layer][0], grad
        )
        down_sum = reduce_line(reduce_chips(down_blocks, chips)).astype(F32)
        gu_sum = own_rows(reduce_line(reduce_chips(gu_blocks, chips)))
        out_sum = reduce_line(reduce_chips(out_blocks, chips)).astype(F32)
        qkv_sum = own_rows(reduce_line(reduce_chips(qkv_blocks, chips)))
        qkv_sum = qkv_sum.reshape(2, block, 3, chips, block).transpose(1, 2, 3, 0, 4)
        qkv_sum = qkv_sum.reshape(block, 3 * width).astype(F32)
        gu_sum = gu_sum.reshape(2, block, 2, chips, hidden_block).transpose(2, 1, 3, 0, 4)
        gu_sum = gu_sum.reshape(2, block, hidden).astype(F32)
        done[layer] = (qkv_sum, out_sum, gu_sum[0], gu_sum[1], down_sum)

    gain_sum = jnp.stack([jnp.concatenate(rows) for rows in gain_grads])
    gain_sum = lax.psum_scatter(gain_sum, "fsdp", scatter_dimension=2, tiled=True)
    gain_sum = lax.psum(gain_sum, "ctx")
    stacked = [jnp.stack([done[layer][n] for layer in range(layers)]) for n in range(5)]
    return (out_tokens, grad[None], gain_sum, *stacked)


def solution(mesh):
    rows = P(None, "fsdp", None)
    tokens = P("fsdp", "ctx", None)
    gains = P(None, None, "fsdp")
    return jax.shard_map(
        body,
        mesh=mesh,
        in_specs=(tokens, P("fsdp", None), tokens, gains, rows, rows, rows, rows, rows),
        out_specs=(tokens, tokens, gains, rows, rows, rows, rows, rows),
        check_vma=False,
    )
```

```python
import math

import jax
import jax.numpy as jnp
from jax import lax
from jax.experimental import pallas as pl
from jax.experimental.pallas import tpu as pltpu
from jax.sharding import PartitionSpec as P

FSDP = "fsdp"
CTX = "ctx"
HEADS = 16
HD = 64
EPSILON = 1e-06
SCORE_SCALE = 0.125
MASK_FILL = -1e30
BF = jnp.bfloat16
F32 = jnp.float32
MIB = 1024 * 1024
ANY = pl.BlockSpec(memory_space=pl.ANY)
VM = pl.BlockSpec(memory_space=pltpu.VMEM)
NT = (((1,), (1,)), ((), ()))
TN = (((0,), (0,)), ((), ()))


def dot(left, right):
    return jnp.dot(left, right, preferred_element_type=F32)


def dot_nt(left, right):
    return lax.dot_general(left, right, NT, preferred_element_type=F32)


def dot_tn(left, right):
    return lax.dot_general(left, right, TN, preferred_element_type=F32)


def swap(array, axis, bit):
    size = lax.axis_size(axis)
    return lax.ppermute(array, axis, [(i, i ^ bit) for i in range(size)])


def call(kernel, outs, out_specs, scratch, args, in_specs, flops, vmem):
    nbytes = sum(a.size * a.dtype.itemsize for a in args)
    nbytes += sum(math.prod(o.shape) * o.dtype.itemsize for o in outs)
    return pl.pallas_call(
        kernel,
        out_shape=outs,
        in_specs=in_specs,
        out_specs=out_specs,
        scratch_shapes=scratch,
        compiler_params=pltpu.CompilerParams(vmem_limit_bytes=vmem * MIB),
        cost_estimate=pl.CostEstimate(flops=flops, bytes_accessed=nbytes, transcendentals=0),
    )(*args)


def shape(dims, kind):
    return jax.ShapeDtypeStruct(tuple(dims), kind)


def chip_index():
    return lax.axis_index(FSDP) // 2


def run_copies(copies):
    for copy in copies:
        copy.start()
    for copy in copies:
        copy.wait()


def weight_copies(plan, refs, buffer, sems, first):
    chip = chip_index()
    rows = plan[0][2]
    copies = []
    for number, ((k, offset, count), ref) in enumerate(zip(plan[1], refs)):
        start = pl.multiple_of(lax.bitwise_xor(chip, k) * rows + offset, 16)
        copies.append(
            pltpu.make_async_copy(
                ref, buffer.at[pl.ds(start, count), :], sems.at[first + number]
            )
        )
    return copies


class Pieces:
    def __init__(self, arrays, where, rows):
        self.arrays = arrays
        self.where = where
        self.rows = rows

    @property
    def plan(self):
        return ((0, 0, self.rows), self.where)


def gather(piece, chips):
    rows = piece.shape[0]
    if chips == 4:
        half = rows // 2
        from_x = swap(piece, FSDP, 2)
        from_y = swap(piece, FSDP, 4)
        far_one = swap(from_x[:half], FSDP, 4)
        far_two = swap(from_y[half:], FSDP, 2)
        return Pieces(
            [piece, from_x, from_y, far_one, far_two],
            [(0, 0, rows), (1, 0, rows), (2, 0, rows), (3, 0, half), (3, half, rows - half)],
            rows,
        )
    arrays = [piece] + [swap(piece, FSDP, 2 * k) for k in range(1, chips)]
    return Pieces(arrays, [(k, 0, rows) for k in range(chips)], rows)


def rope(x, cosines, low_sine, high_sine):
    width = x.shape[-1]
    return (
        x * cosines
        + pltpu.roll(x, width - HD // 2, 1) * low_sine
        + pltpu.roll(x, HD // 2, 1) * high_sine
    )


def project(n_own, n_other, tables, first_value, weight, ctx, last):
    local, width = n_own.shape
    half = width // 2
    group = half // ctx
    pieces = len(weight.arrays)
    plan = weight.plan

    def kernel(*refs):
        own, other, cos, low, high = refs[:5]
        at = 5
        v_in = None
        if first_value is not None:
            v_in = refs[at]
            at += 1
        w_refs = refs[at : at + pieces]
        at += pieces
        slabs = refs[at : at + ctx]
        at += ctx
        v_out = None
        if first_value is None:
            v_out = refs[at]
            at += 1
        buffer, tokens, slab, sems, out_sems = refs[at:]
        copies = weight_copies(plan, w_refs, buffer, sems, 0)
        for copy in copies:
            copy.start()
        tokens[:local] = own[...]
        tokens[local:] = other[...]
        tables_now = [t[...].reshape(2 * local, 128) for t in (cos, low, high)]
        for copy in copies:
            copy.wait()
        for tile in range(3 * half // 256):
            acc = dot(tokens[...], buffer[:, tile * 256 : (tile + 1) * 256])
            kind = tile * 256 // half
            base = tile * 256 - kind * half
            for sub in range(2):
                x = acc[:, sub * 128 : (sub + 1) * 128]
                column = base + sub * 128
                if kind < 2:
                    x = rope(x, *tables_now)
                elif first_value is not None:
                    x = 0.5 * x + 0.5 * v_in[:, column : column + 128].astype(F32)
                x = x.astype(BF)
                if kind == 2 and v_out is not None:
                    v_out[:, column : column + 128] = x
                for part in range(128 // group):
                    slab[column // group + part, kind] = x[
                        :, part * group : (part + 1) * group
                    ].reshape(2, local, group)
        z = lax.axis_index(CTX)
        run_copies(
            [
                pltpu.make_async_copy(slab.at[lax.bitwise_xor(z, k)], slabs[k], out_sems.at[k])
                for k in range(ctx)
            ]
        )

    args = [n_own, n_other, *tables]
    specs = [VM] * 5
    outs = [shape((3, 2, local, group), BF)] * ctx
    out_specs = [ANY] * ctx
    if first_value is not None:
        args.append(first_value)
        specs.append(VM)
    else:
        outs.append(shape((2 * local, half), BF))
        out_specs.append(VM)
    args += weight.arrays
    specs += [ANY] * pieces
    got = call(
        kernel,
        outs,
        out_specs,
        [
            pltpu.VMEM((width, 3 * half), BF),
            pltpu.VMEM((2 * local, width), BF),
            pltpu.VMEM((ctx, 3, 2, local, group), BF),
            pltpu.SemaphoreType.DMA((pieces,)),
            pltpu.SemaphoreType.DMA((ctx,)),
        ],
        args,
        specs,
        2 * 2 * local * width * 3 * half,
        40,
    )
    return got[:ctx], (first_value if first_value is not None else got[ctx])


def exchange(slabs):
    return [slabs[0]] + [swap(slabs[k], CTX, k) for k in range(1, len(slabs))]


def attend(slabs, start_column):
    ctx = len(slabs)
    _, _, local, group = slabs[0].shape
    span = ctx * local
    heads = group // HD

    def kernel(*refs):
        starts = refs[0]
        ins = refs[1 : 1 + ctx]
        outs = refs[1 + ctx : 1 + 2 * ctx]
        whole, mixed, sems, out_sems = refs[1 + 2 * ctx :]
        z = lax.axis_index(CTX)
        copies = []
        for k in range(ctx):
            at = pl.multiple_of(lax.bitwise_xor(z, k) * local, 16)
            copies.append(
                pltpu.make_async_copy(
                    ins[k], whole.at[:, :, pl.ds(at, local), :], sems.at[k]
                )
            )
        run_copies(copies)
        lane = lax.broadcasted_iota(jnp.int32, (1, group), 1) // HD

        def row_step(row, carry):
            for block in range(ctx):
                keys = (block + 1) * local
                here = slice(block * local, keys)
                query = whole[0, row, here, :] * SCORE_SCALE
                key = whole[1, row, :keys, :]
                value = whole[2, row, :keys, :]
                k_at = lax.broadcasted_iota(jnp.int32, (local, keys), 1)
                q_at = lax.broadcasted_iota(jnp.int32, (local, keys), 0) + block * local
                allowed = (k_at <= q_at) & (k_at >= starts[row, here, :])
                result = None
                for head in range(heads):
                    q_head = jnp.where(lane == head, query, jnp.zeros_like(query))
                    scores = jnp.where(allowed, dot_nt(q_head, key), MASK_FILL)
                    top = jnp.max(scores, axis=1, keepdims=True)
                    powers = jnp.exp(scores - top)
                    total = jnp.sum(powers, axis=1, keepdims=True)
                    probs = (powers * (1.0 / total)).astype(BF)
                    out = dot(probs, value)
                    result = out if result is None else jnp.where(lane == head, out, result)
                mixed[block, row] = result.astype(BF)
            return carry

        lax.fori_loop(0, 2, row_step, 0)
        run_copies(
            [
                pltpu.make_async_copy(mixed.at[lax.bitwise_xor(z, k)], outs[k], out_sems.at[k])
                for k in range(ctx)
            ]
        )

    return call(
        kernel,
        [shape((2, local, group), BF)] * ctx,
        [ANY] * ctx,
        [
            pltpu.VMEM((3, 2, span, group), BF),
            pltpu.VMEM((ctx, 2, local, group), BF),
            pltpu.SemaphoreType.DMA((ctx,)),
            pltpu.SemaphoreType.DMA((ctx,)),
        ],
        [start_column, *slabs],
        [VM] + [ANY] * ctx,
        2 * 2 * 2 * heads * span * span * 128,
        40,
    )


def halves_out(product, own_ref, other_ref, columns, local):
    own_ref[:, columns] = product[:local]
    other_ref[:, columns] = product[local:].astype(BF)


def mix_out(slabs, weight):
    ctx = len(slabs)
    _, local, group = slabs[0].shape
    half = ctx * group
    width = weight.arrays[0].shape[1]
    pieces = len(weight.arrays)
    plan = weight.plan

    def kernel(*refs):
        ins = refs[:ctx]
        w_refs = refs[ctx : ctx + pieces]
        own, other, joined, buffer, landed, sems = refs[ctx + pieces :]
        z = lax.axis_index(CTX)
        copies = weight_copies(plan, w_refs, buffer, sems, ctx)
        for k in range(ctx):
            copies.append(
                pltpu.make_async_copy(ins[k], landed.at[lax.bitwise_xor(z, k)], sems.at[k])
            )
        run_copies(copies)
        for k in range(ctx):
            joined[:, k * group : (k + 1) * group] = landed[k].reshape(2 * local, group)
        for tile in range(width // 256):
            columns = slice(tile * 256, (tile + 1) * 256)
            halves_out(dot(joined[...], buffer[:, columns]), own, other, columns, local)

    return call(
        kernel,
        [shape((local, width), F32), shape((local, width), BF), shape((2 * local, half), BF)],
        [VM] * 3,
        [
            pltpu.VMEM((half, width), BF),
            pltpu.VMEM((ctx, 2, local, group), BF),
            pltpu.SemaphoreType.DMA((ctx + pieces,)),
        ],
        [*slabs, *weight.arrays],
        [ANY] * (ctx + pieces),
        2 * 2 * local * half * width,
        24,
    )


def join_norm(base, own, other, gain):
    local, width = base.shape
    fresh = own is not None

    def kernel(*refs):
        if fresh:
            base_ref, own_ref, other_ref, gain_ref, sum_ref, low_ref = refs
            total = base_ref[...].astype(F32) + own_ref[...] + other_ref[...].astype(F32)
            sum_ref[...] = total
        else:
            base_ref, gain_ref, low_ref = refs
            total = base_ref[...].astype(F32)
        factor = lax.rsqrt(jnp.mean(total * total, axis=1, keepdims=True) + EPSILON)
        low_ref[...] = (total * factor * gain_ref[...].astype(F32)).astype(BF)

    outs = [shape((local, width), BF)]
    args = [base, gain]
    if fresh:
        outs = [shape((local, width), F32)] + outs
        args = [base, own, other, gain]
    return call(
        kernel, outs, [VM] * len(outs), [], args, [VM] * len(args), 8 * local * width, 16
    )


def gate_up(n_own, n_other, weight):
    local, width = n_own.shape
    hidden2 = weight.arrays[0].shape[1]
    hidden = hidden2 // 2
    pieces = len(weight.arrays)
    plan = weight.plan

    def kernel(*refs):
        own, other = refs[:2]
        w_refs = refs[2 : 2 + pieces]
        active, kept, buffer, tokens, sems = refs[2 + pieces :]
        copies = weight_copies(plan, w_refs, buffer, sems, 0)
        for copy in copies:
            copy.start()
        tokens[:local] = own[...]
        tokens[local:] = other[...]
        for copy in copies:
            copy.wait()

        def span_step(base, count):
            here, there = pl.ds(base, count), pl.ds(hidden + base, count)
            gate = dot(tokens[...], buffer[:, here])
            up = dot(tokens[...], buffer[:, there])
            kept[:, here] = gate.astype(BF)
            kept[:, there] = up.astype(BF)
            active[:, here] = (gate * jax.nn.sigmoid(gate) * up).astype(BF)

        def step(tile, carry):
            span_step(pl.multiple_of(tile * 256, 128), 256)
            return carry

        lax.fori_loop(0, hidden // 256, step, 0)
        if hidden % 256:
            span_step(hidden // 256 * 256, hidden % 256)

    return call(
        kernel,
        [shape((2 * local, hidden), BF), shape((2 * local, hidden2), BF)],
        [VM] * 2,
        [
            pltpu.VMEM((width, hidden2), BF),
            pltpu.VMEM((2 * local, width), BF),
            pltpu.SemaphoreType.DMA((pieces,)),
        ],
        [n_own, n_other, *weight.arrays],
        [VM] * 2 + [ANY] * pieces,
        2 * 2 * local * width * hidden2,
        40,
    )


def down(active, weight):
    tokens, hidden = active.shape
    local = tokens // 2
    width = weight.arrays[0].shape[1]
    pieces = len(weight.arrays)
    plan = weight.plan

    def kernel(*refs):
        left = refs[0]
        w_refs = refs[1 : 1 + pieces]
        own, other, buffer, sems = refs[1 + pieces :]
        run_copies(weight_copies(plan, w_refs, buffer, sems, 0))

        def step(tile, carry):
            columns = pl.ds(pl.multiple_of(tile * 256, 256), 256)
            halves_out(dot(left[...], buffer[:, columns]), own, other, columns, local)
            return carry

        lax.fori_loop(0, width // 256, step, 0)

    return call(
        kernel,
        [shape((local, width), F32), shape((local, width), BF)],
        [VM] * 2,
        [pltpu.VMEM((hidden, width), BF), pltpu.SemaphoreType.DMA((pieces,))],
        [active, *weight.arrays],
        [VM] + [ANY] * pieces,
        2 * tokens * hidden * width,
        24,
    )


def mlp_back(e_own, e_other, kept, gu_weight, down_weight):
    local, width = e_own.shape
    hidden2 = kept.shape[1]
    hidden = hidden2 // 2
    pieces = len(gu_weight.arrays)
    more = len(down_weight.arrays)
    gu_plan, down_plan = gu_weight.plan, down_weight.plan

    def kernel(*refs):
        e_one, e_two, kept_ref = refs[:3]
        gu_refs = refs[3 : 3 + pieces]
        down_refs = refs[3 + pieces : 3 + pieces + more]
        grads, own, other, gu, wd, tokens, sems = refs[3 + pieces + more :]
        first = weight_copies(down_plan, down_refs, wd, sems, pieces)
        second = weight_copies(gu_plan, gu_refs, gu, sems, 0)
        for copy in first + second:
            copy.start()
        tokens[:local] = e_one[...]
        tokens[local:] = e_two[...]
        for copy in first:
            copy.wait()

        def span_step(base, count):
            here, there = pl.ds(base, count), pl.ds(hidden + base, count)
            flow = dot_nt(tokens[...], wd[here, :])
            gate = kept_ref[:, here].astype(F32)
            up = kept_ref[:, there].astype(F32)
            sig = jax.nn.sigmoid(gate)
            grads[:, here] = (flow * up * sig * (1.0 + gate * (1.0 - sig))).astype(BF)
            grads[:, there] = (flow * gate * sig).astype(BF)

        def step(tile, carry):
            span_step(pl.multiple_of(tile * 256, 128), 256)
            return carry

        lax.fori_loop(0, hidden // 256, step, 0)
        if hidden % 256:
            span_step(hidden // 256 * 256, hidden % 256)
        for copy in second:
            copy.wait()

        def back_step(tile, carry):
            rows = pl.ds(pl.multiple_of(tile * 256, 256), 256)
            halves_out(dot_nt(grads[...], gu[rows, :]), own, other, rows, local)
            return carry

        lax.fori_loop(0, width // 256, back_step, 0)

    return call(
        kernel,
        [
            shape((2 * local, hidden2), BF),
            shape((local, width), F32),
            shape((local, width), BF),
        ],
        [VM] * 3,
        [
            pltpu.VMEM((width, hidden2), BF),
            pltpu.VMEM((hidden, width), BF),
            pltpu.VMEM((2 * local, width), BF),
            pltpu.SemaphoreType.DMA((pieces + more,)),
        ],
        [e_own, e_other, kept, *gu_weight.arrays, *down_weight.arrays],
        [VM] * 3 + [ANY] * (pieces + more),
        2 * 2 * local * width * hidden * 3,
        48,
    )


def norm_back(stream, own, other, gain, grad):
    local, width = stream.shape

    def kernel(x_ref, own_ref, other_ref, gain_ref, grad_ref, out_ref, low_ref, gain_out):
        x = x_ref[...].astype(F32)
        factor = lax.rsqrt(jnp.mean(x * x, axis=1, keepdims=True) + EPSILON)
        flow = own_ref[...] + other_ref[...].astype(F32)
        scaled = flow * gain_ref[...].astype(F32)
        gain_out[...] = jnp.sum(flow * x * factor, axis=0, keepdims=True)
        mean_term = jnp.mean(scaled * x, axis=1, keepdims=True)
        result = (
            grad_ref[...].astype(F32)
            + factor * scaled
            - x * (factor * factor * factor * mean_term)
        )
        out_ref[...] = result
        low_ref[...] = result.astype(BF)

    return call(
        kernel,
        [shape((local, width), F32), shape((local, width), BF), shape((1, width), F32)],
        [VM] * 3,
        [],
        [stream, own, other, gain, grad],
        [VM] * 5,
        12 * local * width,
        24,
    )


def mix_back(f_own, f_other, weight, ctx):
    local, width = f_own.shape
    half = width // 2
    group = half // ctx
    pieces = len(weight.arrays)
    plan = weight.plan

    def kernel(*refs):
        own, other = refs[:2]
        w_refs = refs[2 : 2 + pieces]
        slabs = refs[2 + pieces : 2 + pieces + ctx]
        buffer, tokens, slab, sems, out_sems = refs[2 + pieces + ctx :]
        copies = weight_copies(plan, w_refs, buffer, sems, 0)
        for copy in copies:
            copy.start()
        tokens[:local] = own[...]
        tokens[local:] = other[...]
        for copy in copies:
            copy.wait()
        for tile in range(half // 256):
            flow = dot_nt(tokens[...], buffer[tile * 256 : (tile + 1) * 256, :]).astype(BF)
            for part in range(256 // group):
                slab[tile * 256 // group + part] = flow[
                    :, part * group : (part + 1) * group
                ].reshape(2, local, group)
        z = lax.axis_index(CTX)
        run_copies(
            [
                pltpu.make_async_copy(slab.at[lax.bitwise_xor(z, k)], slabs[k], out_sems.at[k])
                for k in range(ctx)
            ]
        )

    return call(
        kernel,
        [shape((2, local, group), BF)] * ctx,
        [ANY] * ctx,
        [
            pltpu.VMEM((half, width), BF),
            pltpu.VMEM((2 * local, width), BF),
            pltpu.VMEM((ctx, 2, local, group), BF),
            pltpu.SemaphoreType.DMA((pieces,)),
            pltpu.SemaphoreType.DMA((ctx,)),
        ],
        [f_own, f_other, *weight.arrays],
        [VM] * 2 + [ANY] * pieces,
        2 * 2 * local * half * width,
        24,
    )


def attend_back(slabs, grad_slabs, start_row, tables, carried):
    ctx = len(grad_slabs)
    _, local, group = grad_slabs[0].shape
    span = ctx * local
    parts = len(slabs)
    heads = group // HD
    first = carried is not None

    def kernel(*refs):
        starts, cos, low, high = refs[:4]
        at = 4
        carry_in = None
        if first:
            carry_in = refs[at]
            at += 1
        ins = refs[at : at + parts]
        at += parts
        grads = refs[at : at + ctx]
        outs = refs[at + ctx : at + 2 * ctx]
        at += 2 * ctx
        carry_out = None
        if not first:
            carry_out = refs[at]
            at += 1
        whole, flow_in, slab, key_sum, value_sum, sems, out_sems = refs[at:]
        z = lax.axis_index(CTX)
        copies = []
        if parts == 1:
            copies.append(pltpu.make_async_copy(ins[0], whole, sems.at[0]))
        for k in range(ctx):
            to = pl.ds(pl.multiple_of(lax.bitwise_xor(z, k) * local, 16), local)
            if parts > 1:
                copies.append(
                    pltpu.make_async_copy(ins[k], whole.at[:, :, to, :], sems.at[k])
                )
            copies.append(
                pltpu.make_async_copy(grads[k], flow_in.at[:, to, :], sems.at[ctx + k])
            )
        run_copies(copies)
        lane = lax.broadcasted_iota(jnp.int32, (1, group), 1) // HD
        line = lax.broadcasted_iota(jnp.int32, (group, 1), 0) // HD

        def row_step(row, carry):
            key_sum[...] = jnp.zeros_like(key_sum)
            value_sum[...] = jnp.zeros_like(value_sum)
            key_turned = whole[1, row].astype(F32).T.astype(BF)
            for block in range(ctx):
                keys = (block + 1) * local
                here = slice(block * local, keys)
                query = whole[0, row, here, :] * SCORE_SCALE
                grad = flow_in[row, here, :]
                key = whole[1, row, :keys, :]
                value = whole[2, row, :keys, :]
                k_at = lax.broadcasted_iota(jnp.int32, (keys, local), 0)
                q_at = lax.broadcasted_iota(jnp.int32, (keys, local), 1) + block * local
                allowed = (k_at <= q_at) & (k_at >= starts[row, :, here])
                turned = None
                for head in range(heads):
                    mine = lane == head
                    q_head = jnp.where(mine, query, jnp.zeros_like(query))
                    g_head = jnp.where(mine, grad, jnp.zeros_like(grad))
                    scores = jnp.where(allowed, dot_nt(key, q_head), MASK_FILL)
                    top = jnp.max(scores, axis=0, keepdims=True)
                    powers = jnp.exp(scores - top)
                    total = jnp.sum(powers, axis=0, keepdims=True)
                    probs = powers * (1.0 / total)
                    grad_probs = dot_nt(value, g_head)
                    delta = jnp.sum(probs * grad_probs, axis=0, keepdims=True)
                    grad_scores = (probs * (grad_probs - delta)).astype(BF)
                    value_sum[:keys] += dot(probs.astype(BF), g_head)
                    key_sum[:keys] += dot(grad_scores, q_head)
                    part = dot(key_turned[:, :keys], grad_scores)
                    turned = part if turned is None else jnp.where(line == head, part, turned)
                grad_query = turned.T * SCORE_SCALE
                slab[block, 0, row] = rope(
                    grad_query, cos[row, here, :], -low[row, here, :], -high[row, here, :]
                ).astype(BF)
            for block in range(ctx):
                here = slice(block * local, (block + 1) * local)
                slab[block, 1, row] = rope(
                    key_sum[here, :], cos[row, here, :], -low[row, here, :], -high[row, here, :]
                ).astype(BF)
                if first:
                    total_value = value_sum[here, :] + carry_in[row, here, :]
                else:
                    total_value = 0.5 * value_sum[here, :]
                    carry_out[row, here, :] = total_value
                slab[block, 2, row] = total_value.astype(BF)
            return carry

        lax.fori_loop(0, 2, row_step, 0)
        run_copies(
            [
                pltpu.make_async_copy(slab.at[lax.bitwise_xor(z, k)], outs[k], out_sems.at[k])
                for k in range(ctx)
            ]
        )

    args = [start_row, *tables]
    specs = [VM] * 4
    outs = [shape((3, 2, local, group), BF)] * ctx
    out_specs = [ANY] * ctx
    if first:
        args.append(carried)
        specs.append(VM)
    else:
        outs.append(shape((2, span, group), F32))
        out_specs.append(VM)
    got = call(
        kernel,
        outs,
        out_specs,
        [
            pltpu.VMEM((3, 2, span, group), BF),
            pltpu.VMEM((2, span, group), BF),
            pltpu.VMEM((ctx, 3, 2, local, group), BF),
            pltpu.VMEM((span, group), F32),
            pltpu.VMEM((span, group), F32),
            pltpu.SemaphoreType.DMA((2 * ctx,)),
            pltpu.SemaphoreType.DMA((ctx,)),
        ],
        [*args, *slabs, *grad_slabs],
        specs + [ANY] * (parts + ctx),
        2 * 5 * 2 * heads * span * span * 128,
        48,
    )
    return got[:ctx], (None if first else got[ctx])


def project_back(slabs, weight):
    ctx = len(slabs)
    _, _, local, group = slabs[0].shape
    half = ctx * group
    width = 2 * half
    pieces = len(weight.arrays)
    plan = weight.plan

    def kernel(*refs):
        ins = refs[:ctx]
        w_refs = refs[ctx : ctx + pieces]
        own, other, joined, buffer, landed, sems = refs[ctx + pieces :]
        z = lax.axis_index(CTX)
        copies = weight_copies(plan, w_refs, buffer, sems, ctx)
        for k in range(ctx):
            copies.append(
                pltpu.make_async_copy(ins[k], landed.at[lax.bitwise_xor(z, k)], sems.at[k])
            )
        run_copies(copies)
        for k in range(ctx):
            for kind in range(3):
                base = kind * half + k * group
                joined[:, base : base + group] = landed[k, kind].reshape(2 * local, group)

        def step(tile, carry):
            rows = pl.ds(pl.multiple_of(tile * 256, 256), 256)
            halves_out(dot_nt(joined[...], buffer[rows, :]), own, other, rows, local)
            return carry

        lax.fori_loop(0, width // 256, step, 0)

    return call(
        kernel,
        [
            shape((local, width), F32),
            shape((local, width), BF),
            shape((2 * local, 3 * half), BF),
        ],
        [VM] * 3,
        [
            pltpu.VMEM((width, 3 * half), BF),
            pltpu.VMEM((ctx, 3, 2, local, group), BF),
            pltpu.SemaphoreType.DMA((ctx + pieces,)),
        ],
        [*slabs, *weight.arrays],
        [ANY] * (ctx + pieces),
        2 * 2 * local * 3 * half * width,
        40,
    )


def weight_grad(left, right, chips):
    lefts, rights = list(left), list(right)
    tall = lefts[0].shape[1]
    wide = rights[0].shape[1]
    tokens = lefts[0].shape[0] * len(lefts)
    rows = tall // chips
    halved = wide // 2
    split = chips == 4

    def kernel(*refs):
        l_refs = refs[: len(lefts)]
        r_refs = refs[len(lefts) : len(lefts) + len(rights)]
        at = len(lefts) + len(rights)
        count = 4 if split else chips
        outs = refs[at : at + count]
        grads, l_buf, r_buf, sems = refs[at + count :]
        if len(lefts) == 2:
            l_buf[: tokens // 2] = l_refs[0][...]
            l_buf[tokens // 2 :] = l_refs[1][...]
            l_now = l_buf
        else:
            l_now = l_refs[0]
        if len(rights) == 2:
            r_buf[: tokens // 2] = r_refs[0][...]
            r_buf[tokens // 2 :] = r_refs[1][...]
            r_now = r_buf
        else:
            r_now = r_refs[0]

        def tile_step(base, size):
            turned = l_now[:, pl.ds(base, size)]
            for start in range(0, wide, 512):
                stop = min(start + 512, wide)
                grads[pl.ds(base, size), start:stop] = dot_tn(
                    turned, r_now[:, start:stop]
                ).astype(BF)

        def step(tile, carry):
            tile_step(pl.multiple_of(tile * 256, 256), 256)
            return carry

        lax.fori_loop(0, tall // 256, step, 0)
        if tall % 256:
            tile_step(tall // 256 * 256, tall % 256)
        chip = chip_index()

        def block(k):
            return pl.ds(pl.multiple_of(lax.bitwise_xor(chip, k) * rows, 16), rows)

        copies = []
        if split:
            for which, order in enumerate(((1, 3), (0, 2), (2, 3), (0, 1))):
                columns = pl.ds((which // 2) * halved, halved)
                for slot, k in enumerate(order):
                    copies.append(
                        pltpu.make_async_copy(
                            grads.at[block(k), columns],
                            outs[which].at[slot],
                            sems.at[2 * which + slot],
                        )
                    )
        else:
            for k in range(chips):
                copies.append(
                    pltpu.make_async_copy(grads.at[block(k), :], outs[k], sems.at[k])
                )
        run_copies(copies)

    if split:
        outs = [shape((2, rows, halved), BF)] * 4
    else:
        outs = [shape((rows, wide), BF)] * chips
    small = (16, 128)
    return call(
        kernel,
        outs,
        [ANY] * len(outs),
        [
            pltpu.VMEM((tall, wide), BF),
            pltpu.VMEM((tokens, tall) if len(lefts) == 2 else small, BF),
            pltpu.VMEM((tokens, wide) if len(rights) == 2 else small, BF),
            pltpu.SemaphoreType.DMA((8 if split else chips,)),
        ],
        [*lefts, *rights],
        [VM] * (len(lefts) + len(rights)),
        2 * tokens * tall * wide,
        48,
    )


K_B = "B"
K_F = "F"
K_G1 = "G1"
K_G2 = "G2"
K_G3 = "G3"
K_I = "I"
K_O = "O"
K_R = "R"
K_S = "S"
K_T = "T"
K_W = "W"
K_X = "X"
K_att = "att"
K_d = "d"
K_dW = "dW"
K_dn = "dn"
K_dos = "dos"
K_end = "end"
K_g = "g"
K_gW = "gW"
K_ga = "ga"
K_gb = "gb"
K_gu = "gu"
K_mixb = "mixb"
K_mlp = "mlp"
K_n1 = "n1"
K_nrm = "nrm"
K_nrm1 = "nrm1"
K_nrm2 = "nrm2"
K_o = "o"
K_oW = "oW"
K_out = "out"
K_pb = "pb"
K_prj = "prj"
K_q = "q"
K_qW = "qW"
K_qss = "qss"
K_stg0 = "stg0"
K_stg1 = "stg1"
K_tab = "tab"

FORE_ORDER = (
    (K_B, K_q, 0), (K_stg0, 0), (K_n1, 0), (K_tab, 0), (K_F, K_q, 0),
    (K_B, K_o, 0), (K_R, K_q, 0), (K_B, K_g, 0), (K_prj, 0), (K_stg1, 0),
    (K_F, K_o, 0), (K_qss, 0), (K_att, 0, 0), (K_F, K_g, 0), (K_B, K_d, 0),
    (K_att, 0, 1), (K_B, K_q, 1), (K_R, K_g, 0), (K_out, 0), (K_F, K_d, 0),
    (K_nrm, 0), (K_gu, 0), (K_F, K_q, 1), (K_B, K_o, 1), (K_R, K_d, 0),
    (K_dn, 0), (K_R, K_q, 1), (K_end, 0), (K_B, K_g, 1), (K_prj, 1),
    (K_F, K_o, 1), (K_qss, 1), (K_att, 1, 0), (K_F, K_g, 1), (K_B, K_d, 1),
    (K_att, 1, 1), (K_R, K_g, 1), (K_out, 1), (K_F, K_d, 1), (K_nrm, 1),
    (K_R, K_d, 1), (K_gu, 1), (K_dn, 1), (K_end, 1),
)
AIDED = ((K_q, 0), (K_g, 0), (K_d, 0), (K_q, 1), (K_g, 1), (K_d, 1),)


class Link:
    def __init__(self, source, target, arriving, sems, slot, axis, bit):
        device = {axis: lax.bitwise_xor(lax.axis_index(axis), bit)}

        def make(to):
            return pltpu.make_async_remote_copy(
                src_ref=source,
                dst_ref=to,
                send_sem=sems.at[0, slot],
                recv_sem=sems.at[1, slot],
                device_id=device,
                device_id_type=pl.DeviceIdType.MESH,
            )

        self.out = make(target)
        self.into = make(arriving)
        self.flying = False

    def start(self):
        self.out.start()
        self.flying = True
        return self

    def arrived(self):
        self.into.wait_recv()

    def sent(self):
        if self.flying:
            self.out.wait_send()
        self.flying = False


def enter(fsdp_bits, ctx_bits):
    barrier = pltpu.get_barrier_semaphore()
    for axis, bits in ((FSDP, fsdp_bits), (CTX, ctx_bits)):
        for bit in bits:
            pl.semaphore_signal(
                barrier,
                inc=1,
                device_id={axis: lax.bitwise_xor(lax.axis_index(axis), bit)},
                device_id_type=pl.DeviceIdType.MESH,
            )
    pl.semaphore_wait(barrier, len(fsdp_bits) + len(ctx_bits))


def turn(x, cosines, sines, direction):
    width, pairs = x.shape[-1], HD // 2
    lane = lax.broadcasted_iota(jnp.int32, (1, width), 1)
    ahead = pltpu.roll(x, width - pairs, 1)
    behind = pltpu.roll(x, pairs, 1)
    other = jnp.where(lax.rem(lane, HD) < pairs, -ahead, behind)
    return x * cosines + other * (sines if direction > 0 else -sines)


def rms(total, gain):
    factor = lax.rsqrt(jnp.mean(total * total, axis=1, keepdims=True) + EPSILON)
    return (total * factor * gain).astype(BF)


def forward_pass(tokens, doc_lengths, gains, w_qkv, w_out, w_gate, w_up, w_down):
    local, width = tokens.shape
    layers, block, _ = w_qkv.shape
    hidden = w_gate.shape[2]
    hid = hidden // 2
    hid_block = w_down.shape[1]
    half = width // 2
    shards, ctx = lax.axis_size(FSDP), lax.axis_size(CTX)
    chips = shards // 2
    group = half // ctx
    span = ctx * local
    heads = group // HD
    both = 2 * local
    documents = doc_lengths.shape[1]
    def kernel(*refs):
        (tok, lens, gain_in, qkv_in, out_in, gate_in, up_in, down_in) = refs[:8]
        (wq_o, wo_o, wg_o, wd_o, n1_o, n2_o, whole_o, mix_o, mid_o, stream_o) = refs[8:18]
        (act_o, kept_o, gain_o, cos_o, sin_o, start_o, final_o) = refs[18:25]
        (wq, wo, wg, wd, qkv_raw, gu_raw, q_stage, g_stage) = refs[25:33]
        (n1, n2, whole, slab, mixed, landed, value, mix, mid, stream) = refs[33:43]
        (act, kept, part, other, got, gbuf, lens_all, cos, sin, start) = refs[43:53]
        (sems, local_sems, save_sems) = refs[53:]
        f = lax.axis_index(FSDP)
        z = lax.axis_index(CTX)
        core = lax.rem(f, 2)
        chip = f // 2
        flights = []
        saves = []

        def link(source, target, arriving, axis, bit):
            made = Link(source, target, arriving, sems, len(flights), axis, bit)
            flights.append(made)
            return made

        def save(source, target):
            copy = pltpu.make_async_copy(source, target, save_sems.at[len(saves)])
            copy.start()
            saves.append(copy)
            return len(saves) - 1

        def saved(number):
            if saves[number] is not None:
                saves[number].wait()
            saves[number] = None

        def rows(index, count):
            return pl.ds(pl.multiple_of(index * count, 16), count)

        def fx(bit):
            return lax.bitwise_xor(f, bit)

        def cx(bit):
            return lax.bitwise_xor(chip, bit)

        odd = lax.rem(z, 2)

        def spread_far(weight, at, passed_on, far, columns, aided):
            weight.third = []
            if not aided:
                weight.second = [
                    link(at(one), at(one), at(to), FSDP, bit)
                    for one, to, bit in zip(passed_on, far, (4, 2))
                ]
                return
            some = pl.ds(pl.multiple_of(odd * (columns // 2), 128), columns // 2)
            rest = pl.ds(pl.multiple_of((1 - odd) * (columns // 2), 128), columns // 2)
            weight.second = []
            for one, to, bit in zip(passed_on, far, (4, 2)):
                source = at(one).at[:, some]
                weight.second.append(link(source, source, at(to).at[:, some], FSDP, bit))
                mine = at(to).at[:, some]
                weight.third.append(link(mine, mine, at(to).at[:, rest], CTX, 1))

        class Halved:
            def __init__(self, buffer, stage, aided):
                def at(index):
                    return buffer.at[rows(index, block), :]

                self.first = [
                    link(stage, at(f), at(fx(bit)), FSDP, bit) for bit in (1, 3, 5)
                ] + [link(at(f), at(f), at(fx(bit)), FSDP, bit) for bit in (2, 4)]
                far = 2 * cx(3)
                spread_far(self, at, (2 * cx(1), 2 * cx(2) + 1), (far, far + 1), buffer.shape[1], aided)

        class Rowed:
            def __init__(self, buffer, source, count, aided):
                small = count // 2

                def at(index):
                    return buffer.at[rows(index, count), :]

                def side(index, which):
                    begin = pl.multiple_of(index * count + which * small, 16)
                    return buffer.at[pl.ds(begin, small), :]

                self.first = [
                    link(source, at(chip), at(cx(bit // 2)), FSDP, bit) for bit in (2, 4)
                ]
                far = cx(3)
                spread_far(
                    self,
                    lambda spot: side(*spot),
                    ((cx(1), 0), (cx(2), 1)),
                    ((far, 0), (far, 1)),
                    buffer.shape[1],
                    aided,
                )

        def begin(weight):
            for one in weight.first:
                one.start()

        def forward(weight):
            for one in weight.first:
                one.arrived()
            for one in weight.second:
                one.start()

        def relay(weight):
            for one in weight.second:
                one.arrived()
            for one in weight.third:
                one.start()

        def finish(weight):
            for one in weight.third or weight.second:
                one.arrived()

        def aided(name, n):
            return (name, n) in AIDED

        weights = {}
        for n in range(layers):
            weights["q", n] = Halved(wq.at[n], q_stage.at[n], aided("q", n))
            weights["g", n] = Halved(wg.at[n], g_stage.at[n], aided("g", n))
            weights["o", n] = Rowed(wo.at[n], out_in.at[n], block, aided("o", n))
            weights["d", n] = Rowed(wd.at[n], down_in.at[n], hid_block, aided("d", n))

        def local_copy(source, target, slot):
            copy = pltpu.make_async_copy(source, target, local_sems.at[slot])
            copy.start()
            return copy

        def choose(first, second):
            return lax.select(core == 0, first, second)

        def stage_qkv(n):
            for kind in range(3):
                for j in range(chips):
                    at = kind * width + 2 * j * block
                    even = qkv_raw[:, at : at + block]
                    odd = qkv_raw[:, at + block : at + 2 * block]
                    to = kind * half + j * block
                    wq[n, rows(f, block), to : to + block] = choose(even, odd)
                    q_stage[n, :, to : to + block] = choose(odd, even)

        def stage_gu(n):
            for which in range(2):
                sets = []
                for lane_core in range(2):
                    parts = []
                    for j in range(chips):
                        at = (2 * j + lane_core) * hid_block
                        parts.append(gu_raw[which, :, at : at + hid_block])
                    sets.append(jnp.concatenate(parts, axis=1))
                to = slice(which * hid, (which + 1) * hid)
                wg[n, rows(f, block), to] = choose(sets[0], sets[1])
                g_stage[n, :, to] = choose(sets[1], sets[0])

        def load(n):
            return [
                local_copy(qkv_in.at[n], qkv_raw, 0),
                local_copy(gate_in.at[n], gu_raw.at[0], 1),
                local_copy(up_in.at[n], gu_raw.at[1], 2),
            ]

        loads = load(0)
        mine = []
        for n in range(layers):
            mine.append(local_copy(out_in.at[n], wo.at[n, rows(chip, block), :], 3 + n))
            mine.append(
                local_copy(down_in.at[n], wd.at[n, rows(chip, hid_block), :], 3 + layers + n)
            )
        spare = 3 + 2 * layers
        loads[0].wait()
        stage_qkv(0)
        gbuf[f] = jnp.concatenate(
            [gain_in[n].astype(F32) for n in range(layers)]
            + [jnp.zeros((8 - 2 * layers, block), F32)]
        )
        lens_all[0] = jnp.concatenate(
            [jnp.broadcast_to(lens[0:1, n : n + 1], (1, 128)) for n in range(documents)]
            + [jnp.zeros((8 - documents, 128), jnp.int32)]
        )
        gain_links = [
            link(gbuf.at[f], gbuf.at[f], gbuf.at[fx(bit)], FSDP, bit) for bit in range(1, shards)
        ]
        lens_link = link(lens_all.at[0], lens_all.at[1], lens_all.at[1], FSDP, 1)
        enter(list(range(1, shards)), list(range(1, ctx)))
        for one in gain_links:
            one.start()
        lens_link.start()
        state = {"loads": loads, "mine": mine, "slab": [[], []], "mix": [[], []], "held": []}

        def op_stg0(n):
            for copy in state["loads"][1:]:
                copy.wait()
            stage_gu(0)
            state["loads"] = load(1)

        def op_stg1(n):
            for copy in state["loads"]:
                copy.wait()
            stage_qkv(1)
            stage_gu(1)

        def gain_row(n):
            return jnp.concatenate([gbuf[s, n : n + 1, :] for s in range(shards)], axis=1)

        def norm_link(buffer, n):
            upper = buffer.at[n, pl.ds(local, local), :]
            return link(buffer.at[n, pl.ds(0, local), :], upper, upper, FSDP, 1)

        def op_n1(n):
            for one in gain_links:
                one.arrived()
            for row in range(2 * layers):
                gain_o[row : row + 1, :] = gain_row(row)
            n1[0, :local] = rms(tok[...].astype(F32), gain_row(0))
            state["norm"] = norm_link(n1, 0).start()

        pairs = HD // 2
        lane = lax.broadcasted_iota(jnp.int32, (1, 128), 1)
        frequency = jnp.exp((-math.log(10000.0) / pairs) * lax.rem(lane, pairs).astype(F32))

        def table_step(index, carry):
            r = index // ctx
            piece = lax.rem(index, ctx)
            to = rows(piece, local)
            at = lax.broadcasted_iota(jnp.int32, (local, 128), 0) + piece * local
            first = jnp.zeros((local, 128), jnp.int32)
            end = jnp.zeros((1, 128), jnp.int32)
            for j in range(documents):
                end = end + lens_all[r, j : j + 1, :]
                first = jnp.where(at >= end, end, first)
            start[r, to, :] = first
            angle = (at - first).astype(F32) * frequency
            sin[r, to, :] = jnp.sin(angle)
            cos[r, to, :] = jnp.cos(angle)
            return carry

        def op_tab(n):
            lens_link.arrived()
            lax.fori_loop(0, 2 * ctx, table_step, 0)
            for source, target in ((cos, cos_o), (sin, sin_o), (lens_all, start_o)):
                save(source, target)

        here_rows = rows(z, local)
        lane_head = lax.broadcasted_iota(jnp.int32, (1, group), 1) // HD

        def do_project(n):
            for tile in range(3 * half // 256):
                acc = dot(n1[n], wq[n, :, tile * 256 : (tile + 1) * 256])
                kind = tile * 256 // half
                for sub in range(256 // group):
                    column = tile * 256 - kind * half + sub * group
                    for r in range(2):
                        x = acc[r * local : (r + 1) * local, sub * group : (sub + 1) * group]
                        at = (slice(r * local, (r + 1) * local), slice(column, column + group))
                        if kind < 2:
                            x = turn(x, cos[r, here_rows, :], sin[r, here_rows, :], 1)
                        elif n > 0:
                            x = 0.5 * x + 0.5 * value[at].astype(F32)
                        x = x.astype(BF)
                        if kind == 2 and n == 0:
                            value[at] = x
                        slab[column // group, kind, r] = x

        def slab_links(n, r):
            made = []
            for bit in range(1, ctx):
                to = lax.bitwise_xor(z, bit)
                made.append(
                    link(
                        slab.at[to, :, r],
                        whole.at[n, :, r, rows(z, local), :],
                        whole.at[n, :, r, rows(to, local), :],
                        CTX,
                        bit,
                    )
                )
            return made

        def mixed_links(n, r):
            made = []
            for bit in range(1, ctx):
                to = lax.bitwise_xor(z, bit)
                made.append(
                    link(mixed.at[n, to, r], landed.at[n, z, r], landed.at[n, to, r], CTX, bit)
                )
            return made

        def do_attend(n, r):
            if True:
                for piece in range(ctx):
                    keys = (piece + 1) * local
                    here = slice(piece * local, keys)
                    query = whole[n, 0, r, here, :] * SCORE_SCALE
                    key = whole[n, 1, r, :keys, :]
                    val = whole[n, 2, r, :keys, :]
                    k_at = lax.broadcasted_iota(jnp.int32, (local, keys), 1)
                    q_at = lax.broadcasted_iota(jnp.int32, (local, keys), 0) + piece * local
                    allowed = (k_at <= q_at) & (k_at >= start[r, here, 0:1])
                    result = None
                    for head in range(heads):
                        q_head = jnp.where(lane_head == head, query, jnp.zeros_like(query))
                        scores = jnp.where(allowed, dot_nt(q_head, key), MASK_FILL)
                        top = jnp.max(scores, axis=1, keepdims=True)
                        powers = jnp.exp(scores - top)
                        total = jnp.sum(powers, axis=1, keepdims=True)
                        probs = (powers * (1.0 / total)).astype(BF)
                        out = dot(probs, val)
                        result = out if head == 0 else jnp.where(lane_head == head, out, result)
                    mixed[n, piece, r] = result.astype(BF)

        last_sum = [None]

        def partial_sums(n, which, left, weight):
            if last_sum[0] is not None:
                last_sum[0].sent()

            def step(tile, carry):
                columns = rows(tile, 256)
                product = dot(left[...], weight[:, columns])
                part[:, columns] = product[:local]
                other[:, columns] = product[local:].astype(BF)
                return carry

            lax.fori_loop(0, width // 256, step, 0)
            to = got.at[n, which]
            last_sum[0] = link(other, to, to, FSDP, 1).start()
            return last_sum[0]

        def gate_up(n):
            def span_step(base, count):
                here, there = pl.ds(base, count), pl.ds(hid + base, count)
                gate = dot(n2[n], wg[n, :, here])
                up = dot(n2[n], wg[n, :, there])
                kept[:, here] = gate.astype(BF)
                kept[:, there] = up.astype(BF)
                act[:, here] = (gate * jax.nn.sigmoid(gate) * up).astype(BF)

            def step(tile, carry):
                span_step(pl.multiple_of(tile * 256, 128), 256)
                return carry

            lax.fori_loop(0, hid // 256, step, 0)
            if hid % 256:
                span_step(hid // 256 * 256, hid % 256)

        def op_prj(n):
            finish(weights["q", n])
            save(wq.at[n], wq_o.at[n])
            state["norm"].arrived()
            save(n1.at[n], n1_o.at[n])
            for one in state["slab"][0] + state["slab"][1]:
                one.sent()
            do_project(n)
            state["slab"] = [slab_links(n, 0), slab_links(n, 1)]
            for one in state["slab"][0]:
                one.start()
            state["own"] = local_copy(slab.at[z], whole.at[n, :, :, here_rows, :], spare)

        def op_qss(n):
            for one in state["slab"][0]:
                one.arrived()
            for one in state["slab"][1]:
                one.start()

        def op_att(n, r):
            if r:
                for one in state["slab"][1]:
                    one.arrived()
                save(whole.at[n], whole_o.at[n])
            else:
                state["own"].wait()
            do_attend(n, r)
            state["mix"][r] = mixed_links(n, r)
            for one in state["mix"][r]:
                one.start()
            if r:
                state["own"] = local_copy(mixed.at[n, z], landed.at[n, z], spare)

        def op_out(n):
            finish(weights["o", n])
            for copy in state["mine"]:
                copy.wait()
            state["mine"] = []
            save(wo.at[n], wo_o.at[n])
            state["own"].wait()
            for one in state["mix"][0] + state["mix"][1]:
                one.arrived()
            for k in range(ctx):
                mix[n, :, k * group : (k + 1) * group] = landed[n, k].reshape(both, group)
            save(mix.at[n], mix_o.at[n])
            state["sums"] = partial_sums(n, 0, mix.at[n], wo.at[n])

        def op_nrm(n):
            base = tok[...].astype(F32) if n == 0 else stream[...]
            state["sums"].arrived()
            total = base + part[...] + got[n, 0].astype(F32)
            mid[n] = total
            n2[n, :local] = rms(total, gain_row(2 * n + 1))
            state["norm"] = norm_link(n2, n).start()
            save(mid.at[n], mid_o.at[n])

        def op_gu(n):
            finish(weights["g", n])
            save(wg.at[n], wg_o.at[n])
            for number in state["held"]:
                saved(number)
            state["norm"].arrived()
            save(n2.at[n], n2_o.at[n])
            gate_up(n)
            state["held"] = [save(act, act_o.at[n]), save(kept, kept_o.at[n])]

        def op_dn(n):
            finish(weights["d", n])
            save(wd.at[n], wd_o.at[n])
            state["sums"] = partial_sums(n, 1, act, wd.at[n])

        def op_end(n):
            state["sums"].arrived()
            total = mid[n] + part[...] + got[n, 1].astype(F32)
            if n + 1 < layers:
                stream[...] = total
                n1[n + 1, :local] = rms(total, gain_row(2 * n + 2))
                state["norm"] = norm_link(n1, n + 1).start()
                save(stream, stream_o)
            else:
                final_o[...] = total.astype(BF)

        chain = {
            "stg0": op_stg0, "stg1": op_stg1, "n1": op_n1, "tab": op_tab, "prj": op_prj,
            "qss": op_qss, "att": op_att, "out": op_out, "nrm": op_nrm, "gu": op_gu,
            "dn": op_dn, "end": op_end,
        }
        moves = {"B": begin, "F": forward, "R": relay}
        for step in FORE_ORDER:
            if step[0] in chain:
                chain[step[0]](*step[1:])
            else:
                moves[step[0]](weights[step[1], step[2]])
        for one in flights:
            one.sent()
        for number in range(len(saves)):
            saved(number)

    def stacked(*dims):
        return (layers, *dims)

    outs = [
        shape(stacked(width, 3 * half), BF),
        shape(stacked(half, width), BF),
        shape(stacked(width, 2 * hid), BF),
        shape(stacked(hid, width), BF),
        shape(stacked(both, width), BF),
        shape(stacked(both, width), BF),
        shape(stacked(3, 2, span, group), BF),
        shape(stacked(both, half), BF),
        shape(stacked(local, width), F32),
        shape((local, width), F32),
        shape(stacked(both, hid), BF),
        shape(stacked(both, 2 * hid), BF),
        shape((2 * layers, width), F32),
        shape((2, span, 128), F32),
        shape((2, span, 128), F32),
        shape((2, 8, 128), jnp.int32),
        shape((local, width), BF),
    ]
    out_specs = [ANY] * 17
    out_specs[12] = out_specs[16] = VM
    scratch = [
        pltpu.VMEM(stacked(width, 3 * half), BF),
        pltpu.VMEM(stacked(half, width), BF),
        pltpu.VMEM(stacked(width, 2 * hid), BF),
        pltpu.VMEM(stacked(hid, width), BF),
        pltpu.VMEM((block, 3 * width), BF),
        pltpu.VMEM((2, block, hidden), BF),
        pltpu.VMEM(stacked(block, 3 * half), BF),
        pltpu.VMEM(stacked(block, 2 * hid), BF),
        pltpu.VMEM(stacked(both, width), BF),
        pltpu.VMEM(stacked(both, width), BF),
        pltpu.VMEM(stacked(3, 2, span, group), BF),
        pltpu.VMEM((ctx, 3, 2, local, group), BF),
        pltpu.VMEM(stacked(ctx, 2, local, group), BF),
        pltpu.VMEM(stacked(ctx, 2, local, group), BF),
        pltpu.VMEM((both, half), BF),
        pltpu.VMEM(stacked(both, half), BF),
        pltpu.VMEM(stacked(local, width), F32),
        pltpu.VMEM((local, width), F32),
        pltpu.VMEM((both, hid), BF),
        pltpu.VMEM((both, 2 * hid), BF),
        pltpu.VMEM((local, width), F32),
        pltpu.VMEM((local, width), BF),
        pltpu.VMEM(stacked(2, local, width), BF),
        pltpu.VMEM((shards, 8, block), F32),
        pltpu.VMEM((2, 8, 128), jnp.int32),
        pltpu.VMEM((2, span, 128), F32),
        pltpu.VMEM((2, span, 128), F32),
        pltpu.VMEM((2, span, 128), jnp.int32),
        pltpu.SemaphoreType.DMA((2, 112)),
        pltpu.SemaphoreType.DMA((8,)),
        pltpu.SemaphoreType.DMA((32,)),
    ]
    return pl.pallas_call(
        kernel,
        out_shape=outs,
        in_specs=[VM] * 3 + [ANY] * 5,
        out_specs=out_specs,
        scratch_shapes=scratch,
        compiler_params=pltpu.CompilerParams(
            vmem_limit_bytes=62 * MIB, collective_id=0, has_side_effects=True
        ),
        cost_estimate=pl.CostEstimate(
            flops=14 * 10**9, bytes_accessed=60 * MIB, transcendentals=0
        ),
    )(tokens, doc_lengths, gains, w_qkv, w_out, w_gate, w_up, w_down)


BACK_ORDER = (
    (K_dW, 1), (K_mlp, 1), (K_F, K_d, 1, 0), (K_nrm2, 1), (K_F, K_d, 1, 1),
    (K_mixb, 1), (K_gW, 1), (K_oW, 1), (K_T, K_o, 1), (K_dos, 1),
    (K_att, 1, 0), (K_S, K_d, 1, 0), (K_att, 1, 1), (K_T, K_gb, 1), (K_S, K_d, 1, 1),
    (K_F, K_o, 1, 0), (K_F, K_o, 1, 1), (K_F, K_ga, 1, 0), (K_F, K_ga, 1, 1), (K_F, K_gb, 1, 0),
    (K_F, K_gb, 1, 1), (K_pb, 1), (K_qW, 1), (K_nrm1, 1), (K_I, K_d, 1, 0),
    (K_I, K_d, 1, 1), (K_S, K_o, 1, 0), (K_S, K_o, 1, 1), (K_S, K_ga, 1, 0), (K_S, K_ga, 1, 1),
    (K_dW, 0), (K_T, K_d, 0), (K_mlp, 0), (K_I, K_o, 1, 0), (K_X, K_d, 1, 0),
    (K_nrm2, 0), (K_X, K_d, 1, 1), (K_I, K_o, 1, 1), (K_mixb, 0), (K_X, K_o, 1, 0),
    (K_I, K_ga, 1, 0), (K_I, K_ga, 1, 1), (K_F, K_q, 1, 0), (K_F, K_q, 1, 1), (K_X, K_o, 1, 1),
    (K_F, K_d, 0, 0), (K_F, K_d, 0, 1), (K_S, K_gb, 1, 0), (K_S, K_gb, 1, 1), (K_dos, 0),
    (K_att, 0, 0), (K_gW, 0), (K_O, K_d, 1, 0), (K_O, K_o, 1, 0), (K_oW, 0),
    (K_T, K_o, 0), (K_O, K_o, 1, 1), (K_att, 0, 1), (K_W, K_o, 1), (K_O, K_d, 1, 1),
    (K_X, K_ga, 1, 0), (K_X, K_ga, 1, 1), (K_W, K_d, 1), (K_S, K_q, 1, 0), (K_F, K_o, 0, 0),
    (K_F, K_o, 0, 1), (K_S, K_q, 1, 1), (K_I, K_gb, 1, 0), (K_F, K_ga, 0, 0), (K_F, K_ga, 0, 1),
    (K_I, K_gb, 1, 1), (K_F, K_gb, 0, 0), (K_pb, 0), (K_qW, 0), (K_T, K_q, 0),
    (K_nrm1, 0), (K_G1, 0), (K_S, K_d, 0, 0), (K_S, K_d, 0, 1), (K_I, K_q, 1, 0),
    (K_I, K_q, 1, 1), (K_X, K_gb, 1, 0), (K_G2, 0), (K_X, K_gb, 1, 1), (K_O, K_ga, 1, 0),
    (K_O, K_ga, 1, 1), (K_F, K_gb, 0, 1), (K_S, K_o, 0, 0), (K_W, K_ga, 1), (K_S, K_ga, 0, 0),
    (K_S, K_o, 0, 1), (K_S, K_ga, 0, 1), (K_I, K_d, 0, 0), (K_X, K_q, 1, 0), (K_X, K_q, 1, 1),
    (K_O, K_gb, 1, 0), (K_O, K_gb, 1, 1), (K_I, K_d, 0, 1), (K_I, K_o, 0, 0), (K_F, K_q, 0, 0),
    (K_F, K_q, 0, 1), (K_I, K_o, 0, 1), (K_W, K_gb, 1), (K_X, K_d, 0, 0), (K_S, K_gb, 0, 0),
    (K_S, K_gb, 0, 1), (K_X, K_o, 0, 0), (K_I, K_ga, 0, 0), (K_X, K_o, 0, 1), (K_I, K_ga, 0, 1),
    (K_O, K_q, 1, 0), (K_X, K_d, 0, 1), (K_O, K_q, 1, 1), (K_W, K_q, 1), (K_S, K_q, 0, 0),
    (K_S, K_q, 0, 1), (K_O, K_o, 0, 0), (K_O, K_o, 0, 1), (K_I, K_gb, 0, 0), (K_I, K_gb, 0, 1),
    (K_X, K_ga, 0, 0), (K_O, K_d, 0, 0), (K_X, K_ga, 0, 1), (K_W, K_o, 0), (K_O, K_d, 0, 1),
    (K_W, K_d, 0), (K_I, K_q, 0, 0), (K_I, K_q, 0, 1), (K_X, K_gb, 0, 0), (K_X, K_gb, 0, 1),
    (K_O, K_ga, 0, 0), (K_O, K_ga, 0, 1), (K_W, K_ga, 0), (K_X, K_q, 0, 0), (K_X, K_q, 0, 1),
    (K_O, K_gb, 0, 0), (K_O, K_gb, 0, 1), (K_W, K_gb, 0), (K_O, K_q, 0, 0), (K_O, K_q, 0, 1),
    (K_W, K_q, 0), (K_G3, 0),
)
HELD = ((K_o, 1), (K_gb, 1), (K_d, 0), (K_o, 0), (K_q, 0),)
DEFER = True


def backward_pass(saved, tokens, cotangent):
    local, width = tokens.shape
    wq_s, wo_s, wg_s, wd_s = saved[:4]
    layers = wq_s.shape[0]
    half = width // 2
    hid = wd_s.shape[1]
    shards, ctx = lax.axis_size(FSDP), lax.axis_size(CTX)
    chips = shards // 2
    block = width // shards
    hid_block = hid // chips
    group = half // ctx
    span = ctx * local
    heads = group // HD
    both = 2 * local
    documents = 4
    sizes = {
        "d": (hid_block, width),
        "g": (2 * block, 2 * hid),
        "o": (block, width),
        "q": (2 * block, 3 * half),
    }
    names = ("d", "g", "o", "q")
    pieces_of = {"d": ("d",), "g": ("ga", "gb"), "o": ("o",), "q": ("q",)}
    units = [unit for name in names for unit in pieces_of[name]]
    counts = {unit: sizes[unit[0]][0] // len(pieces_of[unit[0]]) for unit in units}

    def kernel(*refs):
        refs = list(refs)

        def take(count):
            out = refs[:count]
            del refs[:count]
            return out

        cot_i, tok_i, lens, gain = take(4)
        wq_i, wo_i, wg_i, wd_i, n1_i, n2_i, whole_i, mix_i, mid_i, stream_i = take(10)
        act_i, kept_i, cos_i, sin_i = take(4)
        grad_o, gain_o, q_o, o_o, gate_o, up_o, d_o = take(7)
        lands = {}
        for unit in units:
            lands[unit] = dict(zip(("x1", "y1", "x2", "y2", "z"), take(5)))
        swap_land = dict(zip(("g", "q"), take(2)))
        wq, wo, wg, wd, act, kept, norm, whole, mix, wide = take(10)
        flow, fgrad, got, do_in, dq_in, part, other, grad, middle = take(9)
        do_out, dq_out, key_sum, value_sum, carry, joined, cos, sin = take(8)
        blocks = dict(zip(names, take(4)))
        finals = dict(zip(names, take(4)))
        tmp, stage, gain_rows, gain_send, gain_land, gain_sum, gain_line = take(7)
        sems, load_sems, tmp_sems, out_sems, own_sems = take(5)
        f = lax.axis_index(FSDP)
        z = lax.axis_index(CTX)
        core = lax.rem(f, 2)
        chip = f // 2
        inner = (z == 1) | (z == 2)
        outer = (z == 0) | (z == 3)
        flights = []

        def link(source, target, arriving, axis, bit):
            made = Link(source, target, arriving, sems, len(flights), axis, bit)
            flights.append(made)
            return made

        def rows(index, count):
            return pl.ds(pl.multiple_of(index * count, 16), count)

        def cx(bit):
            return lax.bitwise_xor(chip, bit)

        loading = {}
        slots = {}

        def load(name, source, target):
            slot = slots.setdefault(name, len(slots))
            copy = pltpu.make_async_copy(source, target, load_sems.at[slot])
            copy.start()
            loading[name] = copy

        def loaded(*wanted):
            for name in wanted:
                if name in loading:
                    loading.pop(name).wait()

        top = layers - 1
        load("cot", cot_i, flow.at[pl.ds(0, local), :])
        load("act", act_i.at[top], act)
        load("wd", wd_i.at[top], wd)
        load("kept", kept_i.at[top], kept)
        load("wg", wg_i.at[top], wg)
        load("wide", mid_i.at[top], wide)
        load("wo", wo_i.at[top], wo)
        load("norm", n2_i.at[top], norm)
        load("mix", mix_i.at[top], mix)
        load("whole", whole_i.at[top], whole)
        load("wq", wq_i.at[top], wq)
        load("cos", cos_i, cos)
        load("sin", sin_i, sin)
        enter(list(range(1, shards)), list(range(1, ctx)))

        def pair_link(buffer):
            upper = buffer.at[pl.ds(local, local), :]
            return link(buffer.at[pl.ds(0, local), :], upper, upper, FSDP, 1)

        loaded("cot")
        e_link = pair_link(flow).start()
        grad[...] = flow[:local].astype(F32)

        class Reduce:
            def __init__(self, unit, n):
                name = unit[0]
                self.name, self.n = name, n
                whole_rows, self.columns = sizes[name]
                self.count = counts[unit]
                self.chunk = pieces_of[name].index(unit) if len(pieces_of[name]) > 1 else None
                self.offset = self.count * (self.chunk or 0)
                self.side = self.columns // 2
                self.blocks, self.final = blocks[name], finals[name]
                self.land = lands[unit]
                left, right = pl.ds(0, self.side), pl.ds(self.side, self.side)
                self.halves = (left, right)

                def row(k):
                    return cx(k) * whole_rows + self.offset

                self.row = row

                def piece(k, columns):
                    at = pl.ds(pl.multiple_of(row(k), 16), self.count)
                    return self.blocks.at[at, columns]

                def into(where, slot=None):
                    ref = self.land[where]
                    return ref.at[n] if slot is None else ref.at[n, slot]

                def hop(source, target, bit):
                    return link(source, target, target, FSDP, bit)

                self.far = (hop(piece(3, left), into("x1", 1), 2), hop(piece(3, right), into("y1", 1), 4))
                self.near = (hop(piece(1, left), into("x1", 0), 2), hop(piece(2, right), into("y1", 0), 4))
                self.next = (hop(piece(2, left), into("y2"), 4), hop(piece(1, right), into("x2"), 2))
                self.line = []
                for side in self.halves:
                    steps = []
                    source = self.final.at[pl.ds(self.offset, self.count), side]
                    for step, bit in ((0, 1), (1, 3), (2, 1)):
                        target = self.land["z"].at[n, step, :, side]
                        steps.append(link(source, target, target, CTX, bit))
                    self.line.append(steps)
                self.swap = None
                if name in swap_land:
                    out = rows(1 - core, block)
                    to = swap_land[name].at[n]
                    self.swap = link(self.final.at[out, :], to, to, FSDP, 1)
                self.complete = 0
                self.held = (unit, n) in HELD

            def fetch(self, *sources):
                copies = []
                for slot, source in enumerate(sources):
                    copy = pltpu.make_async_copy(
                        source,
                        tmp.at[slot, pl.ds(0, self.count), pl.ds(0, self.side)],
                        tmp_sems.at[slot],
                    )
                    copy.start()
                    copies.append(copy)
                for copy in copies:
                    copy.wait()

            def add(self, source, source_row, columns, target, target_row, slots_used):
                def step(tile, carry):
                    at = pl.ds(pl.multiple_of(source_row + tile * 32, 16), 32)
                    total = source[at, columns].astype(F32)
                    here = pl.ds(pl.multiple_of(tile * 32, 16), 32)
                    for slot in slots_used:
                        total = total + tmp[slot, here, : self.side].astype(F32)
                    to = pl.ds(pl.multiple_of(target_row + tile * 32, 16), 32)
                    target[to, columns] = total.astype(BF)
                    return carry

                lax.fori_loop(0, self.count // 32, step, 0)

            def T(self):
                self.far[0].start()
                self.far[1].start()

            def settled(self):
                for one in (*self.far, *self.near, *self.next):
                    one.sent()

            def F(self, h):
                self.far[h].arrived()
                self.fetch(self.land[("x1", "y1")[h]].at[self.n, 1])
                at = self.row(2 - h)
                self.add(self.blocks, at, self.halves[h], self.blocks, at, (0,))
                self.next[h].start()
                if DEFER:
                    self.near[h].start()

            def S(self, h):
                self.near[h].arrived()
                self.next[h].arrived()
                self.fetch(
                    self.land[("x1", "y1")[h]].at[self.n, 0], self.land[("y2", "x2")[h]].at[self.n]
                )
                self.add(self.blocks, self.row(0), self.halves[h], self.final, self.offset, (0, 1))
                pl.when(outer)(self.line[h][0].out.start)

            def I(self, h):
                @pl.when(inner)
                def _():
                    steps = self.line[h]
                    steps[0].into.wait_recv()
                    self.fetch(self.land["z"].at[self.n, 0, :, self.halves[h]])
                    self.add(self.final, self.offset, self.halves[h], self.final, self.offset, (0,))
                    steps[1].out.start()

            def X(self, h):
                @pl.when(inner)
                def _():
                    steps = self.line[h]
                    steps[1].into.wait_recv()
                    self.fetch(self.land["z"].at[self.n, 1, :, self.halves[h]])
                    steps[1].out.wait_send()
                    self.add(self.final, self.offset, self.halves[h], self.final, self.offset, (0,))
                    steps[2].out.start()

            def O(self, h):
                steps = self.line[h]

                @pl.when(outer)
                def _():
                    steps[2].into.wait_recv()
                    steps[0].out.wait_send()
                    copy = pltpu.make_async_copy(
                        self.land["z"].at[self.n, 2, :, self.halves[h]],
                        self.final.at[pl.ds(self.offset, self.count), self.halves[h]],
                        tmp_sems.at[0],
                    )
                    copy.start()
                    copy.wait()

                pl.when(inner)(steps[2].out.wait_send)
                self.complete += 1
                if self.complete == 2 and self.swap is not None:
                    if self.chunk is None:
                        self.swap.out.start()
                    else:
                        pl.when(core != self.chunk)(self.swap.out.start)

            def W(self):
                if self.chunk is None:
                    self.write()
                else:
                    pl.when(core == self.chunk)(self.write)
                    pl.when(core != self.chunk)(self.swap.out.wait_send)

            def write(self):
                n = self.n
                if self.name in ("d", "o"):
                    target = d_o if self.name == "d" else o_o
                    run_copies([pltpu.make_async_copy(self.final, target.at[n], out_sems.at[0])])
                    return
                self.swap.into.wait_recv()
                parts_now = 3 if self.name == "q" else 2
                wide_now = self.columns // parts_now
                places = [
                    (k // 2, pl.ds((k % 2) * block, block), pl.ds(0, wide_now)) for k in range(3)
                ]
                if self.name == "g":
                    places[1] = (1, pl.ds(0, block), pl.ds(0, wide_now))
                run_copies(
                    [
                        pltpu.make_async_copy(
                            swap_land[self.name].at[n, :, pl.ds(k * wide_now, wide_now)],
                            tmp.at[places[k]],
                            out_sems.at[2 + k],
                        )
                        for k in range(parts_now)
                    ]
                )
                mine = rows(core, block)

                def sets(part_now, start_now, count_now):
                    first_at = part_now * wide_now + start_now
                    own = self.final[mine, first_at : first_at + count_now]
                    slot, row_at, _ = places[part_now]
                    theirs = tmp[slot, row_at, start_now : start_now + count_now]
                    return (
                        lax.select(core == 0, own, theirs),
                        lax.select(core == 0, theirs, own),
                    )

                if self.name == "q":
                    for kind in range(3):
                        for j in range(chips):
                            even, odd = sets(kind, j * block, block)
                            to = kind * width + 2 * j * block
                            stage[:, to : to + block] = even
                            stage[:, to + block : to + 2 * block] = odd
                    run_copies([pltpu.make_async_copy(stage, q_o.at[n], out_sems.at[0])])
                else:
                    for which, target in enumerate((gate_o, up_o)):
                        even, odd = sets(which, 0, hid)
                        parts = []
                        for j in range(chips):
                            at = slice(j * hid_block, (j + 1) * hid_block)
                            parts += [even[:, at], odd[:, at]]
                        stage[:, : 2 * hid] = jnp.concatenate(parts, axis=1)
                        run_copies(
                            [
                                pltpu.make_async_copy(
                                    stage.at[:, pl.ds(0, 2 * hid)], target.at[n], out_sems.at[0]
                                )
                            ]
                        )
                if self.chunk is None:
                    self.swap.out.wait_send()

        def grad_tile(target, row, count, left, columns, right, wide_count):
            turned = left[:, columns]
            for begin in range(0, wide_count, 512):
                end = min(begin + 512, wide_count)
                target[pl.ds(row, count), begin:end] = dot_tn(turned, right[:, begin:end]).astype(BF)

        def begin(job, k):
            if k == 3 and not job.held:
                job.T()
            elif k and not DEFER:
                job.near[k - 1].start()

        def compute_blocks(name, n, left, right):
            if not n:
                for unit in pieces_of[name]:
                    jobs[unit, 1].settled()
            count, columns = sizes[name]
            for k in (3, 1, 2, 0):
                row = pl.multiple_of(cx(k) * count, 128)
                grad_tile(blocks[name], row, count, left, pl.ds(row, count), right, columns)
                for unit in pieces_of[name]:
                    begin(jobs[unit, n], k)

        def compute_down(n):
            if not n:
                jobs["d", 1].settled()

            def step(tile, carry):
                row = pl.multiple_of(tile * 256, 128)
                grad_tile(blocks["d"], row, 256, act, pl.ds(row, 256), flow, width)
                return carry

            lax.fori_loop(0, hid // 256, step, 0)
            if hid % 256:
                row = hid // 256 * 256
                grad_tile(blocks["d"], row, hid % 256, act, pl.ds(row, hid % 256), flow, width)
            for k in (3, 1, 2):
                begin(jobs["d", n], k)

        last_sum = [None]

        def partial_sums(which, product):
            if last_sum[0] is not None:
                last_sum[0].sent()

            def step(tile, carry):
                columns = rows(tile, 256)
                value = product(columns)
                part[:, columns] = value[:local]
                other[:, columns] = value[local:].astype(BF)
                return carry

            lax.fori_loop(0, width // 256, step, 0)
            last_sum[0] = link(other, got.at[which], got.at[which], FSDP, 1).start()
            return last_sum[0]

        def norm_step(x, gain_now, gain_row, which, target, low_target):
            factor = lax.rsqrt(jnp.mean(x * x, axis=1, keepdims=True) + EPSILON)
            back = part[...] + got[which].astype(F32)
            scaled = back * gain_now
            gain_rows[gain_row : gain_row + 1, :] = jnp.sum(back * x * factor, axis=0, keepdims=True)
            mean_term = jnp.mean(scaled * x, axis=1, keepdims=True)
            base = grad[...] if target is middle else middle[...]
            result = base + factor * scaled - x * (factor * factor * factor * mean_term)
            target[...] = result
            if low_target is not None:
                low_target[:local] = result.astype(BF)

        def mlp_back():
            def span_step(base, count):
                here, there = pl.ds(base, count), pl.ds(hid + base, count)
                back = dot_nt(flow[...], wd[here, :])
                gate = kept[:, here].astype(F32)
                up = kept[:, there].astype(F32)
                sig = jax.nn.sigmoid(gate)
                kept[:, here] = (back * up * sig * (1.0 + gate * (1.0 - sig))).astype(BF)
                kept[:, there] = (back * gate * sig).astype(BF)

            def step(tile, carry):
                span_step(pl.multiple_of(tile * 256, 128), 256)
                return carry

            lax.fori_loop(0, hid // 256, step, 0)
            if hid % 256:
                span_step(hid // 256 * 256, hid % 256)

        lane_head = lax.broadcasted_iota(jnp.int32, (1, group), 1) // HD
        line_head = lax.broadcasted_iota(jnp.int32, (group, 1), 0) // HD

        def start_row(r):
            at = lax.broadcasted_iota(jnp.int32, (1, span), 1)
            first = jnp.zeros((1, span), jnp.int32)
            end = jnp.zeros((1, 1), jnp.int32)
            for j in range(documents):
                end = end + lens[r, j : j + 1, 0:1]
                first = jnp.where(at >= end, end, first)
            return first

        def attend_row(n, r):
            if True:
                key_sum[...] = jnp.zeros_like(key_sum)
                value_sum[...] = jnp.zeros_like(value_sum)
                key_turned = whole[1, r].astype(F32).T.astype(BF)
                starts = start_row(r)
                for piece in range(ctx):
                    keys = (piece + 1) * local
                    here = slice(piece * local, keys)
                    query = whole[0, r, here, :] * SCORE_SCALE
                    back = do_in[r, here, :]
                    key = whole[1, r, :keys, :]
                    value = whole[2, r, :keys, :]
                    k_at = lax.broadcasted_iota(jnp.int32, (keys, local), 0)
                    q_at = lax.broadcasted_iota(jnp.int32, (keys, local), 1) + piece * local
                    allowed = (k_at <= q_at) & (k_at >= starts[:, here])
                    turned = None
                    for head in range(heads):
                        q_head = jnp.where(lane_head == head, query, jnp.zeros_like(query))
                        b_head = jnp.where(lane_head == head, back, jnp.zeros_like(back))
                        scores = jnp.where(allowed, dot_nt(key, q_head), MASK_FILL)
                        peak = jnp.max(scores, axis=0, keepdims=True)
                        powers = jnp.exp(scores - peak)
                        total = jnp.sum(powers, axis=0, keepdims=True)
                        probs = powers * (1.0 / total)
                        back_probs = dot_nt(value, b_head)
                        delta = jnp.sum(probs * back_probs, axis=0, keepdims=True)
                        back_scores = (probs * (back_probs - delta)).astype(BF)
                        value_sum[:keys] += dot(probs.astype(BF), b_head)
                        key_sum[:keys] += dot(back_scores, q_head)
                        sub = dot(key_turned[:, :keys], back_scores)
                        turned = sub if head == 0 else jnp.where(line_head == head, sub, turned)
                    back_query = turned.T * SCORE_SCALE
                    dq_out[piece, 0, r] = turn(
                        back_query, cos[r, here, :], sin[r, here, :], -1
                    ).astype(BF)
                for piece in range(ctx):
                    here = slice(piece * local, (piece + 1) * local)
                    dq_out[piece, 1, r] = turn(
                        key_sum[here, :], cos[r, here, :], sin[r, here, :], -1
                    ).astype(BF)
                    if n == top:
                        back_value = 0.5 * value_sum[here, :]
                        carry[r, here, :] = back_value
                    else:
                        back_value = value_sum[here, :] + carry[r, here, :]
                    dq_out[piece, 2, r] = back_value.astype(BF)

        def spread(source_of, target_of):
            made = []
            for bit in range(1, ctx):
                to = lax.bitwise_xor(z, bit)
                made.append(link(source_of(to), target_of(z), target_of(to), CTX, bit))
            return made

        def own_copy(r, source, target):
            copy = pltpu.make_async_copy(source, target, own_sems.at[r])
            copy.start()
            return copy

        def do_links(r):
            return spread(lambda to: do_out.at[to, r], lambda at: do_in.at[r, rows(at, local), :])

        def dq_links(r):
            return spread(lambda to: dq_out.at[to, :, r], lambda at: dq_in.at[at, :, r])

        jobs = {(unit, n): Reduce(unit, n) for n in (1, 0) for unit in units}
        state = {"e": e_link, "f": None, "do": [[], []], "dq": [[], []], "own": [None, None]}

        def gain_value(n):
            return gain[n : n + 1, :]

        def await_flow(n):
            if state["e"] is not None:
                state["e"].arrived()
                state["sent"] = state["e"]
                state["e"] = None

        def op_dW(n):
            loaded("act")
            await_flow(n)
            compute_down(n)
            if n:
                load("act", act_i.at[0], act)

        def op_mlp(n):
            loaded("wd", "kept")
            await_flow(n)
            mlp_back()
            if n:
                load("wd", wd_i.at[0], wd)
            loaded("wg")
            state["sums"] = partial_sums(0, lambda columns: dot_nt(kept[...], wg[columns, :]))
            if n:
                load("wg", wg_i.at[0], wg)

        def op_nrm2(n):
            loaded("wide")
            if state["f"] is not None:
                state["f"].sent()
            state["sums"].arrived()
            norm_step(wide[...], gain_value(2 * n + 1), 2 * n + 1, 0, middle, fgrad)
            state["f"] = pair_link(fgrad).start()
            state["fresh"] = True
            if n:
                load("wide", stream_i, wide)

        def await_fgrad():
            if state["fresh"]:
                state["f"].arrived()
            state["fresh"] = False

        def op_mixb(n):
            loaded("wo")
            for one in state["do"][0] + state["do"][1]:
                one.sent()
            await_fgrad()
            for tile in range(half // 256):
                back = dot_nt(fgrad[...], wo[tile * 256 : (tile + 1) * 256, :]).astype(BF)
                for sub in range(256 // group):
                    do_out[tile * 256 // group + sub] = back[
                        :, sub * group : (sub + 1) * group
                    ].reshape(2, local, group)
            if n:
                load("wo", wo_i.at[0], wo)
            state["do"] = [do_links(0), do_links(1)]
            for one in state["do"][0]:
                one.start()
            for r in range(2):
                state["own"][r] = own_copy(r, do_out.at[z, r], do_in.at[r, rows(z, local), :])

        def op_dos(n):
            for one in state["do"][0]:
                one.arrived()
            for one in state["do"][1]:
                one.start()

        def op_gW(n):
            loaded("norm")
            compute_blocks("g", n, norm, kept)
            load("norm", n1_i.at[n], norm)
            if n:
                load("kept", kept_i.at[0], kept)

        def op_oW(n):
            loaded("mix")
            await_fgrad()
            compute_blocks("o", n, mix, fgrad)
            if n:
                load("mix", mix_i.at[0], mix)

        def op_att(n, r):
            loaded("whole", "cos", "sin")
            state["own"][r].wait()
            if r:
                for one in state["do"][r]:
                    one.arrived()
            for one in state["dq"][r]:
                one.sent()
            attend_row(n, r)
            if n and r:
                load("whole", whole_i.at[0], whole)
            state["dq"][r] = dq_links(r)
            for one in state["dq"][r]:
                one.start()
            state["own"][r] = own_copy(r, dq_out.at[z, :, r], dq_in.at[z, :, r])

        def op_pb(n):
            loaded("wq")
            for r in range(2):
                state["own"][r].wait()
                for one in state["dq"][r]:
                    one.arrived()
            for k in range(ctx):
                for kind in range(3):
                    base = kind * half + k * group
                    joined[:, base : base + group] = dq_in[k, kind].reshape(both, group)
            state["sums"] = partial_sums(1, lambda columns: dot_nt(joined[...], wq[columns, :]))
            if n:
                load("wq", wq_i.at[0], wq)

        def op_qW(n):
            loaded("norm")
            compute_blocks("q", n, norm, joined)
            if n:
                load("norm", n2_i.at[0], norm)

        def op_nrm1(n):
            if not n:
                state["f"].sent()
                load("tok", tok_i, fgrad.at[pl.ds(0, local), :])
                loaded("tok")
            loaded("wide")
            state["sent"].sent()
            state["sums"].arrived()
            if n:
                norm_step(wide[...], gain_value(2 * n), 2 * n, 1, grad, flow)
                state["e"] = pair_link(flow).start()
                load("wide", mid_i.at[0], wide)
            else:
                norm_step(fgrad[:local].astype(F32), gain_value(0), 0, 1, grad_o, None)

        def op_G1(n):
            for s in range(shards):
                gain_send[s] = jnp.concatenate(
                    [gain_rows[:4, s * block : (s + 1) * block], jnp.zeros((4, block), F32)]
                )
            state["gain"] = []
            for bit in range(1, shards):
                to = lax.bitwise_xor(f, bit)
                state["gain"].append(
                    link(gain_send.at[to], gain_land.at[f], gain_land.at[to], FSDP, bit).start()
                )
            gain_land[f] = gain_send[f]

        def op_G2(n):
            for one in state["gain"]:
                one.arrived()
            total = gain_land[0]
            for s in range(1, shards):
                total = total + gain_land[s]
            gain_sum[...] = total
            state["line"] = []
            for bit in range(1, ctx):
                to = lax.bitwise_xor(z, bit)
                state["line"].append(
                    link(gain_sum, gain_line.at[z], gain_line.at[to], CTX, bit).start()
                )
            gain_line[z] = total

        def op_G3(n):
            for one in state["line"]:
                one.arrived()
            total = gain_line[0]
            for k in range(1, ctx):
                total = total + gain_line[k]
            gain_o[...] = total[: 2 * layers]

        chain = {
            "dW": op_dW, "mlp": op_mlp, "nrm2": op_nrm2, "mixb": op_mixb, "gW": op_gW,
            "oW": op_oW, "att": op_att, "dos": op_dos, "pb": op_pb, "qW": op_qW, "nrm1": op_nrm1,
            "G1": op_G1, "G2": op_G2, "G3": op_G3,
        }
        for step in BACK_ORDER:
            if step[0] in chain:
                chain[step[0]](*step[1:])
            elif step[0] in ("W", "T"):
                getattr(jobs[step[1], step[2]], step[0])()
            else:
                getattr(jobs[step[1], step[2]], step[0])(step[3])
        for one in flights:
            one.sent()

    def vm(*dims, kind=BF):
        return pltpu.VMEM(dims, kind)

    outs = [
        shape((local, width), F32),
        shape((2 * layers, block), F32),
        shape((layers, block, 3 * width), BF),
        shape((layers, block, width), BF),
        shape((layers, block, 2 * hid), BF),
        shape((layers, block, 2 * hid), BF),
        shape((layers, hid_block, width), BF),
    ]
    for unit in units:
        count, columns = counts[unit], sizes[unit[0]][1]
        outs += [
            shape((layers, 2, count, columns // 2), BF),
            shape((layers, 2, count, columns // 2), BF),
            shape((layers, count, columns // 2), BF),
            shape((layers, count, columns // 2), BF),
            shape((layers, 3, count, columns), BF),
        ]
    outs += [shape((layers, block, sizes[name][1]), BF) for name in ("g", "q")]
    scratch = [
        vm(width, 3 * half),
        vm(half, width),
        vm(width, 2 * hid),
        vm(hid, width),
        vm(both, hid),
        vm(both, 2 * hid),
        vm(both, width),
        vm(3, 2, span, group),
        vm(both, half),
        vm(local, width, kind=F32),
        vm(both, width),
        vm(both, width),
        vm(2, local, width),
        vm(2, span, group),
        vm(ctx, 3, 2, local, group),
        vm(local, width, kind=F32),
        vm(local, width),
        vm(local, width, kind=F32),
        vm(local, width, kind=F32),
        vm(ctx, 2, local, group),
        vm(ctx, 3, 2, local, group),
        vm(span, group, kind=F32),
        vm(span, group, kind=F32),
        vm(2, span, group, kind=F32),
        vm(both, 3 * half),
        vm(2, span, 128, kind=F32),
        vm(2, span, 128, kind=F32),
    ]
    scratch += [vm(chips * sizes[name][0], sizes[name][1]) for name in names]
    scratch += [vm(*sizes[name]) for name in names]
    scratch += [
        vm(2, max(hid_block, 2 * block), hid),
        vm(block, 3 * width),
        vm(8, width, kind=F32),
        vm(shards, 8, block, kind=F32),
        vm(shards, 8, block, kind=F32),
        vm(8, block, kind=F32),
        vm(ctx, 8, block, kind=F32),
        pltpu.SemaphoreType.DMA((2, 192)),
        pltpu.SemaphoreType.DMA((20,)),
        pltpu.SemaphoreType.DMA((2,)),
        pltpu.SemaphoreType.DMA((6,)),
        pltpu.SemaphoreType.DMA((2,)),
    ]
    (wq, wo, wg, wd, n1, n2, whole, mix, mid, stream, act, kept) = saved[:12]
    gain_all, cosines, sines, lens_all = saved[12:16]
    return pl.pallas_call(
        kernel,
        out_shape=outs,
        in_specs=[ANY] * 2 + [VM] * 2 + [ANY] * 14,
        out_specs=[VM] * 2 + [ANY] * (len(outs) - 2),
        scratch_shapes=scratch,
        compiler_params=pltpu.CompilerParams(
            vmem_limit_bytes=63 * MIB, collective_id=1, has_side_effects=True
        ),
        cost_estimate=pl.CostEstimate(
            flops=28 * 10**9, bytes_accessed=100 * MIB, transcendentals=0
        ),
    )(
        cotangent, tokens, lens_all, gain_all, wq, wo, wg, wd, n1, n2, whole, mix, mid, stream,
        act, kept, cosines, sines,
    )


def add_low(left, right):
    return (left.astype(F32) + right.astype(F32)).astype(BF)


def reduce_chips(blocks, chips):
    if chips != 4:
        total = blocks[0].astype(F32)
        for k in range(1, chips):
            total = total + swap(blocks[k], FSDP, 2 * k).astype(F32)
        return total.astype(BF)
    send_x, keep_x, send_y, keep_y = blocks
    got_x = swap(send_x, FSDP, 2)
    got_y = swap(send_y, FSDP, 4)
    on_x = swap(add_low(keep_x[1], got_x[1]), FSDP, 4)
    on_y = swap(add_low(keep_y[1], got_y[1]), FSDP, 2)
    first = add_low(add_low(keep_x[0], got_x[0]), on_x)
    second = add_low(add_low(keep_y[0], got_y[0]), on_y)
    return jnp.concatenate([first, second], axis=1)


def reduce_line(block):
    if lax.axis_size(CTX) != 4:
        return lax.psum(block, CTX)
    z = lax.axis_index(CTX)
    inner = (z == 1) | (z == 2)
    inward = lax.ppermute(block, CTX, [(0, 1), (3, 2)])
    pair = jnp.where(inner, add_low(block, inward), block)
    across = lax.ppermute(pair, CTX, [(1, 2), (2, 1)])
    total = add_low(pair, across)
    outward = lax.ppermute(total, CTX, [(1, 0), (2, 3)])
    return jnp.where(inner, total, outward)


def own_rows(block):
    core = lax.axis_index(FSDP) % 2
    rows = block.shape[0] // 2
    mine = lax.dynamic_slice_in_dim(block, core * rows, rows)
    theirs = swap(lax.dynamic_slice_in_dim(block, (1 - core) * rows, rows), FSDP, 1)
    low = jnp.where(core == 0, mine, theirs)
    high = jnp.where(core == 0, theirs, mine)
    return jnp.stack([low, high])


def chip_piece(mine, other):
    core = lax.axis_index(FSDP) % 2
    got = swap(other, FSDP, 1)
    return jnp.where(
        core == 0, jnp.concatenate([mine, got]), jnp.concatenate([got, mine])
    )


def document_starts(lengths, index):
    ends = []
    total = jnp.int32(0)
    for j in range(lengths.shape[0]):
        total = total + lengths[j]
        ends.append(total)
    start = jnp.zeros_like(index)
    for end in ends:
        start = jnp.where(index >= end, end, start)
    return start


def rotary(positions):
    pairs = HD // 2
    lane = jnp.arange(128, dtype=jnp.int32)
    frequency = jnp.exp(-math.log(10000.0) * jnp.arange(pairs, dtype=F32) / pairs)
    angles = positions.astype(F32)[..., None] * frequency
    cosines = jnp.tile(jnp.cos(angles), 128 // pairs)
    sines = jnp.tile(jnp.sin(angles), 128 // pairs)
    low = jnp.where(lane % HD < pairs, -sines, 0.0)
    high = jnp.where(lane % HD >= pairs, sines, 0.0)
    return [cosines, low, high]


def body(tokens, doc_lengths, cotangent, gains, w_qkv, w_out, w_gate, w_up, w_down):
    _, local, width = tokens.shape
    layers = gains.shape[0]
    shards = lax.axis_size(FSDP)
    ctx = lax.axis_size(CTX)
    chips = shards // 2
    block = width // shards
    hidden = w_gate.shape[2]
    hidden_half = hidden // 2
    hidden_block = hidden // shards
    core = lax.axis_index(FSDP) % 2
    z = lax.axis_index(CTX)
    span = local * ctx

    def pick(array, axis, which):
        return lax.dynamic_index_in_dim(array, which, axis, keepdims=False)

    if chips == 4 and ctx == 4 and layers == 2:
        saved = forward_pass(
            tokens[0], doc_lengths, gains, w_qkv, w_out, w_gate, w_up, w_down
        )
        made = backward_pass(saved, tokens[0], cotangent[0])
        grad, gain_sum, qkv_sum, out_sum, gate_sum, up_sum, down_sum = made[:7]
        sums = [s.astype(F32) for s in (qkv_sum, out_sum, gate_sum, up_sum, down_sum)]
        gain_sum = gain_sum.reshape(layers, 2, block)
        return (saved[16][None], grad[None], gain_sum, *sums)

    qkv_weights, out_weights, gu_weights, down_weights = [], [], [], []
    for layer in range(layers):
        qkv = w_qkv[layer].reshape(block, 3, chips, 2, block)
        sides = [pick(qkv, 3, which).reshape(block, -1) for which in (core, 1 - core)]
        qkv_weights.append(gather(chip_piece(*sides), chips))
        out_weights.append(gather(w_out[layer], chips))
        sides = []
        for which in (core, 1 - core):
            both = [
                pick(w[layer].reshape(block, chips, 2, hidden_block), 2, which).reshape(
                    block, hidden_half
                )
                for w in (w_gate, w_up)
            ]
            sides.append(jnp.concatenate(both, axis=1))
        gu_weights.append(gather(chip_piece(*sides), chips))
        down_weights.append(gather(w_down[layer], chips))

    all_gains = lax.all_gather(gains, FSDP, axis=2, tiled=True)
    gain_rows = [[all_gains[layer, n][None] for n in range(2)] for layer in range(layers)]

    index = jnp.arange(span, dtype=jnp.int32)
    lengths = [doc_lengths[0], swap(doc_lengths, FSDP, 1)[0]]
    starts = jnp.stack([document_starts(row, index) for row in lengths])
    row_tables = rotary(index[None] - starts)
    here_tables = [lax.dynamic_slice_in_dim(t, z * local, local, axis=1) for t in row_tables]
    head_lanes = min(128, width // 2 // ctx)
    head_tables = [t[:, :, :head_lanes] for t in row_tables]
    start_column = starts[:, :, None]
    start_row = starts[:, None, :]

    def pair(array):
        return (array, swap(array, FSDP, 1))

    stream = tokens[0]
    kept = []
    first_value = None
    (low,) = join_norm(stream, None, None, gain_rows[0][0])
    for layer in range(layers):
        normed = pair(low)
        slabs, first_value = project(
            *normed, here_tables, first_value, qkv_weights[layer], ctx, layer == layers - 1
        )
        slabs = exchange(slabs)
        mixed = exchange(attend(slabs, start_column))
        own, other, joined = mix_out(mixed, out_weights[layer])
        middle, low = join_norm(stream, own, swap(other, FSDP, 1), gain_rows[layer][1])
        normed_two = pair(low)
        active, gu_kept = gate_up(*normed_two, gu_weights[layer])
        own, other = down(active, down_weights[layer])
        after = gain_rows[min(layer + 1, layers - 1)][0]
        kept.append((stream, normed, slabs, joined, middle, normed_two, active, gu_kept))
        stream, low = join_norm(middle, own, swap(other, FSDP, 1), after)
    out_tokens = stream.astype(BF)[None]

    grad = cotangent[0]
    low = cotangent[0]
    carried = None
    gain_grads = [[None, None] for _ in range(layers)]
    done = [None] * layers
    for layer in reversed(range(layers)):
        stream, normed, slabs, joined, middle, normed_two, active, gu_kept = kept[layer]
        sent = pair(low)
        down_blocks = weight_grad([active], sent, chips)
        gu_grads, own, other = mlp_back(
            *sent, gu_kept, gu_weights[layer], down_weights[layer]
        )
        grad, low, gain_grads[layer][1] = norm_back(
            middle, own, swap(other, FSDP, 1), gain_rows[layer][1], grad
        )
        gu_blocks = weight_grad(normed_two, [gu_grads], chips)
        mixed_back = pair(low)
        grad_slabs = exchange(mix_back(*mixed_back, out_weights[layer], ctx))
        out_blocks = weight_grad([joined], mixed_back, chips)
        grad_slabs, carry_out = attend_back(slabs, grad_slabs, start_row, head_tables, carried)
        carried = carry_out
        own, other, qkv_grads = project_back(exchange(grad_slabs), qkv_weights[layer])
        qkv_blocks = weight_grad(normed, [qkv_grads], chips)
        grad, low, gain_grads[layer][0] = norm_back(
            stream, own, swap(other, FSDP, 1), gain_rows[layer][0], grad
        )
        down_sum = reduce_line(reduce_chips(down_blocks, chips)).astype(F32)
        gu_sum = own_rows(reduce_line(reduce_chips(gu_blocks, chips)))
        out_sum = reduce_line(reduce_chips(out_blocks, chips)).astype(F32)
        qkv_sum = own_rows(reduce_line(reduce_chips(qkv_blocks, chips)))
        qkv_sum = qkv_sum.reshape(2, block, 3, chips, block).transpose(1, 2, 3, 0, 4)
        qkv_sum = qkv_sum.reshape(block, 3 * width).astype(F32)
        gu_sum = gu_sum.reshape(2, block, 2, chips, hidden_block).transpose(2, 1, 3, 0, 4)
        gu_sum = gu_sum.reshape(2, block, hidden).astype(F32)
        done[layer] = (qkv_sum, out_sum, gu_sum[0], gu_sum[1], down_sum)

    gain_sum = jnp.stack([jnp.concatenate(rows) for rows in gain_grads])
    gain_sum = lax.psum_scatter(gain_sum, FSDP, scatter_dimension=2, tiled=True)
    gain_sum = lax.psum(gain_sum, CTX)
    stacked = [jnp.stack([done[layer][n] for layer in range(layers)]) for n in range(5)]
    return (out_tokens, grad[None], gain_sum, *stacked)


def solution(mesh):
    rows = P(None, FSDP, None)
    tokens = P(FSDP, CTX, None)
    gains = P(None, None, FSDP)
    return jax.shard_map(
        body,
        mesh=mesh,
        in_specs=(tokens, P(FSDP, None), tokens, gains, rows, rows, rows, rows, rows),
        out_specs=(tokens, tokens, gains, rows, rows, rows, rows, rows),
        check_vma=False,
    )
```
